128 devices in a mesh: seq: 16 (over x, z), clu: 8 (over y, core).
Axes of the slice: x: 4, y: 4, z: 4, core: 2. Of those that a mesh axis runs over, the one named last changes fastest.
Arguments:
- queries: bfloat16 [16384, 2048], P(('seq', 'clu')), may hold values from -6 to 6
- key_rows: bfloat16 [16384, 2048], P(('seq', 'clu')), may hold values from -6 to 6
- value_rows: bfloat16 [16384, 2048], P(('seq', 'clu')), may hold values from -6 to 6
- out_grad: bfloat16 [16384, 2048], P(('seq', 'clu')), may hold values from -6 to 6
- cluster_ids: int32 [16384], P(('seq', 'clu')), may hold values from 0 to 127, as said below
Outputs:
- attention_out: bfloat16 [16384, 2048], P(('seq', 'clu'))
- query_grad: bfloat16 [16384, 2048], P(('seq', 'clu'))
- key_grad: bfloat16 [16384, 2048], P(('seq', 'clu'))
- value_grad: bfloat16 [16384, 2048], P(('seq', 'clu'))
The draws below stay inside these ranges and needn't reach their ends.
Inputs may be any that keep to these rules, and one draw needn't show every extreme that they name: `cluster_ids`: each aligned block of 128 rows (the rows of one device) names any one cluster at most 4 times; in every draw one cluster is named exactly 4 times in every block, so that it holds 512 tokens.
All inputs are finite; a program needn't handle non-finite values.
Results may differ from the reference program's by a relative error of at most 0.02.
Values may be sent and summed in bfloat16 or wider, within the bound.
A program may use at most 128 MiB of HBM per device.

```python
import math
import jax
import jax.numpy as jnp
from jax import lax

H = 16
DH = 128
TOK_DEV = 128
TOKENS = 16384
CLUSTERS = 128
MOST = 4
CAP = 512


def route_ids(key):
    key = jax.random.fold_in(key, 101)
    heavy_id = jax.random.randint(jax.random.fold_in(key, 1), (), 0, CLUSTERS).astype(jnp.int32)
    light_count = CLUSTERS - 1
    light_rows = TOK_DEV - MOST
    block_total = TOKENS // TOK_DEV

    def one_block(block_index):
        block_key = jax.random.fold_in(key, block_index + 7)
        increments = jax.random.randint(jax.random.fold_in(block_key, 1), (light_count,), 1, 4).astype(jnp.int32)
        running = jnp.cumsum(increments)
        boundaries = light_rows * running // running[-1]
        row_index = jnp.arange(TOK_DEV, dtype=jnp.int32)
        light_row = row_index - MOST
        light_pick = jnp.sum((boundaries[None, :] <= light_row[:, None]).astype(jnp.int32), axis=1)
        light_pick = light_pick + (light_pick >= heavy_id).astype(jnp.int32)
        chosen = jnp.where(row_index < MOST, heavy_id, light_pick)
        shuffle = jax.random.permutation(jax.random.fold_in(block_key, 2), TOK_DEV)
        return chosen[shuffle]
    blocks = jax.vmap(one_block)(jnp.arange(block_total, dtype=jnp.int32))
    return blocks.reshape(TOKENS).astype(jnp.int32)


def draw_cluster_ids(key, part):
    chosen = route_ids(key)
    return chosen


def draw_queries(key, part):
    key = jax.random.fold_in(key, 3)
    drawn = jnp.clip(1.2 * jax.random.normal(key, (TOKENS, H * DH), jnp.float32), -6.0, 6.0)
    return drawn.astype(jnp.bfloat16)


def draw_key_rows(key, part):
    key = jax.random.fold_in(key, 4)
    drawn = jnp.clip(1.2 * jax.random.normal(key, (TOKENS, H * DH), jnp.float32), -6.0, 6.0)
    return drawn.astype(jnp.bfloat16)


def steps_of(stream_key, shape, pieces, low, largest):
    def one(axis_at, shards_of):
        draws = jax.random.uniform(jax.random.fold_in(jax.random.fold_in(stream_key, 6), axis_at), (shards_of,), jnp.float32, low / len(pieces), largest / len(pieces))
        return jnp.repeat(jnp.exp(draws), shape[axis_at] // shards_of).reshape((-1,) + (1,) * (len(shape) - axis_at - 1))

    gain = one(*pieces[0])
    for cut in pieces[1:]:
        gain = gain * one(*cut)
    return gain


def normal_values(own_key, dims, width, limit, split=(), kind=jnp.bfloat16):
    entries = jax.random.normal(own_key, dims, jnp.float32) * width
    if len(split) > 0:
        entries = steps_of(own_key, dims, split, -0.22, 0.18) * entries
    return jnp.clip(entries, min=-limit, max=limit).astype(kind)


def setup_inputs(seed: int = 0) -> dict:
    keys = jax.random.split(jax.random.key(seed), 6)
    return {
        "queries": draw_queries(jax.random.fold_in(keys[5], 71), 0),
        "key_rows": draw_key_rows(jax.random.fold_in(keys[5], 71), 0),
        "value_rows": normal_values(keys[2], (TOKENS, H * DH), 1.0, 6.0, ((0, 128),)),
        "out_grad": normal_values(keys[3], (TOKENS, H * DH), 1.0, 6.0, ((0, 128),)),
        "cluster_ids": draw_cluster_ids(jax.random.fold_in(keys[5], 71), 0),
    }


tile_rows = 128
masked = -1e+30

def front_pad(array, sorted_order):
    arranged = jnp.take(array, sorted_order, axis=0)
    padding = jnp.zeros((CAP,) + array.shape[1:], array.dtype)
    return jnp.concatenate([padding, arranged], axis=0)

def reference(queries, key_rows, value_rows, out_grad, cluster_ids):
    token_count = queries.shape[0]
    columns = queries.shape[1]
    inv_root = 1.0 / math.sqrt(DH)
    window_len = CAP + tile_rows
    tile_count = token_count // tile_rows
    sorted_order = jnp.argsort(cluster_ids, stable=True).astype(jnp.int32)
    query_pad = front_pad(queries, sorted_order)
    key_pad = front_pad(key_rows, sorted_order)
    value_pad = front_pad(value_rows, sorted_order)
    ident_pad = jnp.concatenate([jnp.full((CAP,), -1, jnp.int32), jnp.take(cluster_ids, sorted_order).astype(jnp.int32)])
    offsets = jnp.arange(tile_rows, dtype=jnp.int32)
    window_offsets = jnp.arange(window_len, dtype=jnp.int32)

    def tile_parts(tile_index):
        first_row = (tile_index * tile_rows).astype(jnp.int32)
        query_tile = lax.dynamic_slice_in_dim(query_pad, first_row + CAP, tile_rows, 0).astype(jnp.float32).reshape(tile_rows, H, DH)
        key_window = lax.dynamic_slice_in_dim(key_pad, first_row, window_len, 0).astype(jnp.float32).reshape(window_len, H, DH)
        value_window = lax.dynamic_slice_in_dim(value_pad, first_row, window_len, 0).astype(jnp.float32).reshape(window_len, H, DH)
        query_ident = lax.dynamic_slice_in_dim(ident_pad, first_row + CAP, tile_rows, 0)
        key_ident = lax.dynamic_slice_in_dim(ident_pad, first_row, window_len, 0)
        allowed = (query_ident[:, None] == key_ident[None, :]) & (window_offsets[None, :] <= offsets[:, None] + CAP)
        scores = jnp.einsum('qhd,khd->hqk', query_tile, key_window) * inv_root
        scores = jnp.where(allowed[None], scores, masked)
        row_max = lax.optimization_barrier(jnp.max(scores, axis=2, keepdims=True))
        weights = jnp.exp(scores - row_max)
        row_sum = lax.optimization_barrier(jnp.sum(weights, axis=2, keepdims=True))
        weights_low = lax.optimization_barrier((weights / row_sum).astype(jnp.bfloat16))
        return (first_row, query_tile, key_window, value_window, weights_low.astype(jnp.float32))

    def forward_tile(tile_index):
        first_row, query_tile, key_window, value_window, prob_wide = tile_parts(tile_index)
        mixed_tile = jnp.einsum('hqk,khd->qhd', prob_wide, value_window)
        return mixed_tile.reshape(tile_rows, columns).astype(jnp.bfloat16)
    tile_ids = jnp.arange(tile_count, dtype=jnp.int32)
    sorted_out = lax.map(forward_tile, tile_ids).reshape(token_count, columns)
    attention_out = jnp.zeros_like(queries).at[sorted_order].set(sorted_out)
    delta_rows = lax.optimization_barrier(jnp.sum((out_grad.astype(jnp.float32) * attention_out.astype(jnp.float32)).reshape(token_count, H, DH), axis=2))
    delta_pad = front_pad(delta_rows, sorted_order)
    grad_pad = front_pad(out_grad, sorted_order)

    def backward_tile(carry, tile_index):
        key_acc, value_acc = carry
        first_row, query_tile, key_window, value_window, prob_wide = tile_parts(tile_index)
        grad_tile = lax.dynamic_slice_in_dim(grad_pad, first_row + CAP, tile_rows, 0).astype(jnp.float32).reshape(tile_rows, H, DH)
        delta_tile = lax.dynamic_slice_in_dim(delta_pad, first_row + CAP, tile_rows, 0)
        prob_grad = jnp.einsum('qhd,khd->hqk', grad_tile, value_window)
        score_low = lax.optimization_barrier((prob_wide * (prob_grad - jnp.transpose(delta_tile)[:, :, None])).astype(jnp.bfloat16))
        score_grad = score_low.astype(jnp.float32)
        query_part = (jnp.einsum('hqk,khd->qhd', score_grad, key_window) * inv_root).reshape(tile_rows, columns).astype(jnp.bfloat16)
        key_part = (jnp.einsum('hqk,qhd->khd', score_grad, query_tile) * inv_root).reshape(window_len, columns)
        value_part = jnp.einsum('hqk,qhd->khd', prob_wide, grad_tile).reshape(window_len, columns)
        key_acc = lax.dynamic_update_slice_in_dim(key_acc, lax.dynamic_slice_in_dim(key_acc, first_row, window_len, 0) + key_part, first_row, 0)
        value_acc = lax.dynamic_update_slice_in_dim(value_acc, lax.dynamic_slice_in_dim(value_acc, first_row, window_len, 0) + value_part, first_row, 0)
        return ((key_acc, value_acc), query_part)
    zero_acc = jnp.zeros((CAP + token_count, columns), jnp.float32)
    (key_acc, value_acc), query_tiles = lax.scan(backward_tile, (zero_acc, zero_acc), tile_ids)
    query_grad = jnp.zeros_like(queries).at[sorted_order].set(query_tiles.reshape(token_count, columns))
    key_grad = jnp.zeros_like(queries).at[sorted_order].set(key_acc[CAP:].astype(jnp.bfloat16))
    value_grad = jnp.zeros_like(queries).at[sorted_order].set(value_acc[CAP:].astype(jnp.bfloat16))
    return (attention_out, query_grad, key_grad, value_grad)
```

```python
import math

import jax
import jax.numpy as jnp
from jax import lax
from jax.experimental import pallas as pl
from jax.experimental.pallas import tpu as pltpu
from jax.sharding import PartitionSpec as P

DH = 128
TOK = 128
OVC = 96
SET = 16
FAR = 1e9
MESH = pl.DeviceIdType.MESH


masked = -1e30


def contract_last(left, right):
    return lax.dot_general(
        left, right, (((1,), (1,)), ((), ())), preferred_element_type=jnp.float32
    )


def contract_first(left, right):
    return lax.dot_general(
        left, right, (((0,), (0,)), ((), ())), preferred_element_type=jnp.float32
    )


def softmax_rows(query_head, key_head, allowed, inv_root):
    scores = contract_last(query_head, key_head) * inv_root
    scores = jnp.where(allowed, scores, masked)
    row_max = jnp.max(scores, axis=1, keepdims=True)
    weights = jnp.exp(scores - row_max)
    row_sum = jnp.sum(weights, axis=1, keepdims=True)
    return (weights / row_sum).astype(jnp.bfloat16)


def head_slice(array, head_index):
    return lax.dynamic_slice_in_dim(array, head_index * DH, DH, 1)


def full_capacity(queries, key_rows, value_rows, out_grad, cluster_ids):
    seq_count = lax.axis_size("seq")
    clu_count = lax.axis_size("clu")
    devices = seq_count * clu_count
    tok_rows = queries.shape[0]
    columns = queries.shape[1]
    head_count = columns // DH
    most_rows = 4 * tok_rows // devices
    capacity = most_rows * devices
    inv_root = 1.0 / math.sqrt(DH)
    owners = jnp.arange(devices, dtype=jnp.int32)
    member = (cluster_ids[:, None] == owners[None, :]).astype(jnp.int32)
    running = jnp.cumsum(member, axis=0) - 1
    slot_rank = jnp.sum(member * running, axis=1)
    sent_counts = jnp.sum(member, axis=0).reshape(devices, 1)
    slot_index = cluster_ids * most_rows + slot_rank
    stacked = jnp.concatenate([queries, key_rows, value_rows], axis=1)
    width_in = stacked.shape[1]
    packed = jnp.zeros((devices * most_rows, width_in), jnp.bfloat16).at[slot_index].set(stacked)
    packed = packed.reshape(devices, most_rows, width_in)
    got_rows, got_counts = (
        lax.all_to_all(packed, ("seq", "clu"), split_axis=0, concat_axis=0, tiled=True),
        lax.all_to_all(sent_counts, ("seq", "clu"), split_axis=0, concat_axis=0, tiled=True),
    )
    got_counts = got_counts.reshape(devices)
    starts = jnp.cumsum(got_counts) - got_counts
    live_total = jnp.sum(got_counts)
    within = jnp.arange(most_rows, dtype=jnp.int32)
    target = jnp.where(
        within[None, :] < got_counts[:, None], starts[:, None] + within[None, :], capacity
    )
    target = target.reshape(devices * most_rows)
    gathered = (
        jnp.zeros((capacity, width_in), jnp.bfloat16)
        .at[target]
        .set(got_rows.reshape(devices * most_rows, width_in), mode="drop")
    )
    query_block = gathered[:, :columns]
    key_block = gathered[:, columns : 2 * columns]
    value_block = gathered[:, 2 * columns : 3 * columns]
    positions = jnp.arange(capacity, dtype=jnp.int32)
    allowed = (positions[None, :] <= positions[:, None]) & (positions[None, :] < live_total)

    def forward_head(head_index, mixed_rows):
        weights_low = softmax_rows(
            head_slice(query_block, head_index),
            head_slice(key_block, head_index),
            allowed,
            inv_root,
        )
        out_head = jnp.dot(
            weights_low, head_slice(value_block, head_index), preferred_element_type=jnp.float32
        ).astype(jnp.bfloat16)
        return lax.dynamic_update_slice_in_dim(mixed_rows, out_head, head_index * DH, 1)

    mixed_rows = lax.fori_loop(
        0, head_count, forward_head, jnp.zeros((capacity, columns), jnp.bfloat16)
    )
    back_index = jnp.minimum(target, capacity - 1)
    outgoing = jnp.take(mixed_rows, back_index, axis=0).reshape(devices, most_rows, columns)
    grad_packed = (
        jnp.zeros((devices * most_rows, columns), jnp.bfloat16).at[slot_index].set(out_grad)
    )
    grad_packed = grad_packed.reshape(devices, most_rows, columns)
    returned = lax.all_to_all(outgoing, ("seq", "clu"), split_axis=0, concat_axis=0, tiled=True)
    got_grad = lax.all_to_all(grad_packed, ("seq", "clu"), split_axis=0, concat_axis=0, tiled=True)
    attention_out = jnp.take(returned.reshape(devices * most_rows, columns), slot_index, axis=0)
    grad_block = (
        jnp.zeros((capacity, columns), jnp.bfloat16)
        .at[target]
        .set(got_grad.reshape(devices * most_rows, columns), mode="drop")
    )
    delta_rows = jnp.sum(
        (grad_block.astype(jnp.float32) * mixed_rows.astype(jnp.float32)).reshape(
            capacity, head_count, DH
        ),
        axis=2,
    )

    def backward_head(head_index, grad_rows):
        query_head = head_slice(query_block, head_index)
        key_head = head_slice(key_block, head_index)
        value_head = head_slice(value_block, head_index)
        grad_head = head_slice(grad_block, head_index)
        weights_low = softmax_rows(query_head, key_head, allowed, inv_root)
        prob_grad = contract_last(grad_head, value_head)
        delta_head = lax.dynamic_slice_in_dim(delta_rows, head_index, 1, 1)
        score_grad = (weights_low.astype(jnp.float32) * (prob_grad - delta_head)).astype(
            jnp.bfloat16
        )
        query_part = (
            jnp.dot(score_grad, key_head, preferred_element_type=jnp.float32) * inv_root
        ).astype(jnp.bfloat16)
        key_part = (contract_first(score_grad, query_head) * inv_root).astype(jnp.bfloat16)
        value_part = contract_first(weights_low, grad_head).astype(jnp.bfloat16)
        grad_rows = lax.dynamic_update_slice_in_dim(grad_rows, query_part, head_index * DH, 1)
        grad_rows = lax.dynamic_update_slice_in_dim(
            grad_rows, key_part, columns + head_index * DH, 1
        )
        return lax.dynamic_update_slice_in_dim(
            grad_rows, value_part, 2 * columns + head_index * DH, 1
        )

    grad_rows = lax.fori_loop(
        0, head_count, backward_head, jnp.zeros((capacity, 3 * columns), jnp.bfloat16)
    )
    outgoing_grads = jnp.take(grad_rows, back_index, axis=0).reshape(
        devices, most_rows, 3 * columns
    )
    returned_grads = lax.all_to_all(
        outgoing_grads, ("seq", "clu"), split_axis=0, concat_axis=0, tiled=True
    )
    picked = jnp.take(returned_grads.reshape(devices * most_rows, 3 * columns), slot_index, axis=0)
    return (
        attention_out,
        picked[:, :columns],
        picked[:, columns : 2 * columns],
        picked[:, 2 * columns :],
    )


def bf16_dot(left, right):
    return jnp.dot(left, right, preferred_element_type=jnp.float32)


def flip_perm():
    row = lax.broadcasted_iota(jnp.int32, (SET * 16, SET * 16), 0)
    col = lax.broadcasted_iota(jnp.int32, (SET * 16, SET * 16), 1)
    swapped = (col % 16) * 16 + col // 16
    return (row == swapped).astype(jnp.float32).astype(jnp.bfloat16)


def attend(q, k, v, g, allowed, inv_root):
    scores = contract_last(q, k) * inv_root
    scores = jnp.where(allowed, scores, masked)
    row_max = jnp.max(scores, axis=1, keepdims=True)
    weights = jnp.exp(scores - row_max)
    row_sum = jnp.sum(weights, axis=1, keepdims=True)
    prob = (weights * (1.0 / row_sum)).astype(jnp.bfloat16)
    out = bf16_dot(prob, v).astype(jnp.bfloat16)
    delta = jnp.sum(
        g.astype(jnp.float32) * out.astype(jnp.float32), axis=1, keepdims=True
    )
    prob_grad = contract_last(g, v)
    score_grad = (prob.astype(jnp.float32) * (prob_grad - delta)).astype(jnp.bfloat16)
    dq = (bf16_dot(score_grad, k) * inv_root).astype(jnp.bfloat16)
    dk = contract_first(score_grad, q) * inv_root
    dv = contract_first(prob, g)
    return out, dq, dk, dv


def fast_kernel(
    ids_ref, q_ref, k_ref, v_ref, g_ref,
    out_ref, dq_ref, dk_ref, dv_ref, flag_ref,
    cnt_send, cnt_recv, pack_mat, unpack_mat, send, recv, table, slots_t, group_t,
    over, over_pos, onehot, over_res, result, back,
    hsend, hrecv, htable, hacc, hresult, hback,
    send_sem, recv_sem, back_send_sem, back_sem, cnt_send_sem, cnt_sem,
    hsend_sem, hrecv_sem, hback_send_sem, hback_sem,
):
    seq_at = lax.axis_index("seq")
    clu_at = lax.axis_index("clu")
    groups = lax.axis_size("clu")
    heads = lax.axis_size("seq")
    devices = heads * groups
    me = seq_at * groups + clu_at
    inv_root = 1.0 / math.sqrt(DH)
    is_heavy_owner = lax.rem(seq_at, groups) == clu_at

    def coords(device):
        return (device // groups, lax.rem(device, groups))

    barrier = pltpu.get_barrier_semaphore()

    def greet(step, carry):
        pl.semaphore_signal(
            barrier, inc=1, device_id=coords(lax.rem(me + step, devices)), device_id_type=MESH
        )
        return carry

    lax.fori_loop(1, devices, greet, 0)

    sub = lax.broadcasted_iota(jnp.int32, (TOK, TOK), 0)
    lane = lax.broadcasted_iota(jnp.int32, (TOK, TOK), 1)
    sub_f = sub.astype(jnp.float32)
    lane_f = lane.astype(jnp.float32)
    ids_l = jnp.broadcast_to(ids_ref[...].astype(jnp.float32), (TOK, TOK))
    ids_s = ids_l.T
    one = jnp.ones((TOK, TOK), jnp.float32)
    zero = jnp.zeros((TOK, TOK), jnp.float32)
    same = ids_l == ids_s
    rank_l = jnp.sum(jnp.where(same & (sub < lane), one, zero), axis=0, keepdims=True)
    rank_s = jnp.sum(jnp.where(same & (lane < sub), one, zero), axis=1, keepdims=True)
    count_l = jnp.sum(jnp.where(same, one, zero), axis=0, keepdims=True)
    counts = jnp.sum(jnp.where(ids_s == lane_f, one, zero), axis=0, keepdims=True)
    cnt_send[...] = jnp.broadcast_to(counts, cnt_send.shape)
    ids_row = ids_l[0:1, :]
    heavy = jnp.min(jnp.where(count_l == 4.0, ids_row, 999.0), axis=1, keepdims=True)
    group_l = jnp.floor(ids_l * (1.0 / 16.0))
    group_s = jnp.floor(ids_s * (1.0 / 16.0))
    before = (group_l == group_s) & (ids_s != heavy) & (rank_s >= 1.0)
    before = before & ((ids_s < ids_l) | (same & (sub < lane)))
    over_at = jnp.sum(jnp.where(before, one, zero), axis=0, keepdims=True)
    light_l = ids_l != heavy
    lower = (sub % 16) < 8
    slot = (sub % 8).astype(jnp.float32)
    slot_group = (sub // 16).astype(jnp.float32)
    picks = []
    for unit in range(2):
        cluster = slot_group * 16.0 + unit * 8.0 + slot
        picks.append((ids_l == cluster) & (rank_l == 0.0) & light_l)
    picks.append((group_l == slot_group) & light_l & (rank_l >= 1.0) & (over_at == slot))
    for unit in range(3):
        for half in range(2):
            chosen = picks[unit] & (lower if half == 0 else ~lower)
            matrix = jnp.where(chosen, one, zero)
            rows = pl.ds(unit * TOK, TOK)
            turned = matrix.T.astype(jnp.bfloat16)
            matrix = matrix.astype(jnp.bfloat16)
            for pair in range(2):
                pack_mat[pair, rows, pl.ds(half * TOK, TOK)] = matrix
                unpack_mat[2 * pair + half, :, rows] = turned
    for array in range(4):
        chosen = (ids_l == heavy) & (rank_l == (sub % 4).astype(jnp.float32))
        chosen = chosen & (sub // 4 == array) & (sub < 16)
        matrix = jnp.where(chosen, one, zero)
        unpack_mat[array, :, pl.ds(3 * TOK, TOK)] = matrix.T.astype(jnp.bfloat16)
        pack_mat[array // 2, pl.ds(3 * TOK, 16), pl.ds((array % 2) * TOK, TOK)] = matrix[
            0:16, :
        ].astype(jnp.bfloat16)

    pl.semaphore_wait(barrier, devices - 1)

    def send_counts(step, carry):
        peer = lax.rem(me + step, devices)
        pltpu.make_async_remote_copy(
            src_ref=cnt_send,
            dst_ref=cnt_recv.at[me],
            send_sem=cnt_send_sem,
            recv_sem=cnt_sem,
            device_id=coords(peer),
            device_id_type=MESH,
        ).start()
        return carry

    lax.fori_loop(1, devices, send_counts, 0)
    pltpu.make_async_copy(cnt_send, cnt_recv.at[me], cnt_sem).start()

    def pack_head(head, carry):
        cols = pl.ds(pl.multiple_of(head * DH, DH), DH)
        extra = None
        for pair, (left, right) in enumerate(((q_ref, k_ref), (v_ref, g_ref))):
            rows = jnp.concatenate([left[:, cols], right[:, cols]], axis=0)
            packed = bf16_dot(pack_mat[pair], rows)
            for unit in range(3):
                piece = packed[unit * TOK : (unit + 1) * TOK].astype(jnp.bfloat16)
                send[pl.ds(head * groups, groups), 2 * unit + pair] = piece.reshape(
                    groups, 16, DH
                )
            part = packed[3 * TOK : 3 * TOK + 16]
            extra = part if extra is None else extra + part
        hsend[head] = extra.astype(jnp.bfloat16)
        return carry

    lax.fori_loop(0, heads, pack_head, 0)

    def send_rows(step, carry):
        peer = lax.rem(me + step, devices)
        pltpu.make_async_remote_copy(
            src_ref=send.at[peer],
            dst_ref=recv.at[me],
            send_sem=send_sem,
            recv_sem=recv_sem,
            device_id=coords(peer),
            device_id_type=MESH,
        ).start()
        return carry

    lax.fori_loop(1, devices, send_rows, 0)
    pltpu.make_async_copy(send.at[me], recv.at[me], recv_sem).start()

    def send_heavy(head, carry):
        peer = head * groups + lax.rem(head, groups)

        @pl.when(peer != me)
        def _():
            pltpu.make_async_remote_copy(
                src_ref=hsend.at[head],
                dst_ref=hrecv.at[me],
                send_sem=hsend_sem,
                recv_sem=hrecv_sem,
                device_id=coords(peer),
                device_id_type=MESH,
            ).start()

        @pl.when(peer == me)
        def _():
            pltpu.make_async_copy(hsend.at[head], hrecv.at[me], hrecv_sem).start()

        return carry

    lax.fori_loop(0, heads, send_heavy, 0)

    pltpu.make_async_copy(cnt_recv, cnt_recv, cnt_sem).wait()
    seen = cnt_recv[...].reshape(TOK, TOK)
    full = jnp.where(seen == 4.0, lane_f, 999.0)
    heavies = jnp.min(full, axis=1, keepdims=True)
    heavy_all = jnp.min(heavies, axis=0, keepdims=True)
    light = lane_f != heavy_all
    more = jnp.where(light, jnp.maximum(seen - 1.0, 0.0), 0.0)
    more_low = more.astype(jnp.bfloat16)
    in_group = jnp.where(sub // 16 == lane, one, zero).astype(jnp.bfloat16)
    per_group = bf16_dot(more_low, in_group)
    bad = jnp.where(per_group > 8.0, one, zero)
    bad = jnp.maximum(bad, jnp.where(heavies != heavy_all, one, zero))
    per_cluster = jnp.sum(more, axis=0, keepdims=True)
    bad = jnp.maximum(bad, jnp.where(per_cluster > OVC, one, zero))
    worst = jnp.max(jnp.max(bad, axis=0, keepdims=True), axis=1, keepdims=True)
    flag_ref[...] = jnp.broadcast_to(worst, flag_ref.shape)

    group_t[0] = more.T
    group_t[1] = jnp.where((seen > 0.0) & light, one, zero).T
    mine = pl.ds(pl.multiple_of(clu_at * 16, 16), 16)
    more_g = group_t[0, mine, :]
    more_g_low = more_g.astype(jnp.bfloat16)
    sub16 = lax.broadcasted_iota(jnp.int32, (16, 16), 0)
    lane16 = lax.broadcasted_iota(jnp.int32, (16, 16), 1)
    earlier = jnp.where(lane16 < sub16, 1.0, 0.0).astype(jnp.bfloat16)
    offset = bf16_dot(earlier, more_g_low)
    ahead = jnp.where(sub < lane, one, zero).astype(jnp.bfloat16)
    start = bf16_dot(more_g_low, ahead)
    at_cluster = lax.broadcasted_iota(jnp.int32, (16, TOK), 0).astype(jnp.float32)
    rows = []
    for s in range(8):
        held = (offset <= float(s)) & (offset + more_g > float(s))
        index = at_cluster * float(OVC) + start + (float(s) - offset) + 1.0
        rows.append(jnp.sum(jnp.where(held, index, 0.0), axis=0, keepdims=True) - 1.0)
    slot_row = jnp.concatenate(rows, axis=0)
    slots_t[...] = jnp.concatenate(
        [slot_row, jnp.full((TOK - 8, TOK), -1.0, jnp.float32)], axis=0
    ).T

    perm = flip_perm()

    def arrange(source, target, units, first):
        def one_set(at, carry):
            blocks = pl.ds(pl.multiple_of(at * SET, SET), SET)
            rows = jnp.concatenate(
                [source(blocks, unit).reshape(SET * 16, DH) for unit in range(units)], axis=1
            )
            turned = bf16_dot(perm, rows).astype(jnp.bfloat16)
            for unit in range(units):
                target(
                    blocks, unit, turned[:, unit * DH : (unit + 1) * DH].reshape(16, SET, DH)
                )
            return carry

        lax.fori_loop(0, devices // SET, one_set, 0)

    def put_table(blocks, unit, value):
        table[unit, :, blocks, :] = value

    pltpu.make_async_copy(recv, recv, recv_sem).wait()
    arrange(lambda blocks, unit: recv[blocks, unit], put_table, 6, 0)

    block_col = jnp.concatenate([sub_f] * 8, axis=0).astype(jnp.bfloat16)
    slot_col = jnp.concatenate([one * float(s + 1) for s in range(8)], axis=0).astype(
        jnp.bfloat16
    )
    loose = jnp.concatenate(
        [
            table[4 + array // 2, (array % 2) * 8 : (array % 2) * 8 + 8].reshape(8 * TOK, DH)
            for array in range(4)
        ]
        + [block_col, slot_col],
        axis=1,
    )
    chunk = 4

    def gather_chunk(at, carry):
        want = (
            lax.broadcasted_iota(jnp.int32, (chunk * OVC, TOK), 0) + at * (chunk * OVC)
        ).astype(jnp.float32)
        pick = jnp.concatenate(
            [jnp.where(slot_row[s : s + 1, :] == want, 1.0, 0.0) for s in range(8)], axis=1
        ).astype(jnp.bfloat16)
        found = bf16_dot(pick, loose)
        for c in range(chunk):
            part = found[c * OVC : (c + 1) * OVC]
            for array in range(4):
                over[array, at * chunk + c] = part[:, array * DH : (array + 1) * DH].astype(
                    jnp.bfloat16
                )
            slot_part = part[:, 5 * DH : 6 * DH]
            where = part[:, 4 * DH : 5 * DH] * 16.0 + slot_part
            over_pos[at * chunk + c] = jnp.where(slot_part > 0.0, where, FAR)
        return carry

    lax.fori_loop(0, 16 // chunk, gather_chunk, 0)

    first_pos = sub_f * 16.0
    first_row = lax.broadcasted_iota(jnp.int32, (1, TOK), 1).astype(jnp.float32) * 16.0
    pad_rows = jnp.zeros((TOK - OVC, DH), jnp.bfloat16)

    def one_cluster(c, carry):
        u2 = (c // 8) * 2
        j = lax.rem(c, 8)
        firsts = [table[u2 + a // 2, (a % 2) * 8 + j] for a in range(4)]
        others = [over[a, c] for a in range(4)]
        q, k, v, g = [jnp.concatenate([f, o], axis=0) for f, o in zip(firsts, others)]
        k = jnp.concatenate([k, pad_rows], axis=0)
        v = jnp.concatenate([v, pad_rows], axis=0)
        pos = over_pos[c]
        pos_q = jnp.concatenate([first_pos, pos], axis=0)
        pos_row = jnp.concatenate([pos, jnp.full((TOK - OVC, TOK), FAR, jnp.float32)], axis=0)
        pos_row = pos_row.T[0:1, :]
        valid = group_t[1, pl.ds(clu_at * 16 + c, 1), :]
        key_first = jnp.where(valid > 0.0, first_row, FAR)
        allowed = jnp.concatenate([key_first <= pos_q, pos_row <= pos_q], axis=1)
        out, dq, dk, dv = attend(q, k, v, g, allowed, inv_root)
        results = [out, dq, dk.astype(jnp.bfloat16), dv.astype(jnp.bfloat16)]
        for a in range(4):
            table[u2 + a // 2, (a % 2) * 8 + j] = results[a][:TOK]
            over_res[pl.ds(pl.multiple_of(c * OVC, 32), OVC), pl.ds(a * DH, DH)] = results[a][
                TOK : TOK + OVC
            ]
        return carry

    lax.fori_loop(0, 16, one_cluster, 0)

    def spread_slot(s, carry):
        pick_s = jnp.max(
            jnp.where(lane == s, slots_t[...], -1.0), axis=1, keepdims=True
        )
        want = lax.broadcasted_iota(jnp.int32, (TOK, 16 * OVC), 1).astype(jnp.float32)
        onehot[pl.ds(pl.multiple_of(s * TOK, TOK), TOK), :] = jnp.where(
            pick_s == want, 1.0, 0.0
        ).astype(jnp.bfloat16)
        return carry

    lax.fori_loop(0, 8, spread_slot, 0)

    def spread_chunk(at, carry):
        found = bf16_dot(
            onehot[pl.ds(pl.multiple_of(at * 256, 256), 256), :], over_res[...]
        ).astype(jnp.bfloat16)
        for array in range(4):
            table[4 + array // 2, pl.ds((array % 2) * 8 + at * 2, 2)] = found[
                :, array * DH : (array + 1) * DH
            ].reshape(2, TOK, DH)
        return carry

    lax.fori_loop(0, 4, spread_chunk, 0)

    def put_result(blocks, unit, value):
        result[blocks, unit] = value

    arrange(lambda blocks, unit: table[unit, :, blocks, :], put_result, 6, 0)

    def send_back(step, carry):
        peer = lax.rem(me + step, devices)
        pltpu.make_async_remote_copy(
            src_ref=result.at[peer],
            dst_ref=back.at[me],
            send_sem=back_send_sem,
            recv_sem=back_sem,
            device_id=coords(peer),
            device_id_type=MESH,
        ).start()
        return carry

    lax.fori_loop(1, devices, send_back, 0)
    pltpu.make_async_copy(result.at[me], back.at[me], back_sem).start()

    @pl.when(is_heavy_owner)
    def _():
        pltpu.make_async_copy(hrecv, hrecv, hrecv_sem).wait()

        def put_heavy(blocks, unit, value):
            htable[:, blocks, :] = value

        arrange(lambda blocks, unit: hrecv[blocks], put_heavy, 1, 0)
        q_h, k_h, v_h, g_h = [
            htable[4 * a : 4 * a + 4].reshape(4 * TOK, DH) for a in range(4)
        ]
        hacc[...] = jnp.zeros_like(hacc)
        key_lane = lax.broadcasted_iota(jnp.int32, (TOK, 4 * TOK), 1)
        key_pos = lax.rem(key_lane, TOK) * 4 + key_lane // TOK
        query_pos = lax.broadcasted_iota(jnp.int32, (TOK, 4 * TOK), 0) * 4

        def heavy_tile(s, carry):
            allowed = key_pos <= query_pos + s
            out, dq, dk, dv = attend(
                htable[s], k_h, v_h, htable[12 + s], allowed, inv_root
            )
            hacc[2, pl.ds(pl.multiple_of(s * TOK, TOK), TOK)] = out.astype(jnp.float32)
            hacc[3, pl.ds(pl.multiple_of(s * TOK, TOK), TOK)] = dq.astype(jnp.float32)
            hacc[0] += dk
            hacc[1] += dv
            return carry

        lax.fori_loop(0, 4, heavy_tile, 0)
        for array, at in enumerate((2, 3, 0, 1)):
            htable[4 * array : 4 * array + 4] = (
                hacc[at].astype(jnp.bfloat16).reshape(4, TOK, DH)
            )

        def put_hresult(blocks, unit, value):
            hresult[blocks] = value

        arrange(lambda blocks, unit: htable[:, blocks, :], put_hresult, 1, 0)

        def send_hback(step, carry):
            peer = lax.rem(me + step, devices)
            pltpu.make_async_remote_copy(
                src_ref=hresult.at[peer],
                dst_ref=hback.at[seq_at],
                send_sem=hback_send_sem,
                recv_sem=hback_sem,
                device_id=coords(peer),
                device_id_type=MESH,
            ).start()
            return carry

        lax.fori_loop(1, devices, send_hback, 0)
        pltpu.make_async_copy(hresult.at[me], hback.at[seq_at], hback_sem).start()

    pltpu.make_async_copy(back, back, back_sem).wait()
    pltpu.make_async_copy(hback, hback, hback_sem).wait()

    def unpack_head(head, carry):
        cols = pl.ds(pl.multiple_of(head * DH, DH), DH)
        heavy_rows = jnp.concatenate(
            [hback[head], jnp.zeros((TOK - 16, DH), jnp.bfloat16)], axis=0
        )
        for pair, refs in enumerate(((out_ref, dq_ref), (dk_ref, dv_ref))):
            rows = jnp.concatenate(
                [
                    back[pl.ds(head * groups, groups), 2 * unit + pair].reshape(TOK, DH)
                    for unit in range(3)
                ]
                + [heavy_rows],
                axis=0,
            )
            for half in range(2):
                refs[half][:, cols] = bf16_dot(unpack_mat[2 * pair + half], rows).astype(
                    jnp.bfloat16
                )
        return carry

    lax.fori_loop(0, heads, unpack_head, 0)

    def drain(ref, sem):
        pltpu.make_async_copy(ref, ref, sem).wait()

    others = pl.ds(0, devices - 1)
    drain(cnt_recv.at[others], cnt_send_sem)
    drain(send.at[others], send_sem)
    drain(result.at[others], back_send_sem)

    @pl.when(is_heavy_owner)
    def _():
        drain(hsend.at[pl.ds(0, heads - 1)], hsend_sem)
        drain(hresult.at[others], hback_send_sem)

    @pl.when(jnp.logical_not(is_heavy_owner))
    def _():
        drain(hsend, hsend_sem)


def fast_path(queries, key_rows, value_rows, out_grad, cluster_ids):
    tok_rows, columns = queries.shape
    heads = columns // DH
    devices = lax.axis_size("seq") * lax.axis_size("clu")
    low = jnp.bfloat16
    wide = jnp.float32
    rows = jax.ShapeDtypeStruct((tok_rows, columns), low)
    vmem = pl.BlockSpec(memory_space=pltpu.VMEM)
    return pl.pallas_call(
        fast_kernel,
        out_shape=[rows] * 4 + [jax.ShapeDtypeStruct((8, TOK), wide)],
        in_specs=[vmem] * 5,
        out_specs=[vmem] * 5,
        scratch_shapes=[
            pltpu.VMEM((1, TOK), wide),
            pltpu.VMEM((devices, 1, TOK), wide),
            pltpu.VMEM((2, 3 * TOK + 16, 2 * TOK), low),
            pltpu.VMEM((4, TOK, 4 * TOK), low),
            pltpu.VMEM((devices, 6, 16, DH), low),
            pltpu.VMEM((devices, 6, 16, DH), low),
            pltpu.VMEM((6, 16, devices, DH), low),
            pltpu.VMEM((TOK, TOK), wide),
            pltpu.VMEM((2, TOK, TOK), wide),
            pltpu.VMEM((4, 16, OVC, DH), low),
            pltpu.VMEM((16, OVC, TOK), wide),
            pltpu.VMEM((8 * TOK, 16 * OVC), low),
            pltpu.VMEM((16 * OVC, 4 * DH), low),
            pltpu.VMEM((devices, 6, 16, DH), low),
            pltpu.VMEM((devices, 6, 16, DH), low),
            pltpu.VMEM((heads, 16, DH), low),
            pltpu.VMEM((devices, 16, DH), low),
            pltpu.VMEM((16, devices, DH), low),
            pltpu.VMEM((4, 4 * TOK, DH), wide),
            pltpu.VMEM((devices, 16, DH), low),
            pltpu.VMEM((heads, 16, DH), low),
        ]
        + [pltpu.SemaphoreType.DMA] * 10,
        compiler_params=pltpu.CompilerParams(
            collective_id=0, has_side_effects=True, vmem_limit_bytes=56 * 1024 * 1024
        ),
    )(cluster_ids.reshape(1, tok_rows), queries, key_rows, value_rows, out_grad)


def per_device(queries, key_rows, value_rows, out_grad, cluster_ids):
    arrays = (queries, key_rows, value_rows, out_grad, cluster_ids)
    *fast, flag = fast_path(*arrays)
    return lax.cond(
        flag[0, 0] > 0.0,
        lambda arrays, fast: full_capacity(*arrays),
        lambda arrays, fast: tuple(fast),
        arrays,
        tuple(fast),
    )


def solution(mesh):
    in_specs = (
        P(("seq", "clu"), None),
        P(("seq", "clu"), None),
        P(("seq", "clu"), None),
        P(("seq", "clu"), None),
        P(("seq", "clu")),
    )
    out_specs = (
        P(("seq", "clu"), None),
        P(("seq", "clu"), None),
        P(("seq", "clu"), None),
        P(("seq", "clu"), None),
    )
    return jax.shard_map(
        per_device, mesh=mesh, in_specs=in_specs, out_specs=out_specs, check_vma=False
    )
```

```python
import math

import jax
import jax.numpy as jnp
from jax import lax
from jax.experimental import pallas as pl
from jax.experimental.pallas import tpu as pltpu
from jax.sharding import PartitionSpec as P

DH = 128
TOK = 128
OVC = 96
SET = 16
FAR = 1e9
MESH = pl.DeviceIdType.MESH


masked = -1e30


def contract_last(left, right):
    return lax.dot_general(
        left, right, (((1,), (1,)), ((), ())), preferred_element_type=jnp.float32
    )


def contract_first(left, right):
    return lax.dot_general(
        left, right, (((0,), (0,)), ((), ())), preferred_element_type=jnp.float32
    )


def softmax_rows(query_head, key_head, allowed, inv_root):
    scores = contract_last(query_head, key_head) * inv_root
    scores = jnp.where(allowed, scores, masked)
    row_max = jnp.max(scores, axis=1, keepdims=True)
    weights = jnp.exp(scores - row_max)
    row_sum = jnp.sum(weights, axis=1, keepdims=True)
    return (weights / row_sum).astype(jnp.bfloat16)


def head_slice(array, head_index):
    return lax.dynamic_slice_in_dim(array, head_index * DH, DH, 1)


def full_capacity(queries, key_rows, value_rows, out_grad, cluster_ids):
    seq_count = lax.axis_size("seq")
    clu_count = lax.axis_size("clu")
    devices = seq_count * clu_count
    tok_rows = queries.shape[0]
    columns = queries.shape[1]
    head_count = columns // DH
    most_rows = 4 * tok_rows // devices
    capacity = most_rows * devices
    inv_root = 1.0 / math.sqrt(DH)
    owners = jnp.arange(devices, dtype=jnp.int32)
    member = (cluster_ids[:, None] == owners[None, :]).astype(jnp.int32)
    running = jnp.cumsum(member, axis=0) - 1
    slot_rank = jnp.sum(member * running, axis=1)
    sent_counts = jnp.sum(member, axis=0).reshape(devices, 1)
    slot_index = cluster_ids * most_rows + slot_rank
    stacked = jnp.concatenate([queries, key_rows, value_rows], axis=1)
    width_in = stacked.shape[1]
    packed = jnp.zeros((devices * most_rows, width_in), jnp.bfloat16).at[slot_index].set(stacked)
    packed = packed.reshape(devices, most_rows, width_in)
    got_rows, got_counts = (
        lax.all_to_all(packed, ("seq", "clu"), split_axis=0, concat_axis=0, tiled=True),
        lax.all_to_all(sent_counts, ("seq", "clu"), split_axis=0, concat_axis=0, tiled=True),
    )
    got_counts = got_counts.reshape(devices)
    starts = jnp.cumsum(got_counts) - got_counts
    live_total = jnp.sum(got_counts)
    within = jnp.arange(most_rows, dtype=jnp.int32)
    target = jnp.where(
        within[None, :] < got_counts[:, None], starts[:, None] + within[None, :], capacity
    )
    target = target.reshape(devices * most_rows)
    gathered = (
        jnp.zeros((capacity, width_in), jnp.bfloat16)
        .at[target]
        .set(got_rows.reshape(devices * most_rows, width_in), mode="drop")
    )
    query_block = gathered[:, :columns]
    key_block = gathered[:, columns : 2 * columns]
    value_block = gathered[:, 2 * columns : 3 * columns]
    positions = jnp.arange(capacity, dtype=jnp.int32)
    allowed = (positions[None, :] <= positions[:, None]) & (positions[None, :] < live_total)

    def forward_head(head_index, mixed_rows):
        weights_low = softmax_rows(
            head_slice(query_block, head_index),
            head_slice(key_block, head_index),
            allowed,
            inv_root,
        )
        out_head = jnp.dot(
            weights_low, head_slice(value_block, head_index), preferred_element_type=jnp.float32
        ).astype(jnp.bfloat16)
        return lax.dynamic_update_slice_in_dim(mixed_rows, out_head, head_index * DH, 1)

    mixed_rows = lax.fori_loop(
        0, head_count, forward_head, jnp.zeros((capacity, columns), jnp.bfloat16)
    )
    back_index = jnp.minimum(target, capacity - 1)
    outgoing = jnp.take(mixed_rows, back_index, axis=0).reshape(devices, most_rows, columns)
    grad_packed = (
        jnp.zeros((devices * most_rows, columns), jnp.bfloat16).at[slot_index].set(out_grad)
    )
    grad_packed = grad_packed.reshape(devices, most_rows, columns)
    returned = lax.all_to_all(outgoing, ("seq", "clu"), split_axis=0, concat_axis=0, tiled=True)
    got_grad = lax.all_to_all(grad_packed, ("seq", "clu"), split_axis=0, concat_axis=0, tiled=True)
    attention_out = jnp.take(returned.reshape(devices * most_rows, columns), slot_index, axis=0)
    grad_block = (
        jnp.zeros((capacity, columns), jnp.bfloat16)
        .at[target]
        .set(got_grad.reshape(devices * most_rows, columns), mode="drop")
    )
    delta_rows = jnp.sum(
        (grad_block.astype(jnp.float32) * mixed_rows.astype(jnp.float32)).reshape(
            capacity, head_count, DH
        ),
        axis=2,
    )

    def backward_head(head_index, grad_rows):
        query_head = head_slice(query_block, head_index)
        key_head = head_slice(key_block, head_index)
        value_head = head_slice(value_block, head_index)
        grad_head = head_slice(grad_block, head_index)
        weights_low = softmax_rows(query_head, key_head, allowed, inv_root)
        prob_grad = contract_last(grad_head, value_head)
        delta_head = lax.dynamic_slice_in_dim(delta_rows, head_index, 1, 1)
        score_grad = (weights_low.astype(jnp.float32) * (prob_grad - delta_head)).astype(
            jnp.bfloat16
        )
        query_part = (
            jnp.dot(score_grad, key_head, preferred_element_type=jnp.float32) * inv_root
        ).astype(jnp.bfloat16)
        key_part = (contract_first(score_grad, query_head) * inv_root).astype(jnp.bfloat16)
        value_part = contract_first(weights_low, grad_head).astype(jnp.bfloat16)
        grad_rows = lax.dynamic_update_slice_in_dim(grad_rows, query_part, head_index * DH, 1)
        grad_rows = lax.dynamic_update_slice_in_dim(
            grad_rows, key_part, columns + head_index * DH, 1
        )
        return lax.dynamic_update_slice_in_dim(
            grad_rows, value_part, 2 * columns + head_index * DH, 1
        )

    grad_rows = lax.fori_loop(
        0, head_count, backward_head, jnp.zeros((capacity, 3 * columns), jnp.bfloat16)
    )
    outgoing_grads = jnp.take(grad_rows, back_index, axis=0).reshape(
        devices, most_rows, 3 * columns
    )
    returned_grads = lax.all_to_all(
        outgoing_grads, ("seq", "clu"), split_axis=0, concat_axis=0, tiled=True
    )
    picked = jnp.take(returned_grads.reshape(devices * most_rows, 3 * columns), slot_index, axis=0)
    return (
        attention_out,
        picked[:, :columns],
        picked[:, columns : 2 * columns],
        picked[:, 2 * columns :],
    )


def bf16_dot(left, right):
    return jnp.dot(left, right, preferred_element_type=jnp.float32)


def flip_perm():
    row = lax.broadcasted_iota(jnp.int32, (SET * 16, SET * 16), 0)
    col = lax.broadcasted_iota(jnp.int32, (SET * 16, SET * 16), 1)
    swapped = (col % 16) * 16 + col // 16
    return (row == swapped).astype(jnp.float32).astype(jnp.bfloat16)


def attend(q, k, v, g, allowed, inv_root):
    raw = jnp.where(allowed, contract_last(q, k), masked)
    row_max = jnp.max(raw, axis=1, keepdims=True)
    weights = jnp.exp2((raw - row_max) * (inv_root * math.log2(math.e)))
    row_sum = jnp.sum(weights, axis=1, keepdims=True)
    prob = weights * (1.0 / row_sum)
    prob_low = prob.astype(jnp.bfloat16)
    out = bf16_dot(prob_low, v).astype(jnp.bfloat16)
    delta = jnp.sum(
        g.astype(jnp.float32) * out.astype(jnp.float32), axis=1, keepdims=True
    )
    prob_grad = contract_last(g, v)
    score_grad = (prob * (prob_grad - delta)).astype(jnp.bfloat16)
    dq = (bf16_dot(score_grad, k) * inv_root).astype(jnp.bfloat16)
    dk = contract_first(score_grad, q) * inv_root
    dv = contract_first(prob_low, g)
    return out, dq, dk, dv


def fast_kernel(
    ids_ref, q_ref, k_ref, v_ref, g_ref,
    out_ref, dq_ref, dk_ref, dv_ref, flag_ref,
    cnt_send, cnt_group, cnt_recv, pack_mat, unpack_mat,
    send_a, send_b, recv_a, recv_b, table, slots_t, group_t,
    over, over_pos, key_pos, pick, onehot, over_res, result_a, result_b, back_a, back_b,
    hsend, hrecv, htable, hacc, hresult, hback,
    cnt_send_sem, cnt_sem, cnt2_send_sem, cnt2_sem,
    send_a_sem, recv_a_sem, send_b_sem, recv_b_sem,
    res_a_sem, back_a_sem, res_b_sem, back_b_sem,
    hsend_sem, hrecv_sem, hres_sem, hback_sem,
):
    seq_at = lax.axis_index("seq")
    clu_at = lax.axis_index("clu")
    groups = lax.axis_size("clu")
    heads = lax.axis_size("seq")
    devices = heads * groups
    me = seq_at * groups + clu_at
    inv_root = 1.0 / math.sqrt(DH)
    is_heavy_owner = lax.rem(seq_at, groups) == clu_at
    at_x, at_z = seq_at // 4, lax.rem(seq_at, 4)
    at_y, at_core = clu_at // 2, lax.rem(clu_at, 2)

    def coords(device):
        return (device // groups, lax.rem(device, groups))

    def moved(at, by):
        return lax.rem(at + by + at_core * (4 - 2 * by), 4)

    def peer_at(step):
        offset = lax.rem(step * 59, devices)
        x = moved(at_x, offset // 32)
        z = moved(at_z, lax.rem(offset // 8, 4))
        y = moved(at_y, lax.rem(offset // 2, 4))
        core = lax.rem(at_core + lax.rem(offset, 2), 2)
        return x * 4 + z, y * 2 + core

    def send_to_all(source, target, send_sem, recv_sem):
        def one_peer(step, carry):
            seq_to, clu_to = peer_at(step)
            pltpu.make_async_remote_copy(
                src_ref=source.at[seq_to * groups + clu_to],
                dst_ref=target,
                send_sem=send_sem,
                recv_sem=recv_sem,
                device_id=(seq_to, clu_to),
                device_id_type=MESH,
            ).start()
            return carry

        lax.fori_loop(1, devices, one_peer, 0)
        pltpu.make_async_copy(source.at[me], target, recv_sem).start()

    def wait_bytes(ref, sem):
        pltpu.make_async_copy(ref, ref, sem).wait()

    barrier = pltpu.get_barrier_semaphore()

    def greet(step, carry):
        pl.semaphore_signal(
            barrier, inc=1, device_id=coords(lax.rem(me + step, devices)), device_id_type=MESH
        )
        return carry

    lax.fori_loop(1, devices, greet, 0)

    sub = lax.broadcasted_iota(jnp.int32, (TOK, TOK), 0)
    lane = lax.broadcasted_iota(jnp.int32, (TOK, TOK), 1)
    sub_f = sub.astype(jnp.float32)
    lane_f = lane.astype(jnp.float32)
    ids_l = jnp.broadcast_to(ids_ref[...].astype(jnp.float32), (TOK, TOK))
    ids_s = ids_l.T
    one = jnp.ones((TOK, TOK), jnp.float32)
    zero = jnp.zeros((TOK, TOK), jnp.float32)
    same = ids_l == ids_s
    rank_l = jnp.sum(jnp.where(same & (sub < lane), one, zero), axis=0, keepdims=True)
    rank_s = jnp.sum(jnp.where(same & (lane < sub), one, zero), axis=1, keepdims=True)
    count_l = jnp.sum(jnp.where(same, one, zero), axis=0, keepdims=True)
    cnt_send[...] = jnp.sum(jnp.where(ids_s == lane_f, one, zero), axis=0, keepdims=True)
    ids_row = ids_l[0:1, :]
    heavy = jnp.min(jnp.where(count_l == 4.0, ids_row, 999.0), axis=1, keepdims=True)
    group_l = jnp.floor(ids_l * (1.0 / 16.0))
    group_s = jnp.floor(ids_s * (1.0 / 16.0))
    before = (group_l == group_s) & (ids_s != heavy) & (rank_s >= 1.0)
    before = before & ((ids_s < ids_l) | (same & (sub < lane)))
    over_at = jnp.sum(jnp.where(before, one, zero), axis=0, keepdims=True)
    light_l = ids_l != heavy
    lower = (sub % 16) < 8
    slot = (sub % 8).astype(jnp.float32)
    slot_group = (sub // 16).astype(jnp.float32)

    def first_rows(half):
        cluster = slot_group * 16.0 + half * 8.0 + slot
        return (ids_l == cluster) & (rank_l == 0.0) & light_l

    later_rows = (group_l == slot_group) & light_l & (rank_l >= 1.0) & (over_at == slot)
    for unit, chosen in enumerate((first_rows(0), later_rows, first_rows(1))):
        at_row = (0, TOK, 2 * TOK + 16)[unit]
        for half in range(2):
            matrix = jnp.where(chosen & (lower if half == 0 else ~lower), one, zero)
            turned = matrix.T.astype(jnp.bfloat16)
            matrix = matrix.astype(jnp.bfloat16)
            for pair in range(2):
                pack_mat[pair, pl.ds(at_row, TOK), pl.ds(half * TOK, TOK)] = matrix
                unpack_mat[pair, pl.ds(half * TOK, TOK), pl.ds(unit * TOK, TOK)] = turned
    for array in range(4):
        chosen = (ids_l == heavy) & (rank_l == (sub % 4).astype(jnp.float32))
        chosen = chosen & (sub // 4 == array) & (sub < 16)
        matrix = jnp.where(chosen, one, zero)
        pair, half = array // 2, array % 2
        unpack_mat[pair, pl.ds(half * TOK, TOK), pl.ds(3 * TOK, TOK)] = matrix.T.astype(
            jnp.bfloat16
        )
        pack_mat[pair, pl.ds(2 * TOK, 16), pl.ds(half * TOK, TOK)] = matrix[0:16, :].astype(
            jnp.bfloat16
        )

    pl.semaphore_wait(barrier, devices - 1)

    def share_counts(source, target, count, to, send_sem, recv_sem):
        def one_peer(step, carry):
            pltpu.make_async_remote_copy(
                src_ref=source,
                dst_ref=target,
                send_sem=send_sem,
                recv_sem=recv_sem,
                device_id=to(step),
                device_id_type=MESH,
            ).start()
            return carry

        lax.fori_loop(1, count, one_peer, 0)
        pltpu.make_async_copy(source, target, recv_sem).start()

    share_counts(
        cnt_send, cnt_group.at[clu_at], groups,
        lambda step: (seq_at, lax.rem(clu_at + step, groups)), cnt_send_sem, cnt_sem,
    )

    def pack_heads(at, first_row, row_count):
        cols = pl.ds(pl.multiple_of(at * 2 * DH, 2 * DH), 2 * DH)
        for pair, (left, right) in enumerate(((q_ref, k_ref), (v_ref, g_ref))):
            rows = jnp.concatenate([left[:, cols], right[:, cols]], axis=0)
            yield pair, bf16_dot(pack_mat[pair, pl.ds(first_row, row_count), :], rows)

    def put_units(target, at, packed, pair, units):
        low = packed.astype(jnp.bfloat16)
        for unit in range(units):
            for k in range(2):
                piece = low[unit * TOK : (unit + 1) * TOK, k * DH : (k + 1) * DH]
                target[pl.ds((2 * at + k) * groups, groups), 2 * unit + pair] = piece.reshape(
                    groups, 16, DH
                )

    def pack_a(at, carry):
        extra = None
        for pair, packed in pack_heads(at, 0, 2 * TOK + 16):
            put_units(send_a, at, packed, pair, 2)
            part = packed[2 * TOK :]
            extra = part if extra is None else extra + part
        for k in range(2):
            hsend[2 * at + k] = extra[:, k * DH : (k + 1) * DH].astype(jnp.bfloat16)
        return carry

    lax.fori_loop(0, heads // 2, pack_a, 0)

    def send_heavy(step, carry):
        head = lax.rem(seq_at + step, heads)
        clu_to = lax.rem(head, groups)

        @pl.when(head * groups + clu_to != me)
        def _():
            pltpu.make_async_remote_copy(
                src_ref=hsend.at[head],
                dst_ref=hrecv.at[me],
                send_sem=hsend_sem,
                recv_sem=hrecv_sem,
                device_id=(head, clu_to),
                device_id_type=MESH,
            ).start()

        @pl.when(head * groups + clu_to == me)
        def _():
            pltpu.make_async_copy(hsend.at[head], hrecv.at[me], hrecv_sem).start()

        return carry

    lax.fori_loop(0, heads, send_heavy, 0)
    send_to_all(send_a, recv_a.at[me], send_a_sem, recv_a_sem)
    wait_bytes(cnt_group, cnt_sem)
    share_counts(
        cnt_group, cnt_recv.at[seq_at], heads,
        lambda step: (lax.rem(seq_at + step, heads), clu_at), cnt2_send_sem, cnt2_sem,
    )

    def pack_b(at, carry):
        for pair, packed in pack_heads(at, 2 * TOK + 16, TOK):
            put_units(send_b, at, packed, pair, 1)
        return carry

    lax.fori_loop(0, heads // 2, pack_b, 0)
    send_to_all(send_b, recv_b.at[me], send_b_sem, recv_b_sem)

    wait_bytes(cnt_recv, cnt2_sem)
    seen = cnt_recv[...].reshape(TOK, TOK)
    heavies = jnp.min(jnp.where(seen == 4.0, lane_f, 999.0), axis=1, keepdims=True)
    heavy_all = jnp.min(heavies, axis=0, keepdims=True)
    light = lane_f != heavy_all
    more = jnp.where(light, jnp.maximum(seen - 1.0, 0.0), 0.0)
    in_group = jnp.where(sub // 16 == lane, one, zero).astype(jnp.bfloat16)
    per_group = bf16_dot(more.astype(jnp.bfloat16), in_group)
    bad = jnp.where((per_group > 8.0) | (heavies != heavy_all), one, zero)
    per_cluster = jnp.sum(more, axis=0, keepdims=True)
    bad = jnp.maximum(bad, jnp.where(per_cluster > OVC, one, zero))
    flag_ref[0, 0] = jnp.max(bad).astype(jnp.int32)

    group_t[0] = more.T
    group_t[1] = jnp.where((seen > 0.0) & light, one, zero).T
    mine = pl.ds(pl.multiple_of(clu_at * 16, 16), 16)
    more_g = group_t[0, mine, :]
    more_g_low = more_g.astype(jnp.bfloat16)
    sub16 = lax.broadcasted_iota(jnp.int32, (16, 16), 0)
    lane16 = lax.broadcasted_iota(jnp.int32, (16, 16), 1)
    earlier = jnp.where(lane16 < sub16, 1.0, 0.0).astype(jnp.bfloat16)
    offset = bf16_dot(earlier, more_g_low)
    ahead = jnp.where(sub < lane, one, zero).astype(jnp.bfloat16)
    start = bf16_dot(more_g_low, ahead)
    at_cluster = lax.broadcasted_iota(jnp.int32, (16, TOK), 0).astype(jnp.float32)
    rows = []
    for s in range(8):
        held = (offset <= float(s)) & (offset + more_g > float(s))
        index = at_cluster * float(OVC) + start + (float(s) - offset) + 1.0
        rows.append(jnp.sum(jnp.where(held, index, 0.0), axis=0, keepdims=True) - 1.0)
    slot_row = jnp.concatenate(rows, axis=0)
    slots_t[...] = jnp.concatenate(
        [slot_row, jnp.full((TOK - 8, TOK), -1.0, jnp.float32)], axis=0
    ).T

    block_col = jnp.concatenate([sub_f] * 8, axis=0).astype(jnp.bfloat16)
    slot_col = jnp.concatenate([one * float(s + 1) for s in range(8)], axis=0).astype(
        jnp.bfloat16
    )
    places = jnp.concatenate([block_col, slot_col], axis=1)
    chunk = 4
    first_row = lax.broadcasted_iota(jnp.int32, (1, TOK), 1).astype(jnp.float32) * 16.0

    def plan_chunk(at, carry):
        want = (
            lax.broadcasted_iota(jnp.int32, (chunk * OVC, TOK), 0) + at * (chunk * OVC)
        ).astype(jnp.float32)
        chosen = jnp.concatenate(
            [jnp.where(slot_row[s : s + 1, :] == want, 1.0, 0.0) for s in range(8)], axis=1
        ).astype(jnp.bfloat16)
        pick[pl.ds(pl.multiple_of(at * chunk * OVC, 128), chunk * OVC), :] = chosen
        found = bf16_dot(chosen, places)
        for c in range(chunk):
            part = found[c * OVC : (c + 1) * OVC]
            slot_part = part[:, DH:]
            where = jnp.where(slot_part > 0.0, part[:, :DH] * 16.0 + slot_part, FAR)
            over_pos[at * chunk + c] = where
            padded = jnp.concatenate(
                [where, jnp.full((TOK - OVC, TOK), FAR, jnp.float32)], axis=0
            )
            valid = group_t[1, pl.ds(clu_at * 16 + at * chunk + c, 1), :]
            key_row = jnp.concatenate(
                [jnp.where(valid > 0.0, first_row, FAR), padded.T[0:1, :]], axis=1
            )
            key_pos[at * chunk + c] = jnp.broadcast_to(key_row, (8, 2 * TOK))
        return carry

    lax.fori_loop(0, 16 // chunk, plan_chunk, 0)

    def plan_slot(s, carry):
        pick_s = jnp.max(jnp.where(lane == s, slots_t[...], -1.0), axis=1, keepdims=True)
        want = lax.broadcasted_iota(jnp.int32, (TOK, 16 * OVC), 1).astype(jnp.float32)
        onehot[pl.ds(pl.multiple_of(s * TOK, TOK), TOK), :] = jnp.where(
            pick_s == want, 1.0, 0.0
        ).astype(jnp.bfloat16)
        return carry

    lax.fori_loop(0, 8, plan_slot, 0)

    perm = flip_perm()

    def arrange(source, target, units):
        def one_set(at, carry):
            blocks = pl.ds(pl.multiple_of(at * SET, SET), SET)
            rows = jnp.concatenate(
                [source(blocks, unit).reshape(SET * 16, DH) for unit in range(units)], axis=1
            )
            turned = bf16_dot(perm, rows).astype(jnp.bfloat16)
            for unit in range(units):
                target(
                    blocks, unit, turned[:, unit * DH : (unit + 1) * DH].reshape(16, SET, DH)
                )
            return carry

        lax.fori_loop(0, devices // SET, one_set, 0)

    def put_table(first):
        def put(blocks, unit, value):
            table[first + unit, :, blocks, :] = value

        return put

    @pl.when(is_heavy_owner)
    def _():
        wait_bytes(hrecv, hrecv_sem)

        def put_heavy(blocks, unit, value):
            htable[:, blocks, :] = value

        arrange(lambda blocks, unit: hrecv[blocks], put_heavy, 1)
        k_h, v_h = [htable[4 * a : 4 * a + 4].reshape(4 * TOK, DH) for a in (1, 2)]
        hacc[...] = jnp.zeros_like(hacc)
        key_lane = lax.broadcasted_iota(jnp.int32, (TOK, 4 * TOK), 1)
        key_at = lax.rem(key_lane, TOK) * 4 + key_lane // TOK
        query_at = lax.broadcasted_iota(jnp.int32, (TOK, 4 * TOK), 0) * 4

        def heavy_tile(s, carry):
            out, dq, dk, dv = attend(
                htable[s], k_h, v_h, htable[12 + s], key_at <= query_at + s, inv_root
            )
            hacc[2, pl.ds(pl.multiple_of(s * TOK, TOK), TOK)] = out.astype(jnp.float32)
            hacc[3, pl.ds(pl.multiple_of(s * TOK, TOK), TOK)] = dq.astype(jnp.float32)
            hacc[0] += dk
            hacc[1] += dv
            return carry

        lax.fori_loop(0, 4, heavy_tile, 0)
        for array, at in enumerate((2, 3, 0, 1)):
            htable[4 * array : 4 * array + 4] = (
                hacc[at].astype(jnp.bfloat16).reshape(4, TOK, DH)
            )

        def put_hresult(blocks, unit, value):
            hresult[blocks] = value

        arrange(lambda blocks, unit: htable[:, blocks, :], put_hresult, 1)
        send_to_all(hresult, hback.at[seq_at], hres_sem, hback_sem)

    wait_bytes(recv_a, recv_a_sem)
    arrange(lambda blocks, unit: recv_a[blocks, unit], put_table(0), 4)

    def over_rows(array):
        return table[2 + array // 2, (array % 2) * 8 : (array % 2) * 8 + 8].reshape(
            8 * TOK, DH
        )

    loose = jnp.concatenate([over_rows(array) for array in range(4)], axis=1)

    def gather_chunk(at, carry):
        chosen = pick[pl.ds(pl.multiple_of(at * chunk * OVC, 128), chunk * OVC), :]
        found = bf16_dot(chosen, loose).astype(jnp.bfloat16)
        for c in range(chunk):
            for array in range(4):
                over[array, at * chunk + c] = found[
                    c * OVC : (c + 1) * OVC, array * DH : (array + 1) * DH
                ]
        return carry

    lax.fori_loop(0, 16 // chunk, gather_chunk, 0)

    first_pos = sub_f * 16.0
    pad_rows = jnp.zeros((TOK - OVC, DH), jnp.bfloat16)

    def one_cluster(c, carry):
        tile = (c // 8) * 4
        j = lax.rem(c, 8)
        q, k, v, g = [
            jnp.concatenate([table[tile + a // 2, (a % 2) * 8 + j], over[a, c]], axis=0)
            for a in range(4)
        ]
        k = jnp.concatenate([k, pad_rows], axis=0)
        v = jnp.concatenate([v, pad_rows], axis=0)
        pos_q = jnp.concatenate([first_pos, over_pos[c]], axis=0)
        allowed = key_pos[c, 0:1, :] <= jnp.concatenate([pos_q, pos_q], axis=1)
        out, dq, dk, dv = attend(q, k, v, g, allowed, inv_root)
        results = [out, dq, dk.astype(jnp.bfloat16), dv.astype(jnp.bfloat16)]
        for a in range(4):
            table[tile + a // 2, (a % 2) * 8 + j] = results[a][:TOK]
            over_res[pl.ds(pl.multiple_of(c * OVC, 32), OVC), pl.ds(a * DH, DH)] = results[a][
                TOK : TOK + OVC
            ]
        return carry

    def put_a(blocks, unit, value):
        result_a[blocks, unit] = value

    def put_b(blocks, unit, value):
        result_b[blocks, unit] = value

    lax.fori_loop(0, 8, one_cluster, 0, unroll=2)
    arrange(lambda blocks, unit: table[unit, :, blocks, :], put_a, 2)
    send_to_all(result_a, back_a.at[me], res_a_sem, back_a_sem)

    wait_bytes(recv_b, recv_b_sem)
    arrange(lambda blocks, unit: recv_b[blocks, unit], put_table(4), 2)
    lax.fori_loop(8, 16, one_cluster, 0, unroll=2)

    def spread_chunk(at, carry):
        found = bf16_dot(
            onehot[pl.ds(pl.multiple_of(at * 256, 256), 256), :], over_res[...]
        ).astype(jnp.bfloat16)
        for array in range(4):
            table[2 + array // 2, pl.ds((array % 2) * 8 + at * 2, 2)] = found[
                :, array * DH : (array + 1) * DH
            ].reshape(2, TOK, DH)
        return carry

    lax.fori_loop(0, 4, spread_chunk, 0)
    arrange(lambda blocks, unit: table[2 + unit, :, blocks, :], put_b, 4)
    send_to_all(result_b, back_b.at[me], res_b_sem, back_b_sem)

    wait_bytes(hback, hback_sem)
    wait_bytes(back_a, back_a_sem)
    wait_bytes(back_b, back_b_sem)

    def unpack_heads(at, carry):
        cols = pl.ds(pl.multiple_of(at * 2 * DH, 2 * DH), 2 * DH)
        for pair, refs in enumerate(((out_ref, dq_ref), (dk_ref, dv_ref))):
            sides = []
            for k in range(2):
                head = 2 * at + k
                owners = pl.ds(head * groups, groups)
                sides.append(
                    jnp.concatenate(
                        [
                            back_a[owners, pair].reshape(TOK, DH),
                            back_b[owners, pair].reshape(TOK, DH),
                            back_b[owners, 2 + pair].reshape(TOK, DH),
                            hback[head],
                            jnp.zeros((TOK - 16, DH), jnp.bfloat16),
                        ],
                        axis=0,
                    )
                )
            found = bf16_dot(unpack_mat[pair], jnp.concatenate(sides, axis=1))
            for half in range(2):
                refs[half][:, cols] = found[half * TOK : (half + 1) * TOK].astype(jnp.bfloat16)
        return carry

    lax.fori_loop(0, heads // 2, unpack_heads, 0)

    others = pl.ds(0, devices - 1)
    wait_bytes(cnt_group.at[pl.ds(0, groups - 1)], cnt_send_sem)
    wait_bytes(cnt_recv.at[pl.ds(0, heads - 1)], cnt2_send_sem)
    wait_bytes(send_a.at[others], send_a_sem)
    wait_bytes(send_b.at[others], send_b_sem)
    wait_bytes(result_a.at[others], res_a_sem)
    wait_bytes(result_b.at[others], res_b_sem)

    @pl.when(is_heavy_owner)
    def _():
        wait_bytes(hsend.at[pl.ds(0, heads - 1)], hsend_sem)
        wait_bytes(hresult.at[others], hres_sem)

    @pl.when(jnp.logical_not(is_heavy_owner))
    def _():
        wait_bytes(hsend, hsend_sem)


def fast_path(queries, key_rows, value_rows, out_grad, cluster_ids):
    tok_rows, columns = queries.shape
    heads = columns // DH
    groups = lax.axis_size("clu")
    devices = lax.axis_size("seq") * groups
    low = jnp.bfloat16
    wide = jnp.float32
    rows = jax.ShapeDtypeStruct((tok_rows, columns), low)
    vmem = pl.BlockSpec(memory_space=pltpu.VMEM)
    smem = pl.BlockSpec(memory_space=pltpu.SMEM)
    return pl.pallas_call(
        fast_kernel,
        out_shape=[rows] * 4 + [jax.ShapeDtypeStruct((1, 1), jnp.int32)],
        in_specs=[vmem] * 5,
        out_specs=[vmem] * 4 + [smem],
        scratch_shapes=[
            pltpu.VMEM((1, TOK), wide),
            pltpu.VMEM((groups, 1, TOK), wide),
            pltpu.VMEM((heads, groups, 1, TOK), wide),
            pltpu.VMEM((2, 3 * TOK + 16, 2 * TOK), low),
            pltpu.VMEM((2, 2 * TOK, 4 * TOK), low),
            pltpu.VMEM((devices, 4, 16, DH), low),
            pltpu.VMEM((devices, 2, 16, DH), low),
            pltpu.VMEM((devices, 4, 16, DH), low),
            pltpu.VMEM((devices, 2, 16, DH), low),
            pltpu.VMEM((6, 16, devices, DH), low),
            pltpu.VMEM((TOK, TOK), wide),
            pltpu.VMEM((2, TOK, TOK), wide),
            pltpu.VMEM((4, 16, OVC, DH), low),
            pltpu.VMEM((16, OVC, TOK), wide),
            pltpu.VMEM((16, 8, 2 * TOK), wide),
            pltpu.VMEM((16 * OVC, 8 * TOK), low),
            pltpu.VMEM((8 * TOK, 16 * OVC), low),
            pltpu.VMEM((16 * OVC, 4 * DH), low),
            pltpu.VMEM((devices, 2, 16, DH), low),
            pltpu.VMEM((devices, 4, 16, DH), low),
            pltpu.VMEM((devices, 2, 16, DH), low),
            pltpu.VMEM((devices, 4, 16, DH), low),
            pltpu.VMEM((heads, 16, DH), low),
            pltpu.VMEM((devices, 16, DH), low),
            pltpu.VMEM((16, devices, DH), low),
            pltpu.VMEM((4, 4 * TOK, DH), wide),
            pltpu.VMEM((devices, 16, DH), low),
            pltpu.VMEM((heads, 16, DH), low),
        ]
        + [pltpu.SemaphoreType.DMA] * 16,
        compiler_params=pltpu.CompilerParams(
            collective_id=0, has_side_effects=True, vmem_limit_bytes=56 * 1024 * 1024
        ),
    )(cluster_ids.reshape(1, tok_rows), queries, key_rows, value_rows, out_grad)


def per_device(queries, key_rows, value_rows, out_grad, cluster_ids):
    arrays = (queries, key_rows, value_rows, out_grad, cluster_ids)
    *fast, flag = fast_path(*arrays)
    return lax.cond(
        flag.reshape(()) != 0,
        lambda arrays, fast: full_capacity(*arrays),
        lambda arrays, fast: tuple(fast),
        arrays,
        tuple(fast),
    )


def solution(mesh):
    in_specs = (
        P(("seq", "clu"), None),
        P(("seq", "clu"), None),
        P(("seq", "clu"), None),
        P(("seq", "clu"), None),
        P(("seq", "clu")),
    )
    out_specs = (
        P(("seq", "clu"), None),
        P(("seq", "clu"), None),
        P(("seq", "clu"), None),
        P(("seq", "clu"), None),
    )
    return jax.shard_map(
        per_device, mesh=mesh, in_specs=in_specs, out_specs=out_specs, check_vma=False
    )
```

```python
import math

import jax
import jax.numpy as jnp
from jax import lax
from jax.experimental import pallas as pl
from jax.experimental.pallas import tpu as pltpu
from jax.sharding import PartitionSpec as P

DH = 128
TOK = 128
OVC = 96
SET = 16
FAR = 1e9
MESH = pl.DeviceIdType.MESH


masked = -1e30


def contract_last(left, right):
    return lax.dot_general(
        left, right, (((1,), (1,)), ((), ())), preferred_element_type=jnp.float32
    )


def contract_first(left, right):
    return lax.dot_general(
        left, right, (((0,), (0,)), ((), ())), preferred_element_type=jnp.float32
    )


def softmax_rows(query_head, key_head, allowed, inv_root):
    scores = contract_last(query_head, key_head) * inv_root
    scores = jnp.where(allowed, scores, masked)
    row_max = jnp.max(scores, axis=1, keepdims=True)
    weights = jnp.exp(scores - row_max)
    row_sum = jnp.sum(weights, axis=1, keepdims=True)
    return (weights / row_sum).astype(jnp.bfloat16)


def head_slice(array, head_index):
    return lax.dynamic_slice_in_dim(array, head_index * DH, DH, 1)


def full_capacity(queries, key_rows, value_rows, out_grad, cluster_ids):
    seq_count = lax.axis_size("seq")
    clu_count = lax.axis_size("clu")
    devices = seq_count * clu_count
    tok_rows = queries.shape[0]
    columns = queries.shape[1]
    head_count = columns // DH
    most_rows = 4 * tok_rows // devices
    capacity = most_rows * devices
    inv_root = 1.0 / math.sqrt(DH)
    owners = jnp.arange(devices, dtype=jnp.int32)
    member = (cluster_ids[:, None] == owners[None, :]).astype(jnp.int32)
    running = jnp.cumsum(member, axis=0) - 1
    slot_rank = jnp.sum(member * running, axis=1)
    sent_counts = jnp.sum(member, axis=0).reshape(devices, 1)
    slot_index = cluster_ids * most_rows + slot_rank
    stacked = jnp.concatenate([queries, key_rows, value_rows], axis=1)
    width_in = stacked.shape[1]
    packed = jnp.zeros((devices * most_rows, width_in), jnp.bfloat16).at[slot_index].set(stacked)
    packed = packed.reshape(devices, most_rows, width_in)
    got_rows, got_counts = (
        lax.all_to_all(packed, ("seq", "clu"), split_axis=0, concat_axis=0, tiled=True),
        lax.all_to_all(sent_counts, ("seq", "clu"), split_axis=0, concat_axis=0, tiled=True),
    )
    got_counts = got_counts.reshape(devices)
    starts = jnp.cumsum(got_counts) - got_counts
    live_total = jnp.sum(got_counts)
    within = jnp.arange(most_rows, dtype=jnp.int32)
    target = jnp.where(
        within[None, :] < got_counts[:, None], starts[:, None] + within[None, :], capacity
    )
    target = target.reshape(devices * most_rows)
    gathered = (
        jnp.zeros((capacity, width_in), jnp.bfloat16)
        .at[target]
        .set(got_rows.reshape(devices * most_rows, width_in), mode="drop")
    )
    query_block = gathered[:, :columns]
    key_block = gathered[:, columns : 2 * columns]
    value_block = gathered[:, 2 * columns : 3 * columns]
    positions = jnp.arange(capacity, dtype=jnp.int32)
    allowed = (positions[None, :] <= positions[:, None]) & (positions[None, :] < live_total)

    def forward_head(head_index, mixed_rows):
        weights_low = softmax_rows(
            head_slice(query_block, head_index),
            head_slice(key_block, head_index),
            allowed,
            inv_root,
        )
        out_head = jnp.dot(
            weights_low, head_slice(value_block, head_index), preferred_element_type=jnp.float32
        ).astype(jnp.bfloat16)
        return lax.dynamic_update_slice_in_dim(mixed_rows, out_head, head_index * DH, 1)

    mixed_rows = lax.fori_loop(
        0, head_count, forward_head, jnp.zeros((capacity, columns), jnp.bfloat16)
    )
    back_index = jnp.minimum(target, capacity - 1)
    outgoing = jnp.take(mixed_rows, back_index, axis=0).reshape(devices, most_rows, columns)
    grad_packed = (
        jnp.zeros((devices * most_rows, columns), jnp.bfloat16).at[slot_index].set(out_grad)
    )
    grad_packed = grad_packed.reshape(devices, most_rows, columns)
    returned = lax.all_to_all(outgoing, ("seq", "clu"), split_axis=0, concat_axis=0, tiled=True)
    got_grad = lax.all_to_all(grad_packed, ("seq", "clu"), split_axis=0, concat_axis=0, tiled=True)
    attention_out = jnp.take(returned.reshape(devices * most_rows, columns), slot_index, axis=0)
    grad_block = (
        jnp.zeros((capacity, columns), jnp.bfloat16)
        .at[target]
        .set(got_grad.reshape(devices * most_rows, columns), mode="drop")
    )
    delta_rows = jnp.sum(
        (grad_block.astype(jnp.float32) * mixed_rows.astype(jnp.float32)).reshape(
            capacity, head_count, DH
        ),
        axis=2,
    )

    def backward_head(head_index, grad_rows):
        query_head = head_slice(query_block, head_index)
        key_head = head_slice(key_block, head_index)
        value_head = head_slice(value_block, head_index)
        grad_head = head_slice(grad_block, head_index)
        weights_low = softmax_rows(query_head, key_head, allowed, inv_root)
        prob_grad = contract_last(grad_head, value_head)
        delta_head = lax.dynamic_slice_in_dim(delta_rows, head_index, 1, 1)
        score_grad = (weights_low.astype(jnp.float32) * (prob_grad - delta_head)).astype(
            jnp.bfloat16
        )
        query_part = (
            jnp.dot(score_grad, key_head, preferred_element_type=jnp.float32) * inv_root
        ).astype(jnp.bfloat16)
        key_part = (contract_first(score_grad, query_head) * inv_root).astype(jnp.bfloat16)
        value_part = contract_first(weights_low, grad_head).astype(jnp.bfloat16)
        grad_rows = lax.dynamic_update_slice_in_dim(grad_rows, query_part, head_index * DH, 1)
        grad_rows = lax.dynamic_update_slice_in_dim(
            grad_rows, key_part, columns + head_index * DH, 1
        )
        return lax.dynamic_update_slice_in_dim(
            grad_rows, value_part, 2 * columns + head_index * DH, 1
        )

    grad_rows = lax.fori_loop(
        0, head_count, backward_head, jnp.zeros((capacity, 3 * columns), jnp.bfloat16)
    )
    outgoing_grads = jnp.take(grad_rows, back_index, axis=0).reshape(
        devices, most_rows, 3 * columns
    )
    returned_grads = lax.all_to_all(
        outgoing_grads, ("seq", "clu"), split_axis=0, concat_axis=0, tiled=True
    )
    picked = jnp.take(returned_grads.reshape(devices * most_rows, 3 * columns), slot_index, axis=0)
    return (
        attention_out,
        picked[:, :columns],
        picked[:, columns : 2 * columns],
        picked[:, 2 * columns :],
    )


def bf16_dot(left, right):
    return jnp.dot(left, right, preferred_element_type=jnp.float32)


def flip_perm():
    row = lax.broadcasted_iota(jnp.int32, (SET * 16, SET * 16), 0)
    col = lax.broadcasted_iota(jnp.int32, (SET * 16, SET * 16), 1)
    swapped = (col % 16) * 16 + col // 16
    return (row == swapped).astype(jnp.float32).astype(jnp.bfloat16)


def attend(q, k, v, g, allowed, inv_root):
    raw = jnp.where(allowed, contract_last(k, q), masked)
    most = jnp.max(raw, axis=0, keepdims=True)
    weights = jnp.exp2((raw - most) * (inv_root * math.log2(math.e)))
    prob = weights * (1.0 / jnp.sum(weights, axis=0, keepdims=True))
    prob_low = prob.astype(jnp.bfloat16)
    prob_grad = contract_last(v, g)
    delta = jnp.sum(prob * prob_grad, axis=0, keepdims=True)
    score_grad = (prob * (prob_grad - delta)).astype(jnp.bfloat16)
    out = contract_first(v, prob_low).T.astype(jnp.bfloat16)
    dq = (contract_first(k, score_grad).T * inv_root).astype(jnp.bfloat16)
    dk = bf16_dot(score_grad, q) * inv_root
    dv = bf16_dot(prob_low, g)
    return out, dq, dk, dv


def fast_kernel(
    ids_ref, q_ref, k_ref, v_ref, g_ref,
    out_ref, dq_ref, dk_ref, dv_ref, flag_ref,
    cnt_send, cnt_group, cnt_recv, pack_mat, unpack_mat,
    send_a, send_b, recv_a, recv_b, table, slots_t, group_t,
    over, key_pos, query_pos, pick, onehot, over_res, result_a, result_b, back_a, back_b,
    hsend, hrecv, htable, hacc, hresult, hback,
    cnt_send_sem, cnt_sem, cnt2_send_sem, cnt2_sem,
    send_a_sem, recv_a_sem, send_b_sem, recv_b_sem,
    res_a_sem, back_a_sem, res_b_sem, back_b_sem,
    hsend_sem, hrecv_sem, hres_sem, hback_sem,
):
    seq_at = lax.axis_index("seq")
    clu_at = lax.axis_index("clu")
    groups = lax.axis_size("clu")
    heads = lax.axis_size("seq")
    devices = heads * groups
    me = seq_at * groups + clu_at
    inv_root = 1.0 / math.sqrt(DH)
    is_heavy_owner = lax.rem(seq_at, groups) == clu_at
    at_x, at_z = lax.div(seq_at, 4), lax.rem(seq_at, 4)
    at_y, at_core = lax.div(clu_at, 2), lax.rem(clu_at, 2)

    def coords(device):
        return (lax.div(device, groups), lax.rem(device, groups))

    def turn(by):
        return by + at_core * (4 - 2 * by)

    eight = []
    for by_x, by_z, by_clu in zip(
        (0, 3, 2, 1, 0, 3, 2, 0), (0, 3, 2, 1, 1, 0, 3, 2), (0, 4, 6, 7, 2, 5, 1, 3)
    ):
        y = lax.rem(at_y + turn(by_clu // 2), 4)
        eight.append((turn(by_x), turn(by_z), y * 2 + lax.rem(at_core + by_clu % 2, 2)))

    def send_to_all(source, target, send_sem, recv_sem):
        def one_eight(step, carry):
            by = lax.rem(step * 11, 16)
            by_x, by_z = lax.div(by, 4), lax.rem(by, 4)
            x = at_x + turn(by_x)
            z = at_z + turn(by_z)
            for j, (more_x, more_z, clu_to) in enumerate(eight):
                seq_to = lax.rem(x + more_x, 4) * 4 + lax.rem(z + more_z, 4)

                def start():
                    pltpu.make_async_remote_copy(
                        src_ref=source.at[seq_to * groups + clu_to],
                        dst_ref=target,
                        send_sem=send_sem,
                        recv_sem=recv_sem,
                        device_id=(seq_to, clu_to),
                        device_id_type=MESH,
                    ).start()

                if j == 0:
                    pl.when(step > 0)(start)
                else:
                    start()
            return carry

        lax.fori_loop(0, devices // 8, one_eight, 0)
        pltpu.make_async_copy(source.at[me], target, recv_sem).start()

    def wait_bytes(ref, sem):
        pltpu.make_async_copy(ref, ref, sem).wait()

    barrier = pltpu.get_barrier_semaphore()

    def greet(step, carry):
        pl.semaphore_signal(
            barrier, inc=1, device_id=coords(lax.rem(me + step, devices)), device_id_type=MESH
        )
        return carry

    lax.fori_loop(1, devices, greet, 0)

    sub = lax.broadcasted_iota(jnp.int32, (TOK, TOK), 0)
    lane = lax.broadcasted_iota(jnp.int32, (TOK, TOK), 1)
    sub_f = sub.astype(jnp.float32)
    lane_f = lane.astype(jnp.float32)
    ids_l = jnp.broadcast_to(ids_ref[...].astype(jnp.float32), (TOK, TOK))
    ids_s = ids_l.T
    one = jnp.ones((TOK, TOK), jnp.float32)
    zero = jnp.zeros((TOK, TOK), jnp.float32)
    same = ids_l == ids_s
    rank_l = jnp.sum(jnp.where(same & (sub < lane), one, zero), axis=0, keepdims=True)
    rank_s = jnp.sum(jnp.where(same & (lane < sub), one, zero), axis=1, keepdims=True)
    count_l = jnp.sum(jnp.where(same, one, zero), axis=0, keepdims=True)
    cnt_send[...] = jnp.sum(jnp.where(ids_s == lane_f, one, zero), axis=0, keepdims=True)
    ids_row = ids_l[0:1, :]
    heavy = jnp.min(jnp.where(count_l == 4.0, ids_row, 999.0), axis=1, keepdims=True)
    group_l = jnp.floor(ids_l * (1.0 / 16.0))
    group_s = jnp.floor(ids_s * (1.0 / 16.0))
    before = (group_l == group_s) & (ids_s != heavy) & (rank_s >= 1.0)
    before = before & ((ids_s < ids_l) | (same & (sub < lane)))
    over_at = jnp.sum(jnp.where(before, one, zero), axis=0, keepdims=True)
    light_l = ids_l != heavy
    lower = (sub % 16) < 8
    slot = (sub % 8).astype(jnp.float32)
    slot_group = (sub // 16).astype(jnp.float32)

    def first_rows(half):
        cluster = slot_group * 16.0 + half * 8.0 + slot
        return (ids_l == cluster) & (rank_l == 0.0) & light_l

    later_rows = (group_l == slot_group) & light_l & (rank_l >= 1.0) & (over_at == slot)
    for unit, chosen in enumerate((first_rows(0), later_rows, first_rows(1))):
        at_row = (0, TOK, 2 * TOK + 16)[unit]
        for half in range(2):
            matrix = jnp.where(chosen & (lower if half == 0 else ~lower), one, zero)
            turned = matrix.T.astype(jnp.bfloat16)
            matrix = matrix.astype(jnp.bfloat16)
            for pair in range(2):
                pack_mat[pair, pl.ds(at_row, TOK), pl.ds(half * TOK, TOK)] = matrix
                unpack_mat[pair, pl.ds(half * TOK, TOK), pl.ds(unit * TOK, TOK)] = turned
    for array in range(4):
        chosen = (ids_l == heavy) & (rank_l == (sub % 4).astype(jnp.float32))
        chosen = chosen & (sub // 4 == array) & (sub < 16)
        matrix = jnp.where(chosen, one, zero)
        pair, half = array // 2, array % 2
        unpack_mat[pair, pl.ds(half * TOK, TOK), pl.ds(3 * TOK, TOK)] = matrix.T.astype(
            jnp.bfloat16
        )
        pack_mat[pair, pl.ds(2 * TOK, 16), pl.ds(half * TOK, TOK)] = matrix[0:16, :].astype(
            jnp.bfloat16
        )

    pl.semaphore_wait(barrier, devices - 1)

    def share_counts(source, target, count, to, send_sem, recv_sem):
        def one_peer(step, carry):
            pltpu.make_async_remote_copy(
                src_ref=source,
                dst_ref=target,
                send_sem=send_sem,
                recv_sem=recv_sem,
                device_id=to(step),
                device_id_type=MESH,
            ).start()
            return carry

        lax.fori_loop(1, count, one_peer, 0)
        pltpu.make_async_copy(source, target, recv_sem).start()

    share_counts(
        cnt_send, cnt_group.at[clu_at], groups,
        lambda step: (seq_at, lax.rem(clu_at + step, groups)), cnt_send_sem, cnt_sem,
    )

    def pack_heads(at, first_row, row_count):
        cols = pl.ds(pl.multiple_of(at * 2 * DH, 2 * DH), 2 * DH)
        for pair, (left, right) in enumerate(((q_ref, k_ref), (v_ref, g_ref))):
            rows = jnp.concatenate([left[:, cols], right[:, cols]], axis=0)
            yield pair, bf16_dot(pack_mat[pair, pl.ds(first_row, row_count), :], rows)

    def put_units(target, at, packed, pair, units):
        low = packed.astype(jnp.bfloat16)
        for unit in range(units):
            for k in range(2):
                piece = low[unit * TOK : (unit + 1) * TOK, k * DH : (k + 1) * DH]
                target[pl.ds((2 * at + k) * groups, groups), 2 * unit + pair] = piece.reshape(
                    groups, 16, DH
                )

    def pack_a(at, carry):
        extra = None
        for pair, packed in pack_heads(at, 0, 2 * TOK + 16):
            put_units(send_a, at, packed, pair, 2)
            part = packed[2 * TOK :]
            extra = part if extra is None else extra + part
        for k in range(2):
            hsend[2 * at + k] = extra[:, k * DH : (k + 1) * DH].astype(jnp.bfloat16)
        return carry

    lax.fori_loop(0, heads // 2, pack_a, 0)

    def send_heavy(step, carry):
        head = lax.rem(seq_at + step, heads)
        clu_to = lax.rem(head, groups)

        @pl.when(head * groups + clu_to != me)
        def _():
            pltpu.make_async_remote_copy(
                src_ref=hsend.at[head],
                dst_ref=hrecv.at[me],
                send_sem=hsend_sem,
                recv_sem=hrecv_sem,
                device_id=(head, clu_to),
                device_id_type=MESH,
            ).start()

        @pl.when(head * groups + clu_to == me)
        def _():
            pltpu.make_async_copy(hsend.at[head], hrecv.at[me], hrecv_sem).start()

        return carry

    lax.fori_loop(0, heads, send_heavy, 0)
    send_to_all(send_a, recv_a.at[me], send_a_sem, recv_a_sem)
    wait_bytes(cnt_group, cnt_sem)
    share_counts(
        cnt_group, cnt_recv.at[seq_at], heads,
        lambda step: (lax.rem(seq_at + step, heads), clu_at), cnt2_send_sem, cnt2_sem,
    )

    def pack_b(at, carry):
        for pair, packed in pack_heads(at, 2 * TOK + 16, TOK):
            put_units(send_b, at, packed, pair, 1)
        return carry

    lax.fori_loop(0, heads // 2, pack_b, 0)
    send_to_all(send_b, recv_b.at[me], send_b_sem, recv_b_sem)

    wait_bytes(cnt_recv, cnt2_sem)
    seen = cnt_recv[...].reshape(TOK, TOK)
    heavies = jnp.min(jnp.where(seen == 4.0, lane_f, 999.0), axis=1, keepdims=True)
    heavy_all = jnp.min(heavies, axis=0, keepdims=True)
    light = lane_f != heavy_all
    more = jnp.where(light, jnp.maximum(seen - 1.0, 0.0), 0.0)
    in_group = jnp.where(sub // 16 == lane, one, zero).astype(jnp.bfloat16)
    per_group = bf16_dot(more.astype(jnp.bfloat16), in_group)
    bad = jnp.where((per_group > 8.0) | (heavies != heavy_all), one, zero)
    per_cluster = jnp.sum(more, axis=0, keepdims=True)
    bad = jnp.maximum(bad, jnp.where(per_cluster > OVC, one, zero))
    flag_ref[0, 0] = jnp.max(bad).astype(jnp.int32)

    valid = jnp.where((seen > 0.0) & light, one, zero)
    group_t[...] = more.T
    mine = pl.ds(pl.multiple_of(clu_at * 16, 16), 16)
    more_g = group_t[mine, :]
    more_g_low = more_g.astype(jnp.bfloat16)
    sub16 = lax.broadcasted_iota(jnp.int32, (16, 16), 0)
    lane16 = lax.broadcasted_iota(jnp.int32, (16, 16), 1)
    earlier = jnp.where(lane16 < sub16, 1.0, 0.0).astype(jnp.bfloat16)
    offset = bf16_dot(earlier, more_g_low)
    ahead = jnp.where(sub < lane, one, zero).astype(jnp.bfloat16)
    start = bf16_dot(more_g_low, ahead)
    at_cluster = lax.broadcasted_iota(jnp.int32, (16, TOK), 0).astype(jnp.float32)
    rows = []
    for s in range(8):
        held = (offset <= float(s)) & (offset + more_g > float(s))
        index = at_cluster * float(OVC) + start + (float(s) - offset) + 1.0
        rows.append(jnp.sum(jnp.where(held, index, 0.0), axis=0, keepdims=True) - 1.0)
    slot_row = jnp.concatenate(rows, axis=0)
    slots_t[...] = jnp.concatenate(
        [slot_row, jnp.full((TOK - 8, TOK), -1.0, jnp.float32)], axis=0
    ).T

    block_col = jnp.concatenate([sub_f] * 8, axis=0).astype(jnp.bfloat16)
    slot_col = jnp.concatenate([one * float(s + 1) for s in range(8)], axis=0).astype(
        jnp.bfloat16
    )
    places = jnp.concatenate([block_col, slot_col], axis=1)
    chunk = 4
    first_row = lax.broadcasted_iota(jnp.int32, (1, TOK), 1).astype(jnp.float32) * 16.0

    def plan_chunk(at, carry):
        want = (
            lax.broadcasted_iota(jnp.int32, (chunk * OVC, TOK), 0) + at * (chunk * OVC)
        ).astype(jnp.float32)
        chosen = jnp.concatenate(
            [jnp.where(slot_row[s : s + 1, :] == want, 1.0, 0.0) for s in range(8)], axis=1
        ).astype(jnp.bfloat16)
        pick[pl.ds(pl.multiple_of(at * chunk * OVC, 128), chunk * OVC), :] = chosen
        found = bf16_dot(chosen, places)
        for c in range(chunk):
            part = found[c * OVC : (c + 1) * OVC]
            slot_part = part[:, DH:]
            where = jnp.where(slot_part > 0.0, part[:, :DH] * 16.0 + slot_part, FAR)
            padded = jnp.concatenate(
                [where, jnp.full((TOK - OVC, TOK), FAR, jnp.float32)], axis=0
            )
            cluster = at * chunk + c
            held = jnp.where(lane == clu_at * 16 + cluster, valid, 0.0)
            held = jnp.max(held, axis=1, keepdims=True) > 0.0
            key_pos[cluster, pl.ds(0, TOK), :] = jnp.where(held, sub_f * 16.0, FAR)
            key_pos[cluster, pl.ds(TOK, OVC), :] = where
            query_row = jnp.concatenate([first_row, padded.T[0:1, :]], axis=1)
            query_pos[cluster] = jnp.broadcast_to(query_row, (8, 2 * TOK))
        return carry

    lax.fori_loop(0, 16 // chunk, plan_chunk, 0)

    def plan_slot(s, carry):
        pick_s = jnp.max(jnp.where(lane == s, slots_t[...], -1.0), axis=1, keepdims=True)
        want = lax.broadcasted_iota(jnp.int32, (TOK, 16 * OVC), 1).astype(jnp.float32)
        onehot[pl.ds(pl.multiple_of(s * TOK, TOK), TOK), :] = jnp.where(
            pick_s == want, 1.0, 0.0
        ).astype(jnp.bfloat16)
        return carry

    lax.fori_loop(0, 8, plan_slot, 0)

    perm = flip_perm()

    def arrange(source, target, units):
        def one_set(at, carry):
            blocks = pl.ds(pl.multiple_of(at * SET, SET), SET)
            rows = jnp.concatenate(
                [source(blocks, unit).reshape(SET * 16, DH) for unit in range(units)], axis=1
            )
            turned = bf16_dot(perm, rows).astype(jnp.bfloat16)
            for unit in range(units):
                target(
                    blocks, unit, turned[:, unit * DH : (unit + 1) * DH].reshape(16, SET, DH)
                )
            return carry

        lax.fori_loop(0, devices // SET, one_set, 0, unroll=2)

    def put_table(first):
        def put(blocks, unit, value):
            table[first + unit, :, blocks, :] = value

        return put

    @pl.when(is_heavy_owner)
    def _():
        wait_bytes(hrecv, hrecv_sem)

        def put_heavy(blocks, unit, value):
            htable[:, blocks, :] = value

        arrange(lambda blocks, unit: hrecv[blocks], put_heavy, 1)
        k_h, v_h = [htable[4 * a : 4 * a + 4].reshape(4 * TOK, DH) for a in (1, 2)]
        hacc[...] = jnp.zeros_like(hacc)
        key_sub = lax.broadcasted_iota(jnp.int32, (4 * TOK, TOK), 0)
        key_at = lax.rem(key_sub, TOK) * 4 + lax.div(key_sub, TOK)
        query_at = lax.broadcasted_iota(jnp.int32, (4 * TOK, TOK), 1) * 4

        def heavy_tile(s, carry):
            out, dq, dk, dv = attend(
                htable[s], k_h, v_h, htable[12 + s], key_at <= query_at + s, inv_root
            )
            hacc[2, pl.ds(pl.multiple_of(s * TOK, TOK), TOK)] = out.astype(jnp.float32)
            hacc[3, pl.ds(pl.multiple_of(s * TOK, TOK), TOK)] = dq.astype(jnp.float32)
            hacc[0] += dk
            hacc[1] += dv
            return carry

        lax.fori_loop(0, 4, heavy_tile, 0)
        for array, at in enumerate((2, 3, 0, 1)):
            htable[4 * array : 4 * array + 4] = (
                hacc[at].astype(jnp.bfloat16).reshape(4, TOK, DH)
            )

        def put_hresult(blocks, unit, value):
            hresult[blocks] = value

        arrange(lambda blocks, unit: htable[:, blocks, :], put_hresult, 1)
        send_to_all(hresult, hback.at[seq_at], hres_sem, hback_sem)

    wait_bytes(recv_a, recv_a_sem)
    arrange(lambda blocks, unit: recv_a[blocks, unit], put_table(0), 4)

    def over_rows(array):
        return table[2 + array // 2, (array % 2) * 8 : (array % 2) * 8 + 8].reshape(
            8 * TOK, DH
        )

    loose = jnp.concatenate([over_rows(array) for array in range(4)], axis=1)

    def gather_chunk(at, carry):
        chosen = pick[pl.ds(pl.multiple_of(at * chunk * OVC, 128), chunk * OVC), :]
        found = bf16_dot(chosen, loose).astype(jnp.bfloat16)
        for c in range(chunk):
            for array in range(4):
                over[array, at * chunk + c] = found[
                    c * OVC : (c + 1) * OVC, array * DH : (array + 1) * DH
                ]
        return carry

    lax.fori_loop(0, 16 // chunk, gather_chunk, 0)

    pad_rows = jnp.zeros((TOK - OVC, DH), jnp.bfloat16)

    def load_cluster(tile, j, c):
        rows = [
            jnp.concatenate([table[tile + a // 2, (a % 2) * 8 + j], over[a, c]], axis=0)
            for a in range(4)
        ]
        for a in (0, 3):
            rows[a] = jnp.concatenate([rows[a], pad_rows], axis=0)
        key_at = key_pos[c]
        allowed = jnp.concatenate([key_at, key_at], axis=1) <= query_pos[c, 0:1, :]
        return rows + [allowed]

    def cluster_pair(tile, first):
        def one_pair(at, carry):
            spots = [(2 * at + i, first + 2 * at + i) for i in range(2)]
            loaded = [load_cluster(tile, j, c) for j, c in spots]
            found = [attend(*arrays, inv_root) for arrays in loaded]
            for (j, c), results in zip(spots, found):
                for a, value in enumerate(results):
                    value = value.astype(jnp.bfloat16)
                    table[tile + a // 2, (a % 2) * 8 + j] = value[:TOK]
                    over_res[
                        pl.ds(pl.multiple_of(c * OVC, 32), OVC), pl.ds(a * DH, DH)
                    ] = value[TOK : TOK + OVC]
            return carry

        lax.fori_loop(0, 4, one_pair, 0)

    def put_a(blocks, unit, value):
        result_a[blocks, unit] = value

    def put_b(blocks, unit, value):
        result_b[blocks, unit] = value

    cluster_pair(0, 0)
    arrange(lambda blocks, unit: table[unit, :, blocks, :], put_a, 2)
    send_to_all(result_a, back_a.at[me], res_a_sem, back_a_sem)

    wait_bytes(recv_b, recv_b_sem)
    arrange(lambda blocks, unit: recv_b[blocks, unit], put_table(4), 2)
    cluster_pair(4, 8)

    def spread_chunk(at, carry):
        found = bf16_dot(
            onehot[pl.ds(pl.multiple_of(at * 256, 256), 256), :], over_res[...]
        ).astype(jnp.bfloat16)
        for array in range(4):
            table[2 + array // 2, pl.ds((array % 2) * 8 + at * 2, 2)] = found[
                :, array * DH : (array + 1) * DH
            ].reshape(2, TOK, DH)
        return carry

    lax.fori_loop(0, 4, spread_chunk, 0)
    arrange(lambda blocks, unit: table[2 + unit, :, blocks, :], put_b, 4)
    send_to_all(result_b, back_b.at[me], res_b_sem, back_b_sem)

    wait_bytes(hback, hback_sem)
    wait_bytes(back_a, back_a_sem)
    wait_bytes(back_b, back_b_sem)

    def unpack_heads(at, carry):
        cols = pl.ds(pl.multiple_of(at * 2 * DH, 2 * DH), 2 * DH)
        for pair, refs in enumerate(((out_ref, dq_ref), (dk_ref, dv_ref))):
            sides = []
            for k in range(2):
                head = 2 * at + k
                owners = pl.ds(head * groups, groups)
                sides.append(
                    jnp.concatenate(
                        [
                            back_a[owners, pair].reshape(TOK, DH),
                            back_b[owners, pair].reshape(TOK, DH),
                            back_b[owners, 2 + pair].reshape(TOK, DH),
                            hback[head],
                            jnp.zeros((TOK - 16, DH), jnp.bfloat16),
                        ],
                        axis=0,
                    )
                )
            found = bf16_dot(unpack_mat[pair], jnp.concatenate(sides, axis=1))
            for half in range(2):
                refs[half][:, cols] = found[half * TOK : (half + 1) * TOK].astype(jnp.bfloat16)
        return carry

    lax.fori_loop(0, heads // 2, unpack_heads, 0, unroll=2)

    others = pl.ds(0, devices - 1)
    wait_bytes(cnt_group.at[pl.ds(0, groups - 1)], cnt_send_sem)
    wait_bytes(cnt_recv.at[pl.ds(0, heads - 1)], cnt2_send_sem)
    wait_bytes(send_a.at[others], send_a_sem)
    wait_bytes(send_b.at[others], send_b_sem)
    wait_bytes(result_a.at[others], res_a_sem)
    wait_bytes(result_b.at[others], res_b_sem)

    @pl.when(is_heavy_owner)
    def _():
        wait_bytes(hsend.at[pl.ds(0, heads - 1)], hsend_sem)
        wait_bytes(hresult.at[others], hres_sem)

    @pl.when(jnp.logical_not(is_heavy_owner))
    def _():
        wait_bytes(hsend, hsend_sem)


def fast_path(queries, key_rows, value_rows, out_grad, cluster_ids):
    tok_rows, columns = queries.shape
    heads = columns // DH
    groups = lax.axis_size("clu")
    devices = lax.axis_size("seq") * groups
    low = jnp.bfloat16
    wide = jnp.float32
    rows = jax.ShapeDtypeStruct((tok_rows, columns), low)
    vmem = pl.BlockSpec(memory_space=pltpu.VMEM)
    smem = pl.BlockSpec(memory_space=pltpu.SMEM)
    return pl.pallas_call(
        fast_kernel,
        out_shape=[rows] * 4 + [jax.ShapeDtypeStruct((1, 1), jnp.int32)],
        in_specs=[vmem] * 5,
        out_specs=[vmem] * 4 + [smem],
        scratch_shapes=[
            pltpu.VMEM((1, TOK), wide),
            pltpu.VMEM((groups, 1, TOK), wide),
            pltpu.VMEM((heads, groups, 1, TOK), wide),
            pltpu.VMEM((2, 3 * TOK + 16, 2 * TOK), low),
            pltpu.VMEM((2, 2 * TOK, 4 * TOK), low),
            pltpu.VMEM((devices, 4, 16, DH), low),
            pltpu.VMEM((devices, 2, 16, DH), low),
            pltpu.VMEM((devices, 4, 16, DH), low),
            pltpu.VMEM((devices, 2, 16, DH), low),
            pltpu.VMEM((6, 16, devices, DH), low),
            pltpu.VMEM((TOK, TOK), wide),
            pltpu.VMEM((TOK, TOK), wide),
            pltpu.VMEM((4, 16, OVC, DH), low),
            pltpu.VMEM((16, TOK + OVC, TOK), wide),
            pltpu.VMEM((16, 8, 2 * TOK), wide),
            pltpu.VMEM((16 * OVC, 8 * TOK), low),
            pltpu.VMEM((8 * TOK, 16 * OVC), low),
            pltpu.VMEM((16 * OVC, 4 * DH), low),
            pltpu.VMEM((devices, 2, 16, DH), low),
            pltpu.VMEM((devices, 4, 16, DH), low),
            pltpu.VMEM((devices, 2, 16, DH), low),
            pltpu.VMEM((devices, 4, 16, DH), low),
            pltpu.VMEM((heads, 16, DH), low),
            pltpu.VMEM((devices, 16, DH), low),
            pltpu.VMEM((16, devices, DH), low),
            pltpu.VMEM((4, 4 * TOK, DH), wide),
            pltpu.VMEM((devices, 16, DH), low),
            pltpu.VMEM((heads, 16, DH), low),
        ]
        + [pltpu.SemaphoreType.DMA] * 16,
        compiler_params=pltpu.CompilerParams(
            collective_id=0, has_side_effects=True, vmem_limit_bytes=56 * 1024 * 1024
        ),
    )(cluster_ids.reshape(1, tok_rows), queries, key_rows, value_rows, out_grad)


def per_device(queries, key_rows, value_rows, out_grad, cluster_ids):
    arrays = (queries, key_rows, value_rows, out_grad, cluster_ids)
    *fast, flag = fast_path(*arrays)
    return lax.cond(
        flag.reshape(()) != 0,
        lambda arrays, fast: full_capacity(*arrays),
        lambda arrays, fast: tuple(fast),
        arrays,
        tuple(fast),
    )


def solution(mesh):
    in_specs = (
        P(("seq", "clu"), None),
        P(("seq", "clu"), None),
        P(("seq", "clu"), None),
        P(("seq", "clu"), None),
        P(("seq", "clu")),
    )
    out_specs = (
        P(("seq", "clu"), None),
        P(("seq", "clu"), None),
        P(("seq", "clu"), None),
        P(("seq", "clu"), None),
    )
    return jax.shard_map(
        per_device, mesh=mesh, in_specs=in_specs, out_specs=out_specs, check_vma=False
    )
```

```python
import math

import jax
import jax.numpy as jnp
from jax import lax
from jax.experimental import pallas as pl
from jax.experimental.pallas import tpu as pltpu
from jax.sharding import PartitionSpec as P

DH = 128
TOK = 128
OVC = 96
SET = 16
FAR = 1e9
MESH = pl.DeviceIdType.MESH


masked = -1e30


def contract_last(left, right):
    return lax.dot_general(
        left, right, (((1,), (1,)), ((), ())), preferred_element_type=jnp.float32
    )


def contract_first(left, right):
    return lax.dot_general(
        left, right, (((0,), (0,)), ((), ())), preferred_element_type=jnp.float32
    )


def softmax_rows(query_head, key_head, allowed, inv_root):
    scores = contract_last(query_head, key_head) * inv_root
    scores = jnp.where(allowed, scores, masked)
    row_max = jnp.max(scores, axis=1, keepdims=True)
    weights = jnp.exp(scores - row_max)
    row_sum = jnp.sum(weights, axis=1, keepdims=True)
    return (weights / row_sum).astype(jnp.bfloat16)


def head_slice(array, head_index):
    return lax.dynamic_slice_in_dim(array, head_index * DH, DH, 1)


def full_capacity(queries, key_rows, value_rows, out_grad, cluster_ids):
    seq_count = lax.axis_size("seq")
    clu_count = lax.axis_size("clu")
    devices = seq_count * clu_count
    tok_rows = queries.shape[0]
    columns = queries.shape[1]
    head_count = columns // DH
    most_rows = 4 * tok_rows // devices
    capacity = most_rows * devices
    inv_root = 1.0 / math.sqrt(DH)
    owners = jnp.arange(devices, dtype=jnp.int32)
    member = (cluster_ids[:, None] == owners[None, :]).astype(jnp.int32)
    running = jnp.cumsum(member, axis=0) - 1
    slot_rank = jnp.sum(member * running, axis=1)
    sent_counts = jnp.sum(member, axis=0).reshape(devices, 1)
    slot_index = cluster_ids * most_rows + slot_rank
    stacked = jnp.concatenate([queries, key_rows, value_rows], axis=1)
    width_in = stacked.shape[1]
    packed = jnp.zeros((devices * most_rows, width_in), jnp.bfloat16).at[slot_index].set(stacked)
    packed = packed.reshape(devices, most_rows, width_in)
    got_rows, got_counts = (
        lax.all_to_all(packed, ("seq", "clu"), split_axis=0, concat_axis=0, tiled=True),
        lax.all_to_all(sent_counts, ("seq", "clu"), split_axis=0, concat_axis=0, tiled=True),
    )
    got_counts = got_counts.reshape(devices)
    starts = jnp.cumsum(got_counts) - got_counts
    live_total = jnp.sum(got_counts)
    within = jnp.arange(most_rows, dtype=jnp.int32)
    target = jnp.where(
        within[None, :] < got_counts[:, None], starts[:, None] + within[None, :], capacity
    )
    target = target.reshape(devices * most_rows)
    gathered = (
        jnp.zeros((capacity, width_in), jnp.bfloat16)
        .at[target]
        .set(got_rows.reshape(devices * most_rows, width_in), mode="drop")
    )
    query_block = gathered[:, :columns]
    key_block = gathered[:, columns : 2 * columns]
    value_block = gathered[:, 2 * columns : 3 * columns]
    positions = jnp.arange(capacity, dtype=jnp.int32)
    allowed = (positions[None, :] <= positions[:, None]) & (positions[None, :] < live_total)

    def forward_head(head_index, mixed_rows):
        weights_low = softmax_rows(
            head_slice(query_block, head_index),
            head_slice(key_block, head_index),
            allowed,
            inv_root,
        )
        out_head = jnp.dot(
            weights_low, head_slice(value_block, head_index), preferred_element_type=jnp.float32
        ).astype(jnp.bfloat16)
        return lax.dynamic_update_slice_in_dim(mixed_rows, out_head, head_index * DH, 1)

    mixed_rows = lax.fori_loop(
        0, head_count, forward_head, jnp.zeros((capacity, columns), jnp.bfloat16)
    )
    back_index = jnp.minimum(target, capacity - 1)
    outgoing = jnp.take(mixed_rows, back_index, axis=0).reshape(devices, most_rows, columns)
    grad_packed = (
        jnp.zeros((devices * most_rows, columns), jnp.bfloat16).at[slot_index].set(out_grad)
    )
    grad_packed = grad_packed.reshape(devices, most_rows, columns)
    returned = lax.all_to_all(outgoing, ("seq", "clu"), split_axis=0, concat_axis=0, tiled=True)
    got_grad = lax.all_to_all(grad_packed, ("seq", "clu"), split_axis=0, concat_axis=0, tiled=True)
    attention_out = jnp.take(returned.reshape(devices * most_rows, columns), slot_index, axis=0)
    grad_block = (
        jnp.zeros((capacity, columns), jnp.bfloat16)
        .at[target]
        .set(got_grad.reshape(devices * most_rows, columns), mode="drop")
    )
    delta_rows = jnp.sum(
        (grad_block.astype(jnp.float32) * mixed_rows.astype(jnp.float32)).reshape(
            capacity, head_count, DH
        ),
        axis=2,
    )

    def backward_head(head_index, grad_rows):
        query_head = head_slice(query_block, head_index)
        key_head = head_slice(key_block, head_index)
        value_head = head_slice(value_block, head_index)
        grad_head = head_slice(grad_block, head_index)
        weights_low = softmax_rows(query_head, key_head, allowed, inv_root)
        prob_grad = contract_last(grad_head, value_head)
        delta_head = lax.dynamic_slice_in_dim(delta_rows, head_index, 1, 1)
        score_grad = (weights_low.astype(jnp.float32) * (prob_grad - delta_head)).astype(
            jnp.bfloat16
        )
        query_part = (
            jnp.dot(score_grad, key_head, preferred_element_type=jnp.float32) * inv_root
        ).astype(jnp.bfloat16)
        key_part = (contract_first(score_grad, query_head) * inv_root).astype(jnp.bfloat16)
        value_part = contract_first(weights_low, grad_head).astype(jnp.bfloat16)
        grad_rows = lax.dynamic_update_slice_in_dim(grad_rows, query_part, head_index * DH, 1)
        grad_rows = lax.dynamic_update_slice_in_dim(
            grad_rows, key_part, columns + head_index * DH, 1
        )
        return lax.dynamic_update_slice_in_dim(
            grad_rows, value_part, 2 * columns + head_index * DH, 1
        )

    grad_rows = lax.fori_loop(
        0, head_count, backward_head, jnp.zeros((capacity, 3 * columns), jnp.bfloat16)
    )
    outgoing_grads = jnp.take(grad_rows, back_index, axis=0).reshape(
        devices, most_rows, 3 * columns
    )
    returned_grads = lax.all_to_all(
        outgoing_grads, ("seq", "clu"), split_axis=0, concat_axis=0, tiled=True
    )
    picked = jnp.take(returned_grads.reshape(devices * most_rows, 3 * columns), slot_index, axis=0)
    return (
        attention_out,
        picked[:, :columns],
        picked[:, columns : 2 * columns],
        picked[:, 2 * columns :],
    )


def bf16_dot(left, right):
    return jnp.dot(left, right, preferred_element_type=jnp.float32)


def flip_perm():
    row = lax.broadcasted_iota(jnp.int32, (SET * 16, SET * 16), 0)
    col = lax.broadcasted_iota(jnp.int32, (SET * 16, SET * 16), 1)
    swapped = (col % 16) * 16 + col // 16
    return (row == swapped).astype(jnp.float32).astype(jnp.bfloat16)


def attend(q, k, v, g, allowed, inv_root):
    raw = jnp.where(allowed, contract_last(k, q), masked)
    most = jnp.max(raw, axis=0, keepdims=True)
    weights = jnp.exp2((raw - most) * (inv_root * math.log2(math.e)))
    prob = weights * (1.0 / jnp.sum(weights, axis=0, keepdims=True))
    prob_low = prob.astype(jnp.bfloat16)
    prob_grad = contract_last(v, g)
    delta = jnp.sum(prob * prob_grad, axis=0, keepdims=True)
    score_grad = (prob * (prob_grad - delta)).astype(jnp.bfloat16)
    out = contract_first(v, prob_low).T.astype(jnp.bfloat16)
    dq = (contract_first(k, score_grad).T * inv_root).astype(jnp.bfloat16)
    dk = bf16_dot(score_grad, q) * inv_root
    dv = bf16_dot(prob_low, g)
    return out, dq, dk, dv


def fast_kernel(
    ids_ref, q_ref, k_ref, v_ref, g_ref,
    out_ref, dq_ref, dk_ref, dv_ref, flag_ref,
    cnt_send, cnt_group, cnt_recv, pack_mat, pack_over, unpack_mat,
    send_a, send_b, send_c, recv_a, recv_b, recv_c, table, slot_col, group_t,
    over, key_pos, query_pos, pick, onehot, loose, over_res,
    result_a, result_b, result_c, back_a, back_b, back_c,
    hsend, hrecv, htable, hacc, hresult, hback,
    cnt_send_sem, cnt_sem, cnt2_send_sem, cnt2_sem,
    send_a_sem, recv_a_sem, send_b_sem, recv_b_sem, send_c_sem, recv_c_sem,
    res_a_sem, back_a_sem, res_b_sem, back_b_sem, res_c_sem, back_c_sem,
    hsend_sem, hrecv_sem, hres_sem, hback_sem,
):
    seq_at = lax.axis_index("seq")
    clu_at = lax.axis_index("clu")
    groups = lax.axis_size("clu")
    heads = lax.axis_size("seq")
    devices = heads * groups
    me = seq_at * groups + clu_at
    inv_root = 1.0 / math.sqrt(DH)
    is_heavy_owner = lax.rem(seq_at, groups) == clu_at
    at_x, at_z = lax.div(seq_at, 4), lax.rem(seq_at, 4)
    at_y, at_core = lax.div(clu_at, 2), lax.rem(clu_at, 2)

    def coords(device):
        return (lax.div(device, groups), lax.rem(device, groups))

    def turn(by):
        return by + at_core * (4 - 2 * by)

    eight = []
    for by_x, by_z, by_clu in zip(
        (0, 3, 2, 1, 0, 3, 2, 0), (0, 3, 2, 1, 1, 0, 3, 2), (0, 4, 6, 7, 2, 5, 1, 3)
    ):
        y = lax.rem(at_y + turn(by_clu // 2), 4)
        eight.append((turn(by_x), turn(by_z), y * 2 + lax.rem(at_core + by_clu % 2, 2)))

    def send_steps(first, count, source, target, send_sem, recv_sem):
        def one_eight(step, carry):
            by = lax.rem(step * 11, 16)
            by_x, by_z = lax.div(by, 4), lax.rem(by, 4)
            x = at_x + turn(by_x)
            z = at_z + turn(by_z)
            for j, (more_x, more_z, clu_to) in enumerate(eight):
                seq_to = lax.rem(x + more_x, 4) * 4 + lax.rem(z + more_z, 4)

                def start():
                    pltpu.make_async_remote_copy(
                        src_ref=source.at[seq_to * groups + clu_to],
                        dst_ref=target,
                        send_sem=send_sem,
                        recv_sem=recv_sem,
                        device_id=(seq_to, clu_to),
                        device_id_type=MESH,
                    ).start()

                if j == 0:
                    pl.when(step > 0)(start)
                else:
                    start()
            return carry

        lax.fori_loop(first, first + count, one_eight, 0)

    def send_own(source, target, recv_sem):
        pltpu.make_async_copy(source.at[me], target, recv_sem).start()

    def send_to_all(source, target, send_sem, recv_sem):
        send_steps(0, devices // 8, source, target, send_sem, recv_sem)
        send_own(source, target, recv_sem)

    def wait_bytes(ref, sem):
        pltpu.make_async_copy(ref, ref, sem).wait()

    barrier = pltpu.get_barrier_semaphore()

    def greet(step, carry):
        pl.semaphore_signal(
            barrier, inc=1, device_id=coords(lax.rem(me + step, devices)), device_id_type=MESH
        )
        return carry

    lax.fori_loop(1, devices, greet, 0)

    sub = lax.broadcasted_iota(jnp.int32, (TOK, TOK), 0)
    lane = lax.broadcasted_iota(jnp.int32, (TOK, TOK), 1)
    sub_f = sub.astype(jnp.float32)
    lane_f = lane.astype(jnp.float32)
    ids_l = jnp.broadcast_to(ids_ref[...].astype(jnp.float32), (TOK, TOK))
    ids_s = ids_l.T
    one = jnp.ones((TOK, TOK), jnp.float32)
    zero = jnp.zeros((TOK, TOK), jnp.float32)
    same = ids_l == ids_s
    rank_l = jnp.sum(jnp.where(same & (sub < lane), one, zero), axis=0, keepdims=True)
    rank_s = jnp.sum(jnp.where(same & (lane < sub), one, zero), axis=1, keepdims=True)
    count_l = jnp.sum(jnp.where(same, one, zero), axis=0, keepdims=True)
    cnt_send[...] = jnp.sum(jnp.where(ids_s == lane_f, one, zero), axis=0, keepdims=True)
    ids_row = ids_l[0:1, :]
    heavy = jnp.min(jnp.where(count_l == 4.0, ids_row, 999.0), axis=1, keepdims=True)
    group_l = jnp.floor(ids_l * (1.0 / 16.0))
    group_s = jnp.floor(ids_s * (1.0 / 16.0))
    before = (group_l == group_s) & (ids_s != heavy) & (rank_s >= 1.0)
    before = before & ((ids_s < ids_l) | (same & (sub < lane)))
    over_at = jnp.sum(jnp.where(before, one, zero), axis=0, keepdims=True)
    light_l = ids_l != heavy
    slot_group = (sub // 16).astype(jnp.float32)
    in_tile = sub % 16
    for tile in range(4):
        cluster = slot_group * 16.0 + (in_tile % 4 + 4 * tile).astype(jnp.float32)
        first_rows = (ids_l == cluster) & (rank_l == 0.0) & light_l
        for array in range(4):
            matrix = jnp.where(first_rows & (in_tile // 4 == array), one, zero)
            at_row = tile * TOK + (16 if tile else 0)
            pack_mat[pl.ds(at_row, TOK), pl.ds(array * TOK, TOK)] = matrix.astype(jnp.bfloat16)
            unpack_mat[
                array // 2, pl.ds((array % 2) * TOK, TOK), pl.ds(tile * TOK, TOK)
            ] = matrix.T.astype(jnp.bfloat16)
    later_rows = (group_l == slot_group) & light_l & (rank_l >= 1.0)
    later_rows = later_rows & (over_at == (sub % 8).astype(jnp.float32))
    for half in range(2):
        matrix = jnp.where(later_rows & (in_tile // 8 == half), one, zero)
        pack_over[:, pl.ds(half * TOK, TOK)] = matrix.astype(jnp.bfloat16)
        turned = matrix.T.astype(jnp.bfloat16)
        for pair in range(2):
            unpack_mat[pair, pl.ds(half * TOK, TOK), pl.ds(4 * TOK, TOK)] = turned
    for array in range(4):
        chosen = (ids_l == heavy) & (rank_l == (sub % 4).astype(jnp.float32))
        chosen = chosen & (sub // 4 == array) & (sub < 16)
        matrix = jnp.where(chosen, one, zero)
        unpack_mat[array // 2, pl.ds((array % 2) * TOK, TOK), pl.ds(5 * TOK, TOK)] = (
            matrix.T.astype(jnp.bfloat16)
        )
        pack_mat[pl.ds(TOK, 16), pl.ds(array * TOK, TOK)] = matrix[0:16, :].astype(jnp.bfloat16)

    pl.semaphore_wait(barrier, devices - 1)

    def share_counts(source, target, count, to, send_sem, recv_sem):
        def one_peer(step, carry):
            pltpu.make_async_remote_copy(
                src_ref=source,
                dst_ref=target,
                send_sem=send_sem,
                recv_sem=recv_sem,
                device_id=to(step),
                device_id_type=MESH,
            ).start()
            return carry

        lax.fori_loop(1, count, one_peer, 0)
        pltpu.make_async_copy(source, target, recv_sem).start()

    share_counts(
        cnt_send, cnt_group.at[clu_at], groups,
        lambda step: (seq_at, lax.rem(clu_at + step, groups)), cnt_send_sem, cnt_sem,
    )

    def head_rows(at):
        cols = pl.ds(pl.multiple_of(at * 2 * DH, 2 * DH), 2 * DH)
        return [ref[:, cols] for ref in (q_ref, k_ref, v_ref, g_ref)]

    def put_tile(target, at, tile, packed):
        low = packed.astype(jnp.bfloat16)
        for k in range(2):
            target[pl.ds((2 * at + k) * groups, groups), tile] = low[
                :, k * DH : (k + 1) * DH
            ].reshape(groups, 16, DH)

    def pack_a(at, carry):
        rows = head_rows(at)
        packed = bf16_dot(pack_mat[pl.ds(0, TOK + 16), :], jnp.concatenate(rows, axis=0))
        put_tile(send_a, at, 0, packed[:TOK])
        for k in range(2):
            hsend[2 * at + k] = packed[TOK:, k * DH : (k + 1) * DH].astype(jnp.bfloat16)
        for pair in range(2):
            both = jnp.concatenate(rows[2 * pair : 2 * pair + 2], axis=0)
            put_tile(send_a, at, 1 + pair, bf16_dot(pack_over[...], both))
        return carry

    lax.fori_loop(0, heads // 2, pack_a, 0, unroll=2)

    def send_heavy(step, carry):
        head = lax.rem(seq_at + step, heads)
        clu_to = lax.rem(head, groups)

        @pl.when(head * groups + clu_to != me)
        def _():
            pltpu.make_async_remote_copy(
                src_ref=hsend.at[head],
                dst_ref=hrecv.at[me],
                send_sem=hsend_sem,
                recv_sem=hrecv_sem,
                device_id=(head, clu_to),
                device_id_type=MESH,
            ).start()

        @pl.when(head * groups + clu_to == me)
        def _():
            pltpu.make_async_copy(hsend.at[head], hrecv.at[me], hrecv_sem).start()

        return carry

    lax.fori_loop(0, heads, send_heavy, 0)
    send_to_all(send_a, recv_a.at[me], send_a_sem, recv_a_sem)
    wait_bytes(cnt_group, cnt_sem)
    share_counts(
        cnt_group, cnt_recv.at[seq_at], heads,
        lambda step: (lax.rem(seq_at + step, heads), clu_at), cnt2_send_sem, cnt2_sem,
    )

    def pack_bc(at, carry):
        rows = jnp.concatenate(head_rows(at), axis=0)
        packed = bf16_dot(pack_mat[pl.ds(TOK + 16, 3 * TOK), :], rows)
        put_tile(send_b, at, 0, packed[:TOK])
        put_tile(send_b, at, 1, packed[TOK : 2 * TOK])
        put_tile(send_c, at, 0, packed[2 * TOK :])
        return carry

    lax.fori_loop(0, heads // 2, pack_bc, 0)
    send_to_all(send_b, recv_b.at[me], send_b_sem, recv_b_sem)
    send_to_all(send_c, recv_c.at[me], send_c_sem, recv_c_sem)

    wait_bytes(cnt_recv, cnt2_sem)
    seen = cnt_recv[...].reshape(TOK, TOK)
    heavies = jnp.min(jnp.where(seen == 4.0, lane_f, 999.0), axis=1, keepdims=True)
    heavy_all = jnp.min(heavies, axis=0, keepdims=True)
    light = lane_f != heavy_all
    more = jnp.where(light, jnp.maximum(seen - 1.0, 0.0), 0.0)
    in_group = jnp.where(sub // 16 == lane, one, zero).astype(jnp.bfloat16)
    per_group = bf16_dot(more.astype(jnp.bfloat16), in_group)
    bad = jnp.where((per_group > 8.0) | (heavies != heavy_all), one, zero)
    per_cluster = jnp.sum(more, axis=0, keepdims=True)
    bad = jnp.maximum(bad, jnp.where(per_cluster > OVC, one, zero))
    flag_ref[0, 0] = jnp.max(bad).astype(jnp.int32)

    valid = jnp.where((seen > 0.0) & light, one, zero)
    group_t[...] = more.T
    mine = pl.ds(pl.multiple_of(clu_at * 16, 16), 16)
    more_g = group_t[mine, :]
    more_g_low = more_g.astype(jnp.bfloat16)
    sub16 = lax.broadcasted_iota(jnp.int32, (16, 16), 0)
    lane16 = lax.broadcasted_iota(jnp.int32, (16, 16), 1)
    earlier = jnp.where(lane16 < sub16, 1.0, 0.0).astype(jnp.bfloat16)
    offset = bf16_dot(earlier, more_g_low)
    ahead = jnp.where(sub < lane, one, zero).astype(jnp.bfloat16)
    start = bf16_dot(more_g_low, ahead)
    at_cluster = lax.broadcasted_iota(jnp.int32, (16, TOK), 0).astype(jnp.float32)
    rows = []
    for s in range(8):
        held = (offset <= float(s)) & (offset + more_g > float(s))
        index = at_cluster * float(OVC) + start + (float(s) - offset) + 1.0
        rows.append(jnp.sum(jnp.where(held, index, 0.0), axis=0, keepdims=True) - 1.0)
    by_slot = jnp.concatenate(rows, axis=0) + 1.0
    high = jnp.floor(by_slot * (1.0 / 32.0))
    split = jnp.concatenate([high, by_slot - high * 32.0], axis=0).astype(jnp.bfloat16)
    wide_sub = lax.broadcasted_iota(jnp.int32, (TOK, 8 * TOK), 0)
    wide_lane = lax.broadcasted_iota(jnp.int32, (TOK, 8 * TOK), 1)
    spaced = bf16_dot(
        split, jnp.where(wide_lane // 8 == wide_sub, 1.0, 0.0).astype(jnp.bfloat16)
    )
    spaced = spaced[:8] * 32.0 + spaced[8:]
    spaced = jnp.where(wide_lane[:8] % 8 == wide_sub[:8], spaced, 0.0)
    slot_row = jnp.sum(spaced, axis=0, keepdims=True) - 1.0
    slot_col[...] = jnp.broadcast_to(slot_row, (TOK, 8 * TOK)).T

    tall = lax.broadcasted_iota(jnp.int32, (8 * TOK, TOK), 0)
    places = jnp.concatenate([tall // 8, tall % 8 + 1], axis=1).astype(jnp.float32)
    places = places.astype(jnp.bfloat16)
    chunk = 4
    first_row = lax.broadcasted_iota(jnp.int32, (1, TOK), 1).astype(jnp.float32) * 16.0

    def plan_chunk(at, carry):
        want = (
            lax.broadcasted_iota(jnp.int32, (chunk * OVC, TOK), 0) + at * (chunk * OVC)
        ).astype(jnp.float32)
        chosen = jnp.concatenate(
            [jnp.where(slot_row[:, s * TOK : (s + 1) * TOK] == want, 1.0, 0.0) for s in range(8)],
            axis=1,
        ).astype(jnp.bfloat16)
        pick[pl.ds(pl.multiple_of(at * chunk * OVC, 128), chunk * OVC), :] = chosen
        found = bf16_dot(chosen, places)
        for c in range(chunk):
            part = found[c * OVC : (c + 1) * OVC]
            slot_part = part[:, DH:]
            where = jnp.where(slot_part > 0.0, part[:, :DH] * 16.0 + slot_part, FAR)
            padded = jnp.concatenate(
                [where, jnp.full((TOK - OVC, TOK), FAR, jnp.float32)], axis=0
            )
            cluster = at * chunk + c
            held = jnp.where(lane == clu_at * 16 + cluster, valid, 0.0)
            held = jnp.max(held, axis=1, keepdims=True) > 0.0
            key_pos[cluster, pl.ds(0, TOK), :] = jnp.where(held, sub_f * 16.0, FAR)
            key_pos[cluster, pl.ds(TOK, OVC), :] = where
            query_row = jnp.concatenate([first_row, padded.T[0:1, :]], axis=1)
            query_pos[cluster] = jnp.broadcast_to(query_row, (8, 2 * TOK))
        return carry

    lax.fori_loop(0, 16 // chunk, plan_chunk, 0)

    def plan_slot(s, carry):
        rows = pl.ds(pl.multiple_of(s * TOK, TOK), TOK)
        for k in range(16 * OVC // TOK):
            onehot[rows, pl.ds(k * TOK, TOK)] = jnp.where(
                slot_col[rows, :] == lane_f + float(k * TOK), 1.0, 0.0
            ).astype(jnp.bfloat16)
        return carry

    lax.fori_loop(0, 8, plan_slot, 0)

    perm = flip_perm()

    def arrange(source, target, units):
        def two_sets(at, carry):
            blocks = [pl.ds(pl.multiple_of((2 * at + i) * SET, SET), SET) for i in range(2)]
            spots = [(held, unit) for held in blocks for unit in range(units)]
            rows = jnp.concatenate(
                [source(held, unit).reshape(SET * 16, DH) for held, unit in spots], axis=1
            )
            turned = bf16_dot(perm, rows).astype(jnp.bfloat16)
            for i, (held, unit) in enumerate(spots):
                target(held, unit, turned[:, i * DH : (i + 1) * DH].reshape(16, SET, DH))
            return carry

        lax.fori_loop(0, devices // (2 * SET), two_sets, 0, unroll=2)

    def put_table(first):
        def put(blocks, unit, value):
            table[first + unit, :, blocks, :] = value

        return put

    @pl.when(is_heavy_owner)
    def _():
        wait_bytes(hrecv, hrecv_sem)

        def put_heavy(blocks, unit, value):
            htable[:, blocks, :] = value

        arrange(lambda blocks, unit: hrecv[blocks], put_heavy, 1)
        k_h, v_h = [htable[4 * a : 4 * a + 4].reshape(4 * TOK, DH) for a in (1, 2)]
        hacc[...] = jnp.zeros_like(hacc)
        key_sub = lax.broadcasted_iota(jnp.int32, (4 * TOK, TOK), 0)
        key_at = lax.rem(key_sub, TOK) * 4 + lax.div(key_sub, TOK)
        query_at = lax.broadcasted_iota(jnp.int32, (4 * TOK, TOK), 1) * 4

        def heavy_tile(s, carry):
            out, dq, dk, dv = attend(
                htable[s], k_h, v_h, htable[12 + s], key_at <= query_at + s, inv_root
            )
            hacc[2, pl.ds(pl.multiple_of(s * TOK, TOK), TOK)] = out.astype(jnp.float32)
            hacc[3, pl.ds(pl.multiple_of(s * TOK, TOK), TOK)] = dq.astype(jnp.float32)
            hacc[0] += dk
            hacc[1] += dv
            return carry

        lax.fori_loop(0, 4, heavy_tile, 0)
        for array, at in enumerate((2, 3, 0, 1)):
            htable[4 * array : 4 * array + 4] = (
                hacc[at].astype(jnp.bfloat16).reshape(4, TOK, DH)
            )

        def put_hresult(blocks, unit, value):
            hresult[blocks] = value

        arrange(lambda blocks, unit: htable[:, blocks, :], put_hresult, 1)
        send_to_all(hresult, hback.at[seq_at], hres_sem, hback_sem)

    wait_bytes(recv_a, recv_a_sem)
    arrange(lambda blocks, unit: recv_a[blocks, 0], put_table(0), 1)

    def part_over(at, carry):
        blocks = pl.ds(pl.multiple_of(at * SET, SET), SET)
        rows = pl.ds(pl.multiple_of(at * TOK, TOK), TOK)
        for pair in range(2):
            held = recv_a[blocks, 1 + pair].astype(jnp.float32)
            for half in range(2):
                loose[rows, pl.ds((2 * pair + half) * DH, DH)] = (
                    held[:, half * 8 : half * 8 + 8, :].reshape(TOK, DH).astype(jnp.bfloat16)
                )
        return carry

    lax.fori_loop(0, devices // SET, part_over, 0, unroll=2)

    def gather_chunk(at, carry):
        chosen = pick[pl.ds(pl.multiple_of(at * chunk * OVC, 128), chunk * OVC), :]
        found = bf16_dot(chosen, loose[...]).astype(jnp.bfloat16)
        for c in range(chunk):
            for array in range(4):
                over[array, at * chunk + c] = found[
                    c * OVC : (c + 1) * OVC, array * DH : (array + 1) * DH
                ]
        return carry

    lax.fori_loop(0, 16 // chunk, gather_chunk, 0)

    pad_rows = jnp.zeros((TOK - OVC, DH), jnp.bfloat16)

    def load_cluster(tile, j):
        c = tile * 4 + j
        rows = [
            jnp.concatenate([table[tile, a * 4 + j], over[a, c]], axis=0) for a in range(4)
        ]
        for a in (0, 3):
            rows[a] = jnp.concatenate([rows[a], pad_rows], axis=0)
        key_at = key_pos[c]
        allowed = jnp.concatenate([key_at, key_at], axis=1) <= query_pos[c, 0:1, :]
        return rows + [allowed]

    def attend_tiles(first, tiles, beside):
        def one_pair(at, carry):
            beside(at)
            tile = first + lax.div(at, 2)
            spots = [lax.rem(at, 2) * 2 + i for i in range(2)]
            loaded = [load_cluster(tile, j) for j in spots]
            found = [attend(*arrays, inv_root) for arrays in loaded]
            for j, results in zip(spots, found):
                c = tile * 4 + j
                for a, value in enumerate(results):
                    value = value.astype(jnp.bfloat16)
                    table[tile, a * 4 + j] = value[:TOK]
                    over_res[
                        pl.ds(pl.multiple_of(c * OVC, 32), OVC), pl.ds(a * DH, DH)
                    ] = value[TOK : TOK + OVC]
            return carry

        lax.fori_loop(0, 2 * tiles, one_pair, 0)

    def put_in(result):
        def put(blocks, unit, value):
            result[blocks, unit] = value

        return put

    def from_table(first):
        return lambda blocks, unit: table[first + unit, :, blocks, :]

    to_a = (result_a, back_a.at[me], res_a_sem, back_a_sem)
    to_b = (result_b, back_b.at[me], res_b_sem, back_b_sem)
    to_c = (result_c, back_c.at[me], res_c_sem, back_c_sem)
    attend_tiles(0, 1, lambda at: None)
    arrange(from_table(0), put_in(result_a), 1)
    send_own(result_a, back_a.at[me], back_a_sem)

    wait_bytes(recv_b, recv_b_sem)
    arrange(lambda blocks, unit: recv_b[blocks, unit], put_table(1), 2)
    attend_tiles(1, 2, lambda at: send_steps(at * 4, 4, *to_a))
    arrange(from_table(1), put_in(result_b), 2)
    send_own(result_b, back_b.at[me], back_b_sem)

    wait_bytes(recv_c, recv_c_sem)
    arrange(lambda blocks, unit: recv_c[blocks, 0], put_table(3), 1)
    attend_tiles(3, 1, lambda at: send_steps(at * 8, 8, *to_b))

    def spread_chunk(at, carry):
        found = bf16_dot(
            onehot[pl.ds(pl.multiple_of(at * 256, 256), 256), :], over_res[...]
        )
        for pair in range(2):
            halves = [
                found[:, a * DH : (a + 1) * DH].reshape(32, 8, DH)
                for a in (2 * pair, 2 * pair + 1)
            ]
            result_c[pl.ds(at * 32, 32), 1 + pair] = jnp.concatenate(halves, axis=1).astype(
                jnp.bfloat16
            )
        return carry

    lax.fori_loop(0, 4, spread_chunk, 0)
    arrange(from_table(3), put_in(result_c), 1)
    send_to_all(*to_c)

    wait_bytes(hback, hback_sem)
    wait_bytes(back_a, back_a_sem)
    wait_bytes(back_b, back_b_sem)
    wait_bytes(back_c, back_c_sem)

    def unpack_heads(at, carry):
        cols = pl.ds(pl.multiple_of(at * 2 * DH, 2 * DH), 2 * DH)
        for pair, refs in enumerate(((out_ref, dq_ref), (dk_ref, dv_ref))):
            sides = []
            for k in range(2):
                head = 2 * at + k
                owners = pl.ds(head * groups, groups)
                sides.append(
                    jnp.concatenate(
                        [
                            back_a[owners, 0].reshape(TOK, DH),
                            back_b[owners, 0].reshape(TOK, DH),
                            back_b[owners, 1].reshape(TOK, DH),
                            back_c[owners, 0].reshape(TOK, DH),
                            back_c[owners, 1 + pair].reshape(TOK, DH),
                            hback[head],
                            jnp.zeros((TOK - 16, DH), jnp.bfloat16),
                        ],
                        axis=0,
                    )
                )
            found = bf16_dot(unpack_mat[pair], jnp.concatenate(sides, axis=1))
            for half in range(2):
                refs[half][:, cols] = found[half * TOK : (half + 1) * TOK].astype(jnp.bfloat16)
        return carry

    lax.fori_loop(0, heads // 2, unpack_heads, 0, unroll=2)

    others = pl.ds(0, devices - 1)
    wait_bytes(cnt_group.at[pl.ds(0, groups - 1)], cnt_send_sem)
    wait_bytes(cnt_recv.at[pl.ds(0, heads - 1)], cnt2_send_sem)
    wait_bytes(send_a.at[others], send_a_sem)
    wait_bytes(send_b.at[others], send_b_sem)
    wait_bytes(send_c.at[others], send_c_sem)
    wait_bytes(result_a.at[others], res_a_sem)
    wait_bytes(result_b.at[others], res_b_sem)
    wait_bytes(result_c.at[others], res_c_sem)

    @pl.when(is_heavy_owner)
    def _():
        wait_bytes(hsend.at[pl.ds(0, heads - 1)], hsend_sem)
        wait_bytes(hresult.at[others], hres_sem)

    @pl.when(jnp.logical_not(is_heavy_owner))
    def _():
        wait_bytes(hsend, hsend_sem)


def fast_path(queries, key_rows, value_rows, out_grad, cluster_ids):
    tok_rows, columns = queries.shape
    heads = columns // DH
    groups = lax.axis_size("clu")
    devices = lax.axis_size("seq") * groups
    low = jnp.bfloat16
    wide = jnp.float32
    rows = jax.ShapeDtypeStruct((tok_rows, columns), low)
    vmem = pl.BlockSpec(memory_space=pltpu.VMEM)
    smem = pl.BlockSpec(memory_space=pltpu.SMEM)
    return pl.pallas_call(
        fast_kernel,
        out_shape=[rows] * 4 + [jax.ShapeDtypeStruct((1, 1), jnp.int32)],
        in_specs=[vmem] * 5,
        out_specs=[vmem] * 4 + [smem],
        scratch_shapes=[
            pltpu.VMEM((1, TOK), wide),
            pltpu.VMEM((groups, 1, TOK), wide),
            pltpu.VMEM((heads, groups, 1, TOK), wide),
            pltpu.VMEM((4 * TOK + 16, 4 * TOK), low),
            pltpu.VMEM((TOK, 2 * TOK), low),
            pltpu.VMEM((2, 2 * TOK, 6 * TOK), low),
            pltpu.VMEM((devices, 3, 16, DH), low),
            pltpu.VMEM((devices, 2, 16, DH), low),
            pltpu.VMEM((devices, 1, 16, DH), low),
            pltpu.VMEM((devices, 3, 16, DH), low),
            pltpu.VMEM((devices, 2, 16, DH), low),
            pltpu.VMEM((devices, 1, 16, DH), low),
            pltpu.VMEM((4, 16, devices, DH), low),
            pltpu.VMEM((8 * TOK, TOK), wide),
            pltpu.VMEM((TOK, TOK), wide),
            pltpu.VMEM((4, 16, OVC, DH), low),
            pltpu.VMEM((16, TOK + OVC, TOK), wide),
            pltpu.VMEM((16, 8, 2 * TOK), wide),
            pltpu.VMEM((16 * OVC, 8 * TOK), low),
            pltpu.VMEM((8 * TOK, 16 * OVC), low),
            pltpu.VMEM((8 * TOK, 4 * DH), low),
            pltpu.VMEM((16 * OVC, 4 * DH), low),
            pltpu.VMEM((devices, 1, 16, DH), low),
            pltpu.VMEM((devices, 2, 16, DH), low),
            pltpu.VMEM((devices, 3, 16, DH), low),
            pltpu.VMEM((devices, 1, 16, DH), low),
            pltpu.VMEM((devices, 2, 16, DH), low),
            pltpu.VMEM((devices, 3, 16, DH), low),
            pltpu.VMEM((heads, 16, DH), low),
            pltpu.VMEM((devices, 16, DH), low),
            pltpu.VMEM((16, devices, DH), low),
            pltpu.VMEM((4, 4 * TOK, DH), wide),
            pltpu.VMEM((devices, 16, DH), low),
            pltpu.VMEM((heads, 16, DH), low),
        ]
        + [pltpu.SemaphoreType.DMA] * 20,
        compiler_params=pltpu.CompilerParams(
            collective_id=0, has_side_effects=True, vmem_limit_bytes=56 * 1024 * 1024
        ),
    )(cluster_ids.reshape(1, tok_rows), queries, key_rows, value_rows, out_grad)


def per_device(queries, key_rows, value_rows, out_grad, cluster_ids):
    arrays = (queries, key_rows, value_rows, out_grad, cluster_ids)
    *fast, flag = fast_path(*arrays)
    return lax.cond(
        flag.reshape(()) != 0,
        lambda arrays, fast: full_capacity(*arrays),
        lambda arrays, fast: tuple(fast),
        arrays,
        tuple(fast),
    )


def solution(mesh):
    in_specs = (
        P(("seq", "clu"), None),
        P(("seq", "clu"), None),
        P(("seq", "clu"), None),
        P(("seq", "clu"), None),
        P(("seq", "clu")),
    )
    out_specs = (
        P(("seq", "clu"), None),
        P(("seq", "clu"), None),
        P(("seq", "clu"), None),
        P(("seq", "clu"), None),
    )
    return jax.shard_map(
        per_device, mesh=mesh, in_specs=in_specs, out_specs=out_specs, check_vma=False
    )
```

```python
import math

import jax
import jax.numpy as jnp
from jax import lax
from jax.experimental import pallas as pl
from jax.experimental.pallas import tpu as pltpu
from jax.sharding import PartitionSpec as P

DH = 128
TOK = 128
OVC = 80
SET = 16
FAR = 1e9
MESH = pl.DeviceIdType.MESH


masked = -1e30


def contract_last(left, right):
    return lax.dot_general(
        left, right, (((1,), (1,)), ((), ())), preferred_element_type=jnp.float32
    )


def contract_first(left, right):
    return lax.dot_general(
        left, right, (((0,), (0,)), ((), ())), preferred_element_type=jnp.float32
    )


def softmax_rows(query_head, key_head, allowed, inv_root):
    scores = contract_last(query_head, key_head) * inv_root
    scores = jnp.where(allowed, scores, masked)
    row_max = jnp.max(scores, axis=1, keepdims=True)
    weights = jnp.exp(scores - row_max)
    row_sum = jnp.sum(weights, axis=1, keepdims=True)
    return (weights / row_sum).astype(jnp.bfloat16)


def head_slice(array, head_index):
    return lax.dynamic_slice_in_dim(array, head_index * DH, DH, 1)


def full_capacity(queries, key_rows, value_rows, out_grad, cluster_ids):
    seq_count = lax.axis_size("seq")
    clu_count = lax.axis_size("clu")
    devices = seq_count * clu_count
    tok_rows = queries.shape[0]
    columns = queries.shape[1]
    head_count = columns // DH
    most_rows = 4 * tok_rows // devices
    capacity = most_rows * devices
    inv_root = 1.0 / math.sqrt(DH)
    owners = jnp.arange(devices, dtype=jnp.int32)
    member = (cluster_ids[:, None] == owners[None, :]).astype(jnp.int32)
    running = jnp.cumsum(member, axis=0) - 1
    slot_rank = jnp.sum(member * running, axis=1)
    sent_counts = jnp.sum(member, axis=0).reshape(devices, 1)
    slot_index = cluster_ids * most_rows + slot_rank
    stacked = jnp.concatenate([queries, key_rows, value_rows], axis=1)
    width_in = stacked.shape[1]
    packed = jnp.zeros((devices * most_rows, width_in), jnp.bfloat16).at[slot_index].set(stacked)
    packed = packed.reshape(devices, most_rows, width_in)
    got_rows, got_counts = (
        lax.all_to_all(packed, ("seq", "clu"), split_axis=0, concat_axis=0, tiled=True),
        lax.all_to_all(sent_counts, ("seq", "clu"), split_axis=0, concat_axis=0, tiled=True),
    )
    got_counts = got_counts.reshape(devices)
    starts = jnp.cumsum(got_counts) - got_counts
    live_total = jnp.sum(got_counts)
    within = jnp.arange(most_rows, dtype=jnp.int32)
    target = jnp.where(
        within[None, :] < got_counts[:, None], starts[:, None] + within[None, :], capacity
    )
    target = target.reshape(devices * most_rows)
    gathered = (
        jnp.zeros((capacity, width_in), jnp.bfloat16)
        .at[target]
        .set(got_rows.reshape(devices * most_rows, width_in), mode="drop")
    )
    query_block = gathered[:, :columns]
    key_block = gathered[:, columns : 2 * columns]
    value_block = gathered[:, 2 * columns : 3 * columns]
    positions = jnp.arange(capacity, dtype=jnp.int32)
    allowed = (positions[None, :] <= positions[:, None]) & (positions[None, :] < live_total)

    def forward_head(head_index, mixed_rows):
        weights_low = softmax_rows(
            head_slice(query_block, head_index),
            head_slice(key_block, head_index),
            allowed,
            inv_root,
        )
        out_head = jnp.dot(
            weights_low, head_slice(value_block, head_index), preferred_element_type=jnp.float32
        ).astype(jnp.bfloat16)
        return lax.dynamic_update_slice_in_dim(mixed_rows, out_head, head_index * DH, 1)

    mixed_rows = lax.fori_loop(
        0, head_count, forward_head, jnp.zeros((capacity, columns), jnp.bfloat16)
    )
    back_index = jnp.minimum(target, capacity - 1)
    outgoing = jnp.take(mixed_rows, back_index, axis=0).reshape(devices, most_rows, columns)
    grad_packed = (
        jnp.zeros((devices * most_rows, columns), jnp.bfloat16).at[slot_index].set(out_grad)
    )
    grad_packed = grad_packed.reshape(devices, most_rows, columns)
    returned = lax.all_to_all(outgoing, ("seq", "clu"), split_axis=0, concat_axis=0, tiled=True)
    got_grad = lax.all_to_all(grad_packed, ("seq", "clu"), split_axis=0, concat_axis=0, tiled=True)
    attention_out = jnp.take(returned.reshape(devices * most_rows, columns), slot_index, axis=0)
    grad_block = (
        jnp.zeros((capacity, columns), jnp.bfloat16)
        .at[target]
        .set(got_grad.reshape(devices * most_rows, columns), mode="drop")
    )
    delta_rows = jnp.sum(
        (grad_block.astype(jnp.float32) * mixed_rows.astype(jnp.float32)).reshape(
            capacity, head_count, DH
        ),
        axis=2,
    )

    def backward_head(head_index, grad_rows):
        query_head = head_slice(query_block, head_index)
        key_head = head_slice(key_block, head_index)
        value_head = head_slice(value_block, head_index)
        grad_head = head_slice(grad_block, head_index)
        weights_low = softmax_rows(query_head, key_head, allowed, inv_root)
        prob_grad = contract_last(grad_head, value_head)
        delta_head = lax.dynamic_slice_in_dim(delta_rows, head_index, 1, 1)
        score_grad = (weights_low.astype(jnp.float32) * (prob_grad - delta_head)).astype(
            jnp.bfloat16
        )
        query_part = (
            jnp.dot(score_grad, key_head, preferred_element_type=jnp.float32) * inv_root
        ).astype(jnp.bfloat16)
        key_part = (contract_first(score_grad, query_head) * inv_root).astype(jnp.bfloat16)
        value_part = contract_first(weights_low, grad_head).astype(jnp.bfloat16)
        grad_rows = lax.dynamic_update_slice_in_dim(grad_rows, query_part, head_index * DH, 1)
        grad_rows = lax.dynamic_update_slice_in_dim(
            grad_rows, key_part, columns + head_index * DH, 1
        )
        return lax.dynamic_update_slice_in_dim(
            grad_rows, value_part, 2 * columns + head_index * DH, 1
        )

    grad_rows = lax.fori_loop(
        0, head_count, backward_head, jnp.zeros((capacity, 3 * columns), jnp.bfloat16)
    )
    outgoing_grads = jnp.take(grad_rows, back_index, axis=0).reshape(
        devices, most_rows, 3 * columns
    )
    returned_grads = lax.all_to_all(
        outgoing_grads, ("seq", "clu"), split_axis=0, concat_axis=0, tiled=True
    )
    picked = jnp.take(returned_grads.reshape(devices * most_rows, 3 * columns), slot_index, axis=0)
    return (
        attention_out,
        picked[:, :columns],
        picked[:, columns : 2 * columns],
        picked[:, 2 * columns :],
    )


def bf16_dot(left, right):
    return jnp.dot(left, right, preferred_element_type=jnp.float32)


def flip_perm():
    row = lax.broadcasted_iota(jnp.int32, (SET * 16, SET * 16), 0)
    col = lax.broadcasted_iota(jnp.int32, (SET * 16, SET * 16), 1)
    swapped = (col % 16) * 16 + col // 16
    return (row == swapped).astype(jnp.float32).astype(jnp.bfloat16)


def attend(q, k, v, g, allowed, inv_root):
    raw = jnp.where(allowed, contract_last(k, q), masked)
    most = jnp.max(raw, axis=0, keepdims=True)
    weights = jnp.exp2((raw - most) * (inv_root * math.log2(math.e)))
    prob = weights * (1.0 / jnp.sum(weights, axis=0, keepdims=True))
    prob_low = prob.astype(jnp.bfloat16)
    prob_grad = contract_last(v, g)
    delta = jnp.sum(prob * prob_grad, axis=0, keepdims=True)
    score_grad = (prob * (prob_grad - delta)).astype(jnp.bfloat16)
    out = contract_first(v, prob_low).T.astype(jnp.bfloat16)
    dq = (contract_first(k, score_grad).T * inv_root).astype(jnp.bfloat16)
    dk = bf16_dot(score_grad, q) * inv_root
    dv = bf16_dot(prob_low, g)
    return out, dq, dk, dv


def fast_kernel(
    ids_ref, q_ref, k_ref, v_ref, g_ref,
    out_ref, dq_ref, dk_ref, dv_ref, flag_ref,
    cnt_send, cnt_group, cnt_recv, pack_mat, unpack_mat,
    send_a, send_b, send_c, recv_a, recv_b, recv_c, table,
    over, key_pos, query_pos, pick, onehot, loose, over_res, to_mate, to_block,
    result_a, result_b, result_c, back_a, back_b, back_c,
    ex_send, ex_recv, ex_send2, ex_recv2, ex_ret2, ex_back2, ex_ret1, ex_back1,
    hsend, hrecv, htable, hacc, hresult, hback,
    cnt_send_sem, cnt_sem, cnt2_send_sem, cnt2_sem,
    send_a_sem, recv_a_sem, send_b_sem, recv_b_sem, send_c_sem, recv_c_sem,
    res_a_sem, back_a_sem, res_b_sem, back_b_sem, res_c_sem, back_c_sem,
    ex_send_sem, ex_recv_sem, ex_send2_sem, ex_recv2_sem,
    ex_ret2_sem, ex_back2_sem, ex_ret1_sem, ex_back1_sem,
    hsend_sem, hrecv_sem, hres_sem, hback_sem,
):
    seq_at = lax.axis_index("seq")
    clu_at = lax.axis_index("clu")
    groups = lax.axis_size("clu")
    heads = lax.axis_size("seq")
    devices = heads * groups
    me = seq_at * groups + clu_at
    inv_root = 1.0 / math.sqrt(DH)
    is_heavy_owner = lax.rem(seq_at, groups) == clu_at
    at_x, at_z = lax.div(seq_at, 4), lax.rem(seq_at, 4)
    at_y, at_core = lax.div(clu_at, 2), lax.rem(clu_at, 2)

    def coords(device):
        return (lax.div(device, groups), lax.rem(device, groups))

    def turn(by):
        return by + at_core * (4 - 2 * by)

    eight = []
    for by_x, by_z, by_clu in zip(
        (0, 3, 2, 1, 0, 3, 2, 0), (0, 3, 2, 1, 1, 0, 3, 2), (0, 4, 6, 7, 2, 5, 1, 3)
    ):
        y = lax.rem(at_y + turn(by_clu // 2), 4)
        eight.append((turn(by_x), turn(by_z), y * 2 + lax.rem(at_core + by_clu % 2, 2)))

    def send_steps(first, count, source, target, send_sem, recv_sem):
        def one_eight(step, carry):
            by = lax.rem(step * 11, 16)
            by_x, by_z = lax.div(by, 4), lax.rem(by, 4)
            x = at_x + turn(by_x)
            z = at_z + turn(by_z)
            for j, (more_x, more_z, clu_to) in enumerate(eight):
                seq_to = lax.rem(x + more_x, 4) * 4 + lax.rem(z + more_z, 4)

                def start():
                    pltpu.make_async_remote_copy(
                        src_ref=source.at[seq_to * groups + clu_to],
                        dst_ref=target,
                        send_sem=send_sem,
                        recv_sem=recv_sem,
                        device_id=(seq_to, clu_to),
                        device_id_type=MESH,
                    ).start()

                if j == 0:
                    pl.when(step > 0)(start)
                else:
                    start()
            return carry

        lax.fori_loop(first, first + count, one_eight, 0)

    def send_own(source, target, recv_sem):
        pltpu.make_async_copy(source.at[me], target, recv_sem).start()

    def send_to_all(source, target, send_sem, recv_sem):
        send_steps(0, devices // 8, source, target, send_sem, recv_sem)
        send_own(source, target, recv_sem)

    def wait_bytes(ref, sem):
        pltpu.make_async_copy(ref, ref, sem).wait()

    barrier = pltpu.get_barrier_semaphore()

    def greet(step, carry):
        pl.semaphore_signal(
            barrier, inc=1, device_id=coords(lax.rem(me + step, devices)), device_id_type=MESH
        )
        return carry

    lax.fori_loop(1, devices, greet, 0)

    sub = lax.broadcasted_iota(jnp.int32, (TOK, TOK), 0)
    lane = lax.broadcasted_iota(jnp.int32, (TOK, TOK), 1)
    sub_f = sub.astype(jnp.float32)
    lane_f = lane.astype(jnp.float32)
    ids_l = jnp.broadcast_to(ids_ref[...].astype(jnp.float32), (TOK, TOK))
    ids_s = ids_l.T
    one = jnp.ones((TOK, TOK), jnp.float32)
    zero = jnp.zeros((TOK, TOK), jnp.float32)
    same = ids_l == ids_s
    rank_l = jnp.sum(jnp.where(same & (sub < lane), one, zero), axis=0, keepdims=True)
    rank_s = jnp.sum(jnp.where(same & (lane < sub), one, zero), axis=1, keepdims=True)
    count_l = jnp.sum(jnp.where(same, one, zero), axis=0, keepdims=True)
    cnt_send[...] = jnp.sum(jnp.where(ids_s == lane_f, one, zero), axis=0, keepdims=True)
    ids_row = ids_l[0:1, :]
    heavy = jnp.min(jnp.where(count_l == 4.0, ids_row, 999.0), axis=1, keepdims=True)
    group_l = jnp.floor(ids_l * (1.0 / 16.0))
    group_s = jnp.floor(ids_s * (1.0 / 16.0))
    earlier = (ids_s < ids_l) | (same & (sub < lane))
    later = (ids_l < ids_s) | (same & (lane < sub))
    before = (group_l == group_s) & (ids_s != heavy) & (rank_s >= 1.0) & earlier
    over_at = jnp.sum(jnp.where(before, one, zero), axis=0, keepdims=True)
    behind = (group_l == group_s) & (ids_l != heavy) & (rank_l >= 1.0) & later
    over_at_s = jnp.sum(jnp.where(behind, one, zero), axis=1, keepdims=True)
    excess_s = (ids_s != heavy) & (rank_s >= 1.0) & (over_at_s >= 4.0)
    excess_at = jnp.sum(jnp.where(excess_s & earlier, one, zero), axis=0, keepdims=True)
    light_l = ids_l != heavy
    slot_group = (sub // 16).astype(jnp.float32)
    in_tile = sub % 16
    over_l = light_l & (rank_l >= 1.0)
    for tile in range(5):
        at_slot = (in_tile % 4).astype(jnp.float32)
        if tile < 4:
            cluster = slot_group * 16.0 + at_slot + 4.0 * tile
            taken = (ids_l == cluster) & (rank_l == 0.0) & light_l
        else:
            taken = (group_l == slot_group) & over_l & (over_at == at_slot)
        at_row = (0, 2 * TOK + 48, 3 * TOK + 48, 4 * TOK + 48, TOK)[tile]
        for array in range(4):
            matrix = jnp.where(taken & (in_tile // 4 == array), one, zero)
            pack_mat[pl.ds(at_row, TOK), pl.ds(array * TOK, TOK)] = matrix.astype(jnp.bfloat16)
            unpack_mat[pl.ds(array * TOK, TOK), pl.ds(tile * TOK, TOK)] = matrix.T.astype(
                jnp.bfloat16
            )
    for array in range(4):
        chosen = (ids_l == heavy) & (rank_l == (sub % 4).astype(jnp.float32))
        chosen = chosen & (sub // 4 == array) & (sub < 16)
        beyond = over_l & (over_at >= 4.0) & (excess_at == (sub % 8).astype(jnp.float32))
        beyond = beyond & (sub // 8 == array + 2)
        matrix = jnp.where(chosen | beyond, one, zero)
        unpack_mat[pl.ds(array * TOK, TOK), pl.ds(5 * TOK, TOK)] = matrix.T.astype(jnp.bfloat16)
        pack_mat[pl.ds(2 * TOK, 48), pl.ds(array * TOK, TOK)] = matrix[0:48, :].astype(
            jnp.bfloat16
        )

    pl.semaphore_wait(barrier, devices - 1)

    def send_line(source, target, count, at, device, send_sem, recv_sem):
        def one_peer(step, carry):
            to = lax.rem(at + step, count)
            pltpu.make_async_remote_copy(
                src_ref=source(to),
                dst_ref=target,
                send_sem=send_sem,
                recv_sem=recv_sem,
                device_id=device(to),
                device_id_type=MESH,
            ).start()
            return carry

        lax.fori_loop(1, count, one_peer, 0)
        pltpu.make_async_copy(source(at), target, recv_sem).start()

    def along_seq(source, target, send_sem, recv_sem):
        send_line(
            source, target.at[seq_at], heads, seq_at, lambda to: (to, clu_at), send_sem, recv_sem
        )

    def along_clu(source, target, send_sem, recv_sem):
        send_line(
            source, target.at[clu_at], groups, clu_at, lambda to: (seq_at, to), send_sem, recv_sem
        )

    along_clu(lambda to: cnt_send, cnt_group, cnt_send_sem, cnt_sem)

    def head_rows(at):
        cols = pl.ds(pl.multiple_of(at * 2 * DH, 2 * DH), 2 * DH)
        return [ref[:, cols] for ref in (q_ref, k_ref, v_ref, g_ref)]

    def put_tile(target, at, tile, packed):
        low = packed.astype(jnp.bfloat16)
        for k in range(2):
            target[pl.ds((2 * at + k) * groups, groups), tile] = low[
                :, k * DH : (k + 1) * DH
            ].reshape(groups, 16, DH)

    def pack_a(at, carry):
        rows = jnp.concatenate(head_rows(at), axis=0)
        packed = bf16_dot(pack_mat[pl.ds(0, 2 * TOK + 48), :], rows)
        put_tile(send_a, at, 0, packed[:TOK])
        put_tile(send_a, at, 1, packed[TOK : 2 * TOK])
        rest = packed[2 * TOK :].astype(jnp.bfloat16)
        for k in range(2):
            hsend[2 * at + k] = rest[:16, k * DH : (k + 1) * DH]
            ex_send[2 * at + k] = rest[16:, k * DH : (k + 1) * DH]
        return carry

    lax.fori_loop(0, heads // 2, pack_a, 0, unroll=2)
    wait_bytes(cnt_group, cnt_sem)
    along_seq(lambda to: cnt_group, cnt_recv, cnt2_send_sem, cnt2_sem)

    def send_heavy(step, carry):
        head = lax.rem(seq_at + step, heads)
        clu_to = lax.rem(head, groups)

        @pl.when(head * groups + clu_to != me)
        def _():
            pltpu.make_async_remote_copy(
                src_ref=hsend.at[head],
                dst_ref=hrecv.at[me],
                send_sem=hsend_sem,
                recv_sem=hrecv_sem,
                device_id=(head, clu_to),
                device_id_type=MESH,
            ).start()

        @pl.when(head * groups + clu_to == me)
        def _():
            pltpu.make_async_copy(hsend.at[head], hrecv.at[me], hrecv_sem).start()

        return carry

    lax.fori_loop(0, heads, send_heavy, 0)
    along_seq(lambda to: ex_send.at[to], ex_recv, ex_send_sem, ex_recv_sem)
    send_to_all(send_a, recv_a.at[me], send_a_sem, recv_a_sem)

    def pack_bc(at, carry):
        rows = jnp.concatenate(head_rows(at), axis=0)
        packed = bf16_dot(pack_mat[pl.ds(2 * TOK + 48, 3 * TOK), :], rows)
        put_tile(send_b, at, 0, packed[:TOK])
        put_tile(send_b, at, 1, packed[TOK : 2 * TOK])
        put_tile(send_c, at, 0, packed[2 * TOK :])
        return carry

    lax.fori_loop(0, heads // 2, pack_bc, 0)

    wait_bytes(cnt_recv, cnt2_sem)
    seen = cnt_recv[...].reshape(TOK, TOK)
    heavies = jnp.min(jnp.where(seen == 4.0, lane_f, 999.0), axis=1, keepdims=True)
    heavy_all = jnp.min(heavies, axis=0, keepdims=True)
    light = lane_f != heavy_all
    more = jnp.where(light, jnp.maximum(seen - 1.0, 0.0), 0.0)
    more_low = more.astype(jnp.bfloat16)
    in_group = jnp.where(sub // 16 == lane, one, zero).astype(jnp.bfloat16)
    ahead = jnp.where(sub < lane, one, zero).astype(jnp.bfloat16)
    prior = jnp.where(lane < sub, one, zero).astype(jnp.bfloat16)
    mates = (lane < sub) & (lane % 8 == sub % 8)
    mates = jnp.where(mates, one, zero).astype(jnp.bfloat16)
    excess = jnp.maximum(bf16_dot(more_low, in_group) - 4.0, 0.0)
    excess_low = excess.astype(jnp.bfloat16)
    excess_off = bf16_dot(excess_low, ahead)
    excess_pre = bf16_dot(mates, excess_low)
    bad = (jnp.sum(excess, axis=1, keepdims=True) > 8.0) | (excess_pre + excess > 16.0)
    bad = bad | (heavies != heavy_all) | (jnp.sum(more, axis=0, keepdims=True) > OVC)
    flag_ref[0, 0] = jnp.max(jnp.where(bad, one, zero)).astype(jnp.int32)

    spot = zero
    for group in range(8):
        off, count, pre = [a[:, group : group + 1] for a in (excess_off, excess, excess_pre)]
        held = (lane_f >= off) & (lane_f < off + count)
        spot = spot + jnp.where(held, lane_f + (group * 16 + 1.0) - off + pre, zero)
    spot = jnp.where(sub % 8 == clu_at, spot, zero).reshape(16, 8, TOK)
    spot = jnp.sum(spot, axis=1).astype(jnp.bfloat16)
    spread8 = jnp.where(lane % 8 == sub, one, zero).astype(jnp.bfloat16)
    spot = jnp.where(lane[:16] // 8 == sub[:16], bf16_dot(spot, spread8), 0.0)
    spot = jnp.sum(spot, axis=0, keepdims=True) - 1.0
    to_mate[...] = jnp.where(sub_f == spot, one, zero).astype(jnp.bfloat16)
    spot = jnp.broadcast_to(spot, (TOK, TOK)).T
    to_block[...] = jnp.where(spot == lane_f, one, zero).astype(jnp.bfloat16)

    wait_bytes(ex_recv, ex_recv_sem)
    held = ex_recv[...].astype(jnp.float32)
    held = [held[:, 8 * a : 8 * a + 8, :].reshape(TOK, DH) for a in range(4)]
    held = jnp.concatenate(held, axis=1).astype(jnp.bfloat16)
    held = bf16_dot(to_mate[...], held).astype(jnp.bfloat16)
    for a in range(4):
        ex_send2[:, a] = held[:, a * DH : (a + 1) * DH].reshape(8, 16, DH)
    along_clu(lambda to: ex_send2.at[to], ex_recv2, ex_send2_sem, ex_recv2_sem)
    send_to_all(send_b, recv_b.at[me], send_b_sem, recv_b_sem)
    send_to_all(send_c, recv_c.at[me], send_c_sem, recv_c_sem)

    valid = jnp.where((seen > 0.0) & light, one, zero).astype(jnp.bfloat16)
    mine = (sub == clu_at * 16 + lane) & (lane < 16)
    mine = jnp.where(mine, one, zero).astype(jnp.bfloat16)
    more_g = bf16_dot(more_low, mine)
    valid_g = bf16_dot(valid, mine)
    more_g_low = more_g.astype(jnp.bfloat16)
    start_g = bf16_dot(prior, more_g_low)
    offset_g = bf16_dot(more_g_low, ahead)
    beyond_g = jnp.maximum(bf16_dot(more_g_low, one.astype(jnp.bfloat16)) - 4.0, 0.0)
    pre_g = bf16_dot(mates, beyond_g.astype(jnp.bfloat16))
    ex_index = lane_f - pre_g + 4.0
    first_row = lax.broadcasted_iota(jnp.int32, (1, TOK), 1).astype(jnp.float32) * 16.0
    in_tile_at = zero
    beyond_at = zero
    for c in range(16):
        count, begin, off, real = [
            a[:, c : c + 1] for a in (more_g, start_g, offset_g, valid_g)
        ]
        place = begin - off + (c * OVC + 1.0)
        held = (lane_f >= off) & (lane_f < off + count) & (lane < 4)
        in_tile_at = in_tile_at + jnp.where(held, lane_f + place, zero)
        held = (ex_index >= off) & (ex_index < off + count) & (ex_index >= 4.0)
        beyond_at = beyond_at + jnp.where(held, ex_index + place, zero)
        held = (lane_f >= begin) & (lane_f < begin + count)
        where = jnp.where(held, sub_f * 16.0 + 1.0 + lane_f - begin, zero)
        where = jnp.sum(where, axis=0, keepdims=True)
        where = jnp.where(where > 0.0, where, FAR)
        query_row = jnp.concatenate([first_row, where], axis=1)
        query_pos[c] = jnp.broadcast_to(query_row, (8, 2 * TOK))
        key_pos[c, pl.ds(0, TOK), :] = jnp.where(real > 0.0, sub_f * 16.0, FAR)
        key_pos[c, pl.ds(TOK, OVC), :] = jnp.broadcast_to(where, (TOK, TOK)).T[:OVC]
    beyond_at = jnp.sum(beyond_at.reshape(16, 8, TOK), axis=0)
    high = jnp.floor(beyond_at * (1.0 / 32.0))
    split = jnp.concatenate([high, beyond_at - high * 32.0], axis=0).astype(jnp.bfloat16)
    spread16 = jnp.where(lane % 16 == sub, one, zero).astype(jnp.bfloat16)
    split = bf16_dot(split, spread16)
    split = jnp.where(lane[:8] // 16 == sub[:8], split[:8] * 32.0 + split[8:], 0.0)
    beyond_row = jnp.sum(split, axis=0, keepdims=True) - 1.0
    tile_rows = in_tile_at.T[0:8, :] - 1.0
    slot_rows = [tile_rows[k : k + 1, :] for k in range(4)] + [beyond_row]
    slot_cols = [in_tile_at[:, k : k + 1] - 1.0 for k in range(4)]
    slot_cols.append(jnp.broadcast_to(beyond_row, (TOK, TOK)).T)

    chunk = 4
    for k in range(5):
        for m in range(16 * OVC // TOK):
            onehot[pl.ds(k * TOK, TOK), pl.ds(m * TOK, TOK)] = jnp.where(
                slot_cols[k] == lane_f + float(m * TOK), one, zero
            ).astype(jnp.bfloat16)
            pick[pl.ds(m * TOK, TOK), pl.ds(k * TOK, TOK)] = jnp.where(
                slot_rows[k] == sub_f + float(m * TOK), one, zero
            ).astype(jnp.bfloat16)

    perm = flip_perm()

    def arrange(source, target, units):
        def two_sets(at, carry):
            blocks = [pl.ds(pl.multiple_of((2 * at + i) * SET, SET), SET) for i in range(2)]
            spots = [(held, unit) for held in blocks for unit in range(units)]
            rows = jnp.concatenate(
                [source(held, unit).reshape(SET * 16, DH) for held, unit in spots], axis=1
            )
            turned = bf16_dot(perm, rows).astype(jnp.bfloat16)
            for i, (held, unit) in enumerate(spots):
                target(held, unit, turned[:, i * DH : (i + 1) * DH].reshape(16, SET, DH))
            return carry

        lax.fori_loop(0, devices // (2 * SET), two_sets, 0, unroll=2)

    def put_table(first):
        def put(blocks, unit, value):
            table[first + unit, :, blocks, :] = value

        return put

    @pl.when(is_heavy_owner)
    def _():
        wait_bytes(hrecv, hrecv_sem)

        def put_heavy(blocks, unit, value):
            htable[:, blocks, :] = value

        arrange(lambda blocks, unit: hrecv[blocks], put_heavy, 1)
        k_h, v_h = [htable[4 * a : 4 * a + 4].reshape(4 * TOK, DH) for a in (1, 2)]
        hacc[...] = jnp.zeros_like(hacc)
        key_sub = lax.broadcasted_iota(jnp.int32, (4 * TOK, TOK), 0)
        key_at = lax.rem(key_sub, TOK) * 4 + lax.div(key_sub, TOK)
        query_at = lax.broadcasted_iota(jnp.int32, (4 * TOK, TOK), 1) * 4

        def heavy_tile(s, carry):
            out, dq, dk, dv = attend(
                htable[s], k_h, v_h, htable[12 + s], key_at <= query_at + s, inv_root
            )
            hacc[2, pl.ds(pl.multiple_of(s * TOK, TOK), TOK)] = out.astype(jnp.float32)
            hacc[3, pl.ds(pl.multiple_of(s * TOK, TOK), TOK)] = dq.astype(jnp.float32)
            hacc[0] += dk
            hacc[1] += dv
            return carry

        lax.fori_loop(0, 4, heavy_tile, 0)
        for array, at in enumerate((2, 3, 0, 1)):
            htable[4 * array : 4 * array + 4] = (
                hacc[at].astype(jnp.bfloat16).reshape(4, TOK, DH)
            )

        def put_hresult(blocks, unit, value):
            hresult[blocks] = value

        arrange(lambda blocks, unit: htable[:, blocks, :], put_hresult, 1)
        send_to_all(hresult, hback.at[seq_at], hres_sem, hback_sem)

    wait_bytes(recv_a, recv_a_sem)
    def put_tile_a(blocks, unit, value):
        table[4 * unit, :, blocks, :] = value

    arrange(lambda blocks, unit: recv_a[blocks, unit], put_tile_a, 2)

    wait_bytes(ex_recv2, ex_recv2_sem)
    for a in range(4):
        cols = pl.ds(a * DH, DH)
        loose[pl.ds(0, 4 * TOK), cols] = table[4, 4 * a : 4 * a + 4].reshape(4 * TOK, DH)
        loose[pl.ds(4 * TOK, TOK), cols] = ex_recv2[:, a].reshape(TOK, DH)

    def gather_chunk(at, carry):
        chosen = pick[pl.ds(pl.multiple_of(at * chunk * OVC, 64), chunk * OVC), :]
        found = bf16_dot(chosen, loose[...]).astype(jnp.bfloat16)
        for c in range(chunk):
            for array in range(4):
                over[array, at * chunk + c] = found[
                    c * OVC : (c + 1) * OVC, array * DH : (array + 1) * DH
                ]
        return carry

    lax.fori_loop(0, 16 // chunk, gather_chunk, 0)

    pad_rows = jnp.zeros((TOK - OVC, DH), jnp.bfloat16)

    def load_cluster(tile, j):
        c = tile * 4 + j
        rows = [
            jnp.concatenate([table[tile, a * 4 + j], over[a, c]], axis=0) for a in range(4)
        ]
        for a in (0, 3):
            rows[a] = jnp.concatenate([rows[a], pad_rows], axis=0)
        key_at = key_pos[c]
        allowed = jnp.concatenate([key_at, key_at], axis=1) <= query_pos[c, 0:1, :]
        return rows + [allowed]

    def attend_tiles(first, tiles, beside):
        def one_pair(at, carry):
            beside(at)
            tile = first + lax.div(at, 2)
            spots = [lax.rem(at, 2) * 2 + i for i in range(2)]
            loaded = [load_cluster(tile, j) for j in spots]
            found = [attend(*arrays, inv_root) for arrays in loaded]
            for j, results in zip(spots, found):
                c = tile * 4 + j
                for a, value in enumerate(results):
                    value = value.astype(jnp.bfloat16)
                    table[tile, a * 4 + j] = value[:TOK]
                    over_res[
                        pl.ds(pl.multiple_of(c * OVC, 16), OVC), pl.ds(a * DH, DH)
                    ] = value[TOK : TOK + OVC]
            return carry

        lax.fori_loop(0, 2 * tiles, one_pair, 0)

    def put_in(result):
        def put(blocks, unit, value):
            result[blocks, unit] = value

        return put

    def from_table(first):
        return lambda blocks, unit: table[first + unit, :, blocks, :]

    to_a = (result_a, back_a.at[me], res_a_sem, back_a_sem)
    to_b = (result_b, back_b.at[me], res_b_sem, back_b_sem)
    to_c = (result_c, back_c.at[me], res_c_sem, back_c_sem)
    attend_tiles(0, 1, lambda at: None)
    arrange(from_table(0), put_in(result_a), 1)
    send_own(result_a, back_a.at[me], back_a_sem)

    wait_bytes(recv_b, recv_b_sem)
    arrange(lambda blocks, unit: recv_b[blocks, unit], put_table(1), 2)
    attend_tiles(1, 2, lambda at: send_steps(at * 4, 4, *to_a))
    arrange(from_table(1), put_in(result_b), 2)
    send_own(result_b, back_b.at[me], back_b_sem)

    wait_bytes(recv_c, recv_c_sem)
    arrange(lambda blocks, unit: recv_c[blocks, 0], put_table(3), 1)
    attend_tiles(3, 1, lambda at: send_steps(at * 8, 8, *to_b))

    found = bf16_dot(onehot[pl.ds(4 * TOK, TOK), :], over_res[...]).astype(jnp.bfloat16)
    for a in range(4):
        ex_ret2[:, a] = found[:, a * DH : (a + 1) * DH].reshape(8, 16, DH)
    along_clu(lambda to: ex_ret2.at[to], ex_back2, ex_ret2_sem, ex_back2_sem)
    found = bf16_dot(onehot[pl.ds(0, 4 * TOK), :], over_res[...]).astype(jnp.bfloat16)
    for a in range(4):
        table[4, 4 * a : 4 * a + 4] = found[:, a * DH : (a + 1) * DH].reshape(4, TOK, DH)
    arrange(from_table(3), put_in(result_c), 2)
    send_to_all(*to_c)

    wait_bytes(ex_back2, ex_back2_sem)
    held = [ex_back2[:, a].reshape(TOK, DH) for a in range(4)]
    held = bf16_dot(to_block[...], jnp.concatenate(held, axis=1))
    held = [held[:, a * DH : (a + 1) * DH].reshape(16, 8, DH) for a in range(4)]
    ex_ret1[...] = jnp.concatenate(held, axis=1).astype(jnp.bfloat16)
    along_seq(lambda to: ex_ret1.at[to], ex_back1, ex_ret1_sem, ex_back1_sem)

    wait_bytes(hback, hback_sem)
    wait_bytes(back_a, back_a_sem)
    wait_bytes(back_b, back_b_sem)
    wait_bytes(back_c, back_c_sem)
    wait_bytes(ex_back1, ex_back1_sem)

    def unpack_heads(at, carry):
        cols = pl.ds(pl.multiple_of(at * 2 * DH, 2 * DH), 2 * DH)
        sides = []
        for k in range(2):
            head = 2 * at + k
            owners = pl.ds(head * groups, groups)
            tiles = [
                back_a[owners, 0], back_b[owners, 0], back_b[owners, 1],
                back_c[owners, 0], back_c[owners, 1],
            ]
            sides.append(
                jnp.concatenate(
                    [tile.reshape(TOK, DH) for tile in tiles]
                    + [hback[head], ex_back1[head], jnp.zeros((TOK - 48, DH), jnp.bfloat16)],
                    axis=0,
                )
            )
        found = bf16_dot(unpack_mat[...], jnp.concatenate(sides, axis=1)).astype(jnp.bfloat16)
        for array, ref in enumerate((out_ref, dq_ref, dk_ref, dv_ref)):
            ref[:, cols] = found[array * TOK : (array + 1) * TOK]
        return carry

    lax.fori_loop(0, heads // 2, unpack_heads, 0, unroll=2)

    others = pl.ds(0, devices - 1)
    wait_bytes(cnt_group.at[pl.ds(0, groups - 1)], cnt_send_sem)
    wait_bytes(cnt_recv.at[pl.ds(0, heads - 1)], cnt2_send_sem)
    for ref, sem in ((ex_send, ex_send_sem), (ex_ret1, ex_ret1_sem)):
        wait_bytes(ref.at[pl.ds(0, heads - 1)], sem)
    for ref, sem in ((ex_send2, ex_send2_sem), (ex_ret2, ex_ret2_sem)):
        wait_bytes(ref.at[pl.ds(0, groups - 1)], sem)
    wait_bytes(send_a.at[others], send_a_sem)
    wait_bytes(send_b.at[others], send_b_sem)
    wait_bytes(send_c.at[others], send_c_sem)
    wait_bytes(result_a.at[others], res_a_sem)
    wait_bytes(result_b.at[others], res_b_sem)
    wait_bytes(result_c.at[others], res_c_sem)

    @pl.when(is_heavy_owner)
    def _():
        wait_bytes(hsend.at[pl.ds(0, heads - 1)], hsend_sem)
        wait_bytes(hresult.at[others], hres_sem)

    @pl.when(jnp.logical_not(is_heavy_owner))
    def _():
        wait_bytes(hsend, hsend_sem)


def fast_path(queries, key_rows, value_rows, out_grad, cluster_ids):
    tok_rows, columns = queries.shape
    heads = columns // DH
    groups = lax.axis_size("clu")
    devices = lax.axis_size("seq") * groups
    low = jnp.bfloat16
    wide = jnp.float32
    rows = jax.ShapeDtypeStruct((tok_rows, columns), low)
    vmem = pl.BlockSpec(memory_space=pltpu.VMEM)
    smem = pl.BlockSpec(memory_space=pltpu.SMEM)
    return pl.pallas_call(
        fast_kernel,
        out_shape=[rows] * 4 + [jax.ShapeDtypeStruct((1, 1), jnp.int32)],
        in_specs=[vmem] * 5,
        out_specs=[vmem] * 4 + [smem],
        scratch_shapes=[
            pltpu.VMEM((1, TOK), wide),
            pltpu.VMEM((groups, 1, TOK), wide),
            pltpu.VMEM((heads, groups, 1, TOK), wide),
            pltpu.VMEM((5 * TOK + 48, 4 * TOK), low),
            pltpu.VMEM((4 * TOK, 6 * TOK), low),
            pltpu.VMEM((devices, 2, 16, DH), low),
            pltpu.VMEM((devices, 2, 16, DH), low),
            pltpu.VMEM((devices, 1, 16, DH), low),
            pltpu.VMEM((devices, 2, 16, DH), low),
            pltpu.VMEM((devices, 2, 16, DH), low),
            pltpu.VMEM((devices, 1, 16, DH), low),
            pltpu.VMEM((5, 16, devices, DH), low),
            pltpu.VMEM((4, 16, OVC, DH), low),
            pltpu.VMEM((16, TOK + OVC, TOK), wide),
            pltpu.VMEM((16, 8, 2 * TOK), wide),
            pltpu.VMEM((16 * OVC, 5 * TOK), low),
            pltpu.VMEM((5 * TOK, 16 * OVC), low),
            pltpu.VMEM((5 * TOK, 4 * DH), low),
            pltpu.VMEM((16 * OVC, 4 * DH), low),
            pltpu.VMEM((TOK, TOK), low),
            pltpu.VMEM((TOK, TOK), low),
            pltpu.VMEM((devices, 1, 16, DH), low),
            pltpu.VMEM((devices, 2, 16, DH), low),
            pltpu.VMEM((devices, 2, 16, DH), low),
            pltpu.VMEM((devices, 1, 16, DH), low),
            pltpu.VMEM((devices, 2, 16, DH), low),
            pltpu.VMEM((devices, 2, 16, DH), low),
            pltpu.VMEM((heads, 32, DH), low),
            pltpu.VMEM((heads, 32, DH), low),
            pltpu.VMEM((groups, 4, 16, DH), low),
            pltpu.VMEM((groups, 4, 16, DH), low),
            pltpu.VMEM((groups, 4, 16, DH), low),
            pltpu.VMEM((groups, 4, 16, DH), low),
            pltpu.VMEM((heads, 32, DH), low),
            pltpu.VMEM((heads, 32, DH), low),
            pltpu.VMEM((heads, 16, DH), low),
            pltpu.VMEM((devices, 16, DH), low),
            pltpu.VMEM((16, devices, DH), low),
            pltpu.VMEM((4, 4 * TOK, DH), wide),
            pltpu.VMEM((devices, 16, DH), low),
            pltpu.VMEM((heads, 16, DH), low),
        ]
        + [pltpu.SemaphoreType.DMA] * 28,
        compiler_params=pltpu.CompilerParams(
            collective_id=0, has_side_effects=True, vmem_limit_bytes=56 * 1024 * 1024
        ),
    )(cluster_ids.reshape(1, tok_rows), queries, key_rows, value_rows, out_grad)


def per_device(queries, key_rows, value_rows, out_grad, cluster_ids):
    arrays = (queries, key_rows, value_rows, out_grad, cluster_ids)
    *fast, flag = fast_path(*arrays)
    return lax.cond(
        flag.reshape(()) != 0,
        lambda arrays, fast: full_capacity(*arrays),
        lambda arrays, fast: tuple(fast),
        arrays,
        tuple(fast),
    )


def solution(mesh):
    in_specs = (
        P(("seq", "clu"), None),
        P(("seq", "clu"), None),
        P(("seq", "clu"), None),
        P(("seq", "clu"), None),
        P(("seq", "clu")),
    )
    out_specs = (
        P(("seq", "clu"), None),
        P(("seq", "clu"), None),
        P(("seq", "clu"), None),
        P(("seq", "clu"), None),
    )
    return jax.shard_map(
        per_device, mesh=mesh, in_specs=in_specs, out_specs=out_specs, check_vma=False
    )
```

```python
import math

import jax
import jax.numpy as jnp
from jax import lax
from jax.experimental import pallas as pl
from jax.experimental.pallas import tpu as pltpu
from jax.sharding import PartitionSpec as P

DH = 128
TOK = 128
OVC = 80
SET = 16
FAR = 1e9
MESH = pl.DeviceIdType.MESH


masked = -1e30


def contract_last(left, right):
    return lax.dot_general(
        left, right, (((1,), (1,)), ((), ())), preferred_element_type=jnp.float32
    )


def contract_first(left, right):
    return lax.dot_general(
        left, right, (((0,), (0,)), ((), ())), preferred_element_type=jnp.float32
    )


def softmax_rows(query_head, key_head, allowed, inv_root):
    scores = contract_last(query_head, key_head) * inv_root
    scores = jnp.where(allowed, scores, masked)
    row_max = jnp.max(scores, axis=1, keepdims=True)
    weights = jnp.exp(scores - row_max)
    row_sum = jnp.sum(weights, axis=1, keepdims=True)
    return (weights / row_sum).astype(jnp.bfloat16)


def head_slice(array, head_index):
    return lax.dynamic_slice_in_dim(array, head_index * DH, DH, 1)


def full_capacity(queries, key_rows, value_rows, out_grad, cluster_ids):
    seq_count = lax.axis_size("seq")
    clu_count = lax.axis_size("clu")
    devices = seq_count * clu_count
    tok_rows = queries.shape[0]
    columns = queries.shape[1]
    head_count = columns // DH
    most_rows = 4 * tok_rows // devices
    capacity = most_rows * devices
    inv_root = 1.0 / math.sqrt(DH)
    owners = jnp.arange(devices, dtype=jnp.int32)
    member = (cluster_ids[:, None] == owners[None, :]).astype(jnp.int32)
    running = jnp.cumsum(member, axis=0) - 1
    slot_rank = jnp.sum(member * running, axis=1)
    sent_counts = jnp.sum(member, axis=0).reshape(devices, 1)
    slot_index = cluster_ids * most_rows + slot_rank
    stacked = jnp.concatenate([queries, key_rows, value_rows], axis=1)
    width_in = stacked.shape[1]
    packed = jnp.zeros((devices * most_rows, width_in), jnp.bfloat16).at[slot_index].set(stacked)
    packed = packed.reshape(devices, most_rows, width_in)
    got_rows, got_counts = (
        lax.all_to_all(packed, ("seq", "clu"), split_axis=0, concat_axis=0, tiled=True),
        lax.all_to_all(sent_counts, ("seq", "clu"), split_axis=0, concat_axis=0, tiled=True),
    )
    got_counts = got_counts.reshape(devices)
    starts = jnp.cumsum(got_counts) - got_counts
    live_total = jnp.sum(got_counts)
    within = jnp.arange(most_rows, dtype=jnp.int32)
    target = jnp.where(
        within[None, :] < got_counts[:, None], starts[:, None] + within[None, :], capacity
    )
    target = target.reshape(devices * most_rows)
    gathered = (
        jnp.zeros((capacity, width_in), jnp.bfloat16)
        .at[target]
        .set(got_rows.reshape(devices * most_rows, width_in), mode="drop")
    )
    query_block = gathered[:, :columns]
    key_block = gathered[:, columns : 2 * columns]
    value_block = gathered[:, 2 * columns : 3 * columns]
    positions = jnp.arange(capacity, dtype=jnp.int32)
    allowed = (positions[None, :] <= positions[:, None]) & (positions[None, :] < live_total)

    def forward_head(head_index, mixed_rows):
        weights_low = softmax_rows(
            head_slice(query_block, head_index),
            head_slice(key_block, head_index),
            allowed,
            inv_root,
        )
        out_head = jnp.dot(
            weights_low, head_slice(value_block, head_index), preferred_element_type=jnp.float32
        ).astype(jnp.bfloat16)
        return lax.dynamic_update_slice_in_dim(mixed_rows, out_head, head_index * DH, 1)

    mixed_rows = lax.fori_loop(
        0, head_count, forward_head, jnp.zeros((capacity, columns), jnp.bfloat16)
    )
    back_index = jnp.minimum(target, capacity - 1)
    outgoing = jnp.take(mixed_rows, back_index, axis=0).reshape(devices, most_rows, columns)
    grad_packed = (
        jnp.zeros((devices * most_rows, columns), jnp.bfloat16).at[slot_index].set(out_grad)
    )
    grad_packed = grad_packed.reshape(devices, most_rows, columns)
    returned = lax.all_to_all(outgoing, ("seq", "clu"), split_axis=0, concat_axis=0, tiled=True)
    got_grad = lax.all_to_all(grad_packed, ("seq", "clu"), split_axis=0, concat_axis=0, tiled=True)
    attention_out = jnp.take(returned.reshape(devices * most_rows, columns), slot_index, axis=0)
    grad_block = (
        jnp.zeros((capacity, columns), jnp.bfloat16)
        .at[target]
        .set(got_grad.reshape(devices * most_rows, columns), mode="drop")
    )
    delta_rows = jnp.sum(
        (grad_block.astype(jnp.float32) * mixed_rows.astype(jnp.float32)).reshape(
            capacity, head_count, DH
        ),
        axis=2,
    )

    def backward_head(head_index, grad_rows):
        query_head = head_slice(query_block, head_index)
        key_head = head_slice(key_block, head_index)
        value_head = head_slice(value_block, head_index)
        grad_head = head_slice(grad_block, head_index)
        weights_low = softmax_rows(query_head, key_head, allowed, inv_root)
        prob_grad = contract_last(grad_head, value_head)
        delta_head = lax.dynamic_slice_in_dim(delta_rows, head_index, 1, 1)
        score_grad = (weights_low.astype(jnp.float32) * (prob_grad - delta_head)).astype(
            jnp.bfloat16
        )
        query_part = (
            jnp.dot(score_grad, key_head, preferred_element_type=jnp.float32) * inv_root
        ).astype(jnp.bfloat16)
        key_part = (contract_first(score_grad, query_head) * inv_root).astype(jnp.bfloat16)
        value_part = contract_first(weights_low, grad_head).astype(jnp.bfloat16)
        grad_rows = lax.dynamic_update_slice_in_dim(grad_rows, query_part, head_index * DH, 1)
        grad_rows = lax.dynamic_update_slice_in_dim(
            grad_rows, key_part, columns + head_index * DH, 1
        )
        return lax.dynamic_update_slice_in_dim(
            grad_rows, value_part, 2 * columns + head_index * DH, 1
        )

    grad_rows = lax.fori_loop(
        0, head_count, backward_head, jnp.zeros((capacity, 3 * columns), jnp.bfloat16)
    )
    outgoing_grads = jnp.take(grad_rows, back_index, axis=0).reshape(
        devices, most_rows, 3 * columns
    )
    returned_grads = lax.all_to_all(
        outgoing_grads, ("seq", "clu"), split_axis=0, concat_axis=0, tiled=True
    )
    picked = jnp.take(returned_grads.reshape(devices * most_rows, 3 * columns), slot_index, axis=0)
    return (
        attention_out,
        picked[:, :columns],
        picked[:, columns : 2 * columns],
        picked[:, 2 * columns :],
    )


def bf16_dot(left, right):
    return jnp.dot(left, right, preferred_element_type=jnp.float32)


def flip_perm():
    row = lax.broadcasted_iota(jnp.int32, (SET * 16, SET * 16), 0)
    col = lax.broadcasted_iota(jnp.int32, (SET * 16, SET * 16), 1)
    swapped = (col % 16) * 16 + col // 16
    return (row == swapped).astype(jnp.float32).astype(jnp.bfloat16)


def attend(q, k, v, g, allowed, inv_root):
    raw = jnp.where(allowed, contract_last(k, q), masked)
    most = jnp.max(raw, axis=0, keepdims=True)
    weights = jnp.exp2((raw - most) * (inv_root * math.log2(math.e)))
    prob = weights * (1.0 / jnp.sum(weights, axis=0, keepdims=True))
    prob_low = prob.astype(jnp.bfloat16)
    prob_grad = contract_last(v, g)
    delta = jnp.sum(prob * prob_grad, axis=0, keepdims=True)
    score_grad = (prob * (prob_grad - delta)).astype(jnp.bfloat16)
    out = contract_first(v, prob_low).T.astype(jnp.bfloat16)
    dq = (contract_first(k, score_grad).T * inv_root).astype(jnp.bfloat16)
    dk = bf16_dot(score_grad, q) * inv_root
    dv = bf16_dot(prob_low, g)
    return out, dq, dk, dv


def fast_kernel(
    ids_ref, q_ref, k_ref, v_ref, g_ref,
    out_ref, dq_ref, dk_ref, dv_ref, flag_ref,
    cnt_send, cnt_group, cnt_recv, pack_mat, unpack_mat,
    send_a, send_b, send_c, recv_a, recv_b, recv_c, table,
    over, key_pos, query_pos, pick, onehot, loose, over_res, to_mate, to_block,
    result_a, result_b, result_c, back_a, back_b, back_c,
    ex_send, ex_recv, ex_send2, ex_recv2, ex_ret2, ex_back2, ex_ret1, ex_back1,
    hsend, hrecv, htable, hacc, hresult, hback, inputs,
    cnt_send_sem, cnt_sem, cnt2_send_sem, cnt2_sem,
    send_a_sem, recv_a_sem, send_b_sem, recv_b_sem, send_c_sem, recv_c_sem,
    res_a_sem, back_a_sem, res_b_sem, back_b_sem, res_c_sem, back_c_sem,
    ex_send_sem, ex_recv_sem, ex_send2_sem, ex_recv2_sem,
    ex_ret2_sem, ex_back2_sem, ex_ret1_sem, ex_back1_sem,
    hsend_sem, hrecv_sem, hres_sem, hback_sem, input_sem,
):
    seq_at = lax.axis_index("seq")
    clu_at = lax.axis_index("clu")
    groups = lax.axis_size("clu")
    heads = lax.axis_size("seq")
    devices = heads * groups
    me = seq_at * groups + clu_at
    inv_root = 1.0 / math.sqrt(DH)
    is_heavy_owner = lax.rem(seq_at, groups) == clu_at
    at_x, at_z = lax.div(seq_at, 4), lax.rem(seq_at, 4)
    at_y, at_core = lax.div(clu_at, 2), lax.rem(clu_at, 2)

    def coords(device):
        return (lax.div(device, groups), lax.rem(device, groups))

    def turn(by):
        return by + at_core * (4 - 2 * by)

    eight = []
    for by_x, by_z, by_clu in zip(
        (0, 3, 2, 1, 0, 3, 2, 0), (0, 3, 2, 1, 1, 0, 3, 2), (0, 4, 6, 7, 2, 5, 1, 3)
    ):
        y = lax.rem(at_y + turn(by_clu // 2), 4)
        eight.append((turn(by_x), turn(by_z), y * 2 + lax.rem(at_core + by_clu % 2, 2)))

    def send_steps(first, count, source, target, send_sem, recv_sem):
        def one_eight(step, carry):
            by = lax.rem(step * 11, 16)
            by_x, by_z = lax.div(by, 4), lax.rem(by, 4)
            x = at_x + turn(by_x)
            z = at_z + turn(by_z)
            for j, (more_x, more_z, clu_to) in enumerate(eight):
                seq_to = lax.rem(x + more_x, 4) * 4 + lax.rem(z + more_z, 4)

                def start():
                    pltpu.make_async_remote_copy(
                        src_ref=source.at[seq_to * groups + clu_to],
                        dst_ref=target,
                        send_sem=send_sem,
                        recv_sem=recv_sem,
                        device_id=(seq_to, clu_to),
                        device_id_type=MESH,
                    ).start()

                if j == 0:
                    pl.when(step > 0)(start)
                else:
                    start()
            return carry

        lax.fori_loop(first, first + count, one_eight, 0)

    def send_own(source, target, recv_sem):
        pltpu.make_async_copy(source.at[me], target, recv_sem).start()

    def send_to_all(source, target, send_sem, recv_sem):
        send_steps(0, devices // 8, source, target, send_sem, recv_sem)
        send_own(source, target, recv_sem)

    def wait_bytes(ref, sem):
        pltpu.make_async_copy(ref, ref, sem).wait()

    for array, ref in enumerate((q_ref, k_ref, v_ref, g_ref)):
        pltpu.make_async_copy(ref, inputs.at[array], input_sem).start()
    barrier = pltpu.get_barrier_semaphore()

    def greet(step, carry):
        pl.semaphore_signal(
            barrier, inc=1, device_id=coords(lax.rem(me + step, devices)), device_id_type=MESH
        )
        return carry

    lax.fori_loop(1, devices, greet, 0)

    sub = lax.broadcasted_iota(jnp.int32, (TOK, TOK), 0)
    lane = lax.broadcasted_iota(jnp.int32, (TOK, TOK), 1)
    sub_f = sub.astype(jnp.float32)
    lane_f = lane.astype(jnp.float32)
    ids_l = jnp.broadcast_to(ids_ref[...].astype(jnp.float32), (TOK, TOK))
    ids_s = ids_l.T
    one = jnp.ones((TOK, TOK), jnp.float32)
    zero = jnp.zeros((TOK, TOK), jnp.float32)
    same = ids_l == ids_s
    rank_l = jnp.sum(jnp.where(same & (sub < lane), one, zero), axis=0, keepdims=True)
    rank_s = jnp.sum(jnp.where(same & (lane < sub), one, zero), axis=1, keepdims=True)
    count_l = jnp.sum(jnp.where(same, one, zero), axis=0, keepdims=True)
    cnt_send[...] = jnp.sum(jnp.where(ids_s == lane_f, one, zero), axis=0, keepdims=True)
    ids_row = ids_l[0:1, :]
    heavy = jnp.min(jnp.where(count_l == 4.0, ids_row, 999.0), axis=1, keepdims=True)
    group_l = jnp.floor(ids_l * (1.0 / 16.0))
    group_s = jnp.floor(ids_s * (1.0 / 16.0))
    earlier = (ids_s < ids_l) | (same & (sub < lane))
    later = (ids_l < ids_s) | (same & (lane < sub))
    before = (group_l == group_s) & (ids_s != heavy) & (rank_s >= 1.0) & earlier
    over_at = jnp.sum(jnp.where(before, one, zero), axis=0, keepdims=True)
    behind = (group_l == group_s) & (ids_l != heavy) & (rank_l >= 1.0) & later
    over_at_s = jnp.sum(jnp.where(behind, one, zero), axis=1, keepdims=True)
    excess_s = (ids_s != heavy) & (rank_s >= 1.0) & (over_at_s >= 4.0)
    excess_at = jnp.sum(jnp.where(excess_s & earlier, one, zero), axis=0, keepdims=True)
    light_l = ids_l != heavy
    slot_group = (sub // 16).astype(jnp.float32)
    in_tile = sub % 16
    over_l = light_l & (rank_l >= 1.0)

    def tile_picks(tile):
        at_slot = (in_tile % 4).astype(jnp.float32)
        if tile < 4:
            cluster = slot_group * 16.0 + at_slot + 4.0 * tile
            taken = (ids_l == cluster) & (rank_l == 0.0) & light_l
        else:
            taken = (group_l == slot_group) & over_l & (over_at == at_slot)
        return [jnp.where(taken & (in_tile // 4 == array), one, zero) for array in range(4)]

    def rest_picks():
        picks = []
        for array in range(4):
            chosen = (ids_l == heavy) & (rank_l == (sub % 4).astype(jnp.float32))
            chosen = chosen & (sub // 4 == array) & (sub < 16)
            beyond = over_l & (over_at >= 4.0) & (excess_at == (sub % 8).astype(jnp.float32))
            beyond = beyond & (sub // 8 == array + 2)
            picks.append(jnp.where(chosen | beyond, one, zero))
        return picks

    def put_pack(at_row, count, picks):
        for array, matrix in enumerate(picks):
            pack_mat[pl.ds(at_row, count), pl.ds(array * TOK, TOK)] = matrix[:count].astype(
                jnp.bfloat16
            )

    put_pack(0, TOK, tile_picks(0))
    put_pack(TOK, TOK, tile_picks(4))
    put_pack(2 * TOK, 48, rest_picks())

    pl.semaphore_wait(barrier, devices - 1)

    def send_line(source, target, count, at, device, send_sem, recv_sem):
        def one_peer(step, carry):
            to = lax.rem(at + step, count)
            pltpu.make_async_remote_copy(
                src_ref=source(to),
                dst_ref=target,
                send_sem=send_sem,
                recv_sem=recv_sem,
                device_id=device(to),
                device_id_type=MESH,
            ).start()
            return carry

        lax.fori_loop(1, count, one_peer, 0)
        pltpu.make_async_copy(source(at), target, recv_sem).start()

    def along_seq(source, target, send_sem, recv_sem):
        send_line(
            source, target.at[seq_at], heads, seq_at, lambda to: (to, clu_at), send_sem, recv_sem
        )

    def along_clu(source, target, send_sem, recv_sem):
        send_line(
            source, target.at[clu_at], groups, clu_at, lambda to: (seq_at, to), send_sem, recv_sem
        )

    along_clu(lambda to: cnt_send, cnt_group, cnt_send_sem, cnt_sem)

    def head_rows(at):
        cols = pl.ds(pl.multiple_of(at * 2 * DH, 2 * DH), 2 * DH)
        return [inputs[array, :, cols] for array in range(4)]

    def put_tile(target, at, tile, packed):
        low = packed.astype(jnp.bfloat16)
        for k in range(2):
            target[pl.ds((2 * at + k) * groups, groups), tile] = low[
                :, k * DH : (k + 1) * DH
            ].reshape(groups, 16, DH)

    def pack_a(at, carry):
        rows = jnp.concatenate(head_rows(at), axis=0)
        packed = bf16_dot(pack_mat[pl.ds(0, 2 * TOK + 48), :], rows)
        put_tile(send_a, at, 0, packed[:TOK])
        put_tile(send_a, at, 1, packed[TOK : 2 * TOK])
        rest = packed[2 * TOK :].astype(jnp.bfloat16)
        for k in range(2):
            hsend[2 * at + k] = rest[:16, k * DH : (k + 1) * DH]
            ex_send[2 * at + k] = rest[16:, k * DH : (k + 1) * DH]
        return carry

    wait_bytes(inputs, input_sem)
    lax.fori_loop(0, heads // 2, pack_a, 0, unroll=2)
    wait_bytes(cnt_group, cnt_sem)
    along_seq(lambda to: cnt_group, cnt_recv, cnt2_send_sem, cnt2_sem)

    def send_heavy(step, carry):
        head = lax.rem(seq_at + step, heads)
        clu_to = lax.rem(head, groups)

        @pl.when(head * groups + clu_to != me)
        def _():
            pltpu.make_async_remote_copy(
                src_ref=hsend.at[head],
                dst_ref=hrecv.at[me],
                send_sem=hsend_sem,
                recv_sem=hrecv_sem,
                device_id=(head, clu_to),
                device_id_type=MESH,
            ).start()

        @pl.when(head * groups + clu_to == me)
        def _():
            pltpu.make_async_copy(hsend.at[head], hrecv.at[me], hrecv_sem).start()

        return carry

    lax.fori_loop(0, heads, send_heavy, 0)
    along_seq(lambda to: ex_send.at[to], ex_recv, ex_send_sem, ex_recv_sem)
    send_to_all(send_a, recv_a.at[me], send_a_sem, recv_a_sem)

    for tile in range(1, 4):
        put_pack((tile + 1) * TOK + 48, TOK, tile_picks(tile))

    def pack_bc(at, carry):
        rows = jnp.concatenate(head_rows(at), axis=0)
        packed = bf16_dot(pack_mat[pl.ds(2 * TOK + 48, 3 * TOK), :], rows)
        put_tile(send_b, at, 0, packed[:TOK])
        put_tile(send_b, at, 1, packed[TOK : 2 * TOK])
        put_tile(send_c, at, 0, packed[2 * TOK :])
        return carry

    lax.fori_loop(0, heads // 2, pack_bc, 0)

    wait_bytes(cnt_recv, cnt2_sem)
    seen = cnt_recv[...].reshape(TOK, TOK)
    heavies = jnp.min(jnp.where(seen == 4.0, lane_f, 999.0), axis=1, keepdims=True)
    heavy_all = jnp.min(heavies, axis=0, keepdims=True)
    light = lane_f != heavy_all
    more = jnp.where(light, jnp.maximum(seen - 1.0, 0.0), 0.0)
    more_low = more.astype(jnp.bfloat16)
    in_group = jnp.where(sub // 16 == lane, one, zero).astype(jnp.bfloat16)
    ahead = jnp.where(sub < lane, one, zero).astype(jnp.bfloat16)
    prior = jnp.where(lane < sub, one, zero).astype(jnp.bfloat16)
    mates = (lane < sub) & (lane % 8 == sub % 8)
    mates = jnp.where(mates, one, zero).astype(jnp.bfloat16)
    excess = jnp.maximum(bf16_dot(more_low, in_group) - 4.0, 0.0)
    excess_low = excess.astype(jnp.bfloat16)
    excess_off = bf16_dot(excess_low, ahead)
    excess_pre = bf16_dot(mates, excess_low)
    bad = (jnp.sum(excess, axis=1, keepdims=True) > 8.0) | (excess_pre + excess > 16.0)
    bad = bad | (heavies != heavy_all) | (jnp.sum(more, axis=0, keepdims=True) > OVC)
    flag_ref[0, 0] = jnp.max(jnp.where(bad, one, zero)).astype(jnp.int32)

    spot = zero
    for group in range(8):
        off, count, pre = [a[:, group : group + 1] for a in (excess_off, excess, excess_pre)]
        held = (lane_f >= off) & (lane_f < off + count)
        spot = spot + jnp.where(held, lane_f + (group * 16 + 1.0) - off + pre, zero)
    spot = jnp.where(sub % 8 == clu_at, spot, zero).reshape(16, 8, TOK)
    spot = jnp.sum(spot, axis=1).astype(jnp.bfloat16)
    spread8 = jnp.where(lane % 8 == sub, one, zero).astype(jnp.bfloat16)
    spot = jnp.where(lane[:16] // 8 == sub[:16], bf16_dot(spot, spread8), 0.0)
    spot = jnp.sum(spot, axis=0, keepdims=True) - 1.0
    to_mate[...] = jnp.where(sub_f == spot, one, zero).astype(jnp.bfloat16)
    spot = jnp.broadcast_to(spot, (TOK, TOK)).T
    to_block[...] = jnp.where(spot == lane_f, one, zero).astype(jnp.bfloat16)

    wait_bytes(ex_recv, ex_recv_sem)
    held = ex_recv[...].astype(jnp.float32)
    held = [held[:, 8 * a : 8 * a + 8, :].reshape(TOK, DH) for a in range(4)]
    held = jnp.concatenate(held, axis=1).astype(jnp.bfloat16)
    held = bf16_dot(to_mate[...], held).astype(jnp.bfloat16)
    for a in range(4):
        ex_send2[:, a] = held[:, a * DH : (a + 1) * DH].reshape(8, 16, DH)
    along_clu(lambda to: ex_send2.at[to], ex_recv2, ex_send2_sem, ex_recv2_sem)
    send_to_all(send_b, recv_b.at[me], send_b_sem, recv_b_sem)
    send_to_all(send_c, recv_c.at[me], send_c_sem, recv_c_sem)

    valid = jnp.where((seen > 0.0) & light, one, zero).astype(jnp.bfloat16)
    mine = (sub == clu_at * 16 + lane) & (lane < 16)
    mine = jnp.where(mine, one, zero).astype(jnp.bfloat16)
    more_g = bf16_dot(more_low, mine)
    valid_g = bf16_dot(valid, mine)
    more_g_low = more_g.astype(jnp.bfloat16)
    start_g = bf16_dot(prior, more_g_low)
    offset_g = bf16_dot(more_g_low, ahead)
    beyond_g = jnp.maximum(bf16_dot(more_g_low, one.astype(jnp.bfloat16)) - 4.0, 0.0)
    pre_g = bf16_dot(mates, beyond_g.astype(jnp.bfloat16))
    ex_index = lane_f - pre_g + 4.0
    first_row = lax.broadcasted_iota(jnp.int32, (1, TOK), 1).astype(jnp.float32) * 16.0
    in_tile_at = zero
    beyond_at = zero
    for c in range(16):
        count, begin, off, real = [
            a[:, c : c + 1] for a in (more_g, start_g, offset_g, valid_g)
        ]
        place = begin - off + (c * OVC + 1.0)
        held = (lane_f >= off) & (lane_f < off + count) & (lane < 4)
        in_tile_at = in_tile_at + jnp.where(held, lane_f + place, zero)
        held = (ex_index >= off) & (ex_index < off + count) & (ex_index >= 4.0)
        beyond_at = beyond_at + jnp.where(held, ex_index + place, zero)
        held = (lane_f >= begin) & (lane_f < begin + count)
        where = jnp.where(held, sub_f * 16.0 + 1.0 + lane_f - begin, zero)
        where = jnp.sum(where, axis=0, keepdims=True)
        where = jnp.where(where > 0.0, where, FAR)
        query_row = jnp.concatenate([first_row, where], axis=1)
        query_pos[c] = jnp.broadcast_to(query_row, (8, 2 * TOK))
        key_pos[c, pl.ds(0, TOK), :] = jnp.where(real > 0.0, sub_f * 16.0, FAR)
        key_pos[c, pl.ds(TOK, OVC), :] = jnp.broadcast_to(where, (TOK, TOK)).T[:OVC]
    beyond_at = jnp.sum(beyond_at.reshape(16, 8, TOK), axis=0)
    high = jnp.floor(beyond_at * (1.0 / 32.0))
    split = jnp.concatenate([high, beyond_at - high * 32.0], axis=0).astype(jnp.bfloat16)
    spread16 = jnp.where(lane % 16 == sub, one, zero).astype(jnp.bfloat16)
    split = bf16_dot(split, spread16)
    split = jnp.where(lane[:8] // 16 == sub[:8], split[:8] * 32.0 + split[8:], 0.0)
    beyond_row = jnp.sum(split, axis=0, keepdims=True) - 1.0
    tile_rows = in_tile_at.T[0:8, :] - 1.0
    slot_rows = [tile_rows[k : k + 1, :] for k in range(4)] + [beyond_row]
    slot_cols = [in_tile_at[:, k : k + 1] - 1.0 for k in range(4)]
    slot_cols.append(jnp.broadcast_to(beyond_row, (TOK, TOK)).T)

    chunk = 4
    for k in range(5):
        for m in range(16 * OVC // TOK):
            onehot[pl.ds(k * TOK, TOK), pl.ds(m * TOK, TOK)] = jnp.where(
                slot_cols[k] == lane_f + float(m * TOK), one, zero
            ).astype(jnp.bfloat16)
            pick[pl.ds(m * TOK, TOK), pl.ds(k * TOK, TOK)] = jnp.where(
                slot_rows[k] == sub_f + float(m * TOK), one, zero
            ).astype(jnp.bfloat16)

    for tile in range(6):
        for array, matrix in enumerate(tile_picks(tile) if tile < 5 else rest_picks()):
            unpack_mat[pl.ds(array * TOK, TOK), pl.ds(tile * TOK, TOK)] = matrix.T.astype(
                jnp.bfloat16
            )

    perm = flip_perm()

    def arrange(source, target, units):
        def two_sets(at, carry):
            blocks = [pl.ds(pl.multiple_of((2 * at + i) * SET, SET), SET) for i in range(2)]
            spots = [(held, unit) for held in blocks for unit in range(units)]
            rows = jnp.concatenate(
                [source(held, unit).reshape(SET * 16, DH) for held, unit in spots], axis=1
            )
            turned = bf16_dot(perm, rows).astype(jnp.bfloat16)
            for i, (held, unit) in enumerate(spots):
                target(held, unit, turned[:, i * DH : (i + 1) * DH].reshape(16, SET, DH))
            return carry

        lax.fori_loop(0, devices // (2 * SET), two_sets, 0, unroll=2)

    def put_table(first):
        def put(blocks, unit, value):
            table[first + unit, :, blocks, :] = value

        return put

    @pl.when(is_heavy_owner)
    def _():
        wait_bytes(hrecv, hrecv_sem)

        def put_heavy(blocks, unit, value):
            htable[:, blocks, :] = value

        arrange(lambda blocks, unit: hrecv[blocks], put_heavy, 1)
        k_h, v_h = [htable[4 * a : 4 * a + 4].reshape(4 * TOK, DH) for a in (1, 2)]
        hacc[...] = jnp.zeros_like(hacc)
        key_sub = lax.broadcasted_iota(jnp.int32, (4 * TOK, TOK), 0)
        key_at = lax.rem(key_sub, TOK) * 4 + lax.div(key_sub, TOK)
        query_at = lax.broadcasted_iota(jnp.int32, (4 * TOK, TOK), 1) * 4

        def heavy_tile(s, carry):
            out, dq, dk, dv = attend(
                htable[s], k_h, v_h, htable[12 + s], key_at <= query_at + s, inv_root
            )
            hacc[2, pl.ds(pl.multiple_of(s * TOK, TOK), TOK)] = out.astype(jnp.float32)
            hacc[3, pl.ds(pl.multiple_of(s * TOK, TOK), TOK)] = dq.astype(jnp.float32)
            hacc[0] += dk
            hacc[1] += dv
            return carry

        lax.fori_loop(0, 4, heavy_tile, 0)
        for array, at in enumerate((2, 3, 0, 1)):
            htable[4 * array : 4 * array + 4] = (
                hacc[at].astype(jnp.bfloat16).reshape(4, TOK, DH)
            )

        def put_hresult(blocks, unit, value):
            hresult[blocks] = value

        arrange(lambda blocks, unit: htable[:, blocks, :], put_hresult, 1)
        send_to_all(hresult, hback.at[seq_at], hres_sem, hback_sem)

    wait_bytes(recv_a, recv_a_sem)
    def put_tile_a(blocks, unit, value):
        table[4 * unit, :, blocks, :] = value

    arrange(lambda blocks, unit: recv_a[blocks, unit], put_tile_a, 2)

    wait_bytes(ex_recv2, ex_recv2_sem)
    for a in range(4):
        cols = pl.ds(a * DH, DH)
        loose[pl.ds(0, 4 * TOK), cols] = table[4, 4 * a : 4 * a + 4].reshape(4 * TOK, DH)
        loose[pl.ds(4 * TOK, TOK), cols] = ex_recv2[:, a].reshape(TOK, DH)

    def gather_chunk(at, carry):
        chosen = pick[pl.ds(pl.multiple_of(at * chunk * OVC, 64), chunk * OVC), :]
        found = bf16_dot(chosen, loose[...]).astype(jnp.bfloat16)
        for c in range(chunk):
            for array in range(4):
                over[array, at * chunk + c] = found[
                    c * OVC : (c + 1) * OVC, array * DH : (array + 1) * DH
                ]
        return carry

    lax.fori_loop(0, 16 // chunk, gather_chunk, 0)

    pad_rows = jnp.zeros((TOK - OVC, DH), jnp.bfloat16)

    def load_cluster(tile, j):
        c = tile * 4 + j
        rows = [
            jnp.concatenate([table[tile, a * 4 + j], over[a, c]], axis=0) for a in range(4)
        ]
        for a in (0, 3):
            rows[a] = jnp.concatenate([rows[a], pad_rows], axis=0)
        key_at = key_pos[c]
        allowed = jnp.concatenate([key_at, key_at], axis=1) <= query_pos[c, 0:1, :]
        return rows + [allowed]

    def attend_tiles(first, tiles, beside):
        def one_pair(at, carry):
            beside(at)
            tile = first + lax.div(at, 2)
            spots = [lax.rem(at, 2) * 2 + i for i in range(2)]
            loaded = [load_cluster(tile, j) for j in spots]
            found = [attend(*arrays, inv_root) for arrays in loaded]
            for j, results in zip(spots, found):
                c = tile * 4 + j
                for a, value in enumerate(results):
                    value = value.astype(jnp.bfloat16)
                    table[tile, a * 4 + j] = value[:TOK]
                    over_res[
                        pl.ds(pl.multiple_of(c * OVC, 16), OVC), pl.ds(a * DH, DH)
                    ] = value[TOK : TOK + OVC]
            return carry

        lax.fori_loop(0, 2 * tiles, one_pair, 0)

    def put_in(result):
        def put(blocks, unit, value):
            result[blocks, unit] = value

        return put

    def from_table(first):
        return lambda blocks, unit: table[first + unit, :, blocks, :]

    to_a = (result_a, back_a.at[me], res_a_sem, back_a_sem)
    to_b = (result_b, back_b.at[me], res_b_sem, back_b_sem)
    to_c = (result_c, back_c.at[me], res_c_sem, back_c_sem)
    attend_tiles(0, 1, lambda at: None)
    arrange(from_table(0), put_in(result_a), 1)
    send_own(result_a, back_a.at[me], back_a_sem)

    wait_bytes(recv_b, recv_b_sem)
    arrange(lambda blocks, unit: recv_b[blocks, unit], put_table(1), 2)
    attend_tiles(1, 2, lambda at: send_steps(at * 4, 4, *to_a))
    arrange(from_table(1), put_in(result_b), 2)
    send_own(result_b, back_b.at[me], back_b_sem)

    wait_bytes(recv_c, recv_c_sem)
    arrange(lambda blocks, unit: recv_c[blocks, 0], put_table(3), 1)
    attend_tiles(3, 1, lambda at: send_steps(at * 8, 8, *to_b))

    found = bf16_dot(onehot[pl.ds(4 * TOK, TOK), :], over_res[...]).astype(jnp.bfloat16)
    for a in range(4):
        ex_ret2[:, a] = found[:, a * DH : (a + 1) * DH].reshape(8, 16, DH)
    along_clu(lambda to: ex_ret2.at[to], ex_back2, ex_ret2_sem, ex_back2_sem)
    found = bf16_dot(onehot[pl.ds(0, 4 * TOK), :], over_res[...]).astype(jnp.bfloat16)
    for a in range(4):
        table[4, 4 * a : 4 * a + 4] = found[:, a * DH : (a + 1) * DH].reshape(4, TOK, DH)
    arrange(from_table(3), put_in(result_c), 2)
    send_to_all(*to_c)

    wait_bytes(ex_back2, ex_back2_sem)
    held = [ex_back2[:, a].reshape(TOK, DH) for a in range(4)]
    held = bf16_dot(to_block[...], jnp.concatenate(held, axis=1))
    held = [held[:, a * DH : (a + 1) * DH].reshape(16, 8, DH) for a in range(4)]
    ex_ret1[...] = jnp.concatenate(held, axis=1).astype(jnp.bfloat16)
    along_seq(lambda to: ex_ret1.at[to], ex_back1, ex_ret1_sem, ex_back1_sem)

    wait_bytes(hback, hback_sem)
    wait_bytes(back_a, back_a_sem)
    wait_bytes(back_b, back_b_sem)
    wait_bytes(back_c, back_c_sem)
    wait_bytes(ex_back1, ex_back1_sem)

    def unpack_heads(at, carry):
        cols = pl.ds(pl.multiple_of(at * 2 * DH, 2 * DH), 2 * DH)
        sides = []
        for k in range(2):
            head = 2 * at + k
            owners = pl.ds(head * groups, groups)
            tiles = [
                back_a[owners, 0], back_b[owners, 0], back_b[owners, 1],
                back_c[owners, 0], back_c[owners, 1],
            ]
            sides.append(
                jnp.concatenate(
                    [tile.reshape(TOK, DH) for tile in tiles]
                    + [hback[head], ex_back1[head], jnp.zeros((TOK - 48, DH), jnp.bfloat16)],
                    axis=0,
                )
            )
        found = bf16_dot(unpack_mat[...], jnp.concatenate(sides, axis=1)).astype(jnp.bfloat16)
        for array, ref in enumerate((out_ref, dq_ref, dk_ref, dv_ref)):
            ref[:, cols] = found[array * TOK : (array + 1) * TOK]
        return carry

    lax.fori_loop(0, heads // 2, unpack_heads, 0, unroll=2)

    others = pl.ds(0, devices - 1)
    wait_bytes(cnt_group.at[pl.ds(0, groups - 1)], cnt_send_sem)
    wait_bytes(cnt_recv.at[pl.ds(0, heads - 1)], cnt2_send_sem)
    for ref, sem in ((ex_send, ex_send_sem), (ex_ret1, ex_ret1_sem)):
        wait_bytes(ref.at[pl.ds(0, heads - 1)], sem)
    for ref, sem in ((ex_send2, ex_send2_sem), (ex_ret2, ex_ret2_sem)):
        wait_bytes(ref.at[pl.ds(0, groups - 1)], sem)
    wait_bytes(send_a.at[others], send_a_sem)
    wait_bytes(send_b.at[others], send_b_sem)
    wait_bytes(send_c.at[others], send_c_sem)
    wait_bytes(result_a.at[others], res_a_sem)
    wait_bytes(result_b.at[others], res_b_sem)
    wait_bytes(result_c.at[others], res_c_sem)

    @pl.when(is_heavy_owner)
    def _():
        wait_bytes(hsend.at[pl.ds(0, heads - 1)], hsend_sem)
        wait_bytes(hresult.at[others], hres_sem)

    @pl.when(jnp.logical_not(is_heavy_owner))
    def _():
        wait_bytes(hsend, hsend_sem)


def fast_path(queries, key_rows, value_rows, out_grad, cluster_ids):
    tok_rows, columns = queries.shape
    heads = columns // DH
    groups = lax.axis_size("clu")
    devices = lax.axis_size("seq") * groups
    low = jnp.bfloat16
    wide = jnp.float32
    rows = pltpu.VMEM((tok_rows, columns), low)
    vmem = pl.BlockSpec(memory_space=pltpu.VMEM)
    smem = pl.BlockSpec(memory_space=pltpu.SMEM)
    return pl.pallas_call(
        fast_kernel,
        out_shape=[rows] * 4 + [jax.ShapeDtypeStruct((1, 1), jnp.int32)],
        in_specs=[vmem] + [pl.BlockSpec(memory_space=pl.ANY)] * 4,
        out_specs=[vmem] * 4 + [smem],
        scratch_shapes=[
            pltpu.VMEM((1, TOK), wide),
            pltpu.VMEM((groups, 1, TOK), wide),
            pltpu.VMEM((heads, groups, 1, TOK), wide),
            pltpu.VMEM((5 * TOK + 48, 4 * TOK), low),
            pltpu.VMEM((4 * TOK, 6 * TOK), low),
            pltpu.VMEM((devices, 2, 16, DH), low),
            pltpu.VMEM((devices, 2, 16, DH), low),
            pltpu.VMEM((devices, 1, 16, DH), low),
            pltpu.VMEM((devices, 2, 16, DH), low),
            pltpu.VMEM((devices, 2, 16, DH), low),
            pltpu.VMEM((devices, 1, 16, DH), low),
            pltpu.VMEM((5, 16, devices, DH), low),
            pltpu.VMEM((4, 16, OVC, DH), low),
            pltpu.VMEM((16, TOK + OVC, TOK), wide),
            pltpu.VMEM((16, 8, 2 * TOK), wide),
            pltpu.VMEM((16 * OVC, 5 * TOK), low),
            pltpu.VMEM((5 * TOK, 16 * OVC), low),
            pltpu.VMEM((5 * TOK, 4 * DH), low),
            pltpu.VMEM((16 * OVC, 4 * DH), low),
            pltpu.VMEM((TOK, TOK), low),
            pltpu.VMEM((TOK, TOK), low),
            pltpu.VMEM((devices, 1, 16, DH), low),
            pltpu.VMEM((devices, 2, 16, DH), low),
            pltpu.VMEM((devices, 2, 16, DH), low),
            pltpu.VMEM((devices, 1, 16, DH), low),
            pltpu.VMEM((devices, 2, 16, DH), low),
            pltpu.VMEM((devices, 2, 16, DH), low),
            pltpu.VMEM((heads, 32, DH), low),
            pltpu.VMEM((heads, 32, DH), low),
            pltpu.VMEM((groups, 4, 16, DH), low),
            pltpu.VMEM((groups, 4, 16, DH), low),
            pltpu.VMEM((groups, 4, 16, DH), low),
            pltpu.VMEM((groups, 4, 16, DH), low),
            pltpu.VMEM((heads, 32, DH), low),
            pltpu.VMEM((heads, 32, DH), low),
            pltpu.VMEM((heads, 16, DH), low),
            pltpu.VMEM((devices, 16, DH), low),
            pltpu.VMEM((16, devices, DH), low),
            pltpu.VMEM((4, 4 * TOK, DH), wide),
            pltpu.VMEM((devices, 16, DH), low),
            pltpu.VMEM((heads, 16, DH), low),
            pltpu.VMEM((4, tok_rows, columns), low),
        ]
        + [pltpu.SemaphoreType.DMA] * 29,
        compiler_params=pltpu.CompilerParams(
            collective_id=0, has_side_effects=True, vmem_limit_bytes=44 * 1024 * 1024
        ),
    )(cluster_ids.reshape(1, tok_rows), queries, key_rows, value_rows, out_grad)


def per_device(queries, key_rows, value_rows, out_grad, cluster_ids):
    arrays = (queries, key_rows, value_rows, out_grad, cluster_ids)
    *fast, flag = fast_path(*arrays)
    return lax.cond(
        flag.reshape(()) != 0,
        lambda arrays, fast: full_capacity(*arrays),
        lambda arrays, fast: tuple(fast),
        arrays,
        tuple(fast),
    )


def solution(mesh):
    in_specs = (
        P(("seq", "clu"), None),
        P(("seq", "clu"), None),
        P(("seq", "clu"), None),
        P(("seq", "clu"), None),
        P(("seq", "clu")),
    )
    out_specs = (
        P(("seq", "clu"), None),
        P(("seq", "clu"), None),
        P(("seq", "clu"), None),
        P(("seq", "clu"), None),
    )
    return jax.shard_map(
        per_device, mesh=mesh, in_specs=in_specs, out_specs=out_specs, check_vma=False
    )
```

```python
import math

import jax
import jax.numpy as jnp
from jax import lax
from jax.experimental import pallas as pl
from jax.experimental.pallas import tpu as pltpu
from jax.sharding import PartitionSpec as P

DH = 128
TOK = 128
OVC = 80
SET = 16
FAR = 1e9
MESH = pl.DeviceIdType.MESH


masked = -1e30


def contract_last(left, right):
    return lax.dot_general(
        left, right, (((1,), (1,)), ((), ())), preferred_element_type=jnp.float32
    )


def contract_first(left, right):
    return lax.dot_general(
        left, right, (((0,), (0,)), ((), ())), preferred_element_type=jnp.float32
    )


def softmax_rows(query_head, key_head, allowed, inv_root):
    scores = contract_last(query_head, key_head) * inv_root
    scores = jnp.where(allowed, scores, masked)
    row_max = jnp.max(scores, axis=1, keepdims=True)
    weights = jnp.exp(scores - row_max)
    row_sum = jnp.sum(weights, axis=1, keepdims=True)
    return (weights / row_sum).astype(jnp.bfloat16)


def head_slice(array, head_index):
    return lax.dynamic_slice_in_dim(array, head_index * DH, DH, 1)


def full_capacity(queries, key_rows, value_rows, out_grad, cluster_ids):
    seq_count = lax.axis_size("seq")
    clu_count = lax.axis_size("clu")
    devices = seq_count * clu_count
    tok_rows = queries.shape[0]
    columns = queries.shape[1]
    head_count = columns // DH
    most_rows = 4 * tok_rows // devices
    capacity = most_rows * devices
    inv_root = 1.0 / math.sqrt(DH)
    owners = jnp.arange(devices, dtype=jnp.int32)
    member = (cluster_ids[:, None] == owners[None, :]).astype(jnp.int32)
    running = jnp.cumsum(member, axis=0) - 1
    slot_rank = jnp.sum(member * running, axis=1)
    sent_counts = jnp.sum(member, axis=0).reshape(devices, 1)
    slot_index = cluster_ids * most_rows + slot_rank
    stacked = jnp.concatenate([queries, key_rows, value_rows], axis=1)
    width_in = stacked.shape[1]
    packed = jnp.zeros((devices * most_rows, width_in), jnp.bfloat16).at[slot_index].set(stacked)
    packed = packed.reshape(devices, most_rows, width_in)
    got_rows, got_counts = (
        lax.all_to_all(packed, ("seq", "clu"), split_axis=0, concat_axis=0, tiled=True),
        lax.all_to_all(sent_counts, ("seq", "clu"), split_axis=0, concat_axis=0, tiled=True),
    )
    got_counts = got_counts.reshape(devices)
    starts = jnp.cumsum(got_counts) - got_counts
    live_total = jnp.sum(got_counts)
    within = jnp.arange(most_rows, dtype=jnp.int32)
    target = jnp.where(
        within[None, :] < got_counts[:, None], starts[:, None] + within[None, :], capacity
    )
    target = target.reshape(devices * most_rows)
    gathered = (
        jnp.zeros((capacity, width_in), jnp.bfloat16)
        .at[target]
        .set(got_rows.reshape(devices * most_rows, width_in), mode="drop")
    )
    query_block = gathered[:, :columns]
    key_block = gathered[:, columns : 2 * columns]
    value_block = gathered[:, 2 * columns : 3 * columns]
    positions = jnp.arange(capacity, dtype=jnp.int32)
    allowed = (positions[None, :] <= positions[:, None]) & (positions[None, :] < live_total)

    def forward_head(head_index, mixed_rows):
        weights_low = softmax_rows(
            head_slice(query_block, head_index),
            head_slice(key_block, head_index),
            allowed,
            inv_root,
        )
        out_head = jnp.dot(
            weights_low, head_slice(value_block, head_index), preferred_element_type=jnp.float32
        ).astype(jnp.bfloat16)
        return lax.dynamic_update_slice_in_dim(mixed_rows, out_head, head_index * DH, 1)

    mixed_rows = lax.fori_loop(
        0, head_count, forward_head, jnp.zeros((capacity, columns), jnp.bfloat16)
    )
    back_index = jnp.minimum(target, capacity - 1)
    outgoing = jnp.take(mixed_rows, back_index, axis=0).reshape(devices, most_rows, columns)
    grad_packed = (
        jnp.zeros((devices * most_rows, columns), jnp.bfloat16).at[slot_index].set(out_grad)
    )
    grad_packed = grad_packed.reshape(devices, most_rows, columns)
    returned = lax.all_to_all(outgoing, ("seq", "clu"), split_axis=0, concat_axis=0, tiled=True)
    got_grad = lax.all_to_all(grad_packed, ("seq", "clu"), split_axis=0, concat_axis=0, tiled=True)
    attention_out = jnp.take(returned.reshape(devices * most_rows, columns), slot_index, axis=0)
    grad_block = (
        jnp.zeros((capacity, columns), jnp.bfloat16)
        .at[target]
        .set(got_grad.reshape(devices * most_rows, columns), mode="drop")
    )
    delta_rows = jnp.sum(
        (grad_block.astype(jnp.float32) * mixed_rows.astype(jnp.float32)).reshape(
            capacity, head_count, DH
        ),
        axis=2,
    )

    def backward_head(head_index, grad_rows):
        query_head = head_slice(query_block, head_index)
        key_head = head_slice(key_block, head_index)
        value_head = head_slice(value_block, head_index)
        grad_head = head_slice(grad_block, head_index)
        weights_low = softmax_rows(query_head, key_head, allowed, inv_root)
        prob_grad = contract_last(grad_head, value_head)
        delta_head = lax.dynamic_slice_in_dim(delta_rows, head_index, 1, 1)
        score_grad = (weights_low.astype(jnp.float32) * (prob_grad - delta_head)).astype(
            jnp.bfloat16
        )
        query_part = (
            jnp.dot(score_grad, key_head, preferred_element_type=jnp.float32) * inv_root
        ).astype(jnp.bfloat16)
        key_part = (contract_first(score_grad, query_head) * inv_root).astype(jnp.bfloat16)
        value_part = contract_first(weights_low, grad_head).astype(jnp.bfloat16)
        grad_rows = lax.dynamic_update_slice_in_dim(grad_rows, query_part, head_index * DH, 1)
        grad_rows = lax.dynamic_update_slice_in_dim(
            grad_rows, key_part, columns + head_index * DH, 1
        )
        return lax.dynamic_update_slice_in_dim(
            grad_rows, value_part, 2 * columns + head_index * DH, 1
        )

    grad_rows = lax.fori_loop(
        0, head_count, backward_head, jnp.zeros((capacity, 3 * columns), jnp.bfloat16)
    )
    outgoing_grads = jnp.take(grad_rows, back_index, axis=0).reshape(
        devices, most_rows, 3 * columns
    )
    returned_grads = lax.all_to_all(
        outgoing_grads, ("seq", "clu"), split_axis=0, concat_axis=0, tiled=True
    )
    picked = jnp.take(returned_grads.reshape(devices * most_rows, 3 * columns), slot_index, axis=0)
    return (
        attention_out,
        picked[:, :columns],
        picked[:, columns : 2 * columns],
        picked[:, 2 * columns :],
    )


def bf16_dot(left, right):
    return jnp.dot(left, right, preferred_element_type=jnp.float32)


def flip_perm():
    row = lax.broadcasted_iota(jnp.int32, (SET * 16, SET * 16), 0)
    col = lax.broadcasted_iota(jnp.int32, (SET * 16, SET * 16), 1)
    swapped = (col % 16) * 16 + col // 16
    return (row == swapped).astype(jnp.float32).astype(jnp.bfloat16)


def attend(q, k, v, g, allowed, inv_root):
    raw = jnp.where(allowed, contract_last(k, q), masked)
    most = jnp.max(raw, axis=0, keepdims=True)
    weights = jnp.exp2((raw - most) * (inv_root * math.log2(math.e)))
    prob = weights * (1.0 / jnp.sum(weights, axis=0, keepdims=True))
    prob_low = prob.astype(jnp.bfloat16)
    prob_grad = contract_last(v, g)
    delta = jnp.sum(prob * prob_grad, axis=0, keepdims=True)
    score_grad = (prob * (prob_grad - delta)).astype(jnp.bfloat16)
    out = contract_first(v, prob_low).T.astype(jnp.bfloat16)
    dq = (contract_first(k, score_grad).T * inv_root).astype(jnp.bfloat16)
    dk = bf16_dot(score_grad, q) * inv_root
    dv = bf16_dot(prob_low, g)
    return out, dq, dk, dv


def fast_kernel(
    ids_ref, q_ref, k_ref, v_ref, g_ref,
    out_ref, dq_ref, dk_ref, dv_ref, flag_ref,
    cnt_send, cnt_group, cnt_recv, pack_mat, unpack_mat,
    send_a, send_b, send_c, recv_a, recv_b, recv_c, table,
    over, key_pos, query_pos, pick, onehot, loose, over_res, to_mate, to_block,
    result_a, result_b, result_c, back_a, back_b, back_c,
    ex_send, ex_recv, ex_send2, ex_recv2, ex_ret2, ex_back2, ex_ret1, ex_back1,
    hsend, hrecv, htable, hacc, hresult, hback, inputs,
    cnt_send_sem, cnt_sem, cnt2_send_sem, cnt2_sem,
    send_a_sem, recv_a_sem, send_b_sem, recv_b_sem, send_c_sem, recv_c_sem,
    res_a_sem, back_a_sem, res_b_sem, back_b_sem, res_c_sem, back_c_sem,
    ex_send_sem, ex_recv_sem, ex_send2_sem, ex_recv2_sem,
    ex_ret2_sem, ex_back2_sem, ex_ret1_sem, ex_back1_sem,
    hsend_sem, hrecv_sem, hres_sem, hback_sem, input_sem,
):
    seq_at = lax.axis_index("seq")
    clu_at = lax.axis_index("clu")
    groups = lax.axis_size("clu")
    heads = lax.axis_size("seq")
    devices = heads * groups
    me = seq_at * groups + clu_at
    inv_root = 1.0 / math.sqrt(DH)
    is_heavy_owner = lax.rem(seq_at, groups) == clu_at
    at_x, at_z = lax.div(seq_at, 4), lax.rem(seq_at, 4)
    at_y, at_core = lax.div(clu_at, 2), lax.rem(clu_at, 2)

    def coords(device):
        return (lax.div(device, groups), lax.rem(device, groups))

    def turn(by):
        return by + at_core * (4 - 2 * by)

    eight = []
    for by_x, by_z, by_clu in zip(
        (0, 3, 2, 1, 0, 3, 2, 0), (0, 3, 2, 1, 1, 0, 3, 2), (0, 4, 6, 7, 2, 5, 1, 3)
    ):
        y = lax.rem(at_y + turn(by_clu // 2), 4)
        eight.append((turn(by_x), turn(by_z), y * 2 + lax.rem(at_core + by_clu % 2, 2)))

    def send_steps(first, count, source, target, send_sem, recv_sem):
        def one_eight(step, carry):
            by = lax.rem(step * 11, 16)
            by_x, by_z = lax.div(by, 4), lax.rem(by, 4)
            x = at_x + turn(by_x)
            z = at_z + turn(by_z)
            for j, (more_x, more_z, clu_to) in enumerate(eight):
                seq_to = lax.rem(x + more_x, 4) * 4 + lax.rem(z + more_z, 4)

                def start():
                    pltpu.make_async_remote_copy(
                        src_ref=source.at[seq_to * groups + clu_to],
                        dst_ref=target,
                        send_sem=send_sem,
                        recv_sem=recv_sem,
                        device_id=(seq_to, clu_to),
                        device_id_type=MESH,
                    ).start()

                if j == 0:
                    pl.when(step > 0)(start)
                else:
                    start()
            return carry

        lax.fori_loop(first, first + count, one_eight, 0)

    def send_own(source, target, recv_sem):
        pltpu.make_async_copy(source.at[me], target, recv_sem).start()

    def send_to_all(source, target, send_sem, recv_sem):
        send_steps(0, devices // 8, source, target, send_sem, recv_sem)
        send_own(source, target, recv_sem)

    def wait_bytes(ref, sem):
        pltpu.make_async_copy(ref, ref, sem).wait()

    for array, ref in enumerate((q_ref, k_ref, v_ref, g_ref)):
        pltpu.make_async_copy(ref, inputs.at[array], input_sem).start()
    barrier = pltpu.get_barrier_semaphore()

    def greet(step, carry):
        pl.semaphore_signal(
            barrier, inc=1, device_id=coords(lax.rem(me + step, devices)), device_id_type=MESH
        )
        return carry

    lax.fori_loop(1, devices, greet, 0)

    sub = lax.broadcasted_iota(jnp.int32, (TOK, TOK), 0)
    lane = lax.broadcasted_iota(jnp.int32, (TOK, TOK), 1)
    sub_f = sub.astype(jnp.float32)
    lane_f = lane.astype(jnp.float32)
    ids_l = jnp.broadcast_to(ids_ref[...].astype(jnp.float32), (TOK, TOK))
    ids_s = ids_l.T
    one = jnp.ones((TOK, TOK), jnp.float32)
    zero = jnp.zeros((TOK, TOK), jnp.float32)
    same = ids_l == ids_s
    rank_l = jnp.sum(jnp.where(same & (sub < lane), one, zero), axis=0, keepdims=True)
    rank_s = jnp.sum(jnp.where(same & (lane < sub), one, zero), axis=1, keepdims=True)
    count_l = jnp.sum(jnp.where(same, one, zero), axis=0, keepdims=True)
    cnt_send[...] = jnp.sum(jnp.where(ids_s == lane_f, one, zero), axis=0, keepdims=True)
    ids_row = ids_l[0:1, :]
    heavy = jnp.min(jnp.where(count_l == 4.0, ids_row, 999.0), axis=1, keepdims=True)
    group_l = jnp.floor(ids_l * (1.0 / 16.0))
    group_s = jnp.floor(ids_s * (1.0 / 16.0))
    earlier = (ids_s < ids_l) | (same & (sub < lane))
    later = (ids_l < ids_s) | (same & (lane < sub))
    before = (group_l == group_s) & (ids_s != heavy) & (rank_s >= 1.0) & earlier
    over_at = jnp.sum(jnp.where(before, one, zero), axis=0, keepdims=True)
    behind = (group_l == group_s) & (ids_l != heavy) & (rank_l >= 1.0) & later
    over_at_s = jnp.sum(jnp.where(behind, one, zero), axis=1, keepdims=True)
    excess_s = (ids_s != heavy) & (rank_s >= 1.0) & (over_at_s >= 4.0)
    excess_at = jnp.sum(jnp.where(excess_s & earlier, one, zero), axis=0, keepdims=True)
    light_l = ids_l != heavy
    slot_group = (sub // 16).astype(jnp.float32)
    in_tile = sub % 16
    over_l = light_l & (rank_l >= 1.0)

    def tile_picks(tile):
        at_slot = (in_tile % 4).astype(jnp.float32)
        if tile < 4:
            cluster = slot_group * 16.0 + at_slot + 4.0 * tile
            taken = (ids_l == cluster) & (rank_l == 0.0) & light_l
        else:
            taken = (group_l == slot_group) & over_l & (over_at == at_slot)
        return [jnp.where(taken & (in_tile // 4 == array), one, zero) for array in range(4)]

    def rest_picks():
        picks = []
        for array in range(4):
            chosen = (ids_l == heavy) & (rank_l == (sub % 4).astype(jnp.float32))
            chosen = chosen & (sub // 4 == array) & (sub < 16)
            beyond = over_l & (over_at >= 4.0) & (excess_at == (sub % 8).astype(jnp.float32))
            beyond = beyond & (sub // 8 == array + 2)
            picks.append(jnp.where(chosen | beyond, one, zero))
        return picks

    def put_pack(at_row, count, picks):
        for array, matrix in enumerate(picks):
            pack_mat[pl.ds(at_row, count), pl.ds(array * TOK, TOK)] = matrix[:count].astype(
                jnp.bfloat16
            )

    put_pack(0, TOK, tile_picks(0))
    put_pack(TOK, TOK, tile_picks(4))
    put_pack(2 * TOK, 48, rest_picks())

    pl.semaphore_wait(barrier, devices - 1)

    def send_line(source, target, count, at, device, send_sem, recv_sem):
        def one_peer(step, carry):
            to = lax.rem(at + step, count)
            pltpu.make_async_remote_copy(
                src_ref=source(to),
                dst_ref=target,
                send_sem=send_sem,
                recv_sem=recv_sem,
                device_id=device(to),
                device_id_type=MESH,
            ).start()
            return carry

        lax.fori_loop(1, count, one_peer, 0)
        pltpu.make_async_copy(source(at), target, recv_sem).start()

    def along_seq(source, target, send_sem, recv_sem):
        send_line(
            source, target.at[seq_at], heads, seq_at, lambda to: (to, clu_at), send_sem, recv_sem
        )

    def along_clu(source, target, send_sem, recv_sem):
        send_line(
            source, target.at[clu_at], groups, clu_at, lambda to: (seq_at, to), send_sem, recv_sem
        )

    along_clu(lambda to: cnt_send, cnt_group, cnt_send_sem, cnt_sem)

    def head_rows(at):
        cols = pl.ds(pl.multiple_of(at * 2 * DH, 2 * DH), 2 * DH)
        return [inputs[array, :, cols] for array in range(4)]

    def put_tile(target, at, tile, packed):
        low = packed.astype(jnp.bfloat16)
        for k in range(2):
            target[pl.ds((2 * at + k) * groups, groups), tile] = low[
                :, k * DH : (k + 1) * DH
            ].reshape(groups, 16, DH)

    def pack_a(at, carry):
        rows = jnp.concatenate(head_rows(at), axis=0)
        packed = bf16_dot(pack_mat[pl.ds(0, 2 * TOK + 48), :], rows)
        put_tile(send_a, at, 0, packed[:TOK])
        put_tile(send_a, at, 1, packed[TOK : 2 * TOK])
        rest = packed[2 * TOK :].astype(jnp.bfloat16)
        for k in range(2):
            hsend[2 * at + k] = rest[:16, k * DH : (k + 1) * DH]
            ex_send[2 * at + k] = rest[16:, k * DH : (k + 1) * DH]
        return carry

    wait_bytes(inputs, input_sem)
    lax.fori_loop(0, heads // 2, pack_a, 0, unroll=2)
    wait_bytes(cnt_group, cnt_sem)
    along_seq(lambda to: cnt_group, cnt_recv, cnt2_send_sem, cnt2_sem)

    def send_heavy(step, carry):
        head = lax.rem(seq_at + step, heads)
        clu_to = lax.rem(head, groups)

        @pl.when(head * groups + clu_to != me)
        def _():
            pltpu.make_async_remote_copy(
                src_ref=hsend.at[head],
                dst_ref=hrecv.at[me],
                send_sem=hsend_sem,
                recv_sem=hrecv_sem,
                device_id=(head, clu_to),
                device_id_type=MESH,
            ).start()

        @pl.when(head * groups + clu_to == me)
        def _():
            pltpu.make_async_copy(hsend.at[head], hrecv.at[me], hrecv_sem).start()

        return carry

    lax.fori_loop(0, heads, send_heavy, 0)
    along_seq(lambda to: ex_send.at[to], ex_recv, ex_send_sem, ex_recv_sem)
    send_to_all(send_a, recv_a.at[me], send_a_sem, recv_a_sem)

    for tile in range(1, 4):
        put_pack((tile + 1) * TOK + 48, TOK, tile_picks(tile))

    def pack_bc(at, carry):
        rows = jnp.concatenate(head_rows(at), axis=0)
        packed = bf16_dot(pack_mat[pl.ds(2 * TOK + 48, 3 * TOK), :], rows)
        put_tile(send_b, at, 0, packed[:TOK])
        put_tile(send_b, at, 1, packed[TOK : 2 * TOK])
        put_tile(send_c, at, 0, packed[2 * TOK :])
        return carry

    lax.fori_loop(0, heads // 2, pack_bc, 0)

    wait_bytes(cnt_recv, cnt2_sem)
    seen = cnt_recv[...].reshape(TOK, TOK)
    heavies = jnp.min(jnp.where(seen == 4.0, lane_f, 999.0), axis=1, keepdims=True)
    heavy_all = jnp.min(heavies, axis=0, keepdims=True)
    light = lane_f != heavy_all
    more = jnp.where(light, jnp.maximum(seen - 1.0, 0.0), 0.0)
    more_low = more.astype(jnp.bfloat16)
    in_group = jnp.where(sub // 16 == lane, one, zero).astype(jnp.bfloat16)
    ahead = jnp.where(sub < lane, one, zero).astype(jnp.bfloat16)
    prior = jnp.where(lane < sub, one, zero).astype(jnp.bfloat16)
    mates = (lane < sub) & (lane % 8 == sub % 8)
    mates = jnp.where(mates, one, zero).astype(jnp.bfloat16)
    excess = jnp.maximum(bf16_dot(more_low, in_group) - 4.0, 0.0)
    excess_low = excess.astype(jnp.bfloat16)
    excess_off = bf16_dot(excess_low, ahead)
    excess_pre = bf16_dot(mates, excess_low)
    bad = (jnp.sum(excess, axis=1, keepdims=True) > 8.0) | (excess_pre + excess > 16.0)
    bad = bad | (heavies != heavy_all) | (jnp.sum(more, axis=0, keepdims=True) > OVC)
    flag_ref[0, 0] = jnp.max(jnp.where(bad, one, zero)).astype(jnp.int32)

    spot = zero
    for group in range(8):
        off, count, pre = [a[:, group : group + 1] for a in (excess_off, excess, excess_pre)]
        held = (lane_f >= off) & (lane_f < off + count)
        spot = spot + jnp.where(held, lane_f + (group * 16 + 1.0) - off + pre, zero)
    spot = jnp.where(sub % 8 == clu_at, spot, zero).reshape(16, 8, TOK)
    spot = jnp.sum(spot, axis=1).astype(jnp.bfloat16)
    spread8 = jnp.where(lane % 8 == sub, one, zero).astype(jnp.bfloat16)
    spot = jnp.where(lane[:16] // 8 == sub[:16], bf16_dot(spot, spread8), 0.0)
    spot = jnp.sum(spot, axis=0, keepdims=True) - 1.0
    to_mate[...] = jnp.where(sub_f == spot, one, zero).astype(jnp.bfloat16)
    spot = jnp.broadcast_to(spot, (TOK, TOK)).T
    to_block[...] = jnp.where(spot == lane_f, one, zero).astype(jnp.bfloat16)

    wait_bytes(ex_recv, ex_recv_sem)
    held = ex_recv[...].astype(jnp.float32)
    held = [held[:, 8 * a : 8 * a + 8, :].reshape(TOK, DH) for a in range(4)]
    held = jnp.concatenate(held, axis=1).astype(jnp.bfloat16)
    held = bf16_dot(to_mate[...], held).astype(jnp.bfloat16)
    for a in range(4):
        ex_send2[:, a] = held[:, a * DH : (a + 1) * DH].reshape(8, 16, DH)
    along_clu(lambda to: ex_send2.at[to], ex_recv2, ex_send2_sem, ex_recv2_sem)
    send_to_all(send_b, recv_b.at[me], send_b_sem, recv_b_sem)
    send_to_all(send_c, recv_c.at[me], send_c_sem, recv_c_sem)

    valid = jnp.where((seen > 0.0) & light, one, zero).astype(jnp.bfloat16)
    mine = (sub == clu_at * 16 + lane) & (lane < 16)
    mine = jnp.where(mine, one, zero).astype(jnp.bfloat16)
    more_g = bf16_dot(more_low, mine)
    valid_g = bf16_dot(valid, mine)
    more_g_low = more_g.astype(jnp.bfloat16)
    start_g = bf16_dot(prior, more_g_low)
    offset_g = bf16_dot(more_g_low, ahead)
    beyond_g = jnp.maximum(bf16_dot(more_g_low, one.astype(jnp.bfloat16)) - 4.0, 0.0)
    pre_g = bf16_dot(mates, beyond_g.astype(jnp.bfloat16))
    ex_index = lane_f - pre_g + 4.0
    first_row = lax.broadcasted_iota(jnp.int32, (1, TOK), 1).astype(jnp.float32) * 16.0
    in_tile_at = zero
    beyond_at = zero
    for c in range(16):
        count, begin, off, real = [
            a[:, c : c + 1] for a in (more_g, start_g, offset_g, valid_g)
        ]
        place = begin - off + (c * OVC + 1.0)
        held = (lane_f >= off) & (lane_f < off + count) & (lane < 4)
        in_tile_at = in_tile_at + jnp.where(held, lane_f + place, zero)
        held = (ex_index >= off) & (ex_index < off + count) & (ex_index >= 4.0)
        beyond_at = beyond_at + jnp.where(held, ex_index + place, zero)
        held = (lane_f >= begin) & (lane_f < begin + count)
        where = jnp.where(held, sub_f * 16.0 + 1.0 + lane_f - begin, zero)
        where = jnp.sum(where, axis=0, keepdims=True)
        where = jnp.where(where > 0.0, where, FAR)
        query_row = jnp.concatenate([first_row, where], axis=1)
        query_pos[c] = jnp.broadcast_to(query_row, (8, 2 * TOK))
        key_pos[c, pl.ds(0, TOK), :] = jnp.where(real > 0.0, sub_f * 16.0, FAR)
        key_pos[c, pl.ds(TOK, OVC), :] = jnp.broadcast_to(where, (TOK, TOK)).T[:OVC]
    beyond_at = jnp.sum(beyond_at.reshape(16, 8, TOK), axis=0)
    high = jnp.floor(beyond_at * (1.0 / 32.0))
    split = jnp.concatenate([high, beyond_at - high * 32.0], axis=0).astype(jnp.bfloat16)
    spread16 = jnp.where(lane % 16 == sub, one, zero).astype(jnp.bfloat16)
    split = bf16_dot(split, spread16)
    split = jnp.where(lane[:8] // 16 == sub[:8], split[:8] * 32.0 + split[8:], 0.0)
    beyond_row = jnp.sum(split, axis=0, keepdims=True) - 1.0
    tile_rows = in_tile_at.T[0:8, :] - 1.0
    slot_rows = [tile_rows[k : k + 1, :] for k in range(4)] + [beyond_row]
    slot_cols = [in_tile_at[:, k : k + 1] - 1.0 for k in range(4)]
    slot_cols.append(jnp.broadcast_to(beyond_row, (TOK, TOK)).T)

    chunk = 4
    for k in range(5):
        for m in range(16 * OVC // TOK):
            onehot[pl.ds(k * TOK, TOK), pl.ds(m * TOK, TOK)] = jnp.where(
                slot_cols[k] == lane_f + float(m * TOK), one, zero
            ).astype(jnp.bfloat16)
            pick[pl.ds(m * TOK, TOK), pl.ds(k * TOK, TOK)] = jnp.where(
                slot_rows[k] == sub_f + float(m * TOK), one, zero
            ).astype(jnp.bfloat16)

    for tile in range(6):
        for array, matrix in enumerate(tile_picks(tile) if tile < 5 else rest_picks()):
            unpack_mat[pl.ds(array * TOK, TOK), pl.ds(tile * TOK, TOK)] = matrix.T.astype(
                jnp.bfloat16
            )

    perm = flip_perm()

    def arrange(source, target, units):
        def two_sets(at, carry):
            blocks = [pl.ds(pl.multiple_of((2 * at + i) * SET, SET), SET) for i in range(2)]
            spots = [(held, unit) for held in blocks for unit in range(units)]
            rows = jnp.concatenate(
                [source(held, unit).reshape(SET * 16, DH) for held, unit in spots], axis=1
            )
            turned = bf16_dot(perm, rows).astype(jnp.bfloat16)
            for i, (held, unit) in enumerate(spots):
                target(held, unit, turned[:, i * DH : (i + 1) * DH].reshape(16, SET, DH))
            return carry

        lax.fori_loop(0, devices // (2 * SET), two_sets, 0, unroll=2)

    def put_table(first):
        def put(blocks, unit, value):
            table[first + unit, :, blocks, :] = value

        return put

    @pl.when(is_heavy_owner)
    def _():
        wait_bytes(hrecv, hrecv_sem)

        def put_heavy(blocks, unit, value):
            htable[:, blocks, :] = value

        arrange(lambda blocks, unit: hrecv[blocks], put_heavy, 1)
        k_h, v_h = [htable[4 * a : 4 * a + 4].reshape(4 * TOK, DH) for a in (1, 2)]
        hacc[...] = jnp.zeros_like(hacc)
        key_sub = lax.broadcasted_iota(jnp.int32, (4 * TOK, TOK), 0)
        key_at = lax.rem(key_sub, TOK) * 4 + lax.div(key_sub, TOK)
        query_at = lax.broadcasted_iota(jnp.int32, (4 * TOK, TOK), 1) * 4

        def heavy_tile(s, carry):
            out, dq, dk, dv = attend(
                htable[s], k_h, v_h, htable[12 + s], key_at <= query_at + s, inv_root
            )
            hacc[2, pl.ds(pl.multiple_of(s * TOK, TOK), TOK)] = out.astype(jnp.float32)
            hacc[3, pl.ds(pl.multiple_of(s * TOK, TOK), TOK)] = dq.astype(jnp.float32)
            hacc[0] += dk
            hacc[1] += dv
            return carry

        lax.fori_loop(0, 4, heavy_tile, 0)
        for array, at in enumerate((2, 3, 0, 1)):
            htable[4 * array : 4 * array + 4] = (
                hacc[at].astype(jnp.bfloat16).reshape(4, TOK, DH)
            )

        def put_hresult(blocks, unit, value):
            hresult[blocks] = value

        arrange(lambda blocks, unit: htable[:, blocks, :], put_hresult, 1)
        send_to_all(hresult, hback.at[seq_at], hres_sem, hback_sem)

    wait_bytes(recv_a, recv_a_sem)
    def put_tile_a(blocks, unit, value):
        table[4 * unit, :, blocks, :] = value

    arrange(lambda blocks, unit: recv_a[blocks, unit], put_tile_a, 2)

    wait_bytes(ex_recv2, ex_recv2_sem)
    for a in range(4):
        cols = pl.ds(a * DH, DH)
        loose[pl.ds(0, 4 * TOK), cols] = table[4, 4 * a : 4 * a + 4].reshape(4 * TOK, DH)
        loose[pl.ds(4 * TOK, TOK), cols] = ex_recv2[:, a].reshape(TOK, DH)

    def gather_chunk(at, carry):
        chosen = pick[pl.ds(pl.multiple_of(at * chunk * OVC, 64), chunk * OVC), :]
        found = bf16_dot(chosen, loose[...]).astype(jnp.bfloat16)
        for c in range(chunk):
            for array in range(4):
                over[array, at * chunk + c] = found[
                    c * OVC : (c + 1) * OVC, array * DH : (array + 1) * DH
                ]
        return carry

    lax.fori_loop(0, 16 // chunk, gather_chunk, 0)

    pad_rows = jnp.zeros((TOK - OVC, DH), jnp.bfloat16)

    def load_cluster(tile, j):
        c = tile * 4 + j
        rows = [
            jnp.concatenate([table[tile, a * 4 + j], over[a, c]], axis=0) for a in range(4)
        ]
        for a in (0, 3):
            rows[a] = jnp.concatenate([rows[a], pad_rows], axis=0)
        key_at = key_pos[c]
        allowed = jnp.concatenate([key_at, key_at], axis=1) <= query_pos[c, 0:1, :]
        return rows + [allowed]

    def attend_tiles(first, tiles, beside):
        def one_pair(at, carry):
            beside(at)
            tile = first + lax.div(at, 2)
            spots = [lax.rem(at, 2) * 2 + i for i in range(2)]
            loaded = [load_cluster(tile, j) for j in spots]
            found = [attend(*arrays, inv_root) for arrays in loaded]
            for j, results in zip(spots, found):
                c = tile * 4 + j
                for a, value in enumerate(results):
                    value = value.astype(jnp.bfloat16)
                    table[tile, a * 4 + j] = value[:TOK]
                    over_res[
                        pl.ds(pl.multiple_of(c * OVC, 16), OVC), pl.ds(a * DH, DH)
                    ] = value[TOK : TOK + OVC]
            return carry

        lax.fori_loop(0, 2 * tiles, one_pair, 0)

    def put_in(result):
        def put(blocks, unit, value):
            result[blocks, unit] = value

        return put

    def from_table(first):
        return lambda blocks, unit: table[first + unit, :, blocks, :]

    to_a = (result_a, back_a.at[me], res_a_sem, back_a_sem)
    to_b = (result_b, back_b.at[me], res_b_sem, back_b_sem)
    to_c = (result_c, back_c.at[me], res_c_sem, back_c_sem)
    attend_tiles(0, 1, lambda at: None)
    arrange(from_table(0), put_in(result_a), 1)
    send_own(result_a, back_a.at[me], back_a_sem)

    wait_bytes(recv_b, recv_b_sem)
    arrange(lambda blocks, unit: recv_b[blocks, unit], put_table(1), 2)
    attend_tiles(1, 2, lambda at: send_steps(at * 4, 4, *to_a))
    arrange(from_table(1), put_in(result_b), 2)
    send_own(result_b, back_b.at[me], back_b_sem)

    wait_bytes(recv_c, recv_c_sem)
    arrange(lambda blocks, unit: recv_c[blocks, 0], put_table(3), 1)
    attend_tiles(3, 1, lambda at: send_steps(at * 8, 8, *to_b))

    found = bf16_dot(onehot[pl.ds(4 * TOK, TOK), :], over_res[...]).astype(jnp.bfloat16)
    for a in range(4):
        ex_ret2[:, a] = found[:, a * DH : (a + 1) * DH].reshape(8, 16, DH)
    along_clu(lambda to: ex_ret2.at[to], ex_back2, ex_ret2_sem, ex_back2_sem)
    found = bf16_dot(onehot[pl.ds(0, 4 * TOK), :], over_res[...]).astype(jnp.bfloat16)
    for a in range(4):
        table[4, 4 * a : 4 * a + 4] = found[:, a * DH : (a + 1) * DH].reshape(4, TOK, DH)
    arrange(from_table(3), put_in(result_c), 2)
    send_to_all(*to_c)

    wait_bytes(ex_back2, ex_back2_sem)
    held = [ex_back2[:, a].reshape(TOK, DH) for a in range(4)]
    held = bf16_dot(to_block[...], jnp.concatenate(held, axis=1))
    held = [held[:, a * DH : (a + 1) * DH].reshape(16, 8, DH) for a in range(4)]
    ex_ret1[...] = jnp.concatenate(held, axis=1).astype(jnp.bfloat16)
    along_seq(lambda to: ex_ret1.at[to], ex_back1, ex_ret1_sem, ex_back1_sem)

    wait_bytes(hback, hback_sem)
    wait_bytes(back_a, back_a_sem)
    wait_bytes(back_b, back_b_sem)
    wait_bytes(back_c, back_c_sem)
    wait_bytes(ex_back1, ex_back1_sem)

    def unpack_heads(at, carry):
        cols = pl.ds(pl.multiple_of(at * 2 * DH, 2 * DH), 2 * DH)
        sides = []
        for k in range(2):
            head = 2 * at + k
            owners = pl.ds(head * groups, groups)
            tiles = [
                back_a[owners, 0], back_b[owners, 0], back_b[owners, 1],
                back_c[owners, 0], back_c[owners, 1],
            ]
            sides.append(
                jnp.concatenate(
                    [tile.reshape(TOK, DH) for tile in tiles]
                    + [hback[head], ex_back1[head], jnp.zeros((TOK - 48, DH), jnp.bfloat16)],
                    axis=0,
                )
            )
        found = bf16_dot(unpack_mat[...], jnp.concatenate(sides, axis=1)).astype(jnp.bfloat16)
        for array, ref in enumerate((out_ref, dq_ref, dk_ref, dv_ref)):
            ref[:, cols] = found[array * TOK : (array + 1) * TOK]
        return carry

    lax.fori_loop(0, heads // 2, unpack_heads, 0, unroll=2)

    others = pl.ds(0, devices - 1)
    wait_bytes(cnt_group.at[pl.ds(0, groups - 1)], cnt_send_sem)
    wait_bytes(cnt_recv.at[pl.ds(0, heads - 1)], cnt2_send_sem)
    for ref, sem in ((ex_send, ex_send_sem), (ex_ret1, ex_ret1_sem)):
        wait_bytes(ref.at[pl.ds(0, heads - 1)], sem)
    for ref, sem in ((ex_send2, ex_send2_sem), (ex_ret2, ex_ret2_sem)):
        wait_bytes(ref.at[pl.ds(0, groups - 1)], sem)
    wait_bytes(send_a.at[others], send_a_sem)
    wait_bytes(send_b.at[others], send_b_sem)
    wait_bytes(send_c.at[others], send_c_sem)
    wait_bytes(result_a.at[others], res_a_sem)
    wait_bytes(result_b.at[others], res_b_sem)
    wait_bytes(result_c.at[others], res_c_sem)

    @pl.when(is_heavy_owner)
    def _():
        wait_bytes(hsend.at[pl.ds(0, heads - 1)], hsend_sem)
        wait_bytes(hresult.at[others], hres_sem)

    @pl.when(jnp.logical_not(is_heavy_owner))
    def _():
        wait_bytes(hsend, hsend_sem)


def fast_path(queries, key_rows, value_rows, out_grad, cluster_ids):
    tok_rows, columns = queries.shape
    heads = columns // DH
    groups = lax.axis_size("clu")
    devices = lax.axis_size("seq") * groups
    low = jnp.bfloat16
    wide = jnp.float32
    rows = pltpu.VMEM((tok_rows, columns), low)
    vmem = pl.BlockSpec(memory_space=pltpu.VMEM)
    smem = pl.BlockSpec(memory_space=pltpu.SMEM)
    return pl.pallas_call(
        fast_kernel,
        out_shape=[rows] * 4 + [jax.ShapeDtypeStruct((1, 1), jnp.int32)],
        in_specs=[vmem] + [pl.BlockSpec(memory_space=pl.ANY)] * 4,
        out_specs=[vmem] * 4 + [smem],
        scratch_shapes=[
            pltpu.VMEM((1, TOK), wide),
            pltpu.VMEM((groups, 1, TOK), wide),
            pltpu.VMEM((heads, groups, 1, TOK), wide),
            pltpu.VMEM((5 * TOK + 48, 4 * TOK), low),
            pltpu.VMEM((4 * TOK, 6 * TOK), low),
            pltpu.VMEM((devices, 2, 16, DH), low),
            pltpu.VMEM((devices, 2, 16, DH), low),
            pltpu.VMEM((devices, 1, 16, DH), low),
            pltpu.VMEM((devices, 2, 16, DH), low),
            pltpu.VMEM((devices, 2, 16, DH), low),
            pltpu.VMEM((devices, 1, 16, DH), low),
            pltpu.VMEM((5, 16, devices, DH), low),
            pltpu.VMEM((4, 16, OVC, DH), low),
            pltpu.VMEM((16, TOK + OVC, TOK), wide),
            pltpu.VMEM((16, 8, 2 * TOK), wide),
            pltpu.VMEM((16 * OVC, 5 * TOK), low),
            pltpu.VMEM((5 * TOK, 16 * OVC), low),
            pltpu.VMEM((5 * TOK, 4 * DH), low),
            pltpu.VMEM((16 * OVC, 4 * DH), low),
            pltpu.VMEM((TOK, TOK), low),
            pltpu.VMEM((TOK, TOK), low),
            pltpu.VMEM((devices, 1, 16, DH), low),
            pltpu.VMEM((devices, 2, 16, DH), low),
            pltpu.VMEM((devices, 2, 16, DH), low),
            pltpu.VMEM((devices, 1, 16, DH), low),
            pltpu.VMEM((devices, 2, 16, DH), low),
            pltpu.VMEM((devices, 2, 16, DH), low),
            pltpu.VMEM((heads, 32, DH), low),
            pltpu.VMEM((heads, 32, DH), low),
            pltpu.VMEM((groups, 4, 16, DH), low),
            pltpu.VMEM((groups, 4, 16, DH), low),
            pltpu.VMEM((groups, 4, 16, DH), low),
            pltpu.VMEM((groups, 4, 16, DH), low),
            pltpu.VMEM((heads, 32, DH), low),
            pltpu.VMEM((heads, 32, DH), low),
            pltpu.VMEM((heads, 16, DH), low),
            pltpu.VMEM((devices, 16, DH), low),
            pltpu.VMEM((16, devices, DH), low),
            pltpu.VMEM((4, 4 * TOK, DH), wide),
            pltpu.VMEM((devices, 16, DH), low),
            pltpu.VMEM((heads, 16, DH), low),
            pltpu.VMEM((4, tok_rows, columns), low),
        ]
        + [pltpu.SemaphoreType.DMA] * 29,
        compiler_params=pltpu.CompilerParams(
            collective_id=0, has_side_effects=True, vmem_limit_bytes=44 * 1024 * 1024
        ),
    )(cluster_ids.reshape(1, tok_rows), queries, key_rows, value_rows, out_grad)


def copy_kernel(*refs):
    sem = refs[-1]
    copies = [
        pltpu.make_async_copy(refs[i], refs[4 + i], sem.at[i]) for i in range(4)
    ]
    for copy in copies:
        copy.start()
    for copy in copies:
        copy.wait()


def copy_out(arrays):
    anywhere = pl.BlockSpec(memory_space=pl.ANY)
    return pl.pallas_call(
        copy_kernel,
        out_shape=[pltpu.HBM(a.shape, a.dtype) for a in arrays],
        in_specs=[anywhere] * 4,
        out_specs=[anywhere] * 4,
        scratch_shapes=[pltpu.SemaphoreType.DMA((4,))],
    )(*arrays)


def per_device(queries, key_rows, value_rows, out_grad, cluster_ids):
    arrays = (queries, key_rows, value_rows, out_grad, cluster_ids)
    *fast, flag = fast_path(*arrays)
    return lax.cond(
        flag.reshape(()) != 0,
        lambda arrays, fast: full_capacity(*arrays),
        lambda arrays, fast: tuple(copy_out(fast)),
        arrays,
        tuple(fast),
    )


def solution(mesh):
    in_specs = (
        P(("seq", "clu"), None),
        P(("seq", "clu"), None),
        P(("seq", "clu"), None),
        P(("seq", "clu"), None),
        P(("seq", "clu")),
    )
    out_specs = (
        P(("seq", "clu"), None),
        P(("seq", "clu"), None),
        P(("seq", "clu"), None),
        P(("seq", "clu"), None),
    )
    return jax.shard_map(
        per_device, mesh=mesh, in_specs=in_specs, out_specs=out_specs, check_vma=False
    )
```

```python
import math

import jax
import jax.numpy as jnp
from jax import lax
from jax.experimental import pallas as pl
from jax.experimental.pallas import tpu as pltpu
from jax.sharding import PartitionSpec as P

DH = 128
TOK = 128
OVC = 80
SET = 16
FAR = 1e9
MESH = pl.DeviceIdType.MESH


masked = -1e30


def contract_last(left, right):
    return lax.dot_general(
        left, right, (((1,), (1,)), ((), ())), preferred_element_type=jnp.float32
    )


def contract_first(left, right):
    return lax.dot_general(
        left, right, (((0,), (0,)), ((), ())), preferred_element_type=jnp.float32
    )


def softmax_rows(query_head, key_head, allowed, inv_root):
    scores = contract_last(query_head, key_head) * inv_root
    scores = jnp.where(allowed, scores, masked)
    row_max = jnp.max(scores, axis=1, keepdims=True)
    weights = jnp.exp(scores - row_max)
    row_sum = jnp.sum(weights, axis=1, keepdims=True)
    return (weights / row_sum).astype(jnp.bfloat16)


def head_slice(array, head_index):
    return lax.dynamic_slice_in_dim(array, head_index * DH, DH, 1)


def full_capacity(queries, key_rows, value_rows, out_grad, cluster_ids):
    seq_count = lax.axis_size("seq")
    clu_count = lax.axis_size("clu")
    devices = seq_count * clu_count
    tok_rows = queries.shape[0]
    columns = queries.shape[1]
    head_count = columns // DH
    most_rows = 4 * tok_rows // devices
    capacity = most_rows * devices
    inv_root = 1.0 / math.sqrt(DH)
    owners = jnp.arange(devices, dtype=jnp.int32)
    member = (cluster_ids[:, None] == owners[None, :]).astype(jnp.int32)
    running = jnp.cumsum(member, axis=0) - 1
    slot_rank = jnp.sum(member * running, axis=1)
    sent_counts = jnp.sum(member, axis=0).reshape(devices, 1)
    slot_index = cluster_ids * most_rows + slot_rank
    stacked = jnp.concatenate([queries, key_rows, value_rows], axis=1)
    width_in = stacked.shape[1]
    packed = jnp.zeros((devices * most_rows, width_in), jnp.bfloat16).at[slot_index].set(stacked)
    packed = packed.reshape(devices, most_rows, width_in)
    got_rows, got_counts = (
        lax.all_to_all(packed, ("seq", "clu"), split_axis=0, concat_axis=0, tiled=True),
        lax.all_to_all(sent_counts, ("seq", "clu"), split_axis=0, concat_axis=0, tiled=True),
    )
    got_counts = got_counts.reshape(devices)
    starts = jnp.cumsum(got_counts) - got_counts
    live_total = jnp.sum(got_counts)
    within = jnp.arange(most_rows, dtype=jnp.int32)
    target = jnp.where(
        within[None, :] < got_counts[:, None], starts[:, None] + within[None, :], capacity
    )
    target = target.reshape(devices * most_rows)
    gathered = (
        jnp.zeros((capacity, width_in), jnp.bfloat16)
        .at[target]
        .set(got_rows.reshape(devices * most_rows, width_in), mode="drop")
    )
    query_block = gathered[:, :columns]
    key_block = gathered[:, columns : 2 * columns]
    value_block = gathered[:, 2 * columns : 3 * columns]
    positions = jnp.arange(capacity, dtype=jnp.int32)
    allowed = (positions[None, :] <= positions[:, None]) & (positions[None, :] < live_total)

    def forward_head(head_index, mixed_rows):
        weights_low = softmax_rows(
            head_slice(query_block, head_index),
            head_slice(key_block, head_index),
            allowed,
            inv_root,
        )
        out_head = jnp.dot(
            weights_low, head_slice(value_block, head_index), preferred_element_type=jnp.float32
        ).astype(jnp.bfloat16)
        return lax.dynamic_update_slice_in_dim(mixed_rows, out_head, head_index * DH, 1)

    mixed_rows = lax.fori_loop(
        0, head_count, forward_head, jnp.zeros((capacity, columns), jnp.bfloat16)
    )
    back_index = jnp.minimum(target, capacity - 1)
    outgoing = jnp.take(mixed_rows, back_index, axis=0).reshape(devices, most_rows, columns)
    grad_packed = (
        jnp.zeros((devices * most_rows, columns), jnp.bfloat16).at[slot_index].set(out_grad)
    )
    grad_packed = grad_packed.reshape(devices, most_rows, columns)
    returned = lax.all_to_all(outgoing, ("seq", "clu"), split_axis=0, concat_axis=0, tiled=True)
    got_grad = lax.all_to_all(grad_packed, ("seq", "clu"), split_axis=0, concat_axis=0, tiled=True)
    attention_out = jnp.take(returned.reshape(devices * most_rows, columns), slot_index, axis=0)
    grad_block = (
        jnp.zeros((capacity, columns), jnp.bfloat16)
        .at[target]
        .set(got_grad.reshape(devices * most_rows, columns), mode="drop")
    )
    delta_rows = jnp.sum(
        (grad_block.astype(jnp.float32) * mixed_rows.astype(jnp.float32)).reshape(
            capacity, head_count, DH
        ),
        axis=2,
    )

    def backward_head(head_index, grad_rows):
        query_head = head_slice(query_block, head_index)
        key_head = head_slice(key_block, head_index)
        value_head = head_slice(value_block, head_index)
        grad_head = head_slice(grad_block, head_index)
        weights_low = softmax_rows(query_head, key_head, allowed, inv_root)
        prob_grad = contract_last(grad_head, value_head)
        delta_head = lax.dynamic_slice_in_dim(delta_rows, head_index, 1, 1)
        score_grad = (weights_low.astype(jnp.float32) * (prob_grad - delta_head)).astype(
            jnp.bfloat16
        )
        query_part = (
            jnp.dot(score_grad, key_head, preferred_element_type=jnp.float32) * inv_root
        ).astype(jnp.bfloat16)
        key_part = (contract_first(score_grad, query_head) * inv_root).astype(jnp.bfloat16)
        value_part = contract_first(weights_low, grad_head).astype(jnp.bfloat16)
        grad_rows = lax.dynamic_update_slice_in_dim(grad_rows, query_part, head_index * DH, 1)
        grad_rows = lax.dynamic_update_slice_in_dim(
            grad_rows, key_part, columns + head_index * DH, 1
        )
        return lax.dynamic_update_slice_in_dim(
            grad_rows, value_part, 2 * columns + head_index * DH, 1
        )

    grad_rows = lax.fori_loop(
        0, head_count, backward_head, jnp.zeros((capacity, 3 * columns), jnp.bfloat16)
    )
    outgoing_grads = jnp.take(grad_rows, back_index, axis=0).reshape(
        devices, most_rows, 3 * columns
    )
    returned_grads = lax.all_to_all(
        outgoing_grads, ("seq", "clu"), split_axis=0, concat_axis=0, tiled=True
    )
    picked = jnp.take(returned_grads.reshape(devices * most_rows, 3 * columns), slot_index, axis=0)
    return (
        attention_out,
        picked[:, :columns],
        picked[:, columns : 2 * columns],
        picked[:, 2 * columns :],
    )


def bf16_dot(left, right):
    return jnp.dot(left, right, preferred_element_type=jnp.float32)


def flip_perm():
    row = lax.broadcasted_iota(jnp.int32, (SET * 16, SET * 16), 0)
    col = lax.broadcasted_iota(jnp.int32, (SET * 16, SET * 16), 1)
    swapped = (col % 16) * 16 + col // 16
    return (row == swapped).astype(jnp.float32).astype(jnp.bfloat16)


def attend(q, k, v, g, allowed, inv_root):
    raw = jnp.where(allowed, contract_last(k, q), masked)
    most = jnp.max(raw, axis=0, keepdims=True)
    weights = jnp.exp2((raw - most) * (inv_root * math.log2(math.e)))
    prob = weights * (1.0 / jnp.sum(weights, axis=0, keepdims=True))
    prob_low = prob.astype(jnp.bfloat16)
    prob_grad = contract_last(v, g)
    delta = jnp.sum(prob * prob_grad, axis=0, keepdims=True)
    score_grad = (prob * (prob_grad - delta)).astype(jnp.bfloat16)
    out = contract_first(v, prob_low).T.astype(jnp.bfloat16)
    dq = (contract_first(k, score_grad).T * inv_root).astype(jnp.bfloat16)
    dk = bf16_dot(score_grad, q) * inv_root
    dv = bf16_dot(prob_low, g)
    return out, dq, dk, dv


def fast_kernel(
    ids_ref, q_ref, k_ref, v_ref, g_ref,
    out_ref, dq_ref, dk_ref, dv_ref, flag_ref,
    cnt_send, cnt_group, cnt_recv, pack_mat, unpack_mat,
    send_a, send_b, send_c, recv_a, recv_b, recv_c, table,
    over, key_pos, query_pos, pick, onehot, loose, over_res, to_mate, to_block,
    result_a, result_b, result_c, back_a, back_b, back_c,
    ex_send, ex_recv, ex_send2, ex_recv2, ex_ret2, ex_back2, ex_ret1, ex_back1,
    hsend, hrecv, htable, hacc, hresult, hback, inputs, early,
    cnt_send_sem, cnt_sem, cnt2_send_sem, cnt2_sem,
    send_a_sem, recv_a_sem, send_b_sem, recv_b_sem, send_c_sem, recv_c_sem,
    res_a_sem, back_a_sem, res_b_sem, back_b_sem, res_c_sem, back_c_sem,
    ex_send_sem, ex_recv_sem, ex_send2_sem, ex_recv2_sem,
    ex_ret2_sem, ex_back2_sem, ex_ret1_sem, ex_back1_sem,
    hsend_sem, hrecv_sem, hres_sem, hback_sem, input_sem,
):
    seq_at = lax.axis_index("seq")
    clu_at = lax.axis_index("clu")
    groups = lax.axis_size("clu")
    heads = lax.axis_size("seq")
    devices = heads * groups
    me = seq_at * groups + clu_at
    inv_root = 1.0 / math.sqrt(DH)
    is_heavy_owner = lax.rem(seq_at, groups) == clu_at
    at_x, at_z = lax.div(seq_at, 4), lax.rem(seq_at, 4)
    at_y, at_core = lax.div(clu_at, 2), lax.rem(clu_at, 2)

    def turn(by):
        return by + at_core * (4 - 2 * by)

    eight = []
    for by_x, by_z, by_clu in zip(
        (0, 3, 2, 1, 0, 3, 2, 0), (0, 3, 2, 1, 1, 0, 3, 2), (0, 4, 6, 7, 2, 5, 1, 3)
    ):
        y = lax.rem(at_y + turn(by_clu // 2), 4)
        eight.append((turn(by_x), turn(by_z), y * 2 + lax.rem(at_core + by_clu % 2, 2)))

    def for_peers(first, count, visit):
        def one_eight(step, carry):
            by = lax.rem(step * 11, 16)
            by_x, by_z = lax.div(by, 4), lax.rem(by, 4)
            x = at_x + turn(by_x)
            z = at_z + turn(by_z)
            for j, (more_x, more_z, clu_to) in enumerate(eight):
                seq_to = lax.rem(x + more_x, 4) * 4 + lax.rem(z + more_z, 4)
                if j == 0:
                    pl.when(step > 0)(lambda: visit(seq_to, clu_to))
                else:
                    visit(seq_to, clu_to)
            return carry

        lax.fori_loop(first, first + count, one_eight, 0)

    def send_steps(first, count, source, target, send_sem, recv_sem):
        def start(seq_to, clu_to):
            pltpu.make_async_remote_copy(
                src_ref=source.at[seq_to * groups + clu_to],
                dst_ref=target,
                send_sem=send_sem,
                recv_sem=recv_sem,
                device_id=(seq_to, clu_to),
                device_id_type=MESH,
            ).start()

        for_peers(first, count, start)

    def send_own(source, target, recv_sem):
        pltpu.make_async_copy(source.at[me], target, recv_sem).start()

    def send_to_all(source, target, send_sem, recv_sem):
        send_steps(0, devices // 8, source, target, send_sem, recv_sem)
        send_own(source, target, recv_sem)

    def wait_bytes(ref, sem):
        pltpu.make_async_copy(ref, ref, sem).wait()

    for array, ref in enumerate((q_ref, k_ref, v_ref, g_ref)):
        pltpu.make_async_copy(ref, inputs.at[array], input_sem).start()
    barrier = pltpu.get_barrier_semaphore()

    def greet(seq_to, clu_to):
        pl.semaphore_signal(barrier, inc=1, device_id=(seq_to, clu_to), device_id_type=MESH)

    for_peers(0, devices // 8, greet)

    sub = lax.broadcasted_iota(jnp.int32, (TOK, TOK), 0)
    lane = lax.broadcasted_iota(jnp.int32, (TOK, TOK), 1)
    sub_f = sub.astype(jnp.float32)
    lane_f = lane.astype(jnp.float32)
    ids_l = jnp.broadcast_to(ids_ref[...].astype(jnp.float32), (TOK, TOK))
    ids_s = ids_l.T
    one = jnp.ones((TOK, TOK), jnp.float32)
    zero = jnp.zeros((TOK, TOK), jnp.float32)
    same = ids_l == ids_s
    rank_l = jnp.sum(jnp.where(same & (sub < lane), one, zero), axis=0, keepdims=True)
    rank_s = jnp.sum(jnp.where(same & (lane < sub), one, zero), axis=1, keepdims=True)
    count_l = jnp.sum(jnp.where(same, one, zero), axis=0, keepdims=True)
    cnt_send[...] = jnp.sum(jnp.where(ids_s == lane_f, one, zero), axis=0, keepdims=True)
    ids_row = ids_l[0:1, :]
    heavy = jnp.min(jnp.where(count_l == 4.0, ids_row, 999.0), axis=1, keepdims=True)
    group_l = jnp.floor(ids_l * (1.0 / 16.0))
    group_s = jnp.floor(ids_s * (1.0 / 16.0))
    earlier = (ids_s < ids_l) | (same & (sub < lane))
    later = (ids_l < ids_s) | (same & (lane < sub))
    before = (group_l == group_s) & (ids_s != heavy) & (rank_s >= 1.0) & earlier
    over_at = jnp.sum(jnp.where(before, one, zero), axis=0, keepdims=True)
    behind = (group_l == group_s) & (ids_l != heavy) & (rank_l >= 1.0) & later
    over_at_s = jnp.sum(jnp.where(behind, one, zero), axis=1, keepdims=True)
    excess_s = (ids_s != heavy) & (rank_s >= 1.0) & (over_at_s >= 4.0)
    excess_at = jnp.sum(jnp.where(excess_s & earlier, one, zero), axis=0, keepdims=True)
    light_l = ids_l != heavy
    slot_group = (sub // 16).astype(jnp.float32)
    in_tile = sub % 16
    over_l = light_l & (rank_l >= 1.0)

    def tile_picks(tile):
        at_slot = (in_tile % 4).astype(jnp.float32)
        if tile < 4:
            cluster = slot_group * 16.0 + at_slot + 4.0 * tile
            taken = (ids_l == cluster) & (rank_l == 0.0) & light_l
        else:
            taken = (group_l == slot_group) & over_l & (over_at == at_slot)
        return [jnp.where(taken & (in_tile // 4 == array), one, zero) for array in range(4)]

    def rest_picks():
        picks = []
        for array in range(4):
            chosen = (ids_l == heavy) & (rank_l == (sub % 4).astype(jnp.float32))
            chosen = chosen & (sub // 4 == array) & (sub < 16)
            beyond = over_l & (over_at >= 4.0) & (excess_at == (sub % 8).astype(jnp.float32))
            beyond = beyond & (sub // 8 == array + 2)
            picks.append(jnp.where(chosen | beyond, one, zero))
        return picks

    def put_pack(at_row, count, picks):
        for array, matrix in enumerate(picks):
            pack_mat[pl.ds(at_row, count), pl.ds(array * TOK, TOK)] = matrix[:count].astype(
                jnp.bfloat16
            )

    put_pack(0, TOK, tile_picks(0))
    put_pack(TOK, TOK, tile_picks(4))
    put_pack(2 * TOK, 48, rest_picks())


    def send_line(source, target, count, at, device, send_sem, recv_sem):
        def one_peer(step, carry):
            to = lax.rem(at + step, count)
            pltpu.make_async_remote_copy(
                src_ref=source(to),
                dst_ref=target,
                send_sem=send_sem,
                recv_sem=recv_sem,
                device_id=device(to),
                device_id_type=MESH,
            ).start()
            return carry

        lax.fori_loop(1, count, one_peer, 0)
        pltpu.make_async_copy(source(at), target, recv_sem).start()

    def along_seq(source, target, send_sem, recv_sem):
        send_line(
            source, target.at[seq_at], heads, seq_at, lambda to: (to, clu_at), send_sem, recv_sem
        )

    def along_clu(source, target, send_sem, recv_sem):
        send_line(
            source, target.at[clu_at], groups, clu_at, lambda to: (seq_at, to), send_sem, recv_sem
        )


    def head_rows(at):
        cols = pl.ds(pl.multiple_of(at * 2 * DH, 2 * DH), 2 * DH)
        return [inputs[array, :, cols] for array in range(4)]

    def put_tile(target, at, tile, packed):
        low = packed.astype(jnp.bfloat16)
        for k in range(2):
            target[pl.ds((2 * at + k) * groups, groups), tile] = low[
                :, k * DH : (k + 1) * DH
            ].reshape(groups, 16, DH)

    def pack_a(at, carry):
        rows = jnp.concatenate(head_rows(at), axis=0)
        packed = bf16_dot(pack_mat[pl.ds(0, 2 * TOK + 48), :], rows)
        put_tile(send_a, at, 0, packed[:TOK])
        put_tile(send_a, at, 1, packed[TOK : 2 * TOK])
        rest = packed[2 * TOK :].astype(jnp.bfloat16)
        for k in range(2):
            hsend[2 * at + k] = rest[:16, k * DH : (k + 1) * DH]
            ex_send[2 * at + k] = rest[16:, k * DH : (k + 1) * DH]
        return carry

    wait_bytes(inputs, input_sem)
    lax.fori_loop(0, heads // 2, pack_a, 0, unroll=2)
    pl.semaphore_wait(barrier, devices - 1)
    along_clu(lambda to: cnt_send, cnt_group, cnt_send_sem, cnt_sem)

    def send_heavy(step, carry):
        head = lax.rem(seq_at + step, heads)
        clu_to = lax.rem(head, groups)

        @pl.when(head * groups + clu_to != me)
        def _():
            pltpu.make_async_remote_copy(
                src_ref=hsend.at[head],
                dst_ref=hrecv.at[me],
                send_sem=hsend_sem,
                recv_sem=hrecv_sem,
                device_id=(head, clu_to),
                device_id_type=MESH,
            ).start()

        @pl.when(head * groups + clu_to == me)
        def _():
            pltpu.make_async_copy(hsend.at[head], hrecv.at[me], hrecv_sem).start()

        return carry

    lax.fori_loop(0, heads, send_heavy, 0)
    along_seq(lambda to: ex_send.at[to], ex_recv, ex_send_sem, ex_recv_sem)
    out_a = (send_a, recv_a.at[me], send_a_sem, recv_a_sem)
    send_steps(0, 4, *out_a)
    wait_bytes(cnt_group, cnt_sem)
    along_seq(lambda to: cnt_group, cnt_recv, cnt2_send_sem, cnt2_sem)
    send_steps(4, devices // 8 - 4, *out_a)
    send_own(send_a, recv_a.at[me], recv_a_sem)

    for tile in range(1, 4):
        put_pack((tile + 1) * TOK + 48, TOK, tile_picks(tile))

    def pack_bc(at, carry):
        rows = jnp.concatenate(head_rows(at), axis=0)
        packed = bf16_dot(pack_mat[pl.ds(2 * TOK + 48, 3 * TOK), :], rows)
        put_tile(send_b, at, 0, packed[:TOK])
        put_tile(send_b, at, 1, packed[TOK : 2 * TOK])
        put_tile(send_c, at, 0, packed[2 * TOK :])
        return carry

    lax.fori_loop(0, heads // 2, pack_bc, 0)

    wait_bytes(cnt_recv, cnt2_sem)
    seen = cnt_recv[...].reshape(TOK, TOK)
    heavies = jnp.min(jnp.where(seen == 4.0, lane_f, 999.0), axis=1, keepdims=True)
    heavy_all = jnp.min(heavies, axis=0, keepdims=True)
    light = lane_f != heavy_all
    more = jnp.where(light, jnp.maximum(seen - 1.0, 0.0), 0.0)
    more_low = more.astype(jnp.bfloat16)
    in_group = jnp.where(sub // 16 == lane, one, zero).astype(jnp.bfloat16)
    ahead = jnp.where(sub < lane, one, zero).astype(jnp.bfloat16)
    prior = jnp.where(lane < sub, one, zero).astype(jnp.bfloat16)
    mates = (lane < sub) & (lane % 8 == sub % 8)
    mates = jnp.where(mates, one, zero).astype(jnp.bfloat16)
    excess = jnp.maximum(bf16_dot(more_low, in_group) - 4.0, 0.0)
    excess_low = excess.astype(jnp.bfloat16)
    excess_off = bf16_dot(excess_low, ahead)
    excess_pre = bf16_dot(mates, excess_low)
    bad = (jnp.sum(excess, axis=1, keepdims=True) > 8.0) | (excess_pre + excess > 16.0)
    bad = bad | (heavies != heavy_all) | (jnp.sum(more, axis=0, keepdims=True) > OVC)
    flag_ref[0, 0] = jnp.max(jnp.where(bad, one, zero)).astype(jnp.int32)

    spot = zero
    for group in range(8):
        off, count, pre = [a[:, group : group + 1] for a in (excess_off, excess, excess_pre)]
        held = (lane_f >= off) & (lane_f < off + count)
        spot = spot + jnp.where(held, lane_f + (group * 16 + 1.0) - off + pre, zero)
    spot = jnp.where(sub % 8 == clu_at, spot, zero).reshape(16, 8, TOK)
    spot = jnp.sum(spot, axis=1).astype(jnp.bfloat16)
    spread8 = jnp.where(lane % 8 == sub, one, zero).astype(jnp.bfloat16)
    spot = jnp.where(lane[:16] // 8 == sub[:16], bf16_dot(spot, spread8), 0.0)
    spot = jnp.sum(spot, axis=0, keepdims=True) - 1.0
    to_mate[...] = jnp.where(sub_f == spot, one, zero).astype(jnp.bfloat16)
    spot = jnp.broadcast_to(spot, (TOK, TOK)).T
    to_block[...] = jnp.where(spot == lane_f, one, zero).astype(jnp.bfloat16)

    wait_bytes(ex_recv, ex_recv_sem)
    held = ex_recv[...].astype(jnp.float32)
    held = [held[:, 8 * a : 8 * a + 8, :].reshape(TOK, DH) for a in range(4)]
    held = jnp.concatenate(held, axis=1).astype(jnp.bfloat16)
    held = bf16_dot(to_mate[...], held).astype(jnp.bfloat16)
    for a in range(4):
        ex_send2[:, a] = held[:, a * DH : (a + 1) * DH].reshape(8, 16, DH)
    along_clu(lambda to: ex_send2.at[to], ex_recv2, ex_send2_sem, ex_recv2_sem)
    send_to_all(send_b, recv_b.at[me], send_b_sem, recv_b_sem)
    send_to_all(send_c, recv_c.at[me], send_c_sem, recv_c_sem)

    valid = jnp.where((seen > 0.0) & light, one, zero).astype(jnp.bfloat16)
    mine = (sub == clu_at * 16 + lane) & (lane < 16)
    mine = jnp.where(mine, one, zero).astype(jnp.bfloat16)
    more_g = bf16_dot(more_low, mine)
    valid_g = bf16_dot(valid, mine)
    more_g_low = more_g.astype(jnp.bfloat16)
    start_g = bf16_dot(prior, more_g_low)
    offset_g = bf16_dot(more_g_low, ahead)
    beyond_g = jnp.maximum(bf16_dot(more_g_low, one.astype(jnp.bfloat16)) - 4.0, 0.0)
    pre_g = bf16_dot(mates, beyond_g.astype(jnp.bfloat16))
    ex_index = lane_f - pre_g + 4.0
    first_row = lax.broadcasted_iota(jnp.int32, (1, TOK), 1).astype(jnp.float32) * 16.0
    in_tile_at = zero
    beyond_at = zero
    for c in range(16):
        count, begin, off, real = [
            a[:, c : c + 1] for a in (more_g, start_g, offset_g, valid_g)
        ]
        place = begin - off + (c * OVC + 1.0)
        held = (lane_f >= off) & (lane_f < off + count) & (lane < 4)
        in_tile_at = in_tile_at + jnp.where(held, lane_f + place, zero)
        held = (ex_index >= off) & (ex_index < off + count) & (ex_index >= 4.0)
        beyond_at = beyond_at + jnp.where(held, ex_index + place, zero)
        held = (lane_f >= begin) & (lane_f < begin + count)
        where = jnp.where(held, sub_f * 16.0 + 1.0 + lane_f - begin, zero)
        where = jnp.sum(where, axis=0, keepdims=True)
        where = jnp.where(where > 0.0, where, FAR)
        query_row = jnp.concatenate([first_row, where], axis=1)
        query_pos[c] = jnp.broadcast_to(query_row, (8, 2 * TOK))
        key_pos[c, pl.ds(0, TOK), :] = jnp.where(real > 0.0, sub_f * 16.0, FAR)
        key_pos[c, pl.ds(TOK, OVC), :] = jnp.broadcast_to(where, (TOK, TOK)).T[:OVC]
    beyond_at = jnp.sum(beyond_at.reshape(16, 8, TOK), axis=0)
    high = jnp.floor(beyond_at * (1.0 / 32.0))
    split = jnp.concatenate([high, beyond_at - high * 32.0], axis=0).astype(jnp.bfloat16)
    spread16 = jnp.where(lane % 16 == sub, one, zero).astype(jnp.bfloat16)
    split = bf16_dot(split, spread16)
    split = jnp.where(lane[:8] // 16 == sub[:8], split[:8] * 32.0 + split[8:], 0.0)
    beyond_row = jnp.sum(split, axis=0, keepdims=True) - 1.0
    tile_rows = in_tile_at.T[0:8, :] - 1.0
    slot_rows = [tile_rows[k : k + 1, :] for k in range(4)] + [beyond_row]
    slot_cols = [in_tile_at[:, k : k + 1] - 1.0 for k in range(4)]
    slot_cols.append(jnp.broadcast_to(beyond_row, (TOK, TOK)).T)

    chunk = 4
    for k in range(5):
        for m in range(16 * OVC // TOK):
            onehot[pl.ds(k * TOK, TOK), pl.ds(m * TOK, TOK)] = jnp.where(
                slot_cols[k] == lane_f + float(m * TOK), one, zero
            ).astype(jnp.bfloat16)
            pick[pl.ds(m * TOK, TOK), pl.ds(k * TOK, TOK)] = jnp.where(
                slot_rows[k] == sub_f + float(m * TOK), one, zero
            ).astype(jnp.bfloat16)

    for at, tile in enumerate((0, 1, 2, None, 3, 4)):
        for array, matrix in enumerate(rest_picks() if tile is None else tile_picks(tile)):
            unpack_mat[pl.ds(array * TOK, TOK), pl.ds(at * TOK, TOK)] = matrix.T.astype(
                jnp.bfloat16
            )

    perm = flip_perm()

    def arrange(source, target, units):
        def two_sets(at, carry):
            blocks = [pl.ds(pl.multiple_of((2 * at + i) * SET, SET), SET) for i in range(2)]
            spots = [(held, unit) for held in blocks for unit in range(units)]
            rows = jnp.concatenate(
                [source(held, unit).reshape(SET * 16, DH) for held, unit in spots], axis=1
            )
            turned = bf16_dot(perm, rows).astype(jnp.bfloat16)
            for i, (held, unit) in enumerate(spots):
                target(held, unit, turned[:, i * DH : (i + 1) * DH].reshape(16, SET, DH))
            return carry

        lax.fori_loop(0, devices // (2 * SET), two_sets, 0, unroll=2)

    def put_table(first):
        def put(blocks, unit, value):
            table[first + unit, :, blocks, :] = value

        return put

    @pl.when(is_heavy_owner)
    def _():
        wait_bytes(hrecv, hrecv_sem)

        def put_heavy(blocks, unit, value):
            htable[:, blocks, :] = value

        arrange(lambda blocks, unit: hrecv[blocks], put_heavy, 1)
        k_h, v_h = [htable[4 * a : 4 * a + 4].reshape(4 * TOK, DH) for a in (1, 2)]
        hacc[...] = jnp.zeros_like(hacc)
        key_sub = lax.broadcasted_iota(jnp.int32, (4 * TOK, TOK), 0)
        key_at = lax.rem(key_sub, TOK) * 4 + lax.div(key_sub, TOK)
        query_at = lax.broadcasted_iota(jnp.int32, (4 * TOK, TOK), 1) * 4

        def heavy_tile(s, carry):
            out, dq, dk, dv = attend(
                htable[s], k_h, v_h, htable[12 + s], key_at <= query_at + s, inv_root
            )
            hacc[2, pl.ds(pl.multiple_of(s * TOK, TOK), TOK)] = out.astype(jnp.float32)
            hacc[3, pl.ds(pl.multiple_of(s * TOK, TOK), TOK)] = dq.astype(jnp.float32)
            hacc[0] += dk
            hacc[1] += dv
            return carry

        lax.fori_loop(0, 4, heavy_tile, 0)
        for array, at in enumerate((2, 3, 0, 1)):
            htable[4 * array : 4 * array + 4] = (
                hacc[at].astype(jnp.bfloat16).reshape(4, TOK, DH)
            )

        def put_hresult(blocks, unit, value):
            hresult[blocks] = value

        arrange(lambda blocks, unit: htable[:, blocks, :], put_hresult, 1)
        send_to_all(hresult, hback.at[seq_at], hres_sem, hback_sem)

    wait_bytes(recv_a, recv_a_sem)
    def put_tile_a(blocks, unit, value):
        table[4 * unit, :, blocks, :] = value

    arrange(lambda blocks, unit: recv_a[blocks, unit], put_tile_a, 2)

    wait_bytes(ex_recv2, ex_recv2_sem)
    for a in range(4):
        cols = pl.ds(a * DH, DH)
        loose[pl.ds(0, 4 * TOK), cols] = table[4, 4 * a : 4 * a + 4].reshape(4 * TOK, DH)
        loose[pl.ds(4 * TOK, TOK), cols] = ex_recv2[:, a].reshape(TOK, DH)

    def gather_chunk(at, carry):
        chosen = pick[pl.ds(pl.multiple_of(at * chunk * OVC, 64), chunk * OVC), :]
        found = bf16_dot(chosen, loose[...]).astype(jnp.bfloat16)
        for c in range(chunk):
            for array in range(4):
                over[array, at * chunk + c] = found[
                    c * OVC : (c + 1) * OVC, array * DH : (array + 1) * DH
                ]
        return carry

    lax.fori_loop(0, 16 // chunk, gather_chunk, 0)

    pad_rows = jnp.zeros((TOK - OVC, DH), jnp.bfloat16)

    def load_cluster(tile, j):
        c = tile * 4 + j
        rows = [
            jnp.concatenate([table[tile, a * 4 + j], over[a, c]], axis=0) for a in range(4)
        ]
        for a in (0, 3):
            rows[a] = jnp.concatenate([rows[a], pad_rows], axis=0)
        key_at = key_pos[c]
        allowed = jnp.concatenate([key_at, key_at], axis=1) <= query_pos[c, 0:1, :]
        return rows + [allowed]

    def attend_tiles(first, tiles, beside):
        def one_pair(at, carry):
            beside(at)
            tile = first + lax.div(at, 2)
            spots = [lax.rem(at, 2) * 2 + i for i in range(2)]
            loaded = [load_cluster(tile, j) for j in spots]
            found = [attend(*arrays, inv_root) for arrays in loaded]
            for j, results in zip(spots, found):
                c = tile * 4 + j
                for a, value in enumerate(results):
                    value = value.astype(jnp.bfloat16)
                    table[tile, a * 4 + j] = value[:TOK]
                    over_res[
                        pl.ds(pl.multiple_of(c * OVC, 16), OVC), pl.ds(a * DH, DH)
                    ] = value[TOK : TOK + OVC]
            return carry

        lax.fori_loop(0, 2 * tiles, one_pair, 0)

    def put_in(result):
        def put(blocks, unit, value):
            result[blocks, unit] = value

        return put

    def from_table(first):
        return lambda blocks, unit: table[first + unit, :, blocks, :]

    to_a = (result_a, back_a.at[me], res_a_sem, back_a_sem)
    to_b = (result_b, back_b.at[me], res_b_sem, back_b_sem)
    to_c = (result_c, back_c.at[me], res_c_sem, back_c_sem)
    attend_tiles(0, 1, lambda at: None)
    arrange(from_table(0), put_in(result_a), 1)
    send_own(result_a, back_a.at[me], back_a_sem)

    wait_bytes(recv_b, recv_b_sem)
    arrange(lambda blocks, unit: recv_b[blocks, unit], put_table(1), 2)
    attend_tiles(1, 2, lambda at: send_steps(at * 4, 4, *to_a))
    arrange(from_table(1), put_in(result_b), 2)
    send_own(result_b, back_b.at[me], back_b_sem)

    wait_bytes(recv_c, recv_c_sem)
    arrange(lambda blocks, unit: recv_c[blocks, 0], put_table(3), 1)
    attend_tiles(3, 1, lambda at: send_steps(at * 8, 8, *to_b))

    found = bf16_dot(onehot[pl.ds(4 * TOK, TOK), :], over_res[...]).astype(jnp.bfloat16)
    for a in range(4):
        ex_ret2[:, a] = found[:, a * DH : (a + 1) * DH].reshape(8, 16, DH)
    along_clu(lambda to: ex_ret2.at[to], ex_back2, ex_ret2_sem, ex_back2_sem)
    found = bf16_dot(onehot[pl.ds(0, 4 * TOK), :], over_res[...]).astype(jnp.bfloat16)
    for a in range(4):
        table[4, 4 * a : 4 * a + 4] = found[:, a * DH : (a + 1) * DH].reshape(4, TOK, DH)
    arrange(from_table(3), put_in(result_c), 2)
    send_steps(0, devices // 16, *to_c)
    send_own(result_c, back_c.at[me], back_c_sem)

    wait_bytes(ex_back2, ex_back2_sem)
    held = [ex_back2[:, a].reshape(TOK, DH) for a in range(4)]
    held = bf16_dot(to_block[...], jnp.concatenate(held, axis=1))
    held = [held[:, a * DH : (a + 1) * DH].reshape(16, 8, DH) for a in range(4)]
    ex_ret1[...] = jnp.concatenate(held, axis=1).astype(jnp.bfloat16)
    along_seq(lambda to: ex_ret1.at[to], ex_back1, ex_ret1_sem, ex_back1_sem)
    send_steps(devices // 16, devices // 16, *to_c)

    def unpack(tiles, rest, first, count):
        sides = []
        for k in range(2):
            sides.append(
                jnp.concatenate(
                    [tile(k).reshape(TOK, DH) for tile in tiles] + [part(k) for part in rest],
                    axis=0,
                )
            )
        return bf16_dot(
            unpack_mat[:, pl.ds(first, count)], jnp.concatenate(sides, axis=1)
        )

    def tile_of(ref, at, tile):
        return lambda k: ref[pl.ds((2 * at + k) * groups, groups), tile]

    def unpack_early(at, carry):
        tiles = [tile_of(back_a, at, 0), tile_of(back_b, at, 0), tile_of(back_b, at, 1)]
        rest = [
            lambda k: hback[2 * at + k],
            lambda k: ex_back1[2 * at + k],
            lambda k: jnp.zeros((TOK - 48, DH), jnp.bfloat16),
        ]
        early[at] = unpack(tiles, rest, 0, 4 * TOK)
        return carry

    def unpack_last(at, carry):
        cols = pl.ds(pl.multiple_of(at * 2 * DH, 2 * DH), 2 * DH)
        tiles = [tile_of(back_c, at, 0), tile_of(back_c, at, 1)]
        found = (early[at] + unpack(tiles, [], 4 * TOK, 2 * TOK)).astype(jnp.bfloat16)
        for array, ref in enumerate((out_ref, dq_ref, dk_ref, dv_ref)):
            ref[:, cols] = found[array * TOK : (array + 1) * TOK]
        return carry

    wait_bytes(hback, hback_sem)
    wait_bytes(back_a, back_a_sem)
    wait_bytes(back_b, back_b_sem)
    wait_bytes(ex_back1, ex_back1_sem)
    lax.fori_loop(0, heads // 2, unpack_early, 0, unroll=2)
    wait_bytes(back_c, back_c_sem)
    lax.fori_loop(0, heads // 2, unpack_last, 0, unroll=2)

    others = pl.ds(0, devices - 1)
    wait_bytes(cnt_group.at[pl.ds(0, groups - 1)], cnt_send_sem)
    wait_bytes(cnt_recv.at[pl.ds(0, heads - 1)], cnt2_send_sem)
    for ref, sem in ((ex_send, ex_send_sem), (ex_ret1, ex_ret1_sem)):
        wait_bytes(ref.at[pl.ds(0, heads - 1)], sem)
    for ref, sem in ((ex_send2, ex_send2_sem), (ex_ret2, ex_ret2_sem)):
        wait_bytes(ref.at[pl.ds(0, groups - 1)], sem)
    wait_bytes(send_a.at[others], send_a_sem)
    wait_bytes(send_b.at[others], send_b_sem)
    wait_bytes(send_c.at[others], send_c_sem)
    wait_bytes(result_a.at[others], res_a_sem)
    wait_bytes(result_b.at[others], res_b_sem)
    wait_bytes(result_c.at[others], res_c_sem)

    @pl.when(is_heavy_owner)
    def _():
        wait_bytes(hsend.at[pl.ds(0, heads - 1)], hsend_sem)
        wait_bytes(hresult.at[others], hres_sem)

    @pl.when(jnp.logical_not(is_heavy_owner))
    def _():
        wait_bytes(hsend, hsend_sem)


def fast_path(queries, key_rows, value_rows, out_grad, cluster_ids):
    tok_rows, columns = queries.shape
    heads = columns // DH
    groups = lax.axis_size("clu")
    devices = lax.axis_size("seq") * groups
    low = jnp.bfloat16
    wide = jnp.float32
    rows = pltpu.VMEM((tok_rows, columns), low)
    vmem = pl.BlockSpec(memory_space=pltpu.VMEM)
    smem = pl.BlockSpec(memory_space=pltpu.SMEM)
    return pl.pallas_call(
        fast_kernel,
        out_shape=[rows] * 4 + [jax.ShapeDtypeStruct((1, 1), jnp.int32)],
        in_specs=[vmem] + [pl.BlockSpec(memory_space=pl.ANY)] * 4,
        out_specs=[vmem] * 4 + [smem],
        scratch_shapes=[
            pltpu.VMEM((1, TOK), wide),
            pltpu.VMEM((groups, 1, TOK), wide),
            pltpu.VMEM((heads, groups, 1, TOK), wide),
            pltpu.VMEM((5 * TOK + 48, 4 * TOK), low),
            pltpu.VMEM((4 * TOK, 6 * TOK), low),
            pltpu.VMEM((devices, 2, 16, DH), low),
            pltpu.VMEM((devices, 2, 16, DH), low),
            pltpu.VMEM((devices, 1, 16, DH), low),
            pltpu.VMEM((devices, 2, 16, DH), low),
            pltpu.VMEM((devices, 2, 16, DH), low),
            pltpu.VMEM((devices, 1, 16, DH), low),
            pltpu.VMEM((5, 16, devices, DH), low),
            pltpu.VMEM((4, 16, OVC, DH), low),
            pltpu.VMEM((16, TOK + OVC, TOK), wide),
            pltpu.VMEM((16, 8, 2 * TOK), wide),
            pltpu.VMEM((16 * OVC, 5 * TOK), low),
            pltpu.VMEM((5 * TOK, 16 * OVC), low),
            pltpu.VMEM((5 * TOK, 4 * DH), low),
            pltpu.VMEM((16 * OVC, 4 * DH), low),
            pltpu.VMEM((TOK, TOK), low),
            pltpu.VMEM((TOK, TOK), low),
            pltpu.VMEM((devices, 1, 16, DH), low),
            pltpu.VMEM((devices, 2, 16, DH), low),
            pltpu.VMEM((devices, 2, 16, DH), low),
            pltpu.VMEM((devices, 1, 16, DH), low),
            pltpu.VMEM((devices, 2, 16, DH), low),
            pltpu.VMEM((devices, 2, 16, DH), low),
            pltpu.VMEM((heads, 32, DH), low),
            pltpu.VMEM((heads, 32, DH), low),
            pltpu.VMEM((groups, 4, 16, DH), low),
            pltpu.VMEM((groups, 4, 16, DH), low),
            pltpu.VMEM((groups, 4, 16, DH), low),
            pltpu.VMEM((groups, 4, 16, DH), low),
            pltpu.VMEM((heads, 32, DH), low),
            pltpu.VMEM((heads, 32, DH), low),
            pltpu.VMEM((heads, 16, DH), low),
            pltpu.VMEM((devices, 16, DH), low),
            pltpu.VMEM((16, devices, DH), low),
            pltpu.VMEM((4, 4 * TOK, DH), wide),
            pltpu.VMEM((devices, 16, DH), low),
            pltpu.VMEM((heads, 16, DH), low),
            pltpu.VMEM((4, tok_rows, columns), low),
            pltpu.VMEM((heads // 2, 4 * tok_rows, 2 * DH), wide),
        ]
        + [pltpu.SemaphoreType.DMA] * 29,
        compiler_params=pltpu.CompilerParams(
            collective_id=0, has_side_effects=True, vmem_limit_bytes=44 * 1024 * 1024
        ),
    )(cluster_ids.reshape(1, tok_rows), queries, key_rows, value_rows, out_grad)


def copy_kernel(*refs):
    sem = refs[-1]
    copies = [
        pltpu.make_async_copy(refs[i], refs[4 + i], sem.at[i]) for i in range(4)
    ]
    for copy in copies:
        copy.start()
    for copy in copies:
        copy.wait()


def copy_out(arrays):
    anywhere = pl.BlockSpec(memory_space=pl.ANY)
    return pl.pallas_call(
        copy_kernel,
        out_shape=[pltpu.HBM(a.shape, a.dtype) for a in arrays],
        in_specs=[anywhere] * 4,
        out_specs=[anywhere] * 4,
        scratch_shapes=[pltpu.SemaphoreType.DMA((4,))],
    )(*arrays)


def per_device(queries, key_rows, value_rows, out_grad, cluster_ids):
    arrays = (queries, key_rows, value_rows, out_grad, cluster_ids)
    *fast, flag = fast_path(*arrays)
    return lax.cond(
        flag.reshape(()) != 0,
        lambda arrays, fast: full_capacity(*arrays),
        lambda arrays, fast: tuple(copy_out(fast)),
        arrays,
        tuple(fast),
    )


def solution(mesh):
    in_specs = (
        P(("seq", "clu"), None),
        P(("seq", "clu"), None),
        P(("seq", "clu"), None),
        P(("seq", "clu"), None),
        P(("seq", "clu")),
    )
    out_specs = (
        P(("seq", "clu"), None),
        P(("seq", "clu"), None),
        P(("seq", "clu"), None),
        P(("seq", "clu"), None),
    )
    return jax.shard_map(
        per_device, mesh=mesh, in_specs=in_specs, out_specs=out_specs, check_vma=False
    )
```

```python
import math

import jax
import jax.numpy as jnp
from jax import lax
from jax.experimental import pallas as pl
from jax.experimental.pallas import tpu as pltpu
from jax.sharding import PartitionSpec as P

DH = 128
TOK = 128
OVC = 80
SET = 16
FAR = 1e9
MESH = pl.DeviceIdType.MESH


masked = -1e30


def contract_last(left, right):
    return lax.dot_general(
        left, right, (((1,), (1,)), ((), ())), preferred_element_type=jnp.float32
    )


def contract_first(left, right):
    return lax.dot_general(
        left, right, (((0,), (0,)), ((), ())), preferred_element_type=jnp.float32
    )


def softmax_rows(query_head, key_head, allowed, inv_root):
    scores = contract_last(query_head, key_head) * inv_root
    scores = jnp.where(allowed, scores, masked)
    row_max = jnp.max(scores, axis=1, keepdims=True)
    weights = jnp.exp(scores - row_max)
    row_sum = jnp.sum(weights, axis=1, keepdims=True)
    return (weights / row_sum).astype(jnp.bfloat16)


def head_slice(array, head_index):
    return lax.dynamic_slice_in_dim(array, head_index * DH, DH, 1)


def full_capacity(queries, key_rows, value_rows, out_grad, cluster_ids):
    seq_count = lax.axis_size("seq")
    clu_count = lax.axis_size("clu")
    devices = seq_count * clu_count
    tok_rows = queries.shape[0]
    columns = queries.shape[1]
    head_count = columns // DH
    most_rows = 4 * tok_rows // devices
    capacity = most_rows * devices
    inv_root = 1.0 / math.sqrt(DH)
    owners = jnp.arange(devices, dtype=jnp.int32)
    member = (cluster_ids[:, None] == owners[None, :]).astype(jnp.int32)
    running = jnp.cumsum(member, axis=0) - 1
    slot_rank = jnp.sum(member * running, axis=1)
    sent_counts = jnp.sum(member, axis=0).reshape(devices, 1)
    slot_index = cluster_ids * most_rows + slot_rank
    stacked = jnp.concatenate([queries, key_rows, value_rows], axis=1)
    width_in = stacked.shape[1]
    packed = jnp.zeros((devices * most_rows, width_in), jnp.bfloat16).at[slot_index].set(stacked)
    packed = packed.reshape(devices, most_rows, width_in)
    got_rows, got_counts = (
        lax.all_to_all(packed, ("seq", "clu"), split_axis=0, concat_axis=0, tiled=True),
        lax.all_to_all(sent_counts, ("seq", "clu"), split_axis=0, concat_axis=0, tiled=True),
    )
    got_counts = got_counts.reshape(devices)
    starts = jnp.cumsum(got_counts) - got_counts
    live_total = jnp.sum(got_counts)
    within = jnp.arange(most_rows, dtype=jnp.int32)
    target = jnp.where(
        within[None, :] < got_counts[:, None], starts[:, None] + within[None, :], capacity
    )
    target = target.reshape(devices * most_rows)
    gathered = (
        jnp.zeros((capacity, width_in), jnp.bfloat16)
        .at[target]
        .set(got_rows.reshape(devices * most_rows, width_in), mode="drop")
    )
    query_block = gathered[:, :columns]
    key_block = gathered[:, columns : 2 * columns]
    value_block = gathered[:, 2 * columns : 3 * columns]
    positions = jnp.arange(capacity, dtype=jnp.int32)
    allowed = (positions[None, :] <= positions[:, None]) & (positions[None, :] < live_total)

    def forward_head(head_index, mixed_rows):
        weights_low = softmax_rows(
            head_slice(query_block, head_index),
            head_slice(key_block, head_index),
            allowed,
            inv_root,
        )
        out_head = jnp.dot(
            weights_low, head_slice(value_block, head_index), preferred_element_type=jnp.float32
        ).astype(jnp.bfloat16)
        return lax.dynamic_update_slice_in_dim(mixed_rows, out_head, head_index * DH, 1)

    mixed_rows = lax.fori_loop(
        0, head_count, forward_head, jnp.zeros((capacity, columns), jnp.bfloat16)
    )
    back_index = jnp.minimum(target, capacity - 1)
    outgoing = jnp.take(mixed_rows, back_index, axis=0).reshape(devices, most_rows, columns)
    grad_packed = (
        jnp.zeros((devices * most_rows, columns), jnp.bfloat16).at[slot_index].set(out_grad)
    )
    grad_packed = grad_packed.reshape(devices, most_rows, columns)
    returned = lax.all_to_all(outgoing, ("seq", "clu"), split_axis=0, concat_axis=0, tiled=True)
    got_grad = lax.all_to_all(grad_packed, ("seq", "clu"), split_axis=0, concat_axis=0, tiled=True)
    attention_out = jnp.take(returned.reshape(devices * most_rows, columns), slot_index, axis=0)
    grad_block = (
        jnp.zeros((capacity, columns), jnp.bfloat16)
        .at[target]
        .set(got_grad.reshape(devices * most_rows, columns), mode="drop")
    )
    delta_rows = jnp.sum(
        (grad_block.astype(jnp.float32) * mixed_rows.astype(jnp.float32)).reshape(
            capacity, head_count, DH
        ),
        axis=2,
    )

    def backward_head(head_index, grad_rows):
        query_head = head_slice(query_block, head_index)
        key_head = head_slice(key_block, head_index)
        value_head = head_slice(value_block, head_index)
        grad_head = head_slice(grad_block, head_index)
        weights_low = softmax_rows(query_head, key_head, allowed, inv_root)
        prob_grad = contract_last(grad_head, value_head)
        delta_head = lax.dynamic_slice_in_dim(delta_rows, head_index, 1, 1)
        score_grad = (weights_low.astype(jnp.float32) * (prob_grad - delta_head)).astype(
            jnp.bfloat16
        )
        query_part = (
            jnp.dot(score_grad, key_head, preferred_element_type=jnp.float32) * inv_root
        ).astype(jnp.bfloat16)
        key_part = (contract_first(score_grad, query_head) * inv_root).astype(jnp.bfloat16)
        value_part = contract_first(weights_low, grad_head).astype(jnp.bfloat16)
        grad_rows = lax.dynamic_update_slice_in_dim(grad_rows, query_part, head_index * DH, 1)
        grad_rows = lax.dynamic_update_slice_in_dim(
            grad_rows, key_part, columns + head_index * DH, 1
        )
        return lax.dynamic_update_slice_in_dim(
            grad_rows, value_part, 2 * columns + head_index * DH, 1
        )

    grad_rows = lax.fori_loop(
        0, head_count, backward_head, jnp.zeros((capacity, 3 * columns), jnp.bfloat16)
    )
    outgoing_grads = jnp.take(grad_rows, back_index, axis=0).reshape(
        devices, most_rows, 3 * columns
    )
    returned_grads = lax.all_to_all(
        outgoing_grads, ("seq", "clu"), split_axis=0, concat_axis=0, tiled=True
    )
    picked = jnp.take(returned_grads.reshape(devices * most_rows, 3 * columns), slot_index, axis=0)
    return (
        attention_out,
        picked[:, :columns],
        picked[:, columns : 2 * columns],
        picked[:, 2 * columns :],
    )


def bf16_dot(left, right):
    return jnp.dot(left, right, preferred_element_type=jnp.float32)


def flip_perm():
    row = lax.broadcasted_iota(jnp.int32, (SET * 16, SET * 16), 0)
    col = lax.broadcasted_iota(jnp.int32, (SET * 16, SET * 16), 1)
    swapped = (col % 16) * 16 + col // 16
    return (row == swapped).astype(jnp.float32).astype(jnp.bfloat16)


def attend(q, k, v, g, allowed, inv_root):
    raw = jnp.where(allowed, contract_last(k, q), masked)
    most = jnp.max(raw, axis=0, keepdims=True)
    weights = jnp.exp2((raw - most) * (inv_root * math.log2(math.e)))
    prob = weights * (1.0 / jnp.sum(weights, axis=0, keepdims=True))
    prob_low = prob.astype(jnp.bfloat16)
    prob_grad = contract_last(v, g)
    delta = jnp.sum(prob * prob_grad, axis=0, keepdims=True)
    score_grad = (prob * (prob_grad - delta)).astype(jnp.bfloat16)
    out = contract_first(v, prob_low).T.astype(jnp.bfloat16)
    dq = (contract_first(k, score_grad).T * inv_root).astype(jnp.bfloat16)
    dk = bf16_dot(score_grad, q) * inv_root
    dv = bf16_dot(prob_low, g)
    return out, dq, dk, dv


def fast_kernel(
    ids_ref, q_ref, k_ref, v_ref, g_ref,
    out_ref, dq_ref, dk_ref, dv_ref, flag_ref,
    cnt_send, cnt_group, cnt_recv, pack_mat, unpack_mat,
    send_a, send_b, send_c, recv_a, recv_b, recv_c, table,
    over, key_pos, query_pos, pick, onehot, loose, over_res, to_mate, to_block,
    result_a, result_b, result_c, back_a, back_b, back_c,
    ex_send, ex_recv, ex_send2, ex_recv2, ex_ret2, ex_back2, ex_ret1, ex_back1,
    hsend, hrecv, htable, hacc, hresult, hback, inputs, early,
    cnt_send_sem, cnt_sem, cnt2_send_sem, cnt2_sem,
    send_a_sem, recv_a_sem, send_b_sem, recv_b_sem, send_c_sem, recv_c_sem,
    res_a_sem, back_a_sem, res_b_sem, back_b_sem, res_c_sem, back_c_sem,
    ex_send_sem, ex_recv_sem, ex_send2_sem, ex_recv2_sem,
    ex_ret2_sem, ex_back2_sem, ex_ret1_sem, ex_back1_sem,
    hsend_sem, hrecv_sem, hres_sem, hback_sem, input_sem,
):
    seq_at = lax.axis_index("seq")
    clu_at = lax.axis_index("clu")
    groups = lax.axis_size("clu")
    heads = lax.axis_size("seq")
    devices = heads * groups
    me = seq_at * groups + clu_at
    inv_root = 1.0 / math.sqrt(DH)
    is_heavy_owner = lax.rem(seq_at, groups) == clu_at
    at_x, at_z = lax.div(seq_at, 4), lax.rem(seq_at, 4)
    at_y, at_core = lax.div(clu_at, 2), lax.rem(clu_at, 2)

    def by_core(first, second):
        return first + at_core * (second - first)

    eight = []
    for by_x, by_z, by_clu in zip(
        zip((3, 2, 3, 1, 3, 0, 2, 0), (2, 2, 1, 0, 2, 3, 0, 2)),
        zip((0, 0, 2, 3, 1, 2, 3, 1), (2, 2, 0, 1, 3, 0, 0, 2)),
        zip((2, 1, 3, 0, 6, 4, 5, 7), (6, 5, 7, 4, 2, 0, 1, 3)),
    ):
        y = lax.rem(at_y + by_core(by_clu[0] // 2, by_clu[1] // 2), 4)
        core = lax.rem(at_core + by_core(by_clu[0] % 2, by_clu[1] % 2), 2)
        eight.append((by_core(*by_x), by_core(*by_z), y * 2 + core))

    def for_peers(first, count, visit):
        def one_eight(step, carry):
            by = lax.rem(step * 13 + at_core * 12, 16)
            x = at_x + lax.div(by, 4)
            z = at_z + lax.rem(by, 4)
            for j, (more_x, more_z, clu_to) in enumerate(eight):
                seq_to = lax.rem(x + more_x, 4) * 4 + lax.rem(z + more_z, 4)
                if j in (3, 5):
                    pl.when(seq_to * groups + clu_to != me)(lambda: visit(seq_to, clu_to))
                else:
                    visit(seq_to, clu_to)
            return carry

        lax.fori_loop(first, first + count, one_eight, 0)

    def send_steps(first, count, source, target, send_sem, recv_sem):
        def start(seq_to, clu_to):
            pltpu.make_async_remote_copy(
                src_ref=source.at[seq_to * groups + clu_to],
                dst_ref=target,
                send_sem=send_sem,
                recv_sem=recv_sem,
                device_id=(seq_to, clu_to),
                device_id_type=MESH,
            ).start()

        for_peers(first, count, start)

    def send_own(source, target, recv_sem):
        pltpu.make_async_copy(source.at[me], target, recv_sem).start()

    def send_to_all(source, target, send_sem, recv_sem):
        send_steps(0, devices // 8, source, target, send_sem, recv_sem)
        send_own(source, target, recv_sem)

    def wait_bytes(ref, sem):
        pltpu.make_async_copy(ref, ref, sem).wait()

    for array, ref in enumerate((q_ref, k_ref, v_ref, g_ref)):
        pltpu.make_async_copy(ref, inputs.at[array], input_sem).start()
    barrier = pltpu.get_barrier_semaphore()

    def greet(seq_to, clu_to):
        pl.semaphore_signal(barrier, inc=1, device_id=(seq_to, clu_to), device_id_type=MESH)

    for_peers(0, devices // 8, greet)

    sub = lax.broadcasted_iota(jnp.int32, (TOK, TOK), 0)
    lane = lax.broadcasted_iota(jnp.int32, (TOK, TOK), 1)
    sub_f = sub.astype(jnp.float32)
    lane_f = lane.astype(jnp.float32)
    ids_l = jnp.broadcast_to(ids_ref[...].astype(jnp.float32), (TOK, TOK))
    ids_s = ids_l.T
    one = jnp.ones((TOK, TOK), jnp.float32)
    zero = jnp.zeros((TOK, TOK), jnp.float32)
    same = ids_l == ids_s
    rank_l = jnp.sum(jnp.where(same & (sub < lane), one, zero), axis=0, keepdims=True)
    rank_s = jnp.sum(jnp.where(same & (lane < sub), one, zero), axis=1, keepdims=True)
    count_l = jnp.sum(jnp.where(same, one, zero), axis=0, keepdims=True)
    cnt_send[...] = jnp.sum(jnp.where(ids_s == lane_f, one, zero), axis=0, keepdims=True)
    ids_row = ids_l[0:1, :]
    heavy = jnp.min(jnp.where(count_l == 4.0, ids_row, 999.0), axis=1, keepdims=True)
    group_l = jnp.floor(ids_l * (1.0 / 16.0))
    group_s = jnp.floor(ids_s * (1.0 / 16.0))
    earlier = (ids_s < ids_l) | (same & (sub < lane))
    later = (ids_l < ids_s) | (same & (lane < sub))
    before = (group_l == group_s) & (ids_s != heavy) & (rank_s >= 1.0) & earlier
    over_at = jnp.sum(jnp.where(before, one, zero), axis=0, keepdims=True)
    behind = (group_l == group_s) & (ids_l != heavy) & (rank_l >= 1.0) & later
    over_at_s = jnp.sum(jnp.where(behind, one, zero), axis=1, keepdims=True)
    excess_s = (ids_s != heavy) & (rank_s >= 1.0) & (over_at_s >= 4.0)
    excess_at = jnp.sum(jnp.where(excess_s & earlier, one, zero), axis=0, keepdims=True)
    light_l = ids_l != heavy
    slot_group = (sub // 16).astype(jnp.float32)
    in_tile = sub % 16
    over_l = light_l & (rank_l >= 1.0)

    def tile_picks(tile):
        at_slot = (in_tile % 4).astype(jnp.float32)
        if tile < 4:
            cluster = slot_group * 16.0 + at_slot + 4.0 * tile
            taken = (ids_l == cluster) & (rank_l == 0.0) & light_l
        else:
            taken = (group_l == slot_group) & over_l & (over_at == at_slot)
        return [jnp.where(taken & (in_tile // 4 == array), one, zero) for array in range(4)]

    def rest_picks():
        picks = []
        for array in range(4):
            chosen = (ids_l == heavy) & (rank_l == (sub % 4).astype(jnp.float32))
            chosen = chosen & (sub // 4 == array) & (sub < 16)
            beyond = over_l & (over_at >= 4.0) & (excess_at == (sub % 8).astype(jnp.float32))
            beyond = beyond & (sub // 8 == array + 2)
            picks.append(jnp.where(chosen | beyond, one, zero))
        return picks

    def put_pack(at_row, count, picks):
        for array, matrix in enumerate(picks):
            pack_mat[pl.ds(at_row, count), pl.ds(array * TOK, TOK)] = matrix[:count].astype(
                jnp.bfloat16
            )

    put_pack(0, TOK, tile_picks(0))
    put_pack(TOK, TOK, tile_picks(4))
    put_pack(2 * TOK, 48, rest_picks())


    def send_line(source, target, count, at, device, send_sem, recv_sem):
        def one_peer(step, carry):
            to = lax.rem(at + step, count)
            pltpu.make_async_remote_copy(
                src_ref=source(to),
                dst_ref=target,
                send_sem=send_sem,
                recv_sem=recv_sem,
                device_id=device(to),
                device_id_type=MESH,
            ).start()
            return carry

        lax.fori_loop(1, count, one_peer, 0)
        pltpu.make_async_copy(source(at), target, recv_sem).start()

    def along_seq(source, target, send_sem, recv_sem):
        send_line(
            source, target.at[seq_at], heads, seq_at, lambda to: (to, clu_at), send_sem, recv_sem
        )

    def along_clu(source, target, send_sem, recv_sem):
        send_line(
            source, target.at[clu_at], groups, clu_at, lambda to: (seq_at, to), send_sem, recv_sem
        )


    def head_rows(at):
        cols = pl.ds(pl.multiple_of(at * 2 * DH, 2 * DH), 2 * DH)
        return [inputs[array, :, cols] for array in range(4)]

    def put_tile(target, at, tile, packed):
        low = packed.astype(jnp.bfloat16)
        for k in range(2):
            target[pl.ds((2 * at + k) * groups, groups), tile] = low[
                :, k * DH : (k + 1) * DH
            ].reshape(groups, 16, DH)

    def pack_a(at, carry):
        rows = jnp.concatenate(head_rows(at), axis=0)
        packed = bf16_dot(pack_mat[pl.ds(0, 2 * TOK + 48), :], rows)
        put_tile(send_a, at, 0, packed[:TOK])
        put_tile(send_a, at, 1, packed[TOK : 2 * TOK])
        rest = packed[2 * TOK :].astype(jnp.bfloat16)
        for k in range(2):
            hsend[2 * at + k] = rest[:16, k * DH : (k + 1) * DH]
            ex_send[2 * at + k] = rest[16:, k * DH : (k + 1) * DH]
        return carry

    wait_bytes(inputs, input_sem)
    lax.fori_loop(0, heads // 2, pack_a, 0, unroll=2)
    pl.semaphore_wait(barrier, devices - 1)
    along_clu(lambda to: cnt_send, cnt_group, cnt_send_sem, cnt_sem)

    def send_heavy(step, carry):
        head = lax.rem(seq_at + step, heads)
        clu_to = lax.rem(head, groups)

        @pl.when(head * groups + clu_to != me)
        def _():
            pltpu.make_async_remote_copy(
                src_ref=hsend.at[head],
                dst_ref=hrecv.at[me],
                send_sem=hsend_sem,
                recv_sem=hrecv_sem,
                device_id=(head, clu_to),
                device_id_type=MESH,
            ).start()

        @pl.when(head * groups + clu_to == me)
        def _():
            pltpu.make_async_copy(hsend.at[head], hrecv.at[me], hrecv_sem).start()

        return carry

    lax.fori_loop(0, heads, send_heavy, 0)
    along_seq(lambda to: ex_send.at[to], ex_recv, ex_send_sem, ex_recv_sem)
    out_a = (send_a, recv_a.at[me], send_a_sem, recv_a_sem)
    send_steps(0, 4, *out_a)
    wait_bytes(cnt_group, cnt_sem)
    along_seq(lambda to: cnt_group, cnt_recv, cnt2_send_sem, cnt2_sem)
    send_steps(4, devices // 8 - 4, *out_a)
    send_own(send_a, recv_a.at[me], recv_a_sem)

    for tile in range(1, 4):
        put_pack((tile + 1) * TOK + 48, TOK, tile_picks(tile))

    def pack_bc(at, carry):
        rows = jnp.concatenate(head_rows(at), axis=0)
        packed = bf16_dot(pack_mat[pl.ds(2 * TOK + 48, 3 * TOK), :], rows)
        put_tile(send_b, at, 0, packed[:TOK])
        put_tile(send_b, at, 1, packed[TOK : 2 * TOK])
        put_tile(send_c, at, 0, packed[2 * TOK :])
        return carry

    lax.fori_loop(0, heads // 2, pack_bc, 0)

    wait_bytes(cnt_recv, cnt2_sem)
    seen = cnt_recv[...].reshape(TOK, TOK)
    heavies = jnp.min(jnp.where(seen == 4.0, lane_f, 999.0), axis=1, keepdims=True)
    heavy_all = jnp.min(heavies, axis=0, keepdims=True)
    light = lane_f != heavy_all
    more = jnp.where(light, jnp.maximum(seen - 1.0, 0.0), 0.0)
    more_low = more.astype(jnp.bfloat16)
    in_group = jnp.where(sub // 16 == lane, one, zero).astype(jnp.bfloat16)
    ahead = jnp.where(sub < lane, one, zero).astype(jnp.bfloat16)
    prior = jnp.where(lane < sub, one, zero).astype(jnp.bfloat16)
    mates = (lane < sub) & (lane % 8 == sub % 8)
    mates = jnp.where(mates, one, zero).astype(jnp.bfloat16)
    excess = jnp.maximum(bf16_dot(more_low, in_group) - 4.0, 0.0)
    excess_low = excess.astype(jnp.bfloat16)
    excess_off = bf16_dot(excess_low, ahead)
    excess_pre = bf16_dot(mates, excess_low)
    bad = (jnp.sum(excess, axis=1, keepdims=True) > 8.0) | (excess_pre + excess > 16.0)
    bad = bad | (heavies != heavy_all) | (jnp.sum(more, axis=0, keepdims=True) > OVC)
    flag_ref[0, 0] = jnp.max(jnp.where(bad, one, zero)).astype(jnp.int32)

    spot = zero
    for group in range(8):
        off, count, pre = [a[:, group : group + 1] for a in (excess_off, excess, excess_pre)]
        held = (lane_f >= off) & (lane_f < off + count)
        spot = spot + jnp.where(held, lane_f + (group * 16 + 1.0) - off + pre, zero)
    spot = jnp.where(sub % 8 == clu_at, spot, zero).reshape(16, 8, TOK)
    spot = jnp.sum(spot, axis=1).astype(jnp.bfloat16)
    spread8 = jnp.where(lane % 8 == sub, one, zero).astype(jnp.bfloat16)
    spot = jnp.where(lane[:16] // 8 == sub[:16], bf16_dot(spot, spread8), 0.0)
    spot = jnp.sum(spot, axis=0, keepdims=True) - 1.0
    to_mate[...] = jnp.where(sub_f == spot, one, zero).astype(jnp.bfloat16)
    spot = jnp.broadcast_to(spot, (TOK, TOK)).T
    to_block[...] = jnp.where(spot == lane_f, one, zero).astype(jnp.bfloat16)

    wait_bytes(ex_recv, ex_recv_sem)
    held = ex_recv[...].astype(jnp.float32)
    held = [held[:, 8 * a : 8 * a + 8, :].reshape(TOK, DH) for a in range(4)]
    held = jnp.concatenate(held, axis=1).astype(jnp.bfloat16)
    held = bf16_dot(to_mate[...], held).astype(jnp.bfloat16)
    for a in range(4):
        ex_send2[:, a] = held[:, a * DH : (a + 1) * DH].reshape(8, 16, DH)
    along_clu(lambda to: ex_send2.at[to], ex_recv2, ex_send2_sem, ex_recv2_sem)
    send_to_all(send_b, recv_b.at[me], send_b_sem, recv_b_sem)
    send_to_all(send_c, recv_c.at[me], send_c_sem, recv_c_sem)

    valid = jnp.where((seen > 0.0) & light, one, zero).astype(jnp.bfloat16)
    mine = (sub == clu_at * 16 + lane) & (lane < 16)
    mine = jnp.where(mine, one, zero).astype(jnp.bfloat16)
    more_g = bf16_dot(more_low, mine)
    valid_g = bf16_dot(valid, mine)
    more_g_low = more_g.astype(jnp.bfloat16)
    start_g = bf16_dot(prior, more_g_low)
    offset_g = bf16_dot(more_g_low, ahead)
    beyond_g = jnp.maximum(bf16_dot(more_g_low, one.astype(jnp.bfloat16)) - 4.0, 0.0)
    pre_g = bf16_dot(mates, beyond_g.astype(jnp.bfloat16))
    ex_index = lane_f - pre_g + 4.0
    first_row = lax.broadcasted_iota(jnp.int32, (1, TOK), 1).astype(jnp.float32) * 16.0
    in_tile_at = zero
    beyond_at = zero
    for c in range(16):
        count, begin, off, real = [
            a[:, c : c + 1] for a in (more_g, start_g, offset_g, valid_g)
        ]
        place = begin - off + (c * OVC + 1.0)
        held = (lane_f >= off) & (lane_f < off + count) & (lane < 4)
        in_tile_at = in_tile_at + jnp.where(held, lane_f + place, zero)
        held = (ex_index >= off) & (ex_index < off + count) & (ex_index >= 4.0)
        beyond_at = beyond_at + jnp.where(held, ex_index + place, zero)
        held = (lane_f >= begin) & (lane_f < begin + count)
        where = jnp.where(held, sub_f * 16.0 + 1.0 + lane_f - begin, zero)
        where = jnp.sum(where, axis=0, keepdims=True)
        where = jnp.where(where > 0.0, where, FAR)
        query_row = jnp.concatenate([first_row, where], axis=1)
        query_pos[c] = jnp.broadcast_to(query_row, (8, 2 * TOK))
        key_pos[c, pl.ds(0, TOK), :] = jnp.where(real > 0.0, sub_f * 16.0, FAR)
        key_pos[c, pl.ds(TOK, OVC), :] = jnp.broadcast_to(where, (TOK, TOK)).T[:OVC]
    beyond_at = jnp.sum(beyond_at.reshape(16, 8, TOK), axis=0)
    high = jnp.floor(beyond_at * (1.0 / 32.0))
    split = jnp.concatenate([high, beyond_at - high * 32.0], axis=0).astype(jnp.bfloat16)
    spread16 = jnp.where(lane % 16 == sub, one, zero).astype(jnp.bfloat16)
    split = bf16_dot(split, spread16)
    split = jnp.where(lane[:8] // 16 == sub[:8], split[:8] * 32.0 + split[8:], 0.0)
    beyond_row = jnp.sum(split, axis=0, keepdims=True) - 1.0
    tile_rows = in_tile_at.T[0:8, :] - 1.0
    slot_rows = [tile_rows[k : k + 1, :] for k in range(4)] + [beyond_row]
    slot_cols = [in_tile_at[:, k : k + 1] - 1.0 for k in range(4)]
    slot_cols.append(jnp.broadcast_to(beyond_row, (TOK, TOK)).T)

    chunk = 4
    for k in range(5):
        for m in range(16 * OVC // TOK):
            onehot[pl.ds(k * TOK, TOK), pl.ds(m * TOK, TOK)] = jnp.where(
                slot_cols[k] == lane_f + float(m * TOK), one, zero
            ).astype(jnp.bfloat16)
            pick[pl.ds(m * TOK, TOK), pl.ds(k * TOK, TOK)] = jnp.where(
                slot_rows[k] == sub_f + float(m * TOK), one, zero
            ).astype(jnp.bfloat16)

    for at, tile in enumerate((0, 1, 2, None, 3, 4)):
        for array, matrix in enumerate(rest_picks() if tile is None else tile_picks(tile)):
            unpack_mat[pl.ds(array * TOK, TOK), pl.ds(at * TOK, TOK)] = matrix.T.astype(
                jnp.bfloat16
            )

    perm = flip_perm()

    def arrange(source, target, units):
        def two_sets(at, carry):
            blocks = [pl.ds(pl.multiple_of((2 * at + i) * SET, SET), SET) for i in range(2)]
            spots = [(held, unit) for held in blocks for unit in range(units)]
            rows = jnp.concatenate(
                [source(held, unit).reshape(SET * 16, DH) for held, unit in spots], axis=1
            )
            turned = bf16_dot(perm, rows).astype(jnp.bfloat16)
            for i, (held, unit) in enumerate(spots):
                target(held, unit, turned[:, i * DH : (i + 1) * DH].reshape(16, SET, DH))
            return carry

        lax.fori_loop(0, devices // (2 * SET), two_sets, 0, unroll=2)

    def put_table(first):
        def put(blocks, unit, value):
            table[first + unit, :, blocks, :] = value

        return put

    @pl.when(is_heavy_owner)
    def _():
        wait_bytes(hrecv, hrecv_sem)

        def put_heavy(blocks, unit, value):
            htable[:, blocks, :] = value

        arrange(lambda blocks, unit: hrecv[blocks], put_heavy, 1)
        k_h, v_h = [htable[4 * a : 4 * a + 4].reshape(4 * TOK, DH) for a in (1, 2)]
        hacc[...] = jnp.zeros_like(hacc)
        key_sub = lax.broadcasted_iota(jnp.int32, (4 * TOK, TOK), 0)
        key_at = lax.rem(key_sub, TOK) * 4 + lax.div(key_sub, TOK)
        query_at = lax.broadcasted_iota(jnp.int32, (4 * TOK, TOK), 1) * 4

        def heavy_tile(s, carry):
            out, dq, dk, dv = attend(
                htable[s], k_h, v_h, htable[12 + s], key_at <= query_at + s, inv_root
            )
            hacc[2, pl.ds(pl.multiple_of(s * TOK, TOK), TOK)] = out.astype(jnp.float32)
            hacc[3, pl.ds(pl.multiple_of(s * TOK, TOK), TOK)] = dq.astype(jnp.float32)
            hacc[0] += dk
            hacc[1] += dv
            return carry

        lax.fori_loop(0, 4, heavy_tile, 0)
        for array, at in enumerate((2, 3, 0, 1)):
            htable[4 * array : 4 * array + 4] = (
                hacc[at].astype(jnp.bfloat16).reshape(4, TOK, DH)
            )

        def put_hresult(blocks, unit, value):
            hresult[blocks] = value

        arrange(lambda blocks, unit: htable[:, blocks, :], put_hresult, 1)
        send_to_all(hresult, hback.at[seq_at], hres_sem, hback_sem)

    wait_bytes(recv_a, recv_a_sem)
    def put_tile_a(blocks, unit, value):
        table[4 * unit, :, blocks, :] = value

    arrange(lambda blocks, unit: recv_a[blocks, unit], put_tile_a, 2)

    wait_bytes(ex_recv2, ex_recv2_sem)
    for a in range(4):
        cols = pl.ds(a * DH, DH)
        loose[pl.ds(0, 4 * TOK), cols] = table[4, 4 * a : 4 * a + 4].reshape(4 * TOK, DH)
        loose[pl.ds(4 * TOK, TOK), cols] = ex_recv2[:, a].reshape(TOK, DH)

    def gather_chunk(at, carry):
        chosen = pick[pl.ds(pl.multiple_of(at * chunk * OVC, 64), chunk * OVC), :]
        found = bf16_dot(chosen, loose[...]).astype(jnp.bfloat16)
        for c in range(chunk):
            for array in range(4):
                over[array, at * chunk + c] = found[
                    c * OVC : (c + 1) * OVC, array * DH : (array + 1) * DH
                ]
        return carry

    lax.fori_loop(0, 16 // chunk, gather_chunk, 0)

    pad_rows = jnp.zeros((TOK - OVC, DH), jnp.bfloat16)

    def load_cluster(tile, j):
        c = tile * 4 + j
        rows = [
            jnp.concatenate([table[tile, a * 4 + j], over[a, c]], axis=0) for a in range(4)
        ]
        for a in (0, 3):
            rows[a] = jnp.concatenate([rows[a], pad_rows], axis=0)
        key_at = key_pos[c]
        allowed = jnp.concatenate([key_at, key_at], axis=1) <= query_pos[c, 0:1, :]
        return rows + [allowed]

    def attend_tiles(first, tiles, beside):
        def one_pair(at, carry):
            beside(at)
            tile = first + lax.div(at, 2)
            spots = [lax.rem(at, 2) * 2 + i for i in range(2)]
            loaded = [load_cluster(tile, j) for j in spots]
            found = [attend(*arrays, inv_root) for arrays in loaded]
            for j, results in zip(spots, found):
                c = tile * 4 + j
                for a, value in enumerate(results):
                    value = value.astype(jnp.bfloat16)
                    table[tile, a * 4 + j] = value[:TOK]
                    over_res[
                        pl.ds(pl.multiple_of(c * OVC, 16), OVC), pl.ds(a * DH, DH)
                    ] = value[TOK : TOK + OVC]
            return carry

        lax.fori_loop(0, 2 * tiles, one_pair, 0)

    def put_in(result):
        def put(blocks, unit, value):
            result[blocks, unit] = value

        return put

    def from_table(first):
        return lambda blocks, unit: table[first + unit, :, blocks, :]

    to_a = (result_a, back_a.at[me], res_a_sem, back_a_sem)
    to_b = (result_b, back_b.at[me], res_b_sem, back_b_sem)
    to_c = (result_c, back_c.at[me], res_c_sem, back_c_sem)
    attend_tiles(0, 1, lambda at: None)
    arrange(from_table(0), put_in(result_a), 1)
    send_own(result_a, back_a.at[me], back_a_sem)

    wait_bytes(recv_b, recv_b_sem)
    arrange(lambda blocks, unit: recv_b[blocks, unit], put_table(1), 2)
    attend_tiles(1, 2, lambda at: send_steps(at * 4, 4, *to_a))
    arrange(from_table(1), put_in(result_b), 2)
    send_own(result_b, back_b.at[me], back_b_sem)

    wait_bytes(recv_c, recv_c_sem)
    arrange(lambda blocks, unit: recv_c[blocks, 0], put_table(3), 1)
    attend_tiles(3, 1, lambda at: send_steps(at * 8, 8, *to_b))

    found = bf16_dot(onehot[pl.ds(4 * TOK, TOK), :], over_res[...]).astype(jnp.bfloat16)
    for a in range(4):
        ex_ret2[:, a] = found[:, a * DH : (a + 1) * DH].reshape(8, 16, DH)
    along_clu(lambda to: ex_ret2.at[to], ex_back2, ex_ret2_sem, ex_back2_sem)
    found = bf16_dot(onehot[pl.ds(0, 4 * TOK), :], over_res[...]).astype(jnp.bfloat16)
    for a in range(4):
        table[4, 4 * a : 4 * a + 4] = found[:, a * DH : (a + 1) * DH].reshape(4, TOK, DH)
    arrange(from_table(3), put_in(result_c), 2)
    send_steps(0, devices // 16, *to_c)
    send_own(result_c, back_c.at[me], back_c_sem)

    wait_bytes(ex_back2, ex_back2_sem)
    held = [ex_back2[:, a].reshape(TOK, DH) for a in range(4)]
    held = bf16_dot(to_block[...], jnp.concatenate(held, axis=1))
    held = [held[:, a * DH : (a + 1) * DH].reshape(16, 8, DH) for a in range(4)]
    ex_ret1[...] = jnp.concatenate(held, axis=1).astype(jnp.bfloat16)
    along_seq(lambda to: ex_ret1.at[to], ex_back1, ex_ret1_sem, ex_back1_sem)
    send_steps(devices // 16, devices // 16, *to_c)

    def unpack(tiles, rest, first, count):
        sides = []
        for k in range(2):
            sides.append(
                jnp.concatenate(
                    [tile(k).reshape(TOK, DH) for tile in tiles] + [part(k) for part in rest],
                    axis=0,
                )
            )
        return bf16_dot(
            unpack_mat[:, pl.ds(first, count)], jnp.concatenate(sides, axis=1)
        )

    def tile_of(ref, at, tile):
        return lambda k: ref[pl.ds((2 * at + k) * groups, groups), tile]

    def unpack_early(at, carry):
        tiles = [tile_of(back_a, at, 0), tile_of(back_b, at, 0), tile_of(back_b, at, 1)]
        rest = [
            lambda k: hback[2 * at + k],
            lambda k: ex_back1[2 * at + k],
            lambda k: jnp.zeros((TOK - 48, DH), jnp.bfloat16),
        ]
        early[at] = unpack(tiles, rest, 0, 4 * TOK)
        return carry

    def unpack_last(at, carry):
        cols = pl.ds(pl.multiple_of(at * 2 * DH, 2 * DH), 2 * DH)
        tiles = [tile_of(back_c, at, 0), tile_of(back_c, at, 1)]
        found = (early[at] + unpack(tiles, [], 4 * TOK, 2 * TOK)).astype(jnp.bfloat16)
        for array, ref in enumerate((out_ref, dq_ref, dk_ref, dv_ref)):
            ref[:, cols] = found[array * TOK : (array + 1) * TOK]
        return carry

    wait_bytes(hback, hback_sem)
    wait_bytes(back_a, back_a_sem)
    wait_bytes(back_b, back_b_sem)
    wait_bytes(ex_back1, ex_back1_sem)
    lax.fori_loop(0, heads // 2, unpack_early, 0, unroll=2)
    wait_bytes(back_c, back_c_sem)
    lax.fori_loop(0, heads // 2, unpack_last, 0, unroll=2)

    others = pl.ds(0, devices - 1)
    wait_bytes(cnt_group.at[pl.ds(0, groups - 1)], cnt_send_sem)
    wait_bytes(cnt_recv.at[pl.ds(0, heads - 1)], cnt2_send_sem)
    for ref, sem in ((ex_send, ex_send_sem), (ex_ret1, ex_ret1_sem)):
        wait_bytes(ref.at[pl.ds(0, heads - 1)], sem)
    for ref, sem in ((ex_send2, ex_send2_sem), (ex_ret2, ex_ret2_sem)):
        wait_bytes(ref.at[pl.ds(0, groups - 1)], sem)
    wait_bytes(send_a.at[others], send_a_sem)
    wait_bytes(send_b.at[others], send_b_sem)
    wait_bytes(send_c.at[others], send_c_sem)
    wait_bytes(result_a.at[others], res_a_sem)
    wait_bytes(result_b.at[others], res_b_sem)
    wait_bytes(result_c.at[others], res_c_sem)

    @pl.when(is_heavy_owner)
    def _():
        wait_bytes(hsend.at[pl.ds(0, heads - 1)], hsend_sem)
        wait_bytes(hresult.at[others], hres_sem)

    @pl.when(jnp.logical_not(is_heavy_owner))
    def _():
        wait_bytes(hsend, hsend_sem)


def fast_path(queries, key_rows, value_rows, out_grad, cluster_ids):
    tok_rows, columns = queries.shape
    heads = columns // DH
    groups = lax.axis_size("clu")
    devices = lax.axis_size("seq") * groups
    low = jnp.bfloat16
    wide = jnp.float32
    rows = pltpu.VMEM((tok_rows, columns), low)
    vmem = pl.BlockSpec(memory_space=pltpu.VMEM)
    smem = pl.BlockSpec(memory_space=pltpu.SMEM)
    return pl.pallas_call(
        fast_kernel,
        out_shape=[rows] * 4 + [jax.ShapeDtypeStruct((1, 1), jnp.int32)],
        in_specs=[vmem] + [pl.BlockSpec(memory_space=pl.ANY)] * 4,
        out_specs=[vmem] * 4 + [smem],
        scratch_shapes=[
            pltpu.VMEM((1, TOK), wide),
            pltpu.VMEM((groups, 1, TOK), wide),
            pltpu.VMEM((heads, groups, 1, TOK), wide),
            pltpu.VMEM((5 * TOK + 48, 4 * TOK), low),
            pltpu.VMEM((4 * TOK, 6 * TOK), low),
            pltpu.VMEM((devices, 2, 16, DH), low),
            pltpu.VMEM((devices, 2, 16, DH), low),
            pltpu.VMEM((devices, 1, 16, DH), low),
            pltpu.VMEM((devices, 2, 16, DH), low),
            pltpu.VMEM((devices, 2, 16, DH), low),
            pltpu.VMEM((devices, 1, 16, DH), low),
            pltpu.VMEM((5, 16, devices, DH), low),
            pltpu.VMEM((4, 16, OVC, DH), low),
            pltpu.VMEM((16, TOK + OVC, TOK), wide),
            pltpu.VMEM((16, 8, 2 * TOK), wide),
            pltpu.VMEM((16 * OVC, 5 * TOK), low),
            pltpu.VMEM((5 * TOK, 16 * OVC), low),
            pltpu.VMEM((5 * TOK, 4 * DH), low),
            pltpu.VMEM((16 * OVC, 4 * DH), low),
            pltpu.VMEM((TOK, TOK), low),
            pltpu.VMEM((TOK, TOK), low),
            pltpu.VMEM((devices, 1, 16, DH), low),
            pltpu.VMEM((devices, 2, 16, DH), low),
            pltpu.VMEM((devices, 2, 16, DH), low),
            pltpu.VMEM((devices, 1, 16, DH), low),
            pltpu.VMEM((devices, 2, 16, DH), low),
            pltpu.VMEM((devices, 2, 16, DH), low),
            pltpu.VMEM((heads, 32, DH), low),
            pltpu.VMEM((heads, 32, DH), low),
            pltpu.VMEM((groups, 4, 16, DH), low),
            pltpu.VMEM((groups, 4, 16, DH), low),
            pltpu.VMEM((groups, 4, 16, DH), low),
            pltpu.VMEM((groups, 4, 16, DH), low),
            pltpu.VMEM((heads, 32, DH), low),
            pltpu.VMEM((heads, 32, DH), low),
            pltpu.VMEM((heads, 16, DH), low),
            pltpu.VMEM((devices, 16, DH), low),
            pltpu.VMEM((16, devices, DH), low),
            pltpu.VMEM((4, 4 * TOK, DH), wide),
            pltpu.VMEM((devices, 16, DH), low),
            pltpu.VMEM((heads, 16, DH), low),
            pltpu.VMEM((4, tok_rows, columns), low),
            pltpu.VMEM((heads // 2, 4 * tok_rows, 2 * DH), wide),
        ]
        + [pltpu.SemaphoreType.DMA] * 29,
        compiler_params=pltpu.CompilerParams(
            collective_id=0, has_side_effects=True, vmem_limit_bytes=44 * 1024 * 1024
        ),
    )(cluster_ids.reshape(1, tok_rows), queries, key_rows, value_rows, out_grad)


def copy_kernel(*refs):
    sem = refs[-1]
    copies = [
        pltpu.make_async_copy(refs[i], refs[4 + i], sem.at[i]) for i in range(4)
    ]
    for copy in copies:
        copy.start()
    for copy in copies:
        copy.wait()


def copy_out(arrays):
    anywhere = pl.BlockSpec(memory_space=pl.ANY)
    return pl.pallas_call(
        copy_kernel,
        out_shape=[pltpu.HBM(a.shape, a.dtype) for a in arrays],
        in_specs=[anywhere] * 4,
        out_specs=[anywhere] * 4,
        scratch_shapes=[pltpu.SemaphoreType.DMA((4,))],
    )(*arrays)


def per_device(queries, key_rows, value_rows, out_grad, cluster_ids):
    arrays = (queries, key_rows, value_rows, out_grad, cluster_ids)
    *fast, flag = fast_path(*arrays)
    return lax.cond(
        flag.reshape(()) != 0,
        lambda arrays, fast: full_capacity(*arrays),
        lambda arrays, fast: tuple(copy_out(fast)),
        arrays,
        tuple(fast),
    )


def solution(mesh):
    in_specs = (
        P(("seq", "clu"), None),
        P(("seq", "clu"), None),
        P(("seq", "clu"), None),
        P(("seq", "clu"), None),
        P(("seq", "clu")),
    )
    out_specs = (
        P(("seq", "clu"), None),
        P(("seq", "clu"), None),
        P(("seq", "clu"), None),
        P(("seq", "clu"), None),
    )
    return jax.shard_map(
        per_device, mesh=mesh, in_specs=in_specs, out_specs=out_specs, check_vma=False
    )
```

```python
import math

import jax
import jax.numpy as jnp
from jax import lax
from jax.experimental import pallas as pl
from jax.experimental.pallas import tpu as pltpu
from jax.sharding import PartitionSpec as P

DH = 128
TOK = 128
OVC = 80
SET = 16
FAR = 1e9
MESH = pl.DeviceIdType.MESH


masked = -1e30


def contract_last(left, right):
    return lax.dot_general(
        left, right, (((1,), (1,)), ((), ())), preferred_element_type=jnp.float32
    )


def contract_first(left, right):
    return lax.dot_general(
        left, right, (((0,), (0,)), ((), ())), preferred_element_type=jnp.float32
    )


def softmax_rows(query_head, key_head, allowed, inv_root):
    scores = contract_last(query_head, key_head) * inv_root
    scores = jnp.where(allowed, scores, masked)
    row_max = jnp.max(scores, axis=1, keepdims=True)
    weights = jnp.exp(scores - row_max)
    row_sum = jnp.sum(weights, axis=1, keepdims=True)
    return (weights / row_sum).astype(jnp.bfloat16)


def head_slice(array, head_index):
    return lax.dynamic_slice_in_dim(array, head_index * DH, DH, 1)


def full_capacity(queries, key_rows, value_rows, out_grad, cluster_ids):
    seq_count = lax.axis_size("seq")
    clu_count = lax.axis_size("clu")
    devices = seq_count * clu_count
    tok_rows = queries.shape[0]
    columns = queries.shape[1]
    head_count = columns // DH
    most_rows = 4 * tok_rows // devices
    capacity = most_rows * devices
    inv_root = 1.0 / math.sqrt(DH)
    owners = jnp.arange(devices, dtype=jnp.int32)
    member = (cluster_ids[:, None] == owners[None, :]).astype(jnp.int32)
    running = jnp.cumsum(member, axis=0) - 1
    slot_rank = jnp.sum(member * running, axis=1)
    sent_counts = jnp.sum(member, axis=0).reshape(devices, 1)
    slot_index = cluster_ids * most_rows + slot_rank
    stacked = jnp.concatenate([queries, key_rows, value_rows], axis=1)
    width_in = stacked.shape[1]
    packed = jnp.zeros((devices * most_rows, width_in), jnp.bfloat16).at[slot_index].set(stacked)
    packed = packed.reshape(devices, most_rows, width_in)
    got_rows, got_counts = (
        lax.all_to_all(packed, ("seq", "clu"), split_axis=0, concat_axis=0, tiled=True),
        lax.all_to_all(sent_counts, ("seq", "clu"), split_axis=0, concat_axis=0, tiled=True),
    )
    got_counts = got_counts.reshape(devices)
    starts = jnp.cumsum(got_counts) - got_counts
    live_total = jnp.sum(got_counts)
    within = jnp.arange(most_rows, dtype=jnp.int32)
    target = jnp.where(
        within[None, :] < got_counts[:, None], starts[:, None] + within[None, :], capacity
    )
    target = target.reshape(devices * most_rows)
    gathered = (
        jnp.zeros((capacity, width_in), jnp.bfloat16)
        .at[target]
        .set(got_rows.reshape(devices * most_rows, width_in), mode="drop")
    )
    query_block = gathered[:, :columns]
    key_block = gathered[:, columns : 2 * columns]
    value_block = gathered[:, 2 * columns : 3 * columns]
    positions = jnp.arange(capacity, dtype=jnp.int32)
    allowed = (positions[None, :] <= positions[:, None]) & (positions[None, :] < live_total)

    def forward_head(head_index, mixed_rows):
        weights_low = softmax_rows(
            head_slice(query_block, head_index),
            head_slice(key_block, head_index),
            allowed,
            inv_root,
        )
        out_head = jnp.dot(
            weights_low, head_slice(value_block, head_index), preferred_element_type=jnp.float32
        ).astype(jnp.bfloat16)
        return lax.dynamic_update_slice_in_dim(mixed_rows, out_head, head_index * DH, 1)

    mixed_rows = lax.fori_loop(
        0, head_count, forward_head, jnp.zeros((capacity, columns), jnp.bfloat16)
    )
    back_index = jnp.minimum(target, capacity - 1)
    outgoing = jnp.take(mixed_rows, back_index, axis=0).reshape(devices, most_rows, columns)
    grad_packed = (
        jnp.zeros((devices * most_rows, columns), jnp.bfloat16).at[slot_index].set(out_grad)
    )
    grad_packed = grad_packed.reshape(devices, most_rows, columns)
    returned = lax.all_to_all(outgoing, ("seq", "clu"), split_axis=0, concat_axis=0, tiled=True)
    got_grad = lax.all_to_all(grad_packed, ("seq", "clu"), split_axis=0, concat_axis=0, tiled=True)
    attention_out = jnp.take(returned.reshape(devices * most_rows, columns), slot_index, axis=0)
    grad_block = (
        jnp.zeros((capacity, columns), jnp.bfloat16)
        .at[target]
        .set(got_grad.reshape(devices * most_rows, columns), mode="drop")
    )
    delta_rows = jnp.sum(
        (grad_block.astype(jnp.float32) * mixed_rows.astype(jnp.float32)).reshape(
            capacity, head_count, DH
        ),
        axis=2,
    )

    def backward_head(head_index, grad_rows):
        query_head = head_slice(query_block, head_index)
        key_head = head_slice(key_block, head_index)
        value_head = head_slice(value_block, head_index)
        grad_head = head_slice(grad_block, head_index)
        weights_low = softmax_rows(query_head, key_head, allowed, inv_root)
        prob_grad = contract_last(grad_head, value_head)
        delta_head = lax.dynamic_slice_in_dim(delta_rows, head_index, 1, 1)
        score_grad = (weights_low.astype(jnp.float32) * (prob_grad - delta_head)).astype(
            jnp.bfloat16
        )
        query_part = (
            jnp.dot(score_grad, key_head, preferred_element_type=jnp.float32) * inv_root
        ).astype(jnp.bfloat16)
        key_part = (contract_first(score_grad, query_head) * inv_root).astype(jnp.bfloat16)
        value_part = contract_first(weights_low, grad_head).astype(jnp.bfloat16)
        grad_rows = lax.dynamic_update_slice_in_dim(grad_rows, query_part, head_index * DH, 1)
        grad_rows = lax.dynamic_update_slice_in_dim(
            grad_rows, key_part, columns + head_index * DH, 1
        )
        return lax.dynamic_update_slice_in_dim(
            grad_rows, value_part, 2 * columns + head_index * DH, 1
        )

    grad_rows = lax.fori_loop(
        0, head_count, backward_head, jnp.zeros((capacity, 3 * columns), jnp.bfloat16)
    )
    outgoing_grads = jnp.take(grad_rows, back_index, axis=0).reshape(
        devices, most_rows, 3 * columns
    )
    returned_grads = lax.all_to_all(
        outgoing_grads, ("seq", "clu"), split_axis=0, concat_axis=0, tiled=True
    )
    picked = jnp.take(returned_grads.reshape(devices * most_rows, 3 * columns), slot_index, axis=0)
    return (
        attention_out,
        picked[:, :columns],
        picked[:, columns : 2 * columns],
        picked[:, 2 * columns :],
    )


def bf16_dot(left, right):
    return jnp.dot(left, right, preferred_element_type=jnp.float32)


def flip_perm():
    row = lax.broadcasted_iota(jnp.int32, (SET * 16, SET * 16), 0)
    col = lax.broadcasted_iota(jnp.int32, (SET * 16, SET * 16), 1)
    swapped = (col % 16) * 16 + col // 16
    return (row == swapped).astype(jnp.float32).astype(jnp.bfloat16)


def attend(q, k, v, g, allowed, inv_root):
    raw = jnp.where(allowed, contract_last(k, q), masked)
    most = jnp.max(raw, axis=0, keepdims=True)
    weights = jnp.exp2((raw - most) * (inv_root * math.log2(math.e)))
    prob = weights * (1.0 / jnp.sum(weights, axis=0, keepdims=True))
    prob_low = prob.astype(jnp.bfloat16)
    prob_grad = contract_last(v, g)
    delta = jnp.sum(prob * prob_grad, axis=0, keepdims=True)
    score_grad = (prob * (prob_grad - delta)).astype(jnp.bfloat16)
    out = contract_first(v, prob_low).T.astype(jnp.bfloat16)
    dq = (contract_first(k, score_grad).T * inv_root).astype(jnp.bfloat16)
    dk = bf16_dot(score_grad, q) * inv_root
    dv = bf16_dot(prob_low, g)
    return out, dq, dk, dv


def fast_kernel(
    ids_ref, q_ref, k_ref, v_ref, g_ref,
    out_ref, dq_ref, dk_ref, dv_ref, flag_ref,
    cnt_send, cnt_group, cnt_recv, pack_mat, unpack_mat,
    send_a, send_b, send_c, recv_a, recv_b, recv_c, table,
    over, key_pos, query_pos, pick, onehot, loose, over_res, to_mate, to_block,
    result_a, result_b, result_c, back_a, back_b, back_c,
    ex_send, ex_recv, ex_send2, ex_recv2, ex_ret2, ex_back2, ex_ret1, ex_back1,
    hsend, hrecv, htable, hacc, hresult, hback, inputs, early,
    cnt_send_sem, cnt_sem, cnt2_send_sem, cnt2_sem,
    send_a_sem, recv_a_sem, send_b_sem, recv_b_sem, send_c_sem, recv_c_sem,
    res_a_sem, back_a_sem, res_b_sem, back_b_sem, res_c_sem, back_c_sem,
    ex_send_sem, ex_recv_sem, ex_send2_sem, ex_recv2_sem,
    ex_ret2_sem, ex_back2_sem, ex_ret1_sem, ex_back1_sem,
    hsend_sem, hrecv_sem, hres_sem, hback_sem, input_sem,
):
    seq_at = lax.axis_index("seq")
    clu_at = lax.axis_index("clu")
    groups = lax.axis_size("clu")
    heads = lax.axis_size("seq")
    devices = heads * groups
    me = seq_at * groups + clu_at
    inv_root = 1.0 / math.sqrt(DH)
    is_heavy_owner = lax.rem(seq_at, groups) == clu_at
    at_x, at_z = lax.div(seq_at, 4), lax.rem(seq_at, 4)
    at_y, at_core = lax.div(clu_at, 2), lax.rem(clu_at, 2)

    def by_core(first, second):
        return first + at_core * (second - first)

    eight = []
    for by_x, by_z, by_clu in zip(
        zip((3, 2, 3, 1, 3, 0, 2, 0), (2, 2, 1, 0, 2, 3, 0, 2)),
        zip((0, 0, 2, 3, 1, 2, 3, 1), (2, 2, 0, 1, 3, 0, 0, 2)),
        zip((2, 1, 3, 0, 6, 4, 5, 7), (6, 5, 7, 4, 2, 0, 1, 3)),
    ):
        y = lax.rem(at_y + by_core(by_clu[0] // 2, by_clu[1] // 2), 4)
        core = lax.rem(at_core + by_core(by_clu[0] % 2, by_clu[1] % 2), 2)
        eight.append((by_core(*by_x), by_core(*by_z), y * 2 + core))

    def for_peers(first, count, visit):
        def one_eight(step, carry):
            by = lax.rem(step * 13 + at_core * 12, 16)
            x = at_x + lax.div(by, 4)
            z = at_z + lax.rem(by, 4)
            for j, (more_x, more_z, clu_to) in enumerate(eight):
                seq_to = lax.rem(x + more_x, 4) * 4 + lax.rem(z + more_z, 4)
                if j in (3, 5):
                    pl.when(seq_to * groups + clu_to != me)(lambda: visit(seq_to, clu_to))
                else:
                    visit(seq_to, clu_to)
            return carry

        lax.fori_loop(first, first + count, one_eight, 0)

    def send_steps(first, count, source, target, send_sem, recv_sem):
        def start(seq_to, clu_to):
            pltpu.make_async_remote_copy(
                src_ref=source.at[seq_to * groups + clu_to],
                dst_ref=target,
                send_sem=send_sem,
                recv_sem=recv_sem,
                device_id=(seq_to, clu_to),
                device_id_type=MESH,
            ).start()

        for_peers(first, count, start)

    def send_own(source, target, recv_sem):
        pltpu.make_async_copy(source.at[me], target, recv_sem).start()

    def send_to_all(source, target, send_sem, recv_sem):
        send_steps(0, devices // 8, source, target, send_sem, recv_sem)
        send_own(source, target, recv_sem)

    def wait_bytes(ref, sem):
        pltpu.make_async_copy(ref, ref, sem).wait()

    for array, ref in enumerate((q_ref, k_ref, v_ref, g_ref)):
        pltpu.make_async_copy(ref, inputs.at[array], input_sem).start()
    barrier = pltpu.get_barrier_semaphore()

    def greet(seq_to, clu_to):
        pl.semaphore_signal(barrier, inc=1, device_id=(seq_to, clu_to), device_id_type=MESH)

    for_peers(0, devices // 8, greet)

    sub = lax.broadcasted_iota(jnp.int32, (TOK, TOK), 0)
    lane = lax.broadcasted_iota(jnp.int32, (TOK, TOK), 1)
    sub_f = sub.astype(jnp.float32)
    lane_f = lane.astype(jnp.float32)
    ids_l = jnp.broadcast_to(ids_ref[...].astype(jnp.float32), (TOK, TOK))
    ids_s = ids_l.T
    one = jnp.ones((TOK, TOK), jnp.float32)
    zero = jnp.zeros((TOK, TOK), jnp.float32)
    same = ids_l == ids_s
    rank_l = jnp.sum(jnp.where(same & (sub < lane), one, zero), axis=0, keepdims=True)
    rank_s = jnp.sum(jnp.where(same & (lane < sub), one, zero), axis=1, keepdims=True)
    count_l = jnp.sum(jnp.where(same, one, zero), axis=0, keepdims=True)
    cnt_send[...] = jnp.sum(jnp.where(ids_s == lane_f, one, zero), axis=0, keepdims=True)
    ids_row = ids_l[0:1, :]
    heavy = jnp.min(jnp.where(count_l == 4.0, ids_row, 999.0), axis=1, keepdims=True)
    group_l = jnp.floor(ids_l * (1.0 / 16.0))
    group_s = jnp.floor(ids_s * (1.0 / 16.0))
    earlier = (ids_s < ids_l) | (same & (sub < lane))
    later = (ids_l < ids_s) | (same & (lane < sub))
    before = (group_l == group_s) & (ids_s != heavy) & (rank_s >= 1.0) & earlier
    over_at = jnp.sum(jnp.where(before, one, zero), axis=0, keepdims=True)
    behind = (group_l == group_s) & (ids_l != heavy) & (rank_l >= 1.0) & later
    over_at_s = jnp.sum(jnp.where(behind, one, zero), axis=1, keepdims=True)
    excess_s = (ids_s != heavy) & (rank_s >= 1.0) & (over_at_s >= 4.0)
    excess_at = jnp.sum(jnp.where(excess_s & earlier, one, zero), axis=0, keepdims=True)
    light_l = ids_l != heavy
    slot_group = (sub // 16).astype(jnp.float32)
    in_tile = sub % 16
    over_l = light_l & (rank_l >= 1.0)

    def tile_picks(tile):
        at_slot = (in_tile % 4).astype(jnp.float32)
        if tile < 4:
            cluster = slot_group * 16.0 + at_slot + 4.0 * tile
            taken = (ids_l == cluster) & (rank_l == 0.0) & light_l
        else:
            taken = (group_l == slot_group) & over_l & (over_at == at_slot)
        return [jnp.where(taken & (in_tile // 4 == array), one, zero) for array in range(4)]

    def rest_picks():
        picks = []
        for array in range(4):
            chosen = (ids_l == heavy) & (rank_l == (sub % 4).astype(jnp.float32))
            chosen = chosen & (sub // 4 == array) & (sub < 16)
            beyond = over_l & (over_at >= 4.0) & (excess_at == (sub % 8).astype(jnp.float32))
            beyond = beyond & (sub // 8 == array + 2)
            picks.append(jnp.where(chosen | beyond, one, zero))
        return picks

    def put_pack(at_row, count, picks):
        for array, matrix in enumerate(picks):
            pack_mat[pl.ds(at_row, count), pl.ds(array * TOK, TOK)] = matrix[:count].astype(
                jnp.bfloat16
            )

    put_pack(0, TOK, tile_picks(0))
    put_pack(TOK, TOK, tile_picks(4))
    put_pack(2 * TOK, 48, rest_picks())


    def send_line(source, target, count, at, device, send_sem, recv_sem):
        def one_peer(step, carry):
            to = lax.rem(at + step, count)
            pltpu.make_async_remote_copy(
                src_ref=source(to),
                dst_ref=target,
                send_sem=send_sem,
                recv_sem=recv_sem,
                device_id=device(to),
                device_id_type=MESH,
            ).start()
            return carry

        lax.fori_loop(1, count, one_peer, 0)
        pltpu.make_async_copy(source(at), target, recv_sem).start()

    def along_seq(source, target, send_sem, recv_sem):
        send_line(
            source, target.at[seq_at], heads, seq_at, lambda to: (to, clu_at), send_sem, recv_sem
        )

    def along_clu(source, target, send_sem, recv_sem):
        send_line(
            source, target.at[clu_at], groups, clu_at, lambda to: (seq_at, to), send_sem, recv_sem
        )


    def head_rows(at):
        cols = pl.ds(pl.multiple_of(at * 2 * DH, 2 * DH), 2 * DH)
        return [inputs[array, :, cols] for array in range(4)]

    def put_tile(target, at, tile, packed):
        low = packed.astype(jnp.bfloat16)
        for k in range(2):
            target[pl.ds((2 * at + k) * groups, groups), tile] = low[
                :, k * DH : (k + 1) * DH
            ].reshape(groups, 16, DH)

    def pack_a(at, carry):
        rows = jnp.concatenate(head_rows(at), axis=0)
        packed = bf16_dot(pack_mat[pl.ds(0, 2 * TOK + 48), :], rows)
        put_tile(send_a, at, 0, packed[:TOK])
        put_tile(send_a, at, 1, packed[TOK : 2 * TOK])
        rest = packed[2 * TOK :].astype(jnp.bfloat16)
        for k in range(2):
            hsend[2 * at + k] = rest[:16, k * DH : (k + 1) * DH]
            ex_send[2 * at + k] = rest[16:, k * DH : (k + 1) * DH]
        return carry

    wait_bytes(inputs, input_sem)
    lax.fori_loop(0, heads // 2, pack_a, 0, unroll=2)
    pl.semaphore_wait(barrier, devices - 1)
    along_clu(lambda to: cnt_send, cnt_group, cnt_send_sem, cnt_sem)

    def send_heavy(step, carry):
        head = lax.rem(seq_at + step, heads)
        clu_to = lax.rem(head, groups)

        @pl.when(head * groups + clu_to != me)
        def _():
            pltpu.make_async_remote_copy(
                src_ref=hsend.at[head],
                dst_ref=hrecv.at[me],
                send_sem=hsend_sem,
                recv_sem=hrecv_sem,
                device_id=(head, clu_to),
                device_id_type=MESH,
            ).start()

        @pl.when(head * groups + clu_to == me)
        def _():
            pltpu.make_async_copy(hsend.at[head], hrecv.at[me], hrecv_sem).start()

        return carry

    lax.fori_loop(0, heads, send_heavy, 0)
    along_seq(lambda to: ex_send.at[to], ex_recv, ex_send_sem, ex_recv_sem)
    out_a = (send_a, recv_a.at[me], send_a_sem, recv_a_sem)
    send_steps(0, 4, *out_a)
    wait_bytes(cnt_group, cnt_sem)
    along_seq(lambda to: cnt_group, cnt_recv, cnt2_send_sem, cnt2_sem)
    send_steps(4, devices // 8 - 4, *out_a)
    send_own(send_a, recv_a.at[me], recv_a_sem)

    for tile in range(1, 4):
        put_pack((tile + 1) * TOK + 48, TOK, tile_picks(tile))

    def pack_bc(at, carry):
        rows = jnp.concatenate(head_rows(at), axis=0)
        packed = bf16_dot(pack_mat[pl.ds(2 * TOK + 48, 3 * TOK), :], rows)
        put_tile(send_b, at, 0, packed[:TOK])
        put_tile(send_b, at, 1, packed[TOK : 2 * TOK])
        put_tile(send_c, at, 0, packed[2 * TOK :])
        return carry

    lax.fori_loop(0, heads // 2, pack_bc, 0)

    wait_bytes(cnt_recv, cnt2_sem)
    seen = cnt_recv[...].reshape(TOK, TOK)
    heavies = jnp.min(jnp.where(seen == 4.0, lane_f, 999.0), axis=1, keepdims=True)
    heavy_all = jnp.min(heavies, axis=0, keepdims=True)
    light = lane_f != heavy_all
    more = jnp.where(light, jnp.maximum(seen - 1.0, 0.0), 0.0)
    more_low = more.astype(jnp.bfloat16)
    in_group = jnp.where(sub // 16 == lane, one, zero).astype(jnp.bfloat16)
    ahead = jnp.where(sub < lane, one, zero).astype(jnp.bfloat16)
    prior = jnp.where(lane < sub, one, zero).astype(jnp.bfloat16)
    mates = (lane < sub) & (lane % 8 == sub % 8)
    mates = jnp.where(mates, one, zero).astype(jnp.bfloat16)
    excess = jnp.maximum(bf16_dot(more_low, in_group) - 4.0, 0.0)
    excess_low = excess.astype(jnp.bfloat16)
    excess_off = bf16_dot(excess_low, ahead)
    excess_pre = bf16_dot(mates, excess_low)
    bad = (jnp.sum(excess, axis=1, keepdims=True) > 8.0) | (excess_pre + excess > 16.0)
    bad = bad | (heavies != heavy_all) | (jnp.sum(more, axis=0, keepdims=True) > OVC)
    flag_ref[0, 0] = jnp.max(jnp.where(bad, one, zero)).astype(jnp.int32)

    spot = zero
    for group in range(8):
        off, count, pre = [a[:, group : group + 1] for a in (excess_off, excess, excess_pre)]
        held = (lane_f >= off) & (lane_f < off + count)
        spot = spot + jnp.where(held, lane_f + (group * 16 + 1.0) - off + pre, zero)
    spot = jnp.where(sub % 8 == clu_at, spot, zero).reshape(16, 8, TOK)
    spot = jnp.sum(spot, axis=1).astype(jnp.bfloat16)
    spread8 = jnp.where(lane % 8 == sub, one, zero).astype(jnp.bfloat16)
    spot = jnp.where(lane[:16] // 8 == sub[:16], bf16_dot(spot, spread8), 0.0)
    spot = jnp.sum(spot, axis=0, keepdims=True) - 1.0
    to_mate[...] = jnp.where(sub_f == spot, one, zero).astype(jnp.bfloat16)
    spot = jnp.broadcast_to(spot, (TOK, TOK)).T
    to_block[...] = jnp.where(spot == lane_f, one, zero).astype(jnp.bfloat16)

    wait_bytes(ex_recv, ex_recv_sem)
    held = ex_recv[...].astype(jnp.float32)
    held = [held[:, 8 * a : 8 * a + 8, :].reshape(TOK, DH) for a in range(4)]
    held = jnp.concatenate(held, axis=1).astype(jnp.bfloat16)
    held = bf16_dot(to_mate[...], held).astype(jnp.bfloat16)
    for a in range(4):
        ex_send2[:, a] = held[:, a * DH : (a + 1) * DH].reshape(8, 16, DH)
    along_clu(lambda to: ex_send2.at[to], ex_recv2, ex_send2_sem, ex_recv2_sem)
    send_to_all(send_b, recv_b.at[me], send_b_sem, recv_b_sem)
    send_to_all(send_c, recv_c.at[me], send_c_sem, recv_c_sem)

    valid = jnp.where((seen > 0.0) & light, one, zero).astype(jnp.bfloat16)
    mine = (sub == clu_at * 16 + lane) & (lane < 16)
    mine = jnp.where(mine, one, zero).astype(jnp.bfloat16)
    more_g = bf16_dot(more_low, mine)
    valid_g = bf16_dot(valid, mine)
    more_g_low = more_g.astype(jnp.bfloat16)
    start_g = bf16_dot(prior, more_g_low)
    offset_g = bf16_dot(more_g_low, ahead)
    beyond_g = jnp.maximum(bf16_dot(more_g_low, one.astype(jnp.bfloat16)) - 4.0, 0.0)
    pre_g = bf16_dot(mates, beyond_g.astype(jnp.bfloat16))
    ex_index = lane_f - pre_g + 4.0
    first_row = lax.broadcasted_iota(jnp.int32, (1, TOK), 1).astype(jnp.float32) * 16.0
    in_tile_at = zero
    beyond_at = zero
    for c in range(16):
        count, begin, off, real = [
            a[:, c : c + 1] for a in (more_g, start_g, offset_g, valid_g)
        ]
        place = begin - off + (c * OVC + 1.0)
        held = (lane_f >= off) & (lane_f < off + count) & (lane < 4)
        in_tile_at = in_tile_at + jnp.where(held, lane_f + place, zero)
        held = (ex_index >= off) & (ex_index < off + count) & (ex_index >= 4.0)
        beyond_at = beyond_at + jnp.where(held, ex_index + place, zero)
        held = (lane_f >= begin) & (lane_f < begin + count)
        where = jnp.where(held, sub_f * 16.0 + 1.0 + lane_f - begin, zero)
        where = jnp.sum(where, axis=0, keepdims=True)
        where = jnp.where(where > 0.0, where, FAR)
        query_row = jnp.concatenate([first_row, where], axis=1)
        query_pos[c] = jnp.broadcast_to(query_row, (8, 2 * TOK))
        key_pos[c, pl.ds(0, TOK), :] = jnp.where(real > 0.0, sub_f * 16.0, FAR)
        key_pos[c, pl.ds(TOK, OVC), :] = jnp.broadcast_to(where, (TOK, TOK)).T[:OVC]
    beyond_at = jnp.sum(beyond_at.reshape(16, 8, TOK), axis=0)
    high = jnp.floor(beyond_at * (1.0 / 32.0))
    split = jnp.concatenate([high, beyond_at - high * 32.0], axis=0).astype(jnp.bfloat16)
    spread16 = jnp.where(lane % 16 == sub, one, zero).astype(jnp.bfloat16)
    split = bf16_dot(split, spread16)
    split = jnp.where(lane[:8] // 16 == sub[:8], split[:8] * 32.0 + split[8:], 0.0)
    beyond_row = jnp.sum(split, axis=0, keepdims=True) - 1.0
    tile_rows = in_tile_at.T[0:8, :] - 1.0
    slot_rows = [tile_rows[k : k + 1, :] for k in range(4)] + [beyond_row]
    slot_cols = [in_tile_at[:, k : k + 1] - 1.0 for k in range(4)]
    slot_cols.append(jnp.broadcast_to(beyond_row, (TOK, TOK)).T)

    chunk = 4
    for k in range(5):
        for m in range(16 * OVC // TOK):
            onehot[pl.ds(k * TOK, TOK), pl.ds(m * TOK, TOK)] = jnp.where(
                slot_cols[k] == lane_f + float(m * TOK), one, zero
            ).astype(jnp.bfloat16)
            pick[pl.ds(m * TOK, TOK), pl.ds(k * TOK, TOK)] = jnp.where(
                slot_rows[k] == sub_f + float(m * TOK), one, zero
            ).astype(jnp.bfloat16)

    for at, tile in enumerate((0, 1, 2, None, 3, 4)):
        for array, matrix in enumerate(rest_picks() if tile is None else tile_picks(tile)):
            unpack_mat[pl.ds(array * TOK, TOK), pl.ds(at * TOK, TOK)] = matrix.T.astype(
                jnp.bfloat16
            )

    perm = flip_perm()

    def arrange(source, target, units):
        def two_sets(at, carry):
            blocks = [pl.ds(pl.multiple_of((2 * at + i) * SET, SET), SET) for i in range(2)]
            spots = [(held, unit) for held in blocks for unit in range(units)]
            rows = jnp.concatenate(
                [source(held, unit).reshape(SET * 16, DH) for held, unit in spots], axis=1
            )
            turned = bf16_dot(perm, rows).astype(jnp.bfloat16)
            for i, (held, unit) in enumerate(spots):
                target(held, unit, turned[:, i * DH : (i + 1) * DH].reshape(16, SET, DH))
            return carry

        lax.fori_loop(0, devices // (2 * SET), two_sets, 0, unroll=2)

    def put_table(first):
        def put(blocks, unit, value):
            table[first + unit, :, blocks, :] = value

        return put

    @pl.when(is_heavy_owner)
    def _():
        wait_bytes(hrecv, hrecv_sem)

        def put_heavy(blocks, unit, value):
            htable[:, blocks, :] = value

        arrange(lambda blocks, unit: hrecv[blocks], put_heavy, 1)
        k_h, v_h = [htable[4 * a : 4 * a + 4].reshape(4 * TOK, DH) for a in (1, 2)]
        hacc[...] = jnp.zeros_like(hacc)
        key_sub = lax.broadcasted_iota(jnp.int32, (4 * TOK, TOK), 0)
        key_at = lax.rem(key_sub, TOK) * 4 + lax.div(key_sub, TOK)
        query_at = lax.broadcasted_iota(jnp.int32, (4 * TOK, TOK), 1) * 4

        def heavy_tile(s, carry):
            out, dq, dk, dv = attend(
                htable[s], k_h, v_h, htable[12 + s], key_at <= query_at + s, inv_root
            )
            hacc[2, pl.ds(pl.multiple_of(s * TOK, TOK), TOK)] = out.astype(jnp.float32)
            hacc[3, pl.ds(pl.multiple_of(s * TOK, TOK), TOK)] = dq.astype(jnp.float32)
            hacc[0] += dk
            hacc[1] += dv
            return carry

        lax.fori_loop(0, 4, heavy_tile, 0)
        for array, at in enumerate((2, 3, 0, 1)):
            htable[4 * array : 4 * array + 4] = (
                hacc[at].astype(jnp.bfloat16).reshape(4, TOK, DH)
            )

        def put_hresult(blocks, unit, value):
            hresult[blocks] = value

        arrange(lambda blocks, unit: htable[:, blocks, :], put_hresult, 1)
        send_to_all(hresult, hback.at[seq_at], hres_sem, hback_sem)

    wait_bytes(recv_a, recv_a_sem)
    def put_tile_a(blocks, unit, value):
        table[4 * unit, :, blocks, :] = value

    arrange(lambda blocks, unit: recv_a[blocks, unit], put_tile_a, 2)

    wait_bytes(ex_recv2, ex_recv2_sem)
    for a in range(4):
        cols = pl.ds(a * DH, DH)
        loose[pl.ds(0, 4 * TOK), cols] = table[4, 4 * a : 4 * a + 4].reshape(4 * TOK, DH)
        loose[pl.ds(4 * TOK, TOK), cols] = ex_recv2[:, a].reshape(TOK, DH)

    def gather_chunk(at, carry):
        chosen = pick[pl.ds(pl.multiple_of(at * chunk * OVC, 64), chunk * OVC), :]
        found = bf16_dot(chosen, loose[...]).astype(jnp.bfloat16)
        for c in range(chunk):
            for array in range(4):
                over[array, at * chunk + c] = found[
                    c * OVC : (c + 1) * OVC, array * DH : (array + 1) * DH
                ]
        return carry

    gather_chunk(0, 0)

    pad_rows = jnp.zeros((TOK - OVC, DH), jnp.bfloat16)

    def load_cluster(tile, j):
        c = tile * 4 + j
        rows = [
            jnp.concatenate([table[tile, a * 4 + j], over[a, c]], axis=0) for a in range(4)
        ]
        for a in (0, 3):
            rows[a] = jnp.concatenate([rows[a], pad_rows], axis=0)
        key_at = key_pos[c]
        allowed = jnp.concatenate([key_at, key_at], axis=1) <= query_pos[c, 0:1, :]
        return rows + [allowed]

    def attend_tiles(first, tiles, beside):
        def one_tile(at, carry):
            beside(at)
            tile = first + at
            spots = range(4)
            loaded = [load_cluster(tile, j) for j in spots]
            found = [attend(*arrays, inv_root) for arrays in loaded]
            for j, results in zip(spots, found):
                c = tile * 4 + j
                for a, value in enumerate(results):
                    value = value.astype(jnp.bfloat16)
                    table[tile, a * 4 + j] = value[:TOK]
                    over_res[
                        pl.ds(pl.multiple_of(c * OVC, 16), OVC), pl.ds(a * DH, DH)
                    ] = value[TOK : TOK + OVC]
            return carry

        lax.fori_loop(0, tiles, one_tile, 0)

    def put_in(result):
        def put(blocks, unit, value):
            result[blocks, unit] = value

        return put

    def from_table(first):
        return lambda blocks, unit: table[first + unit, :, blocks, :]

    to_a = (result_a, back_a.at[me], res_a_sem, back_a_sem)
    to_b = (result_b, back_b.at[me], res_b_sem, back_b_sem)
    to_c = (result_c, back_c.at[me], res_c_sem, back_c_sem)
    attend_tiles(0, 1, lambda at: None)
    arrange(from_table(0), put_in(result_a), 1)
    send_own(result_a, back_a.at[me], back_a_sem)
    lax.fori_loop(1, 16 // chunk, gather_chunk, 0)

    wait_bytes(recv_b, recv_b_sem)
    arrange(lambda blocks, unit: recv_b[blocks, unit], put_table(1), 2)
    attend_tiles(1, 2, lambda at: send_steps(at * 8, 8, *to_a))
    arrange(from_table(1), put_in(result_b), 2)
    send_own(result_b, back_b.at[me], back_b_sem)

    wait_bytes(recv_c, recv_c_sem)
    arrange(lambda blocks, unit: recv_c[blocks, 0], put_table(3), 1)
    attend_tiles(3, 1, lambda at: send_steps(0, 16, *to_b))

    found = bf16_dot(onehot[pl.ds(4 * TOK, TOK), :], over_res[...]).astype(jnp.bfloat16)
    for a in range(4):
        ex_ret2[:, a] = found[:, a * DH : (a + 1) * DH].reshape(8, 16, DH)
    along_clu(lambda to: ex_ret2.at[to], ex_back2, ex_ret2_sem, ex_back2_sem)
    found = bf16_dot(onehot[pl.ds(0, 4 * TOK), :], over_res[...]).astype(jnp.bfloat16)
    for a in range(4):
        table[4, 4 * a : 4 * a + 4] = found[:, a * DH : (a + 1) * DH].reshape(4, TOK, DH)
    arrange(from_table(3), put_in(result_c), 2)
    send_steps(0, devices // 16, *to_c)
    send_own(result_c, back_c.at[me], back_c_sem)

    wait_bytes(ex_back2, ex_back2_sem)
    held = [ex_back2[:, a].reshape(TOK, DH) for a in range(4)]
    held = bf16_dot(to_block[...], jnp.concatenate(held, axis=1))
    held = [held[:, a * DH : (a + 1) * DH].reshape(16, 8, DH) for a in range(4)]
    ex_ret1[...] = jnp.concatenate(held, axis=1).astype(jnp.bfloat16)
    along_seq(lambda to: ex_ret1.at[to], ex_back1, ex_ret1_sem, ex_back1_sem)
    send_steps(devices // 16, devices // 16, *to_c)

    def unpack(tiles, rest, first, count):
        sides = []
        for k in range(2):
            sides.append(
                jnp.concatenate(
                    [tile(k).reshape(TOK, DH) for tile in tiles] + [part(k) for part in rest],
                    axis=0,
                )
            )
        return bf16_dot(
            unpack_mat[:, pl.ds(first, count)], jnp.concatenate(sides, axis=1)
        )

    def tile_of(ref, at, tile):
        return lambda k: ref[pl.ds((2 * at + k) * groups, groups), tile]

    def unpack_early(at, carry):
        tiles = [tile_of(back_a, at, 0), tile_of(back_b, at, 0), tile_of(back_b, at, 1)]
        rest = [
            lambda k: hback[2 * at + k],
            lambda k: ex_back1[2 * at + k],
            lambda k: jnp.zeros((TOK - 48, DH), jnp.bfloat16),
        ]
        early[at] = unpack(tiles, rest, 0, 4 * TOK)
        return carry

    def unpack_last(at, carry):
        cols = pl.ds(pl.multiple_of(at * 2 * DH, 2 * DH), 2 * DH)
        tiles = [tile_of(back_c, at, 0), tile_of(back_c, at, 1)]
        found = (early[at] + unpack(tiles, [], 4 * TOK, 2 * TOK)).astype(jnp.bfloat16)
        for array, ref in enumerate((out_ref, dq_ref, dk_ref, dv_ref)):
            ref[:, cols] = found[array * TOK : (array + 1) * TOK]
        return carry

    wait_bytes(hback, hback_sem)
    wait_bytes(back_a, back_a_sem)
    wait_bytes(back_b, back_b_sem)
    wait_bytes(ex_back1, ex_back1_sem)
    lax.fori_loop(0, heads // 2, unpack_early, 0, unroll=2)
    wait_bytes(back_c, back_c_sem)
    lax.fori_loop(0, heads // 2, unpack_last, 0, unroll=2)

    others = pl.ds(0, devices - 1)
    wait_bytes(cnt_group.at[pl.ds(0, groups - 1)], cnt_send_sem)
    wait_bytes(cnt_recv.at[pl.ds(0, heads - 1)], cnt2_send_sem)
    for ref, sem in ((ex_send, ex_send_sem), (ex_ret1, ex_ret1_sem)):
        wait_bytes(ref.at[pl.ds(0, heads - 1)], sem)
    for ref, sem in ((ex_send2, ex_send2_sem), (ex_ret2, ex_ret2_sem)):
        wait_bytes(ref.at[pl.ds(0, groups - 1)], sem)
    wait_bytes(send_a.at[others], send_a_sem)
    wait_bytes(send_b.at[others], send_b_sem)
    wait_bytes(send_c.at[others], send_c_sem)
    wait_bytes(result_a.at[others], res_a_sem)
    wait_bytes(result_b.at[others], res_b_sem)
    wait_bytes(result_c.at[others], res_c_sem)

    @pl.when(is_heavy_owner)
    def _():
        wait_bytes(hsend.at[pl.ds(0, heads - 1)], hsend_sem)
        wait_bytes(hresult.at[others], hres_sem)

    @pl.when(jnp.logical_not(is_heavy_owner))
    def _():
        wait_bytes(hsend, hsend_sem)


def fast_path(queries, key_rows, value_rows, out_grad, cluster_ids):
    tok_rows, columns = queries.shape
    heads = columns // DH
    groups = lax.axis_size("clu")
    devices = lax.axis_size("seq") * groups
    low = jnp.bfloat16
    wide = jnp.float32
    rows = pltpu.VMEM((tok_rows, columns), low)
    vmem = pl.BlockSpec(memory_space=pltpu.VMEM)
    smem = pl.BlockSpec(memory_space=pltpu.SMEM)
    return pl.pallas_call(
        fast_kernel,
        out_shape=[rows] * 4 + [jax.ShapeDtypeStruct((1, 1), jnp.int32)],
        in_specs=[vmem] + [pl.BlockSpec(memory_space=pl.ANY)] * 4,
        out_specs=[vmem] * 4 + [smem],
        scratch_shapes=[
            pltpu.VMEM((1, TOK), wide),
            pltpu.VMEM((groups, 1, TOK), wide),
            pltpu.VMEM((heads, groups, 1, TOK), wide),
            pltpu.VMEM((5 * TOK + 48, 4 * TOK), low),
            pltpu.VMEM((4 * TOK, 6 * TOK), low),
            pltpu.VMEM((devices, 2, 16, DH), low),
            pltpu.VMEM((devices, 2, 16, DH), low),
            pltpu.VMEM((devices, 1, 16, DH), low),
            pltpu.VMEM((devices, 2, 16, DH), low),
            pltpu.VMEM((devices, 2, 16, DH), low),
            pltpu.VMEM((devices, 1, 16, DH), low),
            pltpu.VMEM((5, 16, devices, DH), low),
            pltpu.VMEM((4, 16, OVC, DH), low),
            pltpu.VMEM((16, TOK + OVC, TOK), wide),
            pltpu.VMEM((16, 8, 2 * TOK), wide),
            pltpu.VMEM((16 * OVC, 5 * TOK), low),
            pltpu.VMEM((5 * TOK, 16 * OVC), low),
            pltpu.VMEM((5 * TOK, 4 * DH), low),
            pltpu.VMEM((16 * OVC, 4 * DH), low),
            pltpu.VMEM((TOK, TOK), low),
            pltpu.VMEM((TOK, TOK), low),
            pltpu.VMEM((devices, 1, 16, DH), low),
            pltpu.VMEM((devices, 2, 16, DH), low),
            pltpu.VMEM((devices, 2, 16, DH), low),
            pltpu.VMEM((devices, 1, 16, DH), low),
            pltpu.VMEM((devices, 2, 16, DH), low),
            pltpu.VMEM((devices, 2, 16, DH), low),
            pltpu.VMEM((heads, 32, DH), low),
            pltpu.VMEM((heads, 32, DH), low),
            pltpu.VMEM((groups, 4, 16, DH), low),
            pltpu.VMEM((groups, 4, 16, DH), low),
            pltpu.VMEM((groups, 4, 16, DH), low),
            pltpu.VMEM((groups, 4, 16, DH), low),
            pltpu.VMEM((heads, 32, DH), low),
            pltpu.VMEM((heads, 32, DH), low),
            pltpu.VMEM((heads, 16, DH), low),
            pltpu.VMEM((devices, 16, DH), low),
            pltpu.VMEM((16, devices, DH), low),
            pltpu.VMEM((4, 4 * TOK, DH), wide),
            pltpu.VMEM((devices, 16, DH), low),
            pltpu.VMEM((heads, 16, DH), low),
            pltpu.VMEM((4, tok_rows, columns), low),
            pltpu.VMEM((heads // 2, 4 * tok_rows, 2 * DH), wide),
        ]
        + [pltpu.SemaphoreType.DMA] * 29,
        compiler_params=pltpu.CompilerParams(
            collective_id=0, has_side_effects=True, vmem_limit_bytes=44 * 1024 * 1024
        ),
    )(cluster_ids.reshape(1, tok_rows), queries, key_rows, value_rows, out_grad)


def copy_kernel(*refs):
    sem = refs[-1]
    copies = [
        pltpu.make_async_copy(refs[i], refs[4 + i], sem.at[i]) for i in range(4)
    ]
    for copy in copies:
        copy.start()
    for copy in copies:
        copy.wait()


def copy_out(arrays):
    anywhere = pl.BlockSpec(memory_space=pl.ANY)
    return pl.pallas_call(
        copy_kernel,
        out_shape=[pltpu.HBM(a.shape, a.dtype) for a in arrays],
        in_specs=[anywhere] * 4,
        out_specs=[anywhere] * 4,
        scratch_shapes=[pltpu.SemaphoreType.DMA((4,))],
    )(*arrays)


def per_device(queries, key_rows, value_rows, out_grad, cluster_ids):
    arrays = (queries, key_rows, value_rows, out_grad, cluster_ids)
    *fast, flag = fast_path(*arrays)
    return lax.cond(
        flag.reshape(()) != 0,
        lambda arrays, fast: full_capacity(*arrays),
        lambda arrays, fast: tuple(copy_out(fast)),
        arrays,
        tuple(fast),
    )


def solution(mesh):
    in_specs = (
        P(("seq", "clu"), None),
        P(("seq", "clu"), None),
        P(("seq", "clu"), None),
        P(("seq", "clu"), None),
        P(("seq", "clu")),
    )
    out_specs = (
        P(("seq", "clu"), None),
        P(("seq", "clu"), None),
        P(("seq", "clu"), None),
        P(("seq", "clu"), None),
    )
    return jax.shard_map(
        per_device, mesh=mesh, in_specs=in_specs, out_specs=out_specs, check_vma=False
    )
```

```python
import math

import jax
import jax.numpy as jnp
from jax import lax
from jax.experimental import pallas as pl
from jax.experimental.pallas import tpu as pltpu
from jax.sharding import PartitionSpec as P

DH = 128
TOK = 128
OVC = 80
SET = 16
FAR = 1e9
MESH = pl.DeviceIdType.MESH


masked = -1e30


def contract_last(left, right):
    return lax.dot_general(
        left, right, (((1,), (1,)), ((), ())), preferred_element_type=jnp.float32
    )


def contract_first(left, right):
    return lax.dot_general(
        left, right, (((0,), (0,)), ((), ())), preferred_element_type=jnp.float32
    )


def softmax_rows(query_head, key_head, allowed, inv_root):
    scores = contract_last(query_head, key_head) * inv_root
    scores = jnp.where(allowed, scores, masked)
    row_max = jnp.max(scores, axis=1, keepdims=True)
    weights = jnp.exp(scores - row_max)
    row_sum = jnp.sum(weights, axis=1, keepdims=True)
    return (weights / row_sum).astype(jnp.bfloat16)


def head_slice(array, head_index):
    return lax.dynamic_slice_in_dim(array, head_index * DH, DH, 1)


def full_capacity(queries, key_rows, value_rows, out_grad, cluster_ids):
    seq_count = lax.axis_size("seq")
    clu_count = lax.axis_size("clu")
    devices = seq_count * clu_count
    tok_rows = queries.shape[0]
    columns = queries.shape[1]
    head_count = columns // DH
    most_rows = 4 * tok_rows // devices
    capacity = most_rows * devices
    inv_root = 1.0 / math.sqrt(DH)
    owners = jnp.arange(devices, dtype=jnp.int32)
    member = (cluster_ids[:, None] == owners[None, :]).astype(jnp.int32)
    running = jnp.cumsum(member, axis=0) - 1
    slot_rank = jnp.sum(member * running, axis=1)
    sent_counts = jnp.sum(member, axis=0).reshape(devices, 1)
    slot_index = cluster_ids * most_rows + slot_rank
    stacked = jnp.concatenate([queries, key_rows, value_rows], axis=1)
    width_in = stacked.shape[1]
    packed = jnp.zeros((devices * most_rows, width_in), jnp.bfloat16).at[slot_index].set(stacked)
    packed = packed.reshape(devices, most_rows, width_in)
    got_rows, got_counts = (
        lax.all_to_all(packed, ("seq", "clu"), split_axis=0, concat_axis=0, tiled=True),
        lax.all_to_all(sent_counts, ("seq", "clu"), split_axis=0, concat_axis=0, tiled=True),
    )
    got_counts = got_counts.reshape(devices)
    starts = jnp.cumsum(got_counts) - got_counts
    live_total = jnp.sum(got_counts)
    within = jnp.arange(most_rows, dtype=jnp.int32)
    target = jnp.where(
        within[None, :] < got_counts[:, None], starts[:, None] + within[None, :], capacity
    )
    target = target.reshape(devices * most_rows)
    gathered = (
        jnp.zeros((capacity, width_in), jnp.bfloat16)
        .at[target]
        .set(got_rows.reshape(devices * most_rows, width_in), mode="drop")
    )
    query_block = gathered[:, :columns]
    key_block = gathered[:, columns : 2 * columns]
    value_block = gathered[:, 2 * columns : 3 * columns]
    positions = jnp.arange(capacity, dtype=jnp.int32)
    allowed = (positions[None, :] <= positions[:, None]) & (positions[None, :] < live_total)

    def forward_head(head_index, mixed_rows):
        weights_low = softmax_rows(
            head_slice(query_block, head_index),
            head_slice(key_block, head_index),
            allowed,
            inv_root,
        )
        out_head = jnp.dot(
            weights_low, head_slice(value_block, head_index), preferred_element_type=jnp.float32
        ).astype(jnp.bfloat16)
        return lax.dynamic_update_slice_in_dim(mixed_rows, out_head, head_index * DH, 1)

    mixed_rows = lax.fori_loop(
        0, head_count, forward_head, jnp.zeros((capacity, columns), jnp.bfloat16)
    )
    back_index = jnp.minimum(target, capacity - 1)
    outgoing = jnp.take(mixed_rows, back_index, axis=0).reshape(devices, most_rows, columns)
    grad_packed = (
        jnp.zeros((devices * most_rows, columns), jnp.bfloat16).at[slot_index].set(out_grad)
    )
    grad_packed = grad_packed.reshape(devices, most_rows, columns)
    returned = lax.all_to_all(outgoing, ("seq", "clu"), split_axis=0, concat_axis=0, tiled=True)
    got_grad = lax.all_to_all(grad_packed, ("seq", "clu"), split_axis=0, concat_axis=0, tiled=True)
    attention_out = jnp.take(returned.reshape(devices * most_rows, columns), slot_index, axis=0)
    grad_block = (
        jnp.zeros((capacity, columns), jnp.bfloat16)
        .at[target]
        .set(got_grad.reshape(devices * most_rows, columns), mode="drop")
    )
    delta_rows = jnp.sum(
        (grad_block.astype(jnp.float32) * mixed_rows.astype(jnp.float32)).reshape(
            capacity, head_count, DH
        ),
        axis=2,
    )

    def backward_head(head_index, grad_rows):
        query_head = head_slice(query_block, head_index)
        key_head = head_slice(key_block, head_index)
        value_head = head_slice(value_block, head_index)
        grad_head = head_slice(grad_block, head_index)
        weights_low = softmax_rows(query_head, key_head, allowed, inv_root)
        prob_grad = contract_last(grad_head, value_head)
        delta_head = lax.dynamic_slice_in_dim(delta_rows, head_index, 1, 1)
        score_grad = (weights_low.astype(jnp.float32) * (prob_grad - delta_head)).astype(
            jnp.bfloat16
        )
        query_part = (
            jnp.dot(score_grad, key_head, preferred_element_type=jnp.float32) * inv_root
        ).astype(jnp.bfloat16)
        key_part = (contract_first(score_grad, query_head) * inv_root).astype(jnp.bfloat16)
        value_part = contract_first(weights_low, grad_head).astype(jnp.bfloat16)
        grad_rows = lax.dynamic_update_slice_in_dim(grad_rows, query_part, head_index * DH, 1)
        grad_rows = lax.dynamic_update_slice_in_dim(
            grad_rows, key_part, columns + head_index * DH, 1
        )
        return lax.dynamic_update_slice_in_dim(
            grad_rows, value_part, 2 * columns + head_index * DH, 1
        )

    grad_rows = lax.fori_loop(
        0, head_count, backward_head, jnp.zeros((capacity, 3 * columns), jnp.bfloat16)
    )
    outgoing_grads = jnp.take(grad_rows, back_index, axis=0).reshape(
        devices, most_rows, 3 * columns
    )
    returned_grads = lax.all_to_all(
        outgoing_grads, ("seq", "clu"), split_axis=0, concat_axis=0, tiled=True
    )
    picked = jnp.take(returned_grads.reshape(devices * most_rows, 3 * columns), slot_index, axis=0)
    return (
        attention_out,
        picked[:, :columns],
        picked[:, columns : 2 * columns],
        picked[:, 2 * columns :],
    )


def bf16_dot(left, right):
    return jnp.dot(left, right, preferred_element_type=jnp.float32)


def flip_perm():
    row = lax.broadcasted_iota(jnp.int32, (SET * 16, SET * 16), 0)
    col = lax.broadcasted_iota(jnp.int32, (SET * 16, SET * 16), 1)
    swapped = (col % 16) * 16 + col // 16
    return (row == swapped).astype(jnp.float32).astype(jnp.bfloat16)


def attend(q, k, v, g, allowed, inv_root):
    raw = jnp.where(allowed, contract_last(k, q), masked)
    most = jnp.max(raw, axis=0, keepdims=True)
    weights = jnp.exp2((raw - most) * (inv_root * math.log2(math.e)))
    prob = weights * (1.0 / jnp.sum(weights, axis=0, keepdims=True))
    prob_low = prob.astype(jnp.bfloat16)
    prob_grad = contract_last(v, g)
    delta = jnp.sum(prob * prob_grad, axis=0, keepdims=True)
    score_grad = (prob * (prob_grad - delta)).astype(jnp.bfloat16)
    out = contract_first(v, prob_low).T.astype(jnp.bfloat16)
    dq = (contract_first(k, score_grad).T * inv_root).astype(jnp.bfloat16)
    dk = bf16_dot(score_grad, q) * inv_root
    dv = bf16_dot(prob_low, g)
    return out, dq, dk, dv


def fast_kernel(
    ids_ref, q_ref, k_ref, v_ref, g_ref,
    out_ref, dq_ref, dk_ref, dv_ref, flag_ref,
    cnt_send, cnt_group, cnt_recv, pack_mat, unpack_mat,
    send_a, send_b, send_c, recv_a, recv_b, recv_c, table,
    over, key_pos, query_pos, pick, onehot, loose, over_res, to_mate, to_block,
    result_a, result_b, result_c, back_a, back_b, back_c,
    ex_send, ex_recv, ex_send2, ex_recv2, ex_ret2, ex_back2, ex_ret1, ex_back1,
    hsend, hrecv, htable, hacc, hresult, hback, inputs, early,
    cnt_send_sem, cnt_sem, cnt2_send_sem, cnt2_sem,
    send_a_sem, recv_a_sem, send_b_sem, recv_b_sem, send_c_sem, recv_c_sem,
    res_a_sem, back_a_sem, res_b_sem, back_b_sem, res_c_sem, back_c_sem,
    ex_send_sem, ex_recv_sem, ex_send2_sem, ex_recv2_sem,
    ex_ret2_sem, ex_back2_sem, ex_ret1_sem, ex_back1_sem,
    hsend_sem, hrecv_sem, hres_sem, hback_sem, input_sem,
):
    seq_at = lax.axis_index("seq")
    clu_at = lax.axis_index("clu")
    groups = lax.axis_size("clu")
    heads = lax.axis_size("seq")
    devices = heads * groups
    me = seq_at * groups + clu_at
    inv_root = 1.0 / math.sqrt(DH)
    is_heavy_owner = lax.rem(seq_at, groups) == clu_at
    at_x, at_z = lax.div(seq_at, 4), lax.rem(seq_at, 4)
    at_y, at_core = lax.div(clu_at, 2), lax.rem(clu_at, 2)

    def by_core(first, second):
        return first + at_core * (second - first)

    eight = []
    for by_x, by_z, by_clu in zip(
        zip((3, 2, 3, 1, 3, 0, 2, 0), (2, 2, 1, 0, 2, 3, 0, 2)),
        zip((0, 0, 2, 3, 1, 2, 3, 1), (2, 2, 0, 1, 3, 0, 0, 2)),
        zip((2, 1, 3, 0, 6, 4, 5, 7), (6, 5, 7, 4, 2, 0, 1, 3)),
    ):
        y = lax.rem(at_y + by_core(by_clu[0] // 2, by_clu[1] // 2), 4)
        core = lax.rem(at_core + by_core(by_clu[0] % 2, by_clu[1] % 2), 2)
        eight.append((by_core(*by_x), by_core(*by_z), y * 2 + core))

    def for_peers(first, count, visit):
        def one_eight(step, carry):
            by = lax.rem(step * 13 + at_core * 12, 16)
            x = at_x + lax.div(by, 4)
            z = at_z + lax.rem(by, 4)
            for j, (more_x, more_z, clu_to) in enumerate(eight):
                seq_to = lax.rem(x + more_x, 4) * 4 + lax.rem(z + more_z, 4)
                if j in (3, 5):
                    pl.when(seq_to * groups + clu_to != me)(lambda: visit(seq_to, clu_to))
                else:
                    visit(seq_to, clu_to)
            return carry

        lax.fori_loop(first, first + count, one_eight, 0)

    def send_steps(first, count, source, target, send_sem, recv_sem):
        def start(seq_to, clu_to):
            pltpu.make_async_remote_copy(
                src_ref=source.at[seq_to * groups + clu_to],
                dst_ref=target,
                send_sem=send_sem,
                recv_sem=recv_sem,
                device_id=(seq_to, clu_to),
                device_id_type=MESH,
            ).start()

        for_peers(first, count, start)

    def send_own(source, target, recv_sem):
        pltpu.make_async_copy(source.at[me], target, recv_sem).start()

    def send_to_all(source, target, send_sem, recv_sem):
        send_steps(0, devices // 8, source, target, send_sem, recv_sem)
        send_own(source, target, recv_sem)

    def wait_bytes(ref, sem):
        pltpu.make_async_copy(ref, ref, sem).wait()

    for array, ref in enumerate((q_ref, k_ref, v_ref, g_ref)):
        pltpu.make_async_copy(ref, inputs.at[array], input_sem).start()
    barrier = pltpu.get_barrier_semaphore()

    def greet(seq_to, clu_to):
        pl.semaphore_signal(barrier, inc=1, device_id=(seq_to, clu_to), device_id_type=MESH)

    for_peers(0, devices // 8, greet)

    sub = lax.broadcasted_iota(jnp.int32, (TOK, TOK), 0)
    lane = lax.broadcasted_iota(jnp.int32, (TOK, TOK), 1)
    sub_f = sub.astype(jnp.float32)
    lane_f = lane.astype(jnp.float32)
    ids_l = jnp.broadcast_to(ids_ref[...].astype(jnp.float32), (TOK, TOK))
    ids_s = ids_l.T
    one = jnp.ones((TOK, TOK), jnp.float32)
    zero = jnp.zeros((TOK, TOK), jnp.float32)
    same = ids_l == ids_s
    rank_l = jnp.sum(jnp.where(same & (sub < lane), one, zero), axis=0, keepdims=True)
    rank_s = jnp.sum(jnp.where(same & (lane < sub), one, zero), axis=1, keepdims=True)
    count_l = jnp.sum(jnp.where(same, one, zero), axis=0, keepdims=True)
    cnt_send[...] = jnp.sum(jnp.where(ids_s == lane_f, one, zero), axis=0, keepdims=True)
    ids_row = ids_l[0:1, :]
    heavy = jnp.min(jnp.where(count_l == 4.0, ids_row, 999.0), axis=1, keepdims=True)
    group_l = jnp.floor(ids_l * (1.0 / 16.0))
    group_s = jnp.floor(ids_s * (1.0 / 16.0))
    earlier = (ids_s < ids_l) | (same & (sub < lane))
    later = (ids_l < ids_s) | (same & (lane < sub))
    before = (group_l == group_s) & (ids_s != heavy) & (rank_s >= 1.0) & earlier
    over_at = jnp.sum(jnp.where(before, one, zero), axis=0, keepdims=True)
    behind = (group_l == group_s) & (ids_l != heavy) & (rank_l >= 1.0) & later
    over_at_s = jnp.sum(jnp.where(behind, one, zero), axis=1, keepdims=True)
    excess_s = (ids_s != heavy) & (rank_s >= 1.0) & (over_at_s >= 4.0)
    excess_at = jnp.sum(jnp.where(excess_s & earlier, one, zero), axis=0, keepdims=True)
    light_l = ids_l != heavy
    slot_group = (sub // 16).astype(jnp.float32)
    in_tile = sub % 16
    over_l = light_l & (rank_l >= 1.0)

    def tile_picks(tile):
        at_slot = (in_tile % 4).astype(jnp.float32)
        if tile < 4:
            cluster = slot_group * 16.0 + at_slot + 4.0 * tile
            taken = (ids_l == cluster) & (rank_l == 0.0) & light_l
        else:
            taken = (group_l == slot_group) & over_l & (over_at == at_slot)
        return [jnp.where(taken & (in_tile // 4 == array), one, zero) for array in range(4)]

    def rest_picks():
        picks = []
        for array in range(4):
            chosen = (ids_l == heavy) & (rank_l == (sub % 4).astype(jnp.float32))
            chosen = chosen & (sub // 4 == array) & (sub < 16)
            beyond = over_l & (over_at >= 4.0) & (excess_at == (sub % 8).astype(jnp.float32))
            beyond = beyond & (sub // 8 == array + 2)
            picks.append(jnp.where(chosen | beyond, one, zero))
        return picks

    def put_pack(at_row, count, picks):
        for array, matrix in enumerate(picks):
            pack_mat[pl.ds(at_row, count), pl.ds(array * TOK, TOK)] = matrix[:count].astype(
                jnp.bfloat16
            )

    put_pack(0, TOK, tile_picks(0))
    put_pack(TOK, TOK, tile_picks(4))
    put_pack(2 * TOK, 48, rest_picks())


    def send_line(source, target, count, at, device, send_sem, recv_sem):
        def one_peer(step, carry):
            to = lax.rem(at + step, count)
            pltpu.make_async_remote_copy(
                src_ref=source(to),
                dst_ref=target,
                send_sem=send_sem,
                recv_sem=recv_sem,
                device_id=device(to),
                device_id_type=MESH,
            ).start()
            return carry

        lax.fori_loop(1, count, one_peer, 0)
        pltpu.make_async_copy(source(at), target, recv_sem).start()

    def along_seq(source, target, send_sem, recv_sem):
        send_line(
            source, target.at[seq_at], heads, seq_at, lambda to: (to, clu_at), send_sem, recv_sem
        )

    def along_clu(source, target, send_sem, recv_sem):
        send_line(
            source, target.at[clu_at], groups, clu_at, lambda to: (seq_at, to), send_sem, recv_sem
        )


    def head_rows(at):
        cols = pl.ds(pl.multiple_of(at * 2 * DH, 2 * DH), 2 * DH)
        return [inputs[array, :, cols] for array in range(4)]

    def put_tile(target, at, tile, packed):
        low = packed.astype(jnp.bfloat16)
        for k in range(2):
            target[pl.ds((2 * at + k) * groups, groups), tile] = low[
                :, k * DH : (k + 1) * DH
            ].reshape(groups, 16, DH)

    def pack_a(at, carry):
        rows = jnp.concatenate(head_rows(at), axis=0)
        packed = bf16_dot(pack_mat[pl.ds(0, 2 * TOK + 48), :], rows)
        put_tile(send_a, at, 0, packed[:TOK])
        put_tile(send_a, at, 1, packed[TOK : 2 * TOK])
        rest = packed[2 * TOK :].astype(jnp.bfloat16)
        for k in range(2):
            hsend[2 * at + k] = rest[:16, k * DH : (k + 1) * DH]
            ex_send[2 * at + k] = rest[16:, k * DH : (k + 1) * DH]
        return carry

    wait_bytes(inputs, input_sem)
    lax.fori_loop(0, heads // 2, pack_a, 0, unroll=4)
    pl.semaphore_wait(barrier, devices - 1)
    along_clu(lambda to: cnt_send, cnt_group, cnt_send_sem, cnt_sem)

    def send_heavy(step, carry):
        head = lax.rem(seq_at + step, heads)
        clu_to = lax.rem(head, groups)

        @pl.when(head * groups + clu_to != me)
        def _():
            pltpu.make_async_remote_copy(
                src_ref=hsend.at[head],
                dst_ref=hrecv.at[me],
                send_sem=hsend_sem,
                recv_sem=hrecv_sem,
                device_id=(head, clu_to),
                device_id_type=MESH,
            ).start()

        @pl.when(head * groups + clu_to == me)
        def _():
            pltpu.make_async_copy(hsend.at[head], hrecv.at[me], hrecv_sem).start()

        return carry

    lax.fori_loop(0, heads, send_heavy, 0)
    along_seq(lambda to: ex_send.at[to], ex_recv, ex_send_sem, ex_recv_sem)
    out_a = (send_a, recv_a.at[me], send_a_sem, recv_a_sem)
    send_steps(0, 4, *out_a)
    wait_bytes(cnt_group, cnt_sem)
    along_seq(lambda to: cnt_group, cnt_recv, cnt2_send_sem, cnt2_sem)
    send_steps(4, devices // 8 - 4, *out_a)
    send_own(send_a, recv_a.at[me], recv_a_sem)

    for tile in range(1, 4):
        put_pack((tile + 1) * TOK + 48, TOK, tile_picks(tile))

    def pack_bc(at, carry):
        rows = jnp.concatenate(head_rows(at), axis=0)
        packed = bf16_dot(pack_mat[pl.ds(2 * TOK + 48, 3 * TOK), :], rows)
        put_tile(send_b, at, 0, packed[:TOK])
        put_tile(send_b, at, 1, packed[TOK : 2 * TOK])
        put_tile(send_c, at, 0, packed[2 * TOK :])
        return carry

    lax.fori_loop(0, heads // 2, pack_bc, 0)

    wait_bytes(cnt_recv, cnt2_sem)
    seen = cnt_recv[...].reshape(TOK, TOK)
    heavies = jnp.min(jnp.where(seen == 4.0, lane_f, 999.0), axis=1, keepdims=True)
    heavy_all = jnp.min(heavies, axis=0, keepdims=True)
    light = lane_f != heavy_all
    more = jnp.where(light, jnp.maximum(seen - 1.0, 0.0), 0.0)
    more_low = more.astype(jnp.bfloat16)
    in_group = jnp.where(sub // 16 == lane, one, zero).astype(jnp.bfloat16)
    ahead = jnp.where(sub < lane, one, zero).astype(jnp.bfloat16)
    prior = jnp.where(lane < sub, one, zero).astype(jnp.bfloat16)
    mates = (lane < sub) & (lane % 8 == sub % 8)
    mates = jnp.where(mates, one, zero).astype(jnp.bfloat16)
    excess = jnp.maximum(bf16_dot(more_low, in_group) - 4.0, 0.0)
    excess_low = excess.astype(jnp.bfloat16)
    excess_off = bf16_dot(excess_low, ahead)
    excess_pre = bf16_dot(mates, excess_low)
    bad = (jnp.sum(excess, axis=1, keepdims=True) > 8.0) | (excess_pre + excess > 16.0)
    bad = bad | (heavies != heavy_all) | (jnp.sum(more, axis=0, keepdims=True) > OVC)
    flag_ref[0, 0] = jnp.max(jnp.where(bad, one, zero)).astype(jnp.int32)

    spot = zero
    for group in range(8):
        off, count, pre = [a[:, group : group + 1] for a in (excess_off, excess, excess_pre)]
        held = (lane_f >= off) & (lane_f < off + count)
        spot = spot + jnp.where(held, lane_f + (group * 16 + 1.0) - off + pre, zero)
    spot = jnp.where(sub % 8 == clu_at, spot, zero).reshape(16, 8, TOK)
    spot = jnp.sum(spot, axis=1).astype(jnp.bfloat16)
    spread8 = jnp.where(lane % 8 == sub, one, zero).astype(jnp.bfloat16)
    spot = jnp.where(lane[:16] // 8 == sub[:16], bf16_dot(spot, spread8), 0.0)
    spot = jnp.sum(spot, axis=0, keepdims=True) - 1.0
    to_mate[...] = jnp.where(sub_f == spot, one, zero).astype(jnp.bfloat16)
    spot = jnp.broadcast_to(spot, (TOK, TOK)).T
    to_block[...] = jnp.where(spot == lane_f, one, zero).astype(jnp.bfloat16)

    wait_bytes(ex_recv, ex_recv_sem)
    held = ex_recv[...].astype(jnp.float32)
    held = [held[:, 8 * a : 8 * a + 8, :].reshape(TOK, DH) for a in range(4)]
    held = jnp.concatenate(held, axis=1).astype(jnp.bfloat16)
    held = bf16_dot(to_mate[...], held).astype(jnp.bfloat16)
    for a in range(4):
        ex_send2[:, a] = held[:, a * DH : (a + 1) * DH].reshape(8, 16, DH)
    along_clu(lambda to: ex_send2.at[to], ex_recv2, ex_send2_sem, ex_recv2_sem)
    send_to_all(send_b, recv_b.at[me], send_b_sem, recv_b_sem)
    send_to_all(send_c, recv_c.at[me], send_c_sem, recv_c_sem)

    valid = jnp.where((seen > 0.0) & light, one, zero).astype(jnp.bfloat16)
    mine = (sub == clu_at * 16 + lane) & (lane < 16)
    mine = jnp.where(mine, one, zero).astype(jnp.bfloat16)
    more_g = bf16_dot(more_low, mine)
    valid_g = bf16_dot(valid, mine)
    more_g_low = more_g.astype(jnp.bfloat16)
    start_g = bf16_dot(prior, more_g_low)
    offset_g = bf16_dot(more_g_low, ahead)
    beyond_g = jnp.maximum(bf16_dot(more_g_low, one.astype(jnp.bfloat16)) - 4.0, 0.0)
    pre_g = bf16_dot(mates, beyond_g.astype(jnp.bfloat16))
    ex_index = lane_f - pre_g + 4.0
    first_row = lax.broadcasted_iota(jnp.int32, (1, TOK), 1).astype(jnp.float32) * 16.0
    in_tile_at = zero
    beyond_at = zero
    for c in range(16):
        count, begin, off, real = [
            a[:, c : c + 1] for a in (more_g, start_g, offset_g, valid_g)
        ]
        place = begin - off + (c * OVC + 1.0)
        held = (lane_f >= off) & (lane_f < off + count) & (lane < 4)
        in_tile_at = in_tile_at + jnp.where(held, lane_f + place, zero)
        held = (ex_index >= off) & (ex_index < off + count) & (ex_index >= 4.0)
        beyond_at = beyond_at + jnp.where(held, ex_index + place, zero)
        held = (lane_f >= begin) & (lane_f < begin + count)
        where = jnp.where(held, sub_f * 16.0 + 1.0 + lane_f - begin, zero)
        where = jnp.sum(where, axis=0, keepdims=True)
        where = jnp.where(where > 0.0, where, FAR)
        query_row = jnp.concatenate([first_row, where], axis=1)
        query_pos[c] = jnp.broadcast_to(query_row, (8, 2 * TOK))
        key_pos[c, pl.ds(0, TOK), :] = jnp.where(real > 0.0, sub_f * 16.0, FAR)
        key_pos[c, pl.ds(TOK, OVC), :] = jnp.broadcast_to(where, (TOK, TOK)).T[:OVC]
    beyond_at = jnp.sum(beyond_at.reshape(16, 8, TOK), axis=0)
    high = jnp.floor(beyond_at * (1.0 / 32.0))
    split = jnp.concatenate([high, beyond_at - high * 32.0], axis=0).astype(jnp.bfloat16)
    spread16 = jnp.where(lane % 16 == sub, one, zero).astype(jnp.bfloat16)
    split = bf16_dot(split, spread16)
    split = jnp.where(lane[:8] // 16 == sub[:8], split[:8] * 32.0 + split[8:], 0.0)
    beyond_row = jnp.sum(split, axis=0, keepdims=True) - 1.0
    tile_rows = in_tile_at.T[0:8, :] - 1.0
    slot_rows = [tile_rows[k : k + 1, :] for k in range(4)] + [beyond_row]
    slot_cols = [in_tile_at[:, k : k + 1] - 1.0 for k in range(4)]
    slot_cols.append(jnp.broadcast_to(beyond_row, (TOK, TOK)).T)

    chunk = 4
    for k in range(5):
        for m in range(16 * OVC // TOK):
            onehot[pl.ds(k * TOK, TOK), pl.ds(m * TOK, TOK)] = jnp.where(
                slot_cols[k] == lane_f + float(m * TOK), one, zero
            ).astype(jnp.bfloat16)
            pick[pl.ds(m * TOK, TOK), pl.ds(k * TOK, TOK)] = jnp.where(
                slot_rows[k] == sub_f + float(m * TOK), one, zero
            ).astype(jnp.bfloat16)

    for at, tile in enumerate((0, 1, 2, None, 3, 4)):
        for array, matrix in enumerate(rest_picks() if tile is None else tile_picks(tile)):
            unpack_mat[pl.ds(array * TOK, TOK), pl.ds(at * TOK, TOK)] = matrix.T.astype(
                jnp.bfloat16
            )

    perm = flip_perm()

    def arrange(source, target, units):
        def two_sets(at, carry):
            blocks = [pl.ds(pl.multiple_of((2 * at + i) * SET, SET), SET) for i in range(2)]
            spots = [(held, unit) for held in blocks for unit in range(units)]
            rows = jnp.concatenate(
                [source(held, unit).reshape(SET * 16, DH) for held, unit in spots], axis=1
            )
            turned = bf16_dot(perm, rows).astype(jnp.bfloat16)
            for i, (held, unit) in enumerate(spots):
                target(held, unit, turned[:, i * DH : (i + 1) * DH].reshape(16, SET, DH))
            return carry

        lax.fori_loop(0, devices // (2 * SET), two_sets, 0, unroll=2)

    def put_table(first):
        def put(blocks, unit, value):
            table[first + unit, :, blocks, :] = value

        return put

    @pl.when(is_heavy_owner)
    def _():
        wait_bytes(hrecv, hrecv_sem)

        def put_heavy(blocks, unit, value):
            htable[:, blocks, :] = value

        arrange(lambda blocks, unit: hrecv[blocks], put_heavy, 1)
        k_h, v_h = [htable[4 * a : 4 * a + 4].reshape(4 * TOK, DH) for a in (1, 2)]
        hacc[...] = jnp.zeros_like(hacc)
        key_sub = lax.broadcasted_iota(jnp.int32, (4 * TOK, TOK), 0)
        key_at = lax.rem(key_sub, TOK) * 4 + lax.div(key_sub, TOK)
        query_at = lax.broadcasted_iota(jnp.int32, (4 * TOK, TOK), 1) * 4

        def heavy_tile(s, carry):
            out, dq, dk, dv = attend(
                htable[s], k_h, v_h, htable[12 + s], key_at <= query_at + s, inv_root
            )
            hacc[2, pl.ds(pl.multiple_of(s * TOK, TOK), TOK)] = out.astype(jnp.float32)
            hacc[3, pl.ds(pl.multiple_of(s * TOK, TOK), TOK)] = dq.astype(jnp.float32)
            hacc[0] += dk
            hacc[1] += dv
            return carry

        lax.fori_loop(0, 4, heavy_tile, 0)
        for array, at in enumerate((2, 3, 0, 1)):
            htable[4 * array : 4 * array + 4] = (
                hacc[at].astype(jnp.bfloat16).reshape(4, TOK, DH)
            )

        def put_hresult(blocks, unit, value):
            hresult[blocks] = value

        arrange(lambda blocks, unit: htable[:, blocks, :], put_hresult, 1)
        send_to_all(hresult, hback.at[seq_at], hres_sem, hback_sem)

    wait_bytes(recv_a, recv_a_sem)
    def put_tile_a(blocks, unit, value):
        table[4 * unit, :, blocks, :] = value

    arrange(lambda blocks, unit: recv_a[blocks, unit], put_tile_a, 2)

    wait_bytes(ex_recv2, ex_recv2_sem)
    for a in range(4):
        cols = pl.ds(a * DH, DH)
        loose[pl.ds(0, 4 * TOK), cols] = table[4, 4 * a : 4 * a + 4].reshape(4 * TOK, DH)
        loose[pl.ds(4 * TOK, TOK), cols] = ex_recv2[:, a].reshape(TOK, DH)

    def gather_chunk(at, carry):
        chosen = pick[pl.ds(pl.multiple_of(at * chunk * OVC, 64), chunk * OVC), :]
        found = bf16_dot(chosen, loose[...]).astype(jnp.bfloat16)
        for c in range(chunk):
            for array in range(4):
                over[array, at * chunk + c] = found[
                    c * OVC : (c + 1) * OVC, array * DH : (array + 1) * DH
                ]
        return carry

    gather_chunk(0, 0)

    pad_rows = jnp.zeros((TOK - OVC, DH), jnp.bfloat16)

    def load_cluster(tile, j):
        c = tile * 4 + j
        rows = [
            jnp.concatenate([table[tile, a * 4 + j], over[a, c]], axis=0) for a in range(4)
        ]
        for a in (0, 3):
            rows[a] = jnp.concatenate([rows[a], pad_rows], axis=0)
        key_at = key_pos[c]
        allowed = jnp.concatenate([key_at, key_at], axis=1) <= query_pos[c, 0:1, :]
        return rows + [allowed]

    def attend_tiles(first, tiles):
        def one_tile(at, carry):
            tile = first + at
            spots = range(4)
            loaded = [load_cluster(tile, j) for j in spots]
            found = [attend(*arrays, inv_root) for arrays in loaded]
            for j, results in zip(spots, found):
                c = tile * 4 + j
                for a, value in enumerate(results):
                    value = value.astype(jnp.bfloat16)
                    table[tile, a * 4 + j] = value[:TOK]
                    over_res[
                        pl.ds(pl.multiple_of(c * OVC, 16), OVC), pl.ds(a * DH, DH)
                    ] = value[TOK : TOK + OVC]
            return carry

        lax.fori_loop(0, tiles, one_tile, 0)

    def put_in(result):
        def put(blocks, unit, value):
            result[blocks, unit] = value

        return put

    def from_table(first):
        return lambda blocks, unit: table[first + unit, :, blocks, :]

    to_a = (result_a, back_a.at[me], res_a_sem, back_a_sem)
    to_b = (result_b, back_b.at[me], res_b_sem, back_b_sem)
    to_c = (result_c, back_c.at[me], res_c_sem, back_c_sem)
    attend_tiles(0, 1)
    arrange(from_table(0), put_in(result_a), 1)
    send_to_all(*to_a)
    lax.fori_loop(1, 16 // chunk, gather_chunk, 0)

    wait_bytes(recv_b, recv_b_sem)
    arrange(lambda blocks, unit: recv_b[blocks, unit], put_table(1), 2)
    attend_tiles(1, 2)
    arrange(from_table(1), put_in(result_b), 2)
    send_to_all(*to_b)

    wait_bytes(recv_c, recv_c_sem)
    arrange(lambda blocks, unit: recv_c[blocks, 0], put_table(3), 1)
    attend_tiles(3, 1)

    found = bf16_dot(onehot[pl.ds(4 * TOK, TOK), :], over_res[...]).astype(jnp.bfloat16)
    for a in range(4):
        ex_ret2[:, a] = found[:, a * DH : (a + 1) * DH].reshape(8, 16, DH)
    along_clu(lambda to: ex_ret2.at[to], ex_back2, ex_ret2_sem, ex_back2_sem)
    found = bf16_dot(onehot[pl.ds(0, 4 * TOK), :], over_res[...]).astype(jnp.bfloat16)
    for a in range(4):
        table[4, 4 * a : 4 * a + 4] = found[:, a * DH : (a + 1) * DH].reshape(4, TOK, DH)
    arrange(from_table(3), put_in(result_c), 2)
    send_steps(0, devices // 16, *to_c)
    send_own(result_c, back_c.at[me], back_c_sem)

    wait_bytes(ex_back2, ex_back2_sem)
    held = [ex_back2[:, a].reshape(TOK, DH) for a in range(4)]
    held = bf16_dot(to_block[...], jnp.concatenate(held, axis=1))
    held = [held[:, a * DH : (a + 1) * DH].reshape(16, 8, DH) for a in range(4)]
    ex_ret1[...] = jnp.concatenate(held, axis=1).astype(jnp.bfloat16)
    along_seq(lambda to: ex_ret1.at[to], ex_back1, ex_ret1_sem, ex_back1_sem)
    send_steps(devices // 16, devices // 16, *to_c)

    def unpack(tiles, rest, first, count):
        sides = []
        for k in range(2):
            sides.append(
                jnp.concatenate(
                    [tile(k).reshape(TOK, DH) for tile in tiles] + [part(k) for part in rest],
                    axis=0,
                )
            )
        return bf16_dot(
            unpack_mat[:, pl.ds(first, count)], jnp.concatenate(sides, axis=1)
        )

    def tile_of(ref, at, tile):
        return lambda k: ref[pl.ds((2 * at + k) * groups, groups), tile]

    def unpack_early(at, carry):
        tiles = [tile_of(back_a, at, 0), tile_of(back_b, at, 0), tile_of(back_b, at, 1)]
        rest = [
            lambda k: hback[2 * at + k],
            lambda k: ex_back1[2 * at + k],
            lambda k: jnp.zeros((TOK - 48, DH), jnp.bfloat16),
        ]
        early[at] = unpack(tiles, rest, 0, 4 * TOK)
        return carry

    def unpack_last(at, carry):
        cols = pl.ds(pl.multiple_of(at * 2 * DH, 2 * DH), 2 * DH)
        tiles = [tile_of(back_c, at, 0), tile_of(back_c, at, 1)]
        found = (early[at] + unpack(tiles, [], 4 * TOK, 2 * TOK)).astype(jnp.bfloat16)
        for array, ref in enumerate((out_ref, dq_ref, dk_ref, dv_ref)):
            ref[:, cols] = found[array * TOK : (array + 1) * TOK]
        return carry

    wait_bytes(hback, hback_sem)
    wait_bytes(back_a, back_a_sem)
    wait_bytes(back_b, back_b_sem)
    wait_bytes(ex_back1, ex_back1_sem)
    lax.fori_loop(0, heads // 2, unpack_early, 0, unroll=2)
    wait_bytes(back_c, back_c_sem)
    lax.fori_loop(0, heads // 2, unpack_last, 0, unroll=2)

    others = pl.ds(0, devices - 1)
    wait_bytes(cnt_group.at[pl.ds(0, groups - 1)], cnt_send_sem)
    wait_bytes(cnt_recv.at[pl.ds(0, heads - 1)], cnt2_send_sem)
    for ref, sem in ((ex_send, ex_send_sem), (ex_ret1, ex_ret1_sem)):
        wait_bytes(ref.at[pl.ds(0, heads - 1)], sem)
    for ref, sem in ((ex_send2, ex_send2_sem), (ex_ret2, ex_ret2_sem)):
        wait_bytes(ref.at[pl.ds(0, groups - 1)], sem)
    wait_bytes(send_a.at[others], send_a_sem)
    wait_bytes(send_b.at[others], send_b_sem)
    wait_bytes(send_c.at[others], send_c_sem)
    wait_bytes(result_a.at[others], res_a_sem)
    wait_bytes(result_b.at[others], res_b_sem)
    wait_bytes(result_c.at[others], res_c_sem)

    @pl.when(is_heavy_owner)
    def _():
        wait_bytes(hsend.at[pl.ds(0, heads - 1)], hsend_sem)
        wait_bytes(hresult.at[others], hres_sem)

    @pl.when(jnp.logical_not(is_heavy_owner))
    def _():
        wait_bytes(hsend, hsend_sem)


def fast_path(queries, key_rows, value_rows, out_grad, cluster_ids):
    tok_rows, columns = queries.shape
    heads = columns // DH
    groups = lax.axis_size("clu")
    devices = lax.axis_size("seq") * groups
    low = jnp.bfloat16
    wide = jnp.float32
    rows = pltpu.VMEM((tok_rows, columns), low)
    vmem = pl.BlockSpec(memory_space=pltpu.VMEM)
    smem = pl.BlockSpec(memory_space=pltpu.SMEM)
    return pl.pallas_call(
        fast_kernel,
        out_shape=[rows] * 4 + [jax.ShapeDtypeStruct((1, 1), jnp.int32)],
        in_specs=[vmem] + [pl.BlockSpec(memory_space=pl.ANY)] * 4,
        out_specs=[vmem] * 4 + [smem],
        scratch_shapes=[
            pltpu.VMEM((1, TOK), wide),
            pltpu.VMEM((groups, 1, TOK), wide),
            pltpu.VMEM((heads, groups, 1, TOK), wide),
            pltpu.VMEM((5 * TOK + 48, 4 * TOK), low),
            pltpu.VMEM((4 * TOK, 6 * TOK), low),
            pltpu.VMEM((devices, 2, 16, DH), low),
            pltpu.VMEM((devices, 2, 16, DH), low),
            pltpu.VMEM((devices, 1, 16, DH), low),
            pltpu.VMEM((devices, 2, 16, DH), low),
            pltpu.VMEM((devices, 2, 16, DH), low),
            pltpu.VMEM((devices, 1, 16, DH), low),
            pltpu.VMEM((5, 16, devices, DH), low),
            pltpu.VMEM((4, 16, OVC, DH), low),
            pltpu.VMEM((16, TOK + OVC, TOK), wide),
            pltpu.VMEM((16, 8, 2 * TOK), wide),
            pltpu.VMEM((16 * OVC, 5 * TOK), low),
            pltpu.VMEM((5 * TOK, 16 * OVC), low),
            pltpu.VMEM((5 * TOK, 4 * DH), low),
            pltpu.VMEM((16 * OVC, 4 * DH), low),
            pltpu.VMEM((TOK, TOK), low),
            pltpu.VMEM((TOK, TOK), low),
            pltpu.VMEM((devices, 1, 16, DH), low),
            pltpu.VMEM((devices, 2, 16, DH), low),
            pltpu.VMEM((devices, 2, 16, DH), low),
            pltpu.VMEM((devices, 1, 16, DH), low),
            pltpu.VMEM((devices, 2, 16, DH), low),
            pltpu.VMEM((devices, 2, 16, DH), low),
            pltpu.VMEM((heads, 32, DH), low),
            pltpu.VMEM((heads, 32, DH), low),
            pltpu.VMEM((groups, 4, 16, DH), low),
            pltpu.VMEM((groups, 4, 16, DH), low),
            pltpu.VMEM((groups, 4, 16, DH), low),
            pltpu.VMEM((groups, 4, 16, DH), low),
            pltpu.VMEM((heads, 32, DH), low),
            pltpu.VMEM((heads, 32, DH), low),
            pltpu.VMEM((heads, 16, DH), low),
            pltpu.VMEM((devices, 16, DH), low),
            pltpu.VMEM((16, devices, DH), low),
            pltpu.VMEM((4, 4 * TOK, DH), wide),
            pltpu.VMEM((devices, 16, DH), low),
            pltpu.VMEM((heads, 16, DH), low),
            pltpu.VMEM((4, tok_rows, columns), low),
            pltpu.VMEM((heads // 2, 4 * tok_rows, 2 * DH), wide),
        ]
        + [pltpu.SemaphoreType.DMA] * 29,
        compiler_params=pltpu.CompilerParams(
            collective_id=0, has_side_effects=True, vmem_limit_bytes=44 * 1024 * 1024
        ),
    )(cluster_ids.reshape(1, tok_rows), queries, key_rows, value_rows, out_grad)


def copy_kernel(*refs):
    sem = refs[-1]
    copies = [
        pltpu.make_async_copy(refs[i], refs[4 + i], sem.at[i]) for i in range(4)
    ]
    for copy in copies:
        copy.start()
    for copy in copies:
        copy.wait()


def copy_out(arrays):
    anywhere = pl.BlockSpec(memory_space=pl.ANY)
    return pl.pallas_call(
        copy_kernel,
        out_shape=[pltpu.HBM(a.shape, a.dtype) for a in arrays],
        in_specs=[anywhere] * 4,
        out_specs=[anywhere] * 4,
        scratch_shapes=[pltpu.SemaphoreType.DMA((4,))],
    )(*arrays)


def per_device(queries, key_rows, value_rows, out_grad, cluster_ids):
    arrays = (queries, key_rows, value_rows, out_grad, cluster_ids)
    *fast, flag = fast_path(*arrays)
    return lax.cond(
        flag.reshape(()) != 0,
        lambda arrays, fast: full_capacity(*arrays),
        lambda arrays, fast: tuple(copy_out(fast)),
        arrays,
        tuple(fast),
    )


def solution(mesh):
    in_specs = (
        P(("seq", "clu"), None),
        P(("seq", "clu"), None),
        P(("seq", "clu"), None),
        P(("seq", "clu"), None),
        P(("seq", "clu")),
    )
    out_specs = (
        P(("seq", "clu"), None),
        P(("seq", "clu"), None),
        P(("seq", "clu"), None),
        P(("seq", "clu"), None),
    )
    return jax.shard_map(
        per_device, mesh=mesh, in_specs=in_specs, out_specs=out_specs, check_vma=False
    )
```

```python
import math

import jax
import jax.numpy as jnp
from jax import lax
from jax.experimental import pallas as pl
from jax.experimental.pallas import tpu as pltpu
from jax.sharding import PartitionSpec as P

DH = 128
TOK = 128
OVC = 80
SET = 16
FAR = 1e9
MESH = pl.DeviceIdType.MESH


masked = -1e30


def contract_last(left, right):
    return lax.dot_general(
        left, right, (((1,), (1,)), ((), ())), preferred_element_type=jnp.float32
    )


def contract_first(left, right):
    return lax.dot_general(
        left, right, (((0,), (0,)), ((), ())), preferred_element_type=jnp.float32
    )


def softmax_rows(query_head, key_head, allowed, inv_root):
    scores = contract_last(query_head, key_head) * inv_root
    scores = jnp.where(allowed, scores, masked)
    row_max = jnp.max(scores, axis=1, keepdims=True)
    weights = jnp.exp(scores - row_max)
    row_sum = jnp.sum(weights, axis=1, keepdims=True)
    return (weights / row_sum).astype(jnp.bfloat16)


def head_slice(array, head_index):
    return lax.dynamic_slice_in_dim(array, head_index * DH, DH, 1)


def full_capacity(queries, key_rows, value_rows, out_grad, cluster_ids):
    seq_count = lax.axis_size("seq")
    clu_count = lax.axis_size("clu")
    devices = seq_count * clu_count
    tok_rows = queries.shape[0]
    columns = queries.shape[1]
    head_count = columns // DH
    most_rows = 4 * tok_rows // devices
    capacity = most_rows * devices
    inv_root = 1.0 / math.sqrt(DH)
    owners = jnp.arange(devices, dtype=jnp.int32)
    member = (cluster_ids[:, None] == owners[None, :]).astype(jnp.int32)
    running = jnp.cumsum(member, axis=0) - 1
    slot_rank = jnp.sum(member * running, axis=1)
    sent_counts = jnp.sum(member, axis=0).reshape(devices, 1)
    slot_index = cluster_ids * most_rows + slot_rank
    stacked = jnp.concatenate([queries, key_rows, value_rows], axis=1)
    width_in = stacked.shape[1]
    packed = jnp.zeros((devices * most_rows, width_in), jnp.bfloat16).at[slot_index].set(stacked)
    packed = packed.reshape(devices, most_rows, width_in)
    got_rows, got_counts = (
        lax.all_to_all(packed, ("seq", "clu"), split_axis=0, concat_axis=0, tiled=True),
        lax.all_to_all(sent_counts, ("seq", "clu"), split_axis=0, concat_axis=0, tiled=True),
    )
    got_counts = got_counts.reshape(devices)
    starts = jnp.cumsum(got_counts) - got_counts
    live_total = jnp.sum(got_counts)
    within = jnp.arange(most_rows, dtype=jnp.int32)
    target = jnp.where(
        within[None, :] < got_counts[:, None], starts[:, None] + within[None, :], capacity
    )
    target = target.reshape(devices * most_rows)
    gathered = (
        jnp.zeros((capacity, width_in), jnp.bfloat16)
        .at[target]
        .set(got_rows.reshape(devices * most_rows, width_in), mode="drop")
    )
    query_block = gathered[:, :columns]
    key_block = gathered[:, columns : 2 * columns]
    value_block = gathered[:, 2 * columns : 3 * columns]
    positions = jnp.arange(capacity, dtype=jnp.int32)
    allowed = (positions[None, :] <= positions[:, None]) & (positions[None, :] < live_total)

    def forward_head(head_index, mixed_rows):
        weights_low = softmax_rows(
            head_slice(query_block, head_index),
            head_slice(key_block, head_index),
            allowed,
            inv_root,
        )
        out_head = jnp.dot(
            weights_low, head_slice(value_block, head_index), preferred_element_type=jnp.float32
        ).astype(jnp.bfloat16)
        return lax.dynamic_update_slice_in_dim(mixed_rows, out_head, head_index * DH, 1)

    mixed_rows = lax.fori_loop(
        0, head_count, forward_head, jnp.zeros((capacity, columns), jnp.bfloat16)
    )
    back_index = jnp.minimum(target, capacity - 1)
    outgoing = jnp.take(mixed_rows, back_index, axis=0).reshape(devices, most_rows, columns)
    grad_packed = (
        jnp.zeros((devices * most_rows, columns), jnp.bfloat16).at[slot_index].set(out_grad)
    )
    grad_packed = grad_packed.reshape(devices, most_rows, columns)
    returned = lax.all_to_all(outgoing, ("seq", "clu"), split_axis=0, concat_axis=0, tiled=True)
    got_grad = lax.all_to_all(grad_packed, ("seq", "clu"), split_axis=0, concat_axis=0, tiled=True)
    attention_out = jnp.take(returned.reshape(devices * most_rows, columns), slot_index, axis=0)
    grad_block = (
        jnp.zeros((capacity, columns), jnp.bfloat16)
        .at[target]
        .set(got_grad.reshape(devices * most_rows, columns), mode="drop")
    )
    delta_rows = jnp.sum(
        (grad_block.astype(jnp.float32) * mixed_rows.astype(jnp.float32)).reshape(
            capacity, head_count, DH
        ),
        axis=2,
    )

    def backward_head(head_index, grad_rows):
        query_head = head_slice(query_block, head_index)
        key_head = head_slice(key_block, head_index)
        value_head = head_slice(value_block, head_index)
        grad_head = head_slice(grad_block, head_index)
        weights_low = softmax_rows(query_head, key_head, allowed, inv_root)
        prob_grad = contract_last(grad_head, value_head)
        delta_head = lax.dynamic_slice_in_dim(delta_rows, head_index, 1, 1)
        score_grad = (weights_low.astype(jnp.float32) * (prob_grad - delta_head)).astype(
            jnp.bfloat16
        )
        query_part = (
            jnp.dot(score_grad, key_head, preferred_element_type=jnp.float32) * inv_root
        ).astype(jnp.bfloat16)
        key_part = (contract_first(score_grad, query_head) * inv_root).astype(jnp.bfloat16)
        value_part = contract_first(weights_low, grad_head).astype(jnp.bfloat16)
        grad_rows = lax.dynamic_update_slice_in_dim(grad_rows, query_part, head_index * DH, 1)
        grad_rows = lax.dynamic_update_slice_in_dim(
            grad_rows, key_part, columns + head_index * DH, 1
        )
        return lax.dynamic_update_slice_in_dim(
            grad_rows, value_part, 2 * columns + head_index * DH, 1
        )

    grad_rows = lax.fori_loop(
        0, head_count, backward_head, jnp.zeros((capacity, 3 * columns), jnp.bfloat16)
    )
    outgoing_grads = jnp.take(grad_rows, back_index, axis=0).reshape(
        devices, most_rows, 3 * columns
    )
    returned_grads = lax.all_to_all(
        outgoing_grads, ("seq", "clu"), split_axis=0, concat_axis=0, tiled=True
    )
    picked = jnp.take(returned_grads.reshape(devices * most_rows, 3 * columns), slot_index, axis=0)
    return (
        attention_out,
        picked[:, :columns],
        picked[:, columns : 2 * columns],
        picked[:, 2 * columns :],
    )


def bf16_dot(left, right):
    return jnp.dot(left, right, preferred_element_type=jnp.float32)


def flip_perm():
    row = lax.broadcasted_iota(jnp.int32, (SET * 16, SET * 16), 0)
    col = lax.broadcasted_iota(jnp.int32, (SET * 16, SET * 16), 1)
    swapped = (col % 16) * 16 + col // 16
    return (row == swapped).astype(jnp.float32).astype(jnp.bfloat16)


def attend(q, k, v, g, allowed, inv_root):
    raw = jnp.where(allowed, contract_last(k, q), masked)
    most = jnp.max(raw, axis=0, keepdims=True)
    weights = jnp.exp2((raw - most) * (inv_root * math.log2(math.e)))
    prob = weights * (1.0 / jnp.sum(weights, axis=0, keepdims=True))
    prob_low = prob.astype(jnp.bfloat16)
    prob_grad = contract_last(v, g)
    delta = jnp.sum(prob * prob_grad, axis=0, keepdims=True)
    score_grad = (prob * (prob_grad - delta)).astype(jnp.bfloat16)
    out = contract_first(v, prob_low).T.astype(jnp.bfloat16)
    dq = (contract_first(k, score_grad).T * inv_root).astype(jnp.bfloat16)
    dk = bf16_dot(score_grad, q) * inv_root
    dv = bf16_dot(prob_low, g)
    return out, dq, dk, dv


def fast_kernel(
    ids_ref, q_ref, k_ref, v_ref, g_ref,
    out_ref, dq_ref, dk_ref, dv_ref, flag_ref,
    cnt_send, cnt_group, cnt_recv, pack_mat, unpack_mat,
    send_a, send_b, send_c, recv_a, recv_b, recv_c, table,
    over, key_pos, query_pos, pick, onehot, loose, over_res, to_mate, to_block,
    result_a, result_b, result_c, back_a, back_b, back_c,
    ex_send, ex_recv, ex_send2, ex_recv2, ex_ret2, ex_back2, ex_ret1, ex_back1,
    hsend, hrecv, htable, hacc, hresult, hback, inputs, early,
    cnt_send_sem, cnt_sem, cnt2_send_sem, cnt2_sem,
    send_a_sem, recv_a_sem, send_b_sem, recv_b_sem, send_c_sem, recv_c_sem,
    res_a_sem, back_a_sem, res_b_sem, back_b_sem, res_c_sem, back_c_sem,
    ex_send_sem, ex_recv_sem, ex_send2_sem, ex_recv2_sem,
    ex_ret2_sem, ex_back2_sem, ex_ret1_sem, ex_back1_sem,
    hsend_sem, hrecv_sem, hres_sem, hback_sem, input_sem,
):
    seq_at = lax.axis_index("seq")
    clu_at = lax.axis_index("clu")
    groups = lax.axis_size("clu")
    heads = lax.axis_size("seq")
    devices = heads * groups
    me = seq_at * groups + clu_at
    inv_root = 1.0 / math.sqrt(DH)
    is_heavy_owner = lax.rem(seq_at, groups) == clu_at
    at_x, at_z = lax.div(seq_at, 4), lax.rem(seq_at, 4)
    at_y, at_core = lax.div(clu_at, 2), lax.rem(clu_at, 2)

    def by_core(first, second):
        return first + at_core * (second - first)

    eight = []
    for by_x, by_z, by_clu in zip(
        zip((3, 2, 3, 1, 3, 0, 2, 0), (2, 2, 1, 0, 2, 3, 0, 2)),
        zip((0, 0, 2, 3, 1, 2, 3, 1), (2, 2, 0, 1, 3, 0, 0, 2)),
        zip((2, 1, 3, 0, 6, 4, 5, 7), (6, 5, 7, 4, 2, 0, 1, 3)),
    ):
        y = lax.rem(at_y + by_core(by_clu[0] // 2, by_clu[1] // 2), 4)
        core = lax.rem(at_core + by_core(by_clu[0] % 2, by_clu[1] % 2), 2)
        eight.append((by_core(*by_x), by_core(*by_z), y * 2 + core))

    def for_peers(first, count, visit):
        def one_eight(step, carry):
            by = lax.rem(step * 13 + at_core * 12, 16)
            x = at_x + lax.div(by, 4)
            z = at_z + lax.rem(by, 4)
            for j, (more_x, more_z, clu_to) in enumerate(eight):
                seq_to = lax.rem(x + more_x, 4) * 4 + lax.rem(z + more_z, 4)
                if j in (3, 5):
                    pl.when(seq_to * groups + clu_to != me)(lambda: visit(seq_to, clu_to))
                else:
                    visit(seq_to, clu_to)
            return carry

        lax.fori_loop(first, first + count, one_eight, 0)

    def send_steps(first, count, source, target, send_sem, recv_sem):
        def start(seq_to, clu_to):
            pltpu.make_async_remote_copy(
                src_ref=source.at[seq_to * groups + clu_to],
                dst_ref=target,
                send_sem=send_sem,
                recv_sem=recv_sem,
                device_id=(seq_to, clu_to),
                device_id_type=MESH,
            ).start()

        for_peers(first, count, start)

    def send_own(source, target, recv_sem):
        pltpu.make_async_copy(source.at[me], target, recv_sem).start()

    def send_to_all(source, target, send_sem, recv_sem):
        send_steps(0, devices // 8, source, target, send_sem, recv_sem)
        send_own(source, target, recv_sem)

    def wait_bytes(ref, sem):
        pltpu.make_async_copy(ref, ref, sem).wait()

    for array, ref in enumerate((q_ref, k_ref, v_ref, g_ref)):
        pltpu.make_async_copy(ref, inputs.at[array], input_sem).start()
    barrier = pltpu.get_barrier_semaphore()

    def greet(seq_to, clu_to):
        pl.semaphore_signal(barrier, inc=1, device_id=(seq_to, clu_to), device_id_type=MESH)

    for_peers(0, devices // 8, greet)

    sub = lax.broadcasted_iota(jnp.int32, (TOK, TOK), 0)
    lane = lax.broadcasted_iota(jnp.int32, (TOK, TOK), 1)
    sub_f = sub.astype(jnp.float32)
    lane_f = lane.astype(jnp.float32)
    ids_l = jnp.broadcast_to(ids_ref[...].astype(jnp.float32), (TOK, TOK))
    ids_s = ids_l.T
    one = jnp.ones((TOK, TOK), jnp.float32)
    zero = jnp.zeros((TOK, TOK), jnp.float32)
    same = ids_l == ids_s
    rank_l = jnp.sum(jnp.where(same & (sub < lane), one, zero), axis=0, keepdims=True)
    rank_s = jnp.sum(jnp.where(same & (lane < sub), one, zero), axis=1, keepdims=True)
    count_l = jnp.sum(jnp.where(same, one, zero), axis=0, keepdims=True)
    cnt_send[...] = jnp.sum(jnp.where(ids_s == lane_f, one, zero), axis=0, keepdims=True)
    ids_row = ids_l[0:1, :]
    heavy = jnp.min(jnp.where(count_l == 4.0, ids_row, 999.0), axis=1, keepdims=True)
    group_l = jnp.floor(ids_l * (1.0 / 16.0))
    group_s = jnp.floor(ids_s * (1.0 / 16.0))
    earlier = (ids_s < ids_l) | (same & (sub < lane))
    later = (ids_l < ids_s) | (same & (lane < sub))
    before = (group_l == group_s) & (ids_s != heavy) & (rank_s >= 1.0) & earlier
    over_at = jnp.sum(jnp.where(before, one, zero), axis=0, keepdims=True)
    behind = (group_l == group_s) & (ids_l != heavy) & (rank_l >= 1.0) & later
    over_at_s = jnp.sum(jnp.where(behind, one, zero), axis=1, keepdims=True)
    excess_s = (ids_s != heavy) & (rank_s >= 1.0) & (over_at_s >= 4.0)
    excess_at = jnp.sum(jnp.where(excess_s & earlier, one, zero), axis=0, keepdims=True)
    light_l = ids_l != heavy
    slot_group = (sub // 16).astype(jnp.float32)
    in_tile = sub % 16
    over_l = light_l & (rank_l >= 1.0)

    def tile_picks(tile):
        at_slot = (in_tile % 4).astype(jnp.float32)
        if tile < 4:
            cluster = slot_group * 16.0 + at_slot + 4.0 * tile
            taken = (ids_l == cluster) & (rank_l == 0.0) & light_l
        else:
            taken = (group_l == slot_group) & over_l & (over_at == at_slot)
        return [jnp.where(taken & (in_tile // 4 == array), one, zero) for array in range(4)]

    def rest_picks():
        picks = []
        for array in range(4):
            chosen = (ids_l == heavy) & (rank_l == (sub % 4).astype(jnp.float32))
            chosen = chosen & (sub // 4 == array) & (sub < 16)
            beyond = over_l & (over_at >= 4.0) & (excess_at == (sub % 8).astype(jnp.float32))
            beyond = beyond & (sub // 8 == array + 2)
            picks.append(jnp.where(chosen | beyond, one, zero))
        return picks

    def put_pack(at_row, count, picks):
        for array, matrix in enumerate(picks):
            pack_mat[pl.ds(at_row, count), pl.ds(array * TOK, TOK)] = matrix[:count].astype(
                jnp.bfloat16
            )

    put_pack(0, TOK, tile_picks(0))
    put_pack(TOK, TOK, tile_picks(4))
    put_pack(2 * TOK, 48, rest_picks())


    def seq_step(step):
        offset = lax.rem(step * 7, 16)
        return by_core(offset, lax.rem(offset, 4) * 4 + lax.div(offset, 4))

    def clu_step(step):
        return lax.rem(step * (3 + 2 * at_core), 8)

    def send_line(source, target, count, at, order, device, send_sem, recv_sem):
        def one_peer(step, carry):
            to = lax.rem(at + order(step), count)
            pltpu.make_async_remote_copy(
                src_ref=source(to),
                dst_ref=target,
                send_sem=send_sem,
                recv_sem=recv_sem,
                device_id=device(to),
                device_id_type=MESH,
            ).start()
            return carry

        lax.fori_loop(1, count, one_peer, 0)
        pltpu.make_async_copy(source(at), target, recv_sem).start()

    def along_seq(source, target, send_sem, recv_sem):
        send_line(
            source, target.at[seq_at], heads, seq_at, seq_step,
            lambda to: (to, clu_at), send_sem, recv_sem,
        )

    def along_clu(source, target, send_sem, recv_sem):
        send_line(
            source, target.at[clu_at], groups, clu_at, clu_step,
            lambda to: (seq_at, to), send_sem, recv_sem,
        )


    def head_rows(at):
        cols = pl.ds(pl.multiple_of(at * 2 * DH, 2 * DH), 2 * DH)
        return [inputs[array, :, cols] for array in range(4)]

    def put_tile(target, at, tile, packed):
        low = packed.astype(jnp.bfloat16)
        for k in range(2):
            target[pl.ds((2 * at + k) * groups, groups), tile] = low[
                :, k * DH : (k + 1) * DH
            ].reshape(groups, 16, DH)

    def pack_a(at, carry):
        rows = jnp.concatenate(head_rows(at), axis=0)
        packed = bf16_dot(pack_mat[pl.ds(0, 2 * TOK + 48), :], rows)
        put_tile(send_a, at, 0, packed[:TOK])
        put_tile(send_a, at, 1, packed[TOK : 2 * TOK])
        rest = packed[2 * TOK :].astype(jnp.bfloat16)
        for k in range(2):
            hsend[2 * at + k] = rest[:16, k * DH : (k + 1) * DH]
            ex_send[2 * at + k] = rest[16:, k * DH : (k + 1) * DH]
        return carry

    wait_bytes(inputs, input_sem)
    lax.fori_loop(0, heads // 2, pack_a, 0, unroll=4)
    pl.semaphore_wait(barrier, devices - 1)
    along_clu(lambda to: cnt_send, cnt_group, cnt_send_sem, cnt_sem)

    def send_heavy(step, carry):
        head = lax.rem(seq_at + seq_step(step), heads)
        clu_to = lax.rem(head, groups)

        @pl.when(head * groups + clu_to != me)
        def _():
            pltpu.make_async_remote_copy(
                src_ref=hsend.at[head],
                dst_ref=hrecv.at[me],
                send_sem=hsend_sem,
                recv_sem=hrecv_sem,
                device_id=(head, clu_to),
                device_id_type=MESH,
            ).start()

        @pl.when(head * groups + clu_to == me)
        def _():
            pltpu.make_async_copy(hsend.at[head], hrecv.at[me], hrecv_sem).start()

        return carry

    lax.fori_loop(0, heads, send_heavy, 0)
    along_seq(lambda to: ex_send.at[to], ex_recv, ex_send_sem, ex_recv_sem)
    out_a = (send_a, recv_a.at[me], send_a_sem, recv_a_sem)
    send_steps(0, 4, *out_a)
    wait_bytes(cnt_group, cnt_sem)
    along_seq(lambda to: cnt_group, cnt_recv, cnt2_send_sem, cnt2_sem)
    send_steps(4, devices // 8 - 4, *out_a)
    send_own(send_a, recv_a.at[me], recv_a_sem)

    for tile in range(1, 4):
        put_pack((tile + 1) * TOK + 48, TOK, tile_picks(tile))

    def pack_bc(at, carry):
        rows = jnp.concatenate(head_rows(at), axis=0)
        packed = bf16_dot(pack_mat[pl.ds(2 * TOK + 48, 3 * TOK), :], rows)
        put_tile(send_b, at, 0, packed[:TOK])
        put_tile(send_b, at, 1, packed[TOK : 2 * TOK])
        put_tile(send_c, at, 0, packed[2 * TOK :])
        return carry

    lax.fori_loop(0, heads // 2, pack_bc, 0)

    wait_bytes(cnt_recv, cnt2_sem)
    seen = cnt_recv[...].reshape(TOK, TOK)
    heavies = jnp.min(jnp.where(seen == 4.0, lane_f, 999.0), axis=1, keepdims=True)
    heavy_all = jnp.min(heavies, axis=0, keepdims=True)
    light = lane_f != heavy_all
    more = jnp.where(light, jnp.maximum(seen - 1.0, 0.0), 0.0)
    more_low = more.astype(jnp.bfloat16)
    in_group = jnp.where(sub // 16 == lane, one, zero).astype(jnp.bfloat16)
    ahead = jnp.where(sub < lane, one, zero).astype(jnp.bfloat16)
    prior = jnp.where(lane < sub, one, zero).astype(jnp.bfloat16)
    mates = (lane < sub) & (lane % 8 == sub % 8)
    mates = jnp.where(mates, one, zero).astype(jnp.bfloat16)
    excess = jnp.maximum(bf16_dot(more_low, in_group) - 4.0, 0.0)
    excess_low = excess.astype(jnp.bfloat16)
    excess_off = bf16_dot(excess_low, ahead)
    excess_pre = bf16_dot(mates, excess_low)
    bad = (jnp.sum(excess, axis=1, keepdims=True) > 8.0) | (excess_pre + excess > 16.0)
    bad = bad | (heavies != heavy_all) | (jnp.sum(more, axis=0, keepdims=True) > OVC)
    flag_ref[0, 0] = jnp.max(jnp.where(bad, one, zero)).astype(jnp.int32)

    spot = zero
    for group in range(8):
        off, count, pre = [a[:, group : group + 1] for a in (excess_off, excess, excess_pre)]
        held = (lane_f >= off) & (lane_f < off + count)
        spot = spot + jnp.where(held, lane_f + (group * 16 + 1.0) - off + pre, zero)
    spot = jnp.where(sub % 8 == clu_at, spot, zero).reshape(16, 8, TOK)
    spot = jnp.sum(spot, axis=1).astype(jnp.bfloat16)
    spread8 = jnp.where(lane % 8 == sub, one, zero).astype(jnp.bfloat16)
    spot = jnp.where(lane[:16] // 8 == sub[:16], bf16_dot(spot, spread8), 0.0)
    spot = jnp.sum(spot, axis=0, keepdims=True) - 1.0
    to_mate[...] = jnp.where(sub_f == spot, one, zero).astype(jnp.bfloat16)
    spot = jnp.broadcast_to(spot, (TOK, TOK)).T
    to_block[...] = jnp.where(spot == lane_f, one, zero).astype(jnp.bfloat16)

    wait_bytes(ex_recv, ex_recv_sem)
    held = ex_recv[...].astype(jnp.float32)
    held = [held[:, 8 * a : 8 * a + 8, :].reshape(TOK, DH) for a in range(4)]
    held = jnp.concatenate(held, axis=1).astype(jnp.bfloat16)
    held = bf16_dot(to_mate[...], held).astype(jnp.bfloat16)
    for a in range(4):
        ex_send2[:, a] = held[:, a * DH : (a + 1) * DH].reshape(8, 16, DH)
    along_clu(lambda to: ex_send2.at[to], ex_recv2, ex_send2_sem, ex_recv2_sem)
    send_to_all(send_b, recv_b.at[me], send_b_sem, recv_b_sem)
    send_to_all(send_c, recv_c.at[me], send_c_sem, recv_c_sem)

    valid = jnp.where((seen > 0.0) & light, one, zero).astype(jnp.bfloat16)
    mine = (sub == clu_at * 16 + lane) & (lane < 16)
    mine = jnp.where(mine, one, zero).astype(jnp.bfloat16)
    more_g = bf16_dot(more_low, mine)
    valid_g = bf16_dot(valid, mine)
    more_g_low = more_g.astype(jnp.bfloat16)
    start_g = bf16_dot(prior, more_g_low)
    offset_g = bf16_dot(more_g_low, ahead)
    beyond_g = jnp.maximum(bf16_dot(more_g_low, one.astype(jnp.bfloat16)) - 4.0, 0.0)
    pre_g = bf16_dot(mates, beyond_g.astype(jnp.bfloat16))
    ex_index = lane_f - pre_g + 4.0
    first_row = lax.broadcasted_iota(jnp.int32, (1, TOK), 1).astype(jnp.float32) * 16.0
    in_tile_at = zero
    beyond_at = zero
    for c in range(16):
        count, begin, off, real = [
            a[:, c : c + 1] for a in (more_g, start_g, offset_g, valid_g)
        ]
        place = begin - off + (c * OVC + 1.0)
        held = (lane_f >= off) & (lane_f < off + count) & (lane < 4)
        in_tile_at = in_tile_at + jnp.where(held, lane_f + place, zero)
        held = (ex_index >= off) & (ex_index < off + count) & (ex_index >= 4.0)
        beyond_at = beyond_at + jnp.where(held, ex_index + place, zero)
        held = (lane_f >= begin) & (lane_f < begin + count)
        where = jnp.where(held, sub_f * 16.0 + 1.0 + lane_f - begin, zero)
        where = jnp.sum(where, axis=0, keepdims=True)
        where = jnp.where(where > 0.0, where, FAR)
        query_row = jnp.concatenate([first_row, where], axis=1)
        query_pos[c] = jnp.broadcast_to(query_row, (8, 2 * TOK))
        key_pos[c, pl.ds(0, TOK), :] = jnp.where(real > 0.0, sub_f * 16.0, FAR)
        key_pos[c, pl.ds(TOK, OVC), :] = jnp.broadcast_to(where, (TOK, TOK)).T[:OVC]
    beyond_at = jnp.sum(beyond_at.reshape(16, 8, TOK), axis=0)
    high = jnp.floor(beyond_at * (1.0 / 32.0))
    split = jnp.concatenate([high, beyond_at - high * 32.0], axis=0).astype(jnp.bfloat16)
    spread16 = jnp.where(lane % 16 == sub, one, zero).astype(jnp.bfloat16)
    split = bf16_dot(split, spread16)
    split = jnp.where(lane[:8] // 16 == sub[:8], split[:8] * 32.0 + split[8:], 0.0)
    beyond_row = jnp.sum(split, axis=0, keepdims=True) - 1.0
    tile_rows = in_tile_at.T[0:8, :] - 1.0
    slot_rows = [tile_rows[k : k + 1, :] for k in range(4)] + [beyond_row]
    slot_cols = [in_tile_at[:, k : k + 1] - 1.0 for k in range(4)]
    slot_cols.append(jnp.broadcast_to(beyond_row, (TOK, TOK)).T)

    chunk = 4
    for k in range(5):
        for m in range(16 * OVC // TOK):
            onehot[pl.ds(k * TOK, TOK), pl.ds(m * TOK, TOK)] = jnp.where(
                slot_cols[k] == lane_f + float(m * TOK), one, zero
            ).astype(jnp.bfloat16)
            pick[pl.ds(m * TOK, TOK), pl.ds(k * TOK, TOK)] = jnp.where(
                slot_rows[k] == sub_f + float(m * TOK), one, zero
            ).astype(jnp.bfloat16)

    for at, tile in enumerate((0, 1, 2, None, 3, 4)):
        for array, matrix in enumerate(rest_picks() if tile is None else tile_picks(tile)):
            unpack_mat[pl.ds(array * TOK, TOK), pl.ds(at * TOK, TOK)] = matrix.T.astype(
                jnp.bfloat16
            )

    perm = flip_perm()

    def arrange(source, target, units):
        def two_sets(at, carry):
            blocks = [pl.ds(pl.multiple_of((2 * at + i) * SET, SET), SET) for i in range(2)]
            spots = [(held, unit) for held in blocks for unit in range(units)]
            rows = jnp.concatenate(
                [source(held, unit).reshape(SET * 16, DH) for held, unit in spots], axis=1
            )
            turned = bf16_dot(perm, rows).astype(jnp.bfloat16)
            for i, (held, unit) in enumerate(spots):
                target(held, unit, turned[:, i * DH : (i + 1) * DH].reshape(16, SET, DH))
            return carry

        lax.fori_loop(0, devices // (2 * SET), two_sets, 0, unroll=2)

    def put_table(first):
        def put(blocks, unit, value):
            table[first + unit, :, blocks, :] = value

        return put

    @pl.when(is_heavy_owner)
    def _():
        wait_bytes(hrecv, hrecv_sem)

        def put_heavy(blocks, unit, value):
            htable[:, blocks, :] = value

        arrange(lambda blocks, unit: hrecv[blocks], put_heavy, 1)
        k_h, v_h = [htable[4 * a : 4 * a + 4].reshape(4 * TOK, DH) for a in (1, 2)]
        hacc[...] = jnp.zeros_like(hacc)
        key_sub = lax.broadcasted_iota(jnp.int32, (4 * TOK, TOK), 0)
        key_at = lax.rem(key_sub, TOK) * 4 + lax.div(key_sub, TOK)
        query_at = lax.broadcasted_iota(jnp.int32, (4 * TOK, TOK), 1) * 4

        def heavy_tile(s, carry):
            out, dq, dk, dv = attend(
                htable[s], k_h, v_h, htable[12 + s], key_at <= query_at + s, inv_root
            )
            hacc[2, pl.ds(pl.multiple_of(s * TOK, TOK), TOK)] = out.astype(jnp.float32)
            hacc[3, pl.ds(pl.multiple_of(s * TOK, TOK), TOK)] = dq.astype(jnp.float32)
            hacc[0] += dk
            hacc[1] += dv
            return carry

        lax.fori_loop(0, 4, heavy_tile, 0)
        for array, at in enumerate((2, 3, 0, 1)):
            htable[4 * array : 4 * array + 4] = (
                hacc[at].astype(jnp.bfloat16).reshape(4, TOK, DH)
            )

        def put_hresult(blocks, unit, value):
            hresult[blocks] = value

        arrange(lambda blocks, unit: htable[:, blocks, :], put_hresult, 1)
        send_to_all(hresult, hback.at[seq_at], hres_sem, hback_sem)

    wait_bytes(recv_a, recv_a_sem)
    def put_tile_a(blocks, unit, value):
        table[4 * unit, :, blocks, :] = value

    arrange(lambda blocks, unit: recv_a[blocks, unit], put_tile_a, 2)

    wait_bytes(ex_recv2, ex_recv2_sem)
    for a in range(4):
        cols = pl.ds(a * DH, DH)
        loose[pl.ds(0, 4 * TOK), cols] = table[4, 4 * a : 4 * a + 4].reshape(4 * TOK, DH)
        loose[pl.ds(4 * TOK, TOK), cols] = ex_recv2[:, a].reshape(TOK, DH)

    def gather_chunk(at, carry):
        chosen = pick[pl.ds(pl.multiple_of(at * chunk * OVC, 64), chunk * OVC), :]
        found = bf16_dot(chosen, loose[...]).astype(jnp.bfloat16)
        for c in range(chunk):
            for array in range(4):
                over[array, at * chunk + c] = found[
                    c * OVC : (c + 1) * OVC, array * DH : (array + 1) * DH
                ]
        return carry

    gather_chunk(0, 0)

    pad_rows = jnp.zeros((TOK - OVC, DH), jnp.bfloat16)

    def load_cluster(tile, j):
        c = tile * 4 + j
        rows = [
            jnp.concatenate([table[tile, a * 4 + j], over[a, c]], axis=0) for a in range(4)
        ]
        for a in (0, 3):
            rows[a] = jnp.concatenate([rows[a], pad_rows], axis=0)
        key_at = key_pos[c]
        allowed = jnp.concatenate([key_at, key_at], axis=1) <= query_pos[c, 0:1, :]
        return rows + [allowed]

    def attend_tiles(first, tiles):
        def one_tile(at, carry):
            tile = first + at
            spots = range(4)
            loaded = [load_cluster(tile, j) for j in spots]
            found = [attend(*arrays, inv_root) for arrays in loaded]
            for j, results in zip(spots, found):
                c = tile * 4 + j
                for a, value in enumerate(results):
                    value = value.astype(jnp.bfloat16)
                    table[tile, a * 4 + j] = value[:TOK]
                    over_res[
                        pl.ds(pl.multiple_of(c * OVC, 16), OVC), pl.ds(a * DH, DH)
                    ] = value[TOK : TOK + OVC]
            return carry

        lax.fori_loop(0, tiles, one_tile, 0)

    def put_in(result):
        def put(blocks, unit, value):
            result[blocks, unit] = value

        return put

    def from_table(first):
        return lambda blocks, unit: table[first + unit, :, blocks, :]

    to_a = (result_a, back_a.at[me], res_a_sem, back_a_sem)
    to_b = (result_b, back_b.at[me], res_b_sem, back_b_sem)
    to_c = (result_c, back_c.at[me], res_c_sem, back_c_sem)
    attend_tiles(0, 1)
    arrange(from_table(0), put_in(result_a), 1)
    send_to_all(*to_a)
    lax.fori_loop(1, 16 // chunk, gather_chunk, 0)

    wait_bytes(recv_b, recv_b_sem)
    arrange(lambda blocks, unit: recv_b[blocks, unit], put_table(1), 2)
    attend_tiles(1, 2)
    arrange(from_table(1), put_in(result_b), 2)
    send_to_all(*to_b)

    wait_bytes(recv_c, recv_c_sem)
    arrange(lambda blocks, unit: recv_c[blocks, 0], put_table(3), 1)
    attend_tiles(3, 1)

    found = bf16_dot(onehot[pl.ds(4 * TOK, TOK), :], over_res[...]).astype(jnp.bfloat16)
    for a in range(4):
        ex_ret2[:, a] = found[:, a * DH : (a + 1) * DH].reshape(8, 16, DH)
    along_clu(lambda to: ex_ret2.at[to], ex_back2, ex_ret2_sem, ex_back2_sem)
    found = bf16_dot(onehot[pl.ds(0, 4 * TOK), :], over_res[...]).astype(jnp.bfloat16)
    for a in range(4):
        table[4, 4 * a : 4 * a + 4] = found[:, a * DH : (a + 1) * DH].reshape(4, TOK, DH)
    arrange(from_table(3), put_in(result_c), 2)
    send_steps(0, devices // 16, *to_c)
    send_own(result_c, back_c.at[me], back_c_sem)

    wait_bytes(ex_back2, ex_back2_sem)
    held = [ex_back2[:, a].reshape(TOK, DH) for a in range(4)]
    held = bf16_dot(to_block[...], jnp.concatenate(held, axis=1))
    held = [held[:, a * DH : (a + 1) * DH].reshape(16, 8, DH) for a in range(4)]
    ex_ret1[...] = jnp.concatenate(held, axis=1).astype(jnp.bfloat16)
    along_seq(lambda to: ex_ret1.at[to], ex_back1, ex_ret1_sem, ex_back1_sem)
    send_steps(devices // 16, devices // 16, *to_c)

    def unpack(tiles, rest, first, count):
        sides = []
        for k in range(2):
            sides.append(
                jnp.concatenate(
                    [tile(k).reshape(TOK, DH) for tile in tiles] + [part(k) for part in rest],
                    axis=0,
                )
            )
        return bf16_dot(
            unpack_mat[:, pl.ds(first, count)], jnp.concatenate(sides, axis=1)
        )

    def tile_of(ref, at, tile):
        return lambda k: ref[pl.ds((2 * at + k) * groups, groups), tile]

    def unpack_early(at, carry):
        tiles = [tile_of(back_a, at, 0), tile_of(back_b, at, 0), tile_of(back_b, at, 1)]
        rest = [
            lambda k: hback[2 * at + k],
            lambda k: ex_back1[2 * at + k],
            lambda k: jnp.zeros((TOK - 48, DH), jnp.bfloat16),
        ]
        early[at] = unpack(tiles, rest, 0, 4 * TOK)
        return carry

    def unpack_last(at, carry):
        cols = pl.ds(pl.multiple_of(at * 2 * DH, 2 * DH), 2 * DH)
        tiles = [tile_of(back_c, at, 0), tile_of(back_c, at, 1)]
        found = (early[at] + unpack(tiles, [], 4 * TOK, 2 * TOK)).astype(jnp.bfloat16)
        for array, ref in enumerate((out_ref, dq_ref, dk_ref, dv_ref)):
            ref[:, cols] = found[array * TOK : (array + 1) * TOK]
        return carry

    wait_bytes(hback, hback_sem)
    wait_bytes(back_a, back_a_sem)
    wait_bytes(back_b, back_b_sem)
    wait_bytes(ex_back1, ex_back1_sem)
    lax.fori_loop(0, heads // 2, unpack_early, 0, unroll=2)
    wait_bytes(back_c, back_c_sem)
    lax.fori_loop(0, heads // 2, unpack_last, 0, unroll=2)

    others = pl.ds(0, devices - 1)
    wait_bytes(cnt_group.at[pl.ds(0, groups - 1)], cnt_send_sem)
    wait_bytes(cnt_recv.at[pl.ds(0, heads - 1)], cnt2_send_sem)
    for ref, sem in ((ex_send, ex_send_sem), (ex_ret1, ex_ret1_sem)):
        wait_bytes(ref.at[pl.ds(0, heads - 1)], sem)
    for ref, sem in ((ex_send2, ex_send2_sem), (ex_ret2, ex_ret2_sem)):
        wait_bytes(ref.at[pl.ds(0, groups - 1)], sem)
    wait_bytes(send_a.at[others], send_a_sem)
    wait_bytes(send_b.at[others], send_b_sem)
    wait_bytes(send_c.at[others], send_c_sem)
    wait_bytes(result_a.at[others], res_a_sem)
    wait_bytes(result_b.at[others], res_b_sem)
    wait_bytes(result_c.at[others], res_c_sem)

    @pl.when(is_heavy_owner)
    def _():
        wait_bytes(hsend.at[pl.ds(0, heads - 1)], hsend_sem)
        wait_bytes(hresult.at[others], hres_sem)

    @pl.when(jnp.logical_not(is_heavy_owner))
    def _():
        wait_bytes(hsend, hsend_sem)


def fast_path(queries, key_rows, value_rows, out_grad, cluster_ids):
    tok_rows, columns = queries.shape
    heads = columns // DH
    groups = lax.axis_size("clu")
    devices = lax.axis_size("seq") * groups
    low = jnp.bfloat16
    wide = jnp.float32
    rows = pltpu.VMEM((tok_rows, columns), low)
    vmem = pl.BlockSpec(memory_space=pltpu.VMEM)
    smem = pl.BlockSpec(memory_space=pltpu.SMEM)
    return pl.pallas_call(
        fast_kernel,
        out_shape=[rows] * 4 + [jax.ShapeDtypeStruct((1, 1), jnp.int32)],
        in_specs=[vmem] + [pl.BlockSpec(memory_space=pl.ANY)] * 4,
        out_specs=[vmem] * 4 + [smem],
        scratch_shapes=[
            pltpu.VMEM((1, TOK), wide),
            pltpu.VMEM((groups, 1, TOK), wide),
            pltpu.VMEM((heads, groups, 1, TOK), wide),
            pltpu.VMEM((5 * TOK + 48, 4 * TOK), low),
            pltpu.VMEM((4 * TOK, 6 * TOK), low),
            pltpu.VMEM((devices, 2, 16, DH), low),
            pltpu.VMEM((devices, 2, 16, DH), low),
            pltpu.VMEM((devices, 1, 16, DH), low),
            pltpu.VMEM((devices, 2, 16, DH), low),
            pltpu.VMEM((devices, 2, 16, DH), low),
            pltpu.VMEM((devices, 1, 16, DH), low),
            pltpu.VMEM((5, 16, devices, DH), low),
            pltpu.VMEM((4, 16, OVC, DH), low),
            pltpu.VMEM((16, TOK + OVC, TOK), wide),
            pltpu.VMEM((16, 8, 2 * TOK), wide),
            pltpu.VMEM((16 * OVC, 5 * TOK), low),
            pltpu.VMEM((5 * TOK, 16 * OVC), low),
            pltpu.VMEM((5 * TOK, 4 * DH), low),
            pltpu.VMEM((16 * OVC, 4 * DH), low),
            pltpu.VMEM((TOK, TOK), low),
            pltpu.VMEM((TOK, TOK), low),
            pltpu.VMEM((devices, 1, 16, DH), low),
            pltpu.VMEM((devices, 2, 16, DH), low),
            pltpu.VMEM((devices, 2, 16, DH), low),
            pltpu.VMEM((devices, 1, 16, DH), low),
            pltpu.VMEM((devices, 2, 16, DH), low),
            pltpu.VMEM((devices, 2, 16, DH), low),
            pltpu.VMEM((heads, 32, DH), low),
            pltpu.VMEM((heads, 32, DH), low),
            pltpu.VMEM((groups, 4, 16, DH), low),
            pltpu.VMEM((groups, 4, 16, DH), low),
            pltpu.VMEM((groups, 4, 16, DH), low),
            pltpu.VMEM((groups, 4, 16, DH), low),
            pltpu.VMEM((heads, 32, DH), low),
            pltpu.VMEM((heads, 32, DH), low),
            pltpu.VMEM((heads, 16, DH), low),
            pltpu.VMEM((devices, 16, DH), low),
            pltpu.VMEM((16, devices, DH), low),
            pltpu.VMEM((4, 4 * TOK, DH), wide),
            pltpu.VMEM((devices, 16, DH), low),
            pltpu.VMEM((heads, 16, DH), low),
            pltpu.VMEM((4, tok_rows, columns), low),
            pltpu.VMEM((heads // 2, 4 * tok_rows, 2 * DH), wide),
        ]
        + [pltpu.SemaphoreType.DMA] * 29,
        compiler_params=pltpu.CompilerParams(
            collective_id=0, has_side_effects=True, vmem_limit_bytes=44 * 1024 * 1024
        ),
    )(cluster_ids.reshape(1, tok_rows), queries, key_rows, value_rows, out_grad)


def copy_kernel(*refs):
    sem = refs[-1]
    copies = [
        pltpu.make_async_copy(refs[i], refs[4 + i], sem.at[i]) for i in range(4)
    ]
    for copy in copies:
        copy.start()
    for copy in copies:
        copy.wait()


def copy_out(arrays):
    anywhere = pl.BlockSpec(memory_space=pl.ANY)
    return pl.pallas_call(
        copy_kernel,
        out_shape=[pltpu.HBM(a.shape, a.dtype) for a in arrays],
        in_specs=[anywhere] * 4,
        out_specs=[anywhere] * 4,
        scratch_shapes=[pltpu.SemaphoreType.DMA((4,))],
    )(*arrays)


def per_device(queries, key_rows, value_rows, out_grad, cluster_ids):
    arrays = (queries, key_rows, value_rows, out_grad, cluster_ids)
    *fast, flag = fast_path(*arrays)
    return lax.cond(
        flag.reshape(()) != 0,
        lambda arrays, fast: full_capacity(*arrays),
        lambda arrays, fast: tuple(copy_out(fast)),
        arrays,
        tuple(fast),
    )


def solution(mesh):
    in_specs = (
        P(("seq", "clu"), None),
        P(("seq", "clu"), None),
        P(("seq", "clu"), None),
        P(("seq", "clu"), None),
        P(("seq", "clu")),
    )
    out_specs = (
        P(("seq", "clu"), None),
        P(("seq", "clu"), None),
        P(("seq", "clu"), None),
        P(("seq", "clu"), None),
    )
    return jax.shard_map(
        per_device, mesh=mesh, in_specs=in_specs, out_specs=out_specs, check_vma=False
    )
```

```python
import math

import jax
import jax.numpy as jnp
from jax import lax
from jax.experimental import pallas as pl
from jax.experimental.pallas import tpu as pltpu
from jax.sharding import PartitionSpec as P

DH = 128
TOK = 128
OVC = 80
SET = 16
FAR = 1e9
MESH = pl.DeviceIdType.MESH


masked = -1e30


def contract_last(left, right):
    return lax.dot_general(
        left, right, (((1,), (1,)), ((), ())), preferred_element_type=jnp.float32
    )


def contract_first(left, right):
    return lax.dot_general(
        left, right, (((0,), (0,)), ((), ())), preferred_element_type=jnp.float32
    )


def softmax_rows(query_head, key_head, allowed, inv_root):
    scores = contract_last(query_head, key_head) * inv_root
    scores = jnp.where(allowed, scores, masked)
    row_max = jnp.max(scores, axis=1, keepdims=True)
    weights = jnp.exp(scores - row_max)
    row_sum = jnp.sum(weights, axis=1, keepdims=True)
    return (weights / row_sum).astype(jnp.bfloat16)


def head_slice(array, head_index):
    return lax.dynamic_slice_in_dim(array, head_index * DH, DH, 1)


def full_capacity(queries, key_rows, value_rows, out_grad, cluster_ids):
    seq_count = lax.axis_size("seq")
    clu_count = lax.axis_size("clu")
    devices = seq_count * clu_count
    tok_rows = queries.shape[0]
    columns = queries.shape[1]
    head_count = columns // DH
    most_rows = 4 * tok_rows // devices
    capacity = most_rows * devices
    inv_root = 1.0 / math.sqrt(DH)
    owners = jnp.arange(devices, dtype=jnp.int32)
    member = (cluster_ids[:, None] == owners[None, :]).astype(jnp.int32)
    running = jnp.cumsum(member, axis=0) - 1
    slot_rank = jnp.sum(member * running, axis=1)
    sent_counts = jnp.sum(member, axis=0).reshape(devices, 1)
    slot_index = cluster_ids * most_rows + slot_rank
    stacked = jnp.concatenate([queries, key_rows, value_rows], axis=1)
    width_in = stacked.shape[1]
    packed = jnp.zeros((devices * most_rows, width_in), jnp.bfloat16).at[slot_index].set(stacked)
    packed = packed.reshape(devices, most_rows, width_in)
    got_rows, got_counts = (
        lax.all_to_all(packed, ("seq", "clu"), split_axis=0, concat_axis=0, tiled=True),
        lax.all_to_all(sent_counts, ("seq", "clu"), split_axis=0, concat_axis=0, tiled=True),
    )
    got_counts = got_counts.reshape(devices)
    starts = jnp.cumsum(got_counts) - got_counts
    live_total = jnp.sum(got_counts)
    within = jnp.arange(most_rows, dtype=jnp.int32)
    target = jnp.where(
        within[None, :] < got_counts[:, None], starts[:, None] + within[None, :], capacity
    )
    target = target.reshape(devices * most_rows)
    gathered = (
        jnp.zeros((capacity, width_in), jnp.bfloat16)
        .at[target]
        .set(got_rows.reshape(devices * most_rows, width_in), mode="drop")
    )
    query_block = gathered[:, :columns]
    key_block = gathered[:, columns : 2 * columns]
    value_block = gathered[:, 2 * columns : 3 * columns]
    positions = jnp.arange(capacity, dtype=jnp.int32)
    allowed = (positions[None, :] <= positions[:, None]) & (positions[None, :] < live_total)

    def forward_head(head_index, mixed_rows):
        weights_low = softmax_rows(
            head_slice(query_block, head_index),
            head_slice(key_block, head_index),
            allowed,
            inv_root,
        )
        out_head = jnp.dot(
            weights_low, head_slice(value_block, head_index), preferred_element_type=jnp.float32
        ).astype(jnp.bfloat16)
        return lax.dynamic_update_slice_in_dim(mixed_rows, out_head, head_index * DH, 1)

    mixed_rows = lax.fori_loop(
        0, head_count, forward_head, jnp.zeros((capacity, columns), jnp.bfloat16)
    )
    back_index = jnp.minimum(target, capacity - 1)
    outgoing = jnp.take(mixed_rows, back_index, axis=0).reshape(devices, most_rows, columns)
    grad_packed = (
        jnp.zeros((devices * most_rows, columns), jnp.bfloat16).at[slot_index].set(out_grad)
    )
    grad_packed = grad_packed.reshape(devices, most_rows, columns)
    returned = lax.all_to_all(outgoing, ("seq", "clu"), split_axis=0, concat_axis=0, tiled=True)
    got_grad = lax.all_to_all(grad_packed, ("seq", "clu"), split_axis=0, concat_axis=0, tiled=True)
    attention_out = jnp.take(returned.reshape(devices * most_rows, columns), slot_index, axis=0)
    grad_block = (
        jnp.zeros((capacity, columns), jnp.bfloat16)
        .at[target]
        .set(got_grad.reshape(devices * most_rows, columns), mode="drop")
    )
    delta_rows = jnp.sum(
        (grad_block.astype(jnp.float32) * mixed_rows.astype(jnp.float32)).reshape(
            capacity, head_count, DH
        ),
        axis=2,
    )

    def backward_head(head_index, grad_rows):
        query_head = head_slice(query_block, head_index)
        key_head = head_slice(key_block, head_index)
        value_head = head_slice(value_block, head_index)
        grad_head = head_slice(grad_block, head_index)
        weights_low = softmax_rows(query_head, key_head, allowed, inv_root)
        prob_grad = contract_last(grad_head, value_head)
        delta_head = lax.dynamic_slice_in_dim(delta_rows, head_index, 1, 1)
        score_grad = (weights_low.astype(jnp.float32) * (prob_grad - delta_head)).astype(
            jnp.bfloat16
        )
        query_part = (
            jnp.dot(score_grad, key_head, preferred_element_type=jnp.float32) * inv_root
        ).astype(jnp.bfloat16)
        key_part = (contract_first(score_grad, query_head) * inv_root).astype(jnp.bfloat16)
        value_part = contract_first(weights_low, grad_head).astype(jnp.bfloat16)
        grad_rows = lax.dynamic_update_slice_in_dim(grad_rows, query_part, head_index * DH, 1)
        grad_rows = lax.dynamic_update_slice_in_dim(
            grad_rows, key_part, columns + head_index * DH, 1
        )
        return lax.dynamic_update_slice_in_dim(
            grad_rows, value_part, 2 * columns + head_index * DH, 1
        )

    grad_rows = lax.fori_loop(
        0, head_count, backward_head, jnp.zeros((capacity, 3 * columns), jnp.bfloat16)
    )
    outgoing_grads = jnp.take(grad_rows, back_index, axis=0).reshape(
        devices, most_rows, 3 * columns
    )
    returned_grads = lax.all_to_all(
        outgoing_grads, ("seq", "clu"), split_axis=0, concat_axis=0, tiled=True
    )
    picked = jnp.take(returned_grads.reshape(devices * most_rows, 3 * columns), slot_index, axis=0)
    return (
        attention_out,
        picked[:, :columns],
        picked[:, columns : 2 * columns],
        picked[:, 2 * columns :],
    )


def bf16_dot(left, right):
    return jnp.dot(left, right, preferred_element_type=jnp.float32)


def flip_perm():
    row = lax.broadcasted_iota(jnp.int32, (SET * 16, SET * 16), 0)
    col = lax.broadcasted_iota(jnp.int32, (SET * 16, SET * 16), 1)
    swapped = (col % 16) * 16 + col // 16
    return (row == swapped).astype(jnp.float32).astype(jnp.bfloat16)


def attend(q, k, v, g, allowed, inv_root):
    raw = jnp.where(allowed, contract_last(k, q), masked)
    most = jnp.max(raw, axis=0, keepdims=True)
    weights = jnp.exp2((raw - most) * (inv_root * math.log2(math.e)))
    prob = weights * (1.0 / jnp.sum(weights, axis=0, keepdims=True))
    prob_low = prob.astype(jnp.bfloat16)
    prob_grad = contract_last(v, g)
    delta = jnp.sum(prob * prob_grad, axis=0, keepdims=True)
    score_grad = (prob * (prob_grad - delta)).astype(jnp.bfloat16)
    out = contract_first(v, prob_low).T.astype(jnp.bfloat16)
    dq = (contract_first(k, score_grad).T * inv_root).astype(jnp.bfloat16)
    dk = bf16_dot(score_grad, q) * inv_root
    dv = bf16_dot(prob_low, g)
    return out, dq, dk, dv


def fast_kernel(
    ids_ref, q_ref, k_ref, v_ref, g_ref,
    out_ref, dq_ref, dk_ref, dv_ref, flag_ref,
    cnt_send, cnt_group, cnt_recv, pack_mat, unpack_mat,
    send_a, send_b, send_c, recv_a, recv_b, recv_c, table,
    over, key_pos, query_pos, pick, onehot, loose, over_res, to_mate, to_block,
    result_a, result_b, result_c, back_a, back_b, back_c,
    ex_send, ex_recv, ex_send2, ex_recv2, ex_ret2, ex_back2, ex_ret1, ex_back1,
    hsend, hrecv, htable, hacc, hresult, hback, inputs, early,
    cnt_send_sem, cnt_sem, cnt2_send_sem, cnt2_sem,
    send_a_sem, recv_a_sem, send_b_sem, recv_b_sem, send_c_sem, recv_c_sem,
    res_a_sem, back_a_sem, res_b_sem, back_b_sem, res_c_sem, back_c_sem,
    ex_send_sem, ex_recv_sem, ex_send2_sem, ex_recv2_sem,
    ex_ret2_sem, ex_back2_sem, ex_ret1_sem, ex_back1_sem,
    hsend_sem, hrecv_sem, hres_sem, hback_sem, input_sem,
):
    seq_at = lax.axis_index("seq")
    clu_at = lax.axis_index("clu")
    groups = lax.axis_size("clu")
    heads = lax.axis_size("seq")
    devices = heads * groups
    me = seq_at * groups + clu_at
    inv_root = 1.0 / math.sqrt(DH)
    is_heavy_owner = lax.rem(seq_at, groups) == clu_at
    at_x, at_z = lax.div(seq_at, 4), lax.rem(seq_at, 4)
    at_y, at_core = lax.div(clu_at, 2), lax.rem(clu_at, 2)

    def by_core(first, second):
        return first + at_core * (second - first)

    eight = []
    for by_x, by_z, by_clu in zip(
        zip((3, 2, 3, 1, 3, 0, 2, 0), (2, 2, 1, 0, 2, 3, 0, 2)),
        zip((0, 0, 2, 3, 1, 2, 3, 1), (2, 2, 0, 1, 3, 0, 0, 2)),
        zip((2, 1, 3, 0, 6, 4, 5, 7), (6, 5, 7, 4, 2, 0, 1, 3)),
    ):
        y = lax.rem(at_y + by_core(by_clu[0] // 2, by_clu[1] // 2), 4)
        core = lax.rem(at_core + by_core(by_clu[0] % 2, by_clu[1] % 2), 2)
        eight.append((by_core(*by_x), by_core(*by_z), y * 2 + core))

    def for_peers(first, count, visit):
        def one_eight(step, carry):
            by = lax.rem(step * 13 + at_core * 12, 16)
            x = at_x + lax.div(by, 4)
            z = at_z + lax.rem(by, 4)
            for j, (more_x, more_z, clu_to) in enumerate(eight):
                seq_to = lax.rem(x + more_x, 4) * 4 + lax.rem(z + more_z, 4)
                if j in (3, 5):
                    pl.when(seq_to * groups + clu_to != me)(lambda: visit(seq_to, clu_to))
                else:
                    visit(seq_to, clu_to)
            return carry

        lax.fori_loop(first, first + count, one_eight, 0)

    def send_steps(first, count, source, target, send_sem, recv_sem):
        def start(seq_to, clu_to):
            pltpu.make_async_remote_copy(
                src_ref=source.at[seq_to * groups + clu_to],
                dst_ref=target,
                send_sem=send_sem,
                recv_sem=recv_sem,
                device_id=(seq_to, clu_to),
                device_id_type=MESH,
            ).start()

        for_peers(first, count, start)

    def send_own(source, target, recv_sem):
        pltpu.make_async_copy(source.at[me], target, recv_sem).start()

    def send_to_all(source, target, send_sem, recv_sem):
        send_steps(0, devices // 8, source, target, send_sem, recv_sem)
        send_own(source, target, recv_sem)

    def wait_bytes(ref, sem):
        pltpu.make_async_copy(ref, ref, sem).wait()

    for array, ref in enumerate((q_ref, k_ref, v_ref, g_ref)):
        pltpu.make_async_copy(ref, inputs.at[array], input_sem).start()
    barrier = pltpu.get_barrier_semaphore()

    def greet(seq_to, clu_to):
        pl.semaphore_signal(barrier, inc=1, device_id=(seq_to, clu_to), device_id_type=MESH)

    for_peers(0, devices // 8, greet)

    sub = lax.broadcasted_iota(jnp.int32, (TOK, TOK), 0)
    lane = lax.broadcasted_iota(jnp.int32, (TOK, TOK), 1)
    sub_f = sub.astype(jnp.float32)
    lane_f = lane.astype(jnp.float32)
    ids_l = jnp.broadcast_to(ids_ref[...].astype(jnp.float32), (TOK, TOK))
    ids_s = ids_l.T
    one = jnp.ones((TOK, TOK), jnp.float32)
    zero = jnp.zeros((TOK, TOK), jnp.float32)
    same = ids_l == ids_s
    rank_l = jnp.sum(jnp.where(same & (sub < lane), one, zero), axis=0, keepdims=True)
    rank_s = jnp.sum(jnp.where(same & (lane < sub), one, zero), axis=1, keepdims=True)
    count_l = jnp.sum(jnp.where(same, one, zero), axis=0, keepdims=True)
    cnt_send[...] = jnp.sum(jnp.where(ids_s == lane_f, one, zero), axis=0, keepdims=True)
    ids_row = ids_l[0:1, :]
    heavy = jnp.min(jnp.where(count_l == 4.0, ids_row, 999.0), axis=1, keepdims=True)
    group_l = jnp.floor(ids_l * (1.0 / 16.0))
    group_s = jnp.floor(ids_s * (1.0 / 16.0))
    earlier = (ids_s < ids_l) | (same & (sub < lane))
    later = (ids_l < ids_s) | (same & (lane < sub))
    before = (group_l == group_s) & (ids_s != heavy) & (rank_s >= 1.0) & earlier
    over_at = jnp.sum(jnp.where(before, one, zero), axis=0, keepdims=True)
    behind = (group_l == group_s) & (ids_l != heavy) & (rank_l >= 1.0) & later
    over_at_s = jnp.sum(jnp.where(behind, one, zero), axis=1, keepdims=True)
    excess_s = (ids_s != heavy) & (rank_s >= 1.0) & (over_at_s >= 4.0)
    excess_at = jnp.sum(jnp.where(excess_s & earlier, one, zero), axis=0, keepdims=True)
    light_l = ids_l != heavy
    slot_group = (sub // 16).astype(jnp.float32)
    in_tile = sub % 16
    over_l = light_l & (rank_l >= 1.0)

    def tile_picks(tile):
        at_slot = (in_tile % 4).astype(jnp.float32)
        if tile < 4:
            cluster = slot_group * 16.0 + at_slot + 4.0 * tile
            taken = (ids_l == cluster) & (rank_l == 0.0) & light_l
        else:
            taken = (group_l == slot_group) & over_l & (over_at == at_slot)
        return [jnp.where(taken & (in_tile // 4 == array), one, zero) for array in range(4)]

    def rest_picks():
        picks = []
        for array in range(4):
            chosen = (ids_l == heavy) & (rank_l == (sub % 4).astype(jnp.float32))
            chosen = chosen & (sub // 4 == array) & (sub < 16)
            beyond = over_l & (over_at >= 4.0) & (excess_at == (sub % 8).astype(jnp.float32))
            beyond = beyond & (sub // 8 == array + 2)
            picks.append(jnp.where(chosen | beyond, one, zero))
        return picks

    def put_pack(at_row, count, picks):
        for array, matrix in enumerate(picks):
            pack_mat[pl.ds(at_row, count), pl.ds(array * TOK, TOK)] = matrix[:count].astype(
                jnp.bfloat16
            )

    put_pack(0, TOK, tile_picks(0))
    put_pack(TOK, TOK, tile_picks(4))
    put_pack(2 * TOK, 48, rest_picks())


    def send_line(source, target, count, at, device, send_sem, recv_sem):
        def one_peer(step, carry):
            to = lax.rem(at + step, count)
            pltpu.make_async_remote_copy(
                src_ref=source(to),
                dst_ref=target,
                send_sem=send_sem,
                recv_sem=recv_sem,
                device_id=device(to),
                device_id_type=MESH,
            ).start()
            return carry

        lax.fori_loop(1, count, one_peer, 0)
        pltpu.make_async_copy(source(at), target, recv_sem).start()

    def along_seq(source, target, send_sem, recv_sem):
        send_line(
            source, target.at[seq_at], heads, seq_at, lambda to: (to, clu_at), send_sem, recv_sem
        )

    def along_clu(source, target, send_sem, recv_sem):
        send_line(
            source, target.at[clu_at], groups, clu_at, lambda to: (seq_at, to), send_sem, recv_sem
        )


    def head_rows(at):
        cols = pl.ds(pl.multiple_of(at * 2 * DH, 2 * DH), 2 * DH)
        return [inputs[array, :, cols] for array in range(4)]

    def put_tile(target, at, tile, packed):
        low = packed.astype(jnp.bfloat16)
        for k in range(2):
            target[pl.ds((2 * at + k) * groups, groups), tile] = low[
                :, k * DH : (k + 1) * DH
            ].reshape(groups, 16, DH)

    def pack_a(at, carry):
        rows = jnp.concatenate(head_rows(at), axis=0)
        packed = bf16_dot(pack_mat[pl.ds(0, 2 * TOK + 48), :], rows)
        put_tile(send_a, at, 0, packed[:TOK])
        put_tile(send_a, at, 1, packed[TOK : 2 * TOK])
        rest = packed[2 * TOK :].astype(jnp.bfloat16)
        for k in range(2):
            hsend[2 * at + k] = rest[:16, k * DH : (k + 1) * DH]
            ex_send[2 * at + k] = rest[16:, k * DH : (k + 1) * DH]
        return carry

    wait_bytes(inputs, input_sem)
    lax.fori_loop(0, heads // 2, pack_a, 0, unroll=4)
    pl.semaphore_wait(barrier, devices - 1)
    along_clu(lambda to: cnt_send, cnt_group, cnt_send_sem, cnt_sem)

    def send_heavy(step, carry):
        head = lax.rem(seq_at + step, heads)
        clu_to = lax.rem(head, groups)

        @pl.when(head * groups + clu_to != me)
        def _():
            pltpu.make_async_remote_copy(
                src_ref=hsend.at[head],
                dst_ref=hrecv.at[me],
                send_sem=hsend_sem,
                recv_sem=hrecv_sem,
                device_id=(head, clu_to),
                device_id_type=MESH,
            ).start()

        @pl.when(head * groups + clu_to == me)
        def _():
            pltpu.make_async_copy(hsend.at[head], hrecv.at[me], hrecv_sem).start()

        return carry

    lax.fori_loop(0, heads, send_heavy, 0)
    along_seq(lambda to: ex_send.at[to], ex_recv, ex_send_sem, ex_recv_sem)
    out_a = (send_a, recv_a.at[me], send_a_sem, recv_a_sem)
    send_steps(0, 4, *out_a)
    wait_bytes(cnt_group, cnt_sem)
    along_seq(lambda to: cnt_group, cnt_recv, cnt2_send_sem, cnt2_sem)
    send_steps(4, devices // 8 - 4, *out_a)
    send_own(send_a, recv_a.at[me], recv_a_sem)

    for tile in range(1, 4):
        put_pack((tile + 1) * TOK + 48, TOK, tile_picks(tile))

    def pack_bc(at, carry):
        rows = jnp.concatenate(head_rows(at), axis=0)
        packed = bf16_dot(pack_mat[pl.ds(2 * TOK + 48, 3 * TOK), :], rows)
        put_tile(send_b, at, 0, packed[:TOK])
        put_tile(send_b, at, 1, packed[TOK : 2 * TOK])
        put_tile(send_c, at, 0, packed[2 * TOK :])
        return carry

    lax.fori_loop(0, heads // 2, pack_bc, 0)

    wait_bytes(cnt_recv, cnt2_sem)
    seen = cnt_recv[...].reshape(TOK, TOK)
    heavies = jnp.min(jnp.where(seen == 4.0, lane_f, 999.0), axis=1, keepdims=True)
    heavy_all = jnp.min(heavies, axis=0, keepdims=True)
    light = lane_f != heavy_all
    more = jnp.where(light, jnp.maximum(seen - 1.0, 0.0), 0.0)
    more_low = more.astype(jnp.bfloat16)
    in_group = jnp.where(sub // 16 == lane, one, zero).astype(jnp.bfloat16)
    ahead = jnp.where(sub < lane, one, zero).astype(jnp.bfloat16)
    prior = jnp.where(lane < sub, one, zero).astype(jnp.bfloat16)
    mates = (lane < sub) & (lane % 8 == sub % 8)
    mates = jnp.where(mates, one, zero).astype(jnp.bfloat16)
    excess = jnp.maximum(bf16_dot(more_low, in_group) - 4.0, 0.0)
    excess_low = excess.astype(jnp.bfloat16)
    excess_off = bf16_dot(excess_low, ahead)
    excess_pre = bf16_dot(mates, excess_low)
    bad = (jnp.sum(excess, axis=1, keepdims=True) > 8.0) | (excess_pre + excess > 16.0)
    bad = bad | (heavies != heavy_all) | (jnp.sum(more, axis=0, keepdims=True) > OVC)
    flag_ref[0, 0] = jnp.max(jnp.where(bad, one, zero)).astype(jnp.int32)

    spot = zero
    for group in range(8):
        off, count, pre = [a[:, group : group + 1] for a in (excess_off, excess, excess_pre)]
        held = (lane_f >= off) & (lane_f < off + count)
        spot = spot + jnp.where(held, lane_f + (group * 16 + 1.0) - off + pre, zero)
    spot = jnp.where(sub % 8 == clu_at, spot, zero).reshape(16, 8, TOK)
    spot = jnp.sum(spot, axis=1).astype(jnp.bfloat16)
    spread8 = jnp.where(lane % 8 == sub, one, zero).astype(jnp.bfloat16)
    spot = jnp.where(lane[:16] // 8 == sub[:16], bf16_dot(spot, spread8), 0.0)
    spot = jnp.sum(spot, axis=0, keepdims=True) - 1.0
    to_mate[...] = jnp.where(sub_f == spot, one, zero).astype(jnp.bfloat16)
    spot = jnp.broadcast_to(spot, (TOK, TOK)).T
    to_block[...] = jnp.where(spot == lane_f, one, zero).astype(jnp.bfloat16)

    wait_bytes(ex_recv, ex_recv_sem)
    held = ex_recv[...].astype(jnp.float32)
    held = [held[:, 8 * a : 8 * a + 8, :].reshape(TOK, DH) for a in range(4)]
    held = jnp.concatenate(held, axis=1).astype(jnp.bfloat16)
    held = bf16_dot(to_mate[...], held).astype(jnp.bfloat16)
    for a in range(4):
        ex_send2[:, a] = held[:, a * DH : (a + 1) * DH].reshape(8, 16, DH)
    along_clu(lambda to: ex_send2.at[to], ex_recv2, ex_send2_sem, ex_recv2_sem)
    send_to_all(send_b, recv_b.at[me], send_b_sem, recv_b_sem)
    send_to_all(send_c, recv_c.at[me], send_c_sem, recv_c_sem)

    valid = jnp.where((seen > 0.0) & light, one, zero).astype(jnp.bfloat16)
    mine = (sub == clu_at * 16 + lane) & (lane < 16)
    mine = jnp.where(mine, one, zero).astype(jnp.bfloat16)
    more_g = bf16_dot(more_low, mine)
    valid_g = bf16_dot(valid, mine)
    more_g_low = more_g.astype(jnp.bfloat16)
    start_g = bf16_dot(prior, more_g_low)
    offset_g = bf16_dot(more_g_low, ahead)
    beyond_g = jnp.maximum(bf16_dot(more_g_low, one.astype(jnp.bfloat16)) - 4.0, 0.0)
    pre_g = bf16_dot(mates, beyond_g.astype(jnp.bfloat16))
    ex_index = lane_f - pre_g + 4.0
    first_row = lax.broadcasted_iota(jnp.int32, (1, TOK), 1).astype(jnp.float32) * 16.0
    in_tile_at = zero
    beyond_at = zero
    for c in range(16):
        count, begin, off, real = [
            a[:, c : c + 1] for a in (more_g, start_g, offset_g, valid_g)
        ]
        place = begin - off + (c * OVC + 1.0)
        held = (lane_f >= off) & (lane_f < off + count) & (lane < 4)
        in_tile_at = in_tile_at + jnp.where(held, lane_f + place, zero)
        held = (ex_index >= off) & (ex_index < off + count) & (ex_index >= 4.0)
        beyond_at = beyond_at + jnp.where(held, ex_index + place, zero)
        held = (lane_f >= begin) & (lane_f < begin + count)
        where = jnp.where(held, sub_f * 16.0 + 1.0 + lane_f - begin, zero)
        where = jnp.sum(where, axis=0, keepdims=True)
        where = jnp.where(where > 0.0, where, FAR)
        query_row = jnp.concatenate([first_row, where], axis=1)
        query_pos[c] = jnp.broadcast_to(query_row, (8, 2 * TOK))
        key_pos[c, pl.ds(0, TOK), :] = jnp.where(real > 0.0, sub_f * 16.0, FAR)
        key_pos[c, pl.ds(TOK, OVC), :] = jnp.broadcast_to(where, (TOK, TOK)).T[:OVC]
    beyond_at = jnp.sum(beyond_at.reshape(16, 8, TOK), axis=0)
    high = jnp.floor(beyond_at * (1.0 / 32.0))
    split = jnp.concatenate([high, beyond_at - high * 32.0], axis=0).astype(jnp.bfloat16)
    spread16 = jnp.where(lane % 16 == sub, one, zero).astype(jnp.bfloat16)
    split = bf16_dot(split, spread16)
    split = jnp.where(lane[:8] // 16 == sub[:8], split[:8] * 32.0 + split[8:], 0.0)
    beyond_row = jnp.sum(split, axis=0, keepdims=True) - 1.0
    tile_rows = in_tile_at.T[0:8, :] - 1.0
    slot_rows = [tile_rows[k : k + 1, :] for k in range(4)] + [beyond_row]
    slot_cols = [in_tile_at[:, k : k + 1] - 1.0 for k in range(4)]
    slot_cols.append(jnp.broadcast_to(beyond_row, (TOK, TOK)).T)

    chunk = 4
    for k in range(5):
        for m in range(16 * OVC // TOK):
            onehot[pl.ds(k * TOK, TOK), pl.ds(m * TOK, TOK)] = jnp.where(
                slot_cols[k] == lane_f + float(m * TOK), one, zero
            ).astype(jnp.bfloat16)
            pick[pl.ds(m * TOK, TOK), pl.ds(k * TOK, TOK)] = jnp.where(
                slot_rows[k] == sub_f + float(m * TOK), one, zero
            ).astype(jnp.bfloat16)

    for at, tile in enumerate((0, 1, 2, 3, 4, None)):
        for array, matrix in enumerate(rest_picks() if tile is None else tile_picks(tile)):
            unpack_mat[pl.ds(array * TOK, TOK), pl.ds(at * TOK, TOK)] = matrix.T.astype(
                jnp.bfloat16
            )

    perm = flip_perm()

    def arrange(source, target, units):
        def two_sets(at, carry):
            blocks = [pl.ds(pl.multiple_of((2 * at + i) * SET, SET), SET) for i in range(2)]
            spots = [(held, unit) for held in blocks for unit in range(units)]
            rows = jnp.concatenate(
                [source(held, unit).reshape(SET * 16, DH) for held, unit in spots], axis=1
            )
            turned = bf16_dot(perm, rows).astype(jnp.bfloat16)
            for i, (held, unit) in enumerate(spots):
                target(held, unit, turned[:, i * DH : (i + 1) * DH].reshape(16, SET, DH))
            return carry

        lax.fori_loop(0, devices // (2 * SET), two_sets, 0, unroll=2)

    def put_table(first):
        def put(blocks, unit, value):
            table[first + unit, :, blocks, :] = value

        return put

    wait_bytes(recv_a, recv_a_sem)
    def put_tile_a(blocks, unit, value):
        table[4 * unit, :, blocks, :] = value

    arrange(lambda blocks, unit: recv_a[blocks, unit], put_tile_a, 2)

    wait_bytes(ex_recv2, ex_recv2_sem)
    for a in range(4):
        cols = pl.ds(a * DH, DH)
        loose[pl.ds(0, 4 * TOK), cols] = table[4, 4 * a : 4 * a + 4].reshape(4 * TOK, DH)
        loose[pl.ds(4 * TOK, TOK), cols] = ex_recv2[:, a].reshape(TOK, DH)

    def gather_chunk(at, carry):
        chosen = pick[pl.ds(pl.multiple_of(at * chunk * OVC, 64), chunk * OVC), :]
        found = bf16_dot(chosen, loose[...]).astype(jnp.bfloat16)
        for c in range(chunk):
            for array in range(4):
                over[array, at * chunk + c] = found[
                    c * OVC : (c + 1) * OVC, array * DH : (array + 1) * DH
                ]
        return carry

    gather_chunk(0, 0)

    pad_rows = jnp.zeros((TOK - OVC, DH), jnp.bfloat16)

    def load_cluster(tile, j):
        c = tile * 4 + j
        rows = [
            jnp.concatenate([table[tile, a * 4 + j], over[a, c]], axis=0) for a in range(4)
        ]
        for a in (0, 3):
            rows[a] = jnp.concatenate([rows[a], pad_rows], axis=0)
        key_at = key_pos[c]
        allowed = jnp.concatenate([key_at, key_at], axis=1) <= query_pos[c, 0:1, :]
        return rows + [allowed]

    def attend_tiles(first, tiles):
        def one_tile(at, carry):
            tile = first + at
            spots = range(4)
            loaded = [load_cluster(tile, j) for j in spots]
            found = [attend(*arrays, inv_root) for arrays in loaded]
            for j, results in zip(spots, found):
                c = tile * 4 + j
                for a, value in enumerate(results):
                    value = value.astype(jnp.bfloat16)
                    table[tile, a * 4 + j] = value[:TOK]
                    over_res[
                        pl.ds(pl.multiple_of(c * OVC, 16), OVC), pl.ds(a * DH, DH)
                    ] = value[TOK : TOK + OVC]
            return carry

        lax.fori_loop(0, tiles, one_tile, 0)

    def put_in(result):
        def put(blocks, unit, value):
            result[blocks, unit] = value

        return put

    def from_table(first):
        return lambda blocks, unit: table[first + unit, :, blocks, :]

    to_a = (result_a, back_a.at[me], res_a_sem, back_a_sem)
    to_b = (result_b, back_b.at[me], res_b_sem, back_b_sem)
    to_c = (result_c, back_c.at[me], res_c_sem, back_c_sem)
    attend_tiles(0, 1)
    arrange(from_table(0), put_in(result_a), 1)
    send_to_all(*to_a)
    lax.fori_loop(1, 16 // chunk, gather_chunk, 0)

    wait_bytes(recv_b, recv_b_sem)
    arrange(lambda blocks, unit: recv_b[blocks, unit], put_table(1), 2)
    attend_tiles(1, 2)
    arrange(from_table(1), put_in(result_b), 2)
    send_to_all(*to_b)

    wait_bytes(recv_c, recv_c_sem)
    arrange(lambda blocks, unit: recv_c[blocks, 0], put_table(3), 1)
    attend_tiles(3, 1)

    found = bf16_dot(onehot[pl.ds(4 * TOK, TOK), :], over_res[...]).astype(jnp.bfloat16)
    for a in range(4):
        ex_ret2[:, a] = found[:, a * DH : (a + 1) * DH].reshape(8, 16, DH)
    along_clu(lambda to: ex_ret2.at[to], ex_back2, ex_ret2_sem, ex_back2_sem)
    found = bf16_dot(onehot[pl.ds(0, 4 * TOK), :], over_res[...]).astype(jnp.bfloat16)
    for a in range(4):
        table[4, 4 * a : 4 * a + 4] = found[:, a * DH : (a + 1) * DH].reshape(4, TOK, DH)
    arrange(from_table(3), put_in(result_c), 2)
    send_steps(0, devices // 16, *to_c)
    send_own(result_c, back_c.at[me], back_c_sem)

    wait_bytes(ex_back2, ex_back2_sem)
    held = [ex_back2[:, a].reshape(TOK, DH) for a in range(4)]
    held = bf16_dot(to_block[...], jnp.concatenate(held, axis=1))
    held = [held[:, a * DH : (a + 1) * DH].reshape(16, 8, DH) for a in range(4)]
    ex_ret1[...] = jnp.concatenate(held, axis=1).astype(jnp.bfloat16)
    along_seq(lambda to: ex_ret1.at[to], ex_back1, ex_ret1_sem, ex_back1_sem)
    send_steps(devices // 16, devices // 16, *to_c)

    @pl.when(is_heavy_owner)
    def _():
        wait_bytes(hrecv, hrecv_sem)

        def put_heavy(blocks, unit, value):
            htable[:, blocks, :] = value

        arrange(lambda blocks, unit: hrecv[blocks], put_heavy, 1)
        k_h, v_h = [htable[4 * a : 4 * a + 4].reshape(4 * TOK, DH) for a in (1, 2)]
        hacc[...] = jnp.zeros_like(hacc)
        key_sub = lax.broadcasted_iota(jnp.int32, (4 * TOK, TOK), 0)
        key_at = lax.rem(key_sub, TOK) * 4 + lax.div(key_sub, TOK)
        query_at = lax.broadcasted_iota(jnp.int32, (4 * TOK, TOK), 1) * 4

        def heavy_tile(s, carry):
            out, dq, dk, dv = attend(
                htable[s], k_h, v_h, htable[12 + s], key_at <= query_at + s, inv_root
            )
            hacc[2, pl.ds(pl.multiple_of(s * TOK, TOK), TOK)] = out.astype(jnp.float32)
            hacc[3, pl.ds(pl.multiple_of(s * TOK, TOK), TOK)] = dq.astype(jnp.float32)
            hacc[0] += dk
            hacc[1] += dv
            return carry

        lax.fori_loop(0, 4, heavy_tile, 0)
        for array, at in enumerate((2, 3, 0, 1)):
            htable[4 * array : 4 * array + 4] = (
                hacc[at].astype(jnp.bfloat16).reshape(4, TOK, DH)
            )

        def put_hresult(blocks, unit, value):
            hresult[blocks] = value

        arrange(lambda blocks, unit: htable[:, blocks, :], put_hresult, 1)
        send_to_all(hresult, hback.at[seq_at], hres_sem, hback_sem)

    def unpack(tiles, rest, first, count):
        sides = []
        for k in range(2):
            sides.append(
                jnp.concatenate(
                    [tile(k).reshape(TOK, DH) for tile in tiles] + [part(k) for part in rest],
                    axis=0,
                )
            )
        return bf16_dot(
            unpack_mat[:, pl.ds(first, count)], jnp.concatenate(sides, axis=1)
        )

    def tile_of(ref, at, tile):
        return lambda k: ref[pl.ds((2 * at + k) * groups, groups), tile]

    def unpack_early(at, carry):
        tiles = [tile_of(back_a, at, 0), tile_of(back_b, at, 0), tile_of(back_b, at, 1)]
        early[at] = unpack(tiles, [], 0, 3 * TOK)
        return carry

    def unpack_last(at, carry):
        cols = pl.ds(pl.multiple_of(at * 2 * DH, 2 * DH), 2 * DH)
        tiles = [tile_of(back_c, at, 0), tile_of(back_c, at, 1)]
        rest = [
            lambda k: hback[2 * at + k],
            lambda k: ex_back1[2 * at + k],
            lambda k: jnp.zeros((TOK - 48, DH), jnp.bfloat16),
        ]
        found = (early[at] + unpack(tiles, rest, 3 * TOK, 3 * TOK)).astype(jnp.bfloat16)
        for array, ref in enumerate((out_ref, dq_ref, dk_ref, dv_ref)):
            ref[:, cols] = found[array * TOK : (array + 1) * TOK]
        return carry

    wait_bytes(back_a, back_a_sem)
    wait_bytes(back_b, back_b_sem)
    lax.fori_loop(0, heads // 2, unpack_early, 0, unroll=2)
    wait_bytes(ex_back1, ex_back1_sem)
    wait_bytes(hback, hback_sem)
    wait_bytes(back_c, back_c_sem)
    lax.fori_loop(0, heads // 2, unpack_last, 0, unroll=2)

    others = pl.ds(0, devices - 1)
    wait_bytes(cnt_group.at[pl.ds(0, groups - 1)], cnt_send_sem)
    wait_bytes(cnt_recv.at[pl.ds(0, heads - 1)], cnt2_send_sem)
    for ref, sem in ((ex_send, ex_send_sem), (ex_ret1, ex_ret1_sem)):
        wait_bytes(ref.at[pl.ds(0, heads - 1)], sem)
    for ref, sem in ((ex_send2, ex_send2_sem), (ex_ret2, ex_ret2_sem)):
        wait_bytes(ref.at[pl.ds(0, groups - 1)], sem)
    wait_bytes(send_a.at[others], send_a_sem)
    wait_bytes(send_b.at[others], send_b_sem)
    wait_bytes(send_c.at[others], send_c_sem)
    wait_bytes(result_a.at[others], res_a_sem)
    wait_bytes(result_b.at[others], res_b_sem)
    wait_bytes(result_c.at[others], res_c_sem)

    @pl.when(is_heavy_owner)
    def _():
        wait_bytes(hsend.at[pl.ds(0, heads - 1)], hsend_sem)
        wait_bytes(hresult.at[others], hres_sem)

    @pl.when(jnp.logical_not(is_heavy_owner))
    def _():
        wait_bytes(hsend, hsend_sem)


def fast_path(queries, key_rows, value_rows, out_grad, cluster_ids):
    tok_rows, columns = queries.shape
    heads = columns // DH
    groups = lax.axis_size("clu")
    devices = lax.axis_size("seq") * groups
    low = jnp.bfloat16
    wide = jnp.float32
    rows = pltpu.VMEM((tok_rows, columns), low)
    vmem = pl.BlockSpec(memory_space=pltpu.VMEM)
    smem = pl.BlockSpec(memory_space=pltpu.SMEM)
    return pl.pallas_call(
        fast_kernel,
        out_shape=[rows] * 4 + [jax.ShapeDtypeStruct((1, 1), jnp.int32)],
        in_specs=[vmem] + [pl.BlockSpec(memory_space=pl.ANY)] * 4,
        out_specs=[vmem] * 4 + [smem],
        scratch_shapes=[
            pltpu.VMEM((1, TOK), wide),
            pltpu.VMEM((groups, 1, TOK), wide),
            pltpu.VMEM((heads, groups, 1, TOK), wide),
            pltpu.VMEM((5 * TOK + 48, 4 * TOK), low),
            pltpu.VMEM((4 * TOK, 6 * TOK), low),
            pltpu.VMEM((devices, 2, 16, DH), low),
            pltpu.VMEM((devices, 2, 16, DH), low),
            pltpu.VMEM((devices, 1, 16, DH), low),
            pltpu.VMEM((devices, 2, 16, DH), low),
            pltpu.VMEM((devices, 2, 16, DH), low),
            pltpu.VMEM((devices, 1, 16, DH), low),
            pltpu.VMEM((5, 16, devices, DH), low),
            pltpu.VMEM((4, 16, OVC, DH), low),
            pltpu.VMEM((16, TOK + OVC, TOK), wide),
            pltpu.VMEM((16, 8, 2 * TOK), wide),
            pltpu.VMEM((16 * OVC, 5 * TOK), low),
            pltpu.VMEM((5 * TOK, 16 * OVC), low),
            pltpu.VMEM((5 * TOK, 4 * DH), low),
            pltpu.VMEM((16 * OVC, 4 * DH), low),
            pltpu.VMEM((TOK, TOK), low),
            pltpu.VMEM((TOK, TOK), low),
            pltpu.VMEM((devices, 1, 16, DH), low),
            pltpu.VMEM((devices, 2, 16, DH), low),
            pltpu.VMEM((devices, 2, 16, DH), low),
            pltpu.VMEM((devices, 1, 16, DH), low),
            pltpu.VMEM((devices, 2, 16, DH), low),
            pltpu.VMEM((devices, 2, 16, DH), low),
            pltpu.VMEM((heads, 32, DH), low),
            pltpu.VMEM((heads, 32, DH), low),
            pltpu.VMEM((groups, 4, 16, DH), low),
            pltpu.VMEM((groups, 4, 16, DH), low),
            pltpu.VMEM((groups, 4, 16, DH), low),
            pltpu.VMEM((groups, 4, 16, DH), low),
            pltpu.VMEM((heads, 32, DH), low),
            pltpu.VMEM((heads, 32, DH), low),
            pltpu.VMEM((heads, 16, DH), low),
            pltpu.VMEM((devices, 16, DH), low),
            pltpu.VMEM((16, devices, DH), low),
            pltpu.VMEM((4, 4 * TOK, DH), wide),
            pltpu.VMEM((devices, 16, DH), low),
            pltpu.VMEM((heads, 16, DH), low),
            pltpu.VMEM((4, tok_rows, columns), low),
            pltpu.VMEM((heads // 2, 4 * tok_rows, 2 * DH), wide),
        ]
        + [pltpu.SemaphoreType.DMA] * 29,
        compiler_params=pltpu.CompilerParams(
            collective_id=0, has_side_effects=True, vmem_limit_bytes=44 * 1024 * 1024
        ),
    )(cluster_ids.reshape(1, tok_rows), queries, key_rows, value_rows, out_grad)


def copy_kernel(*refs):
    sem = refs[-1]
    copies = [
        pltpu.make_async_copy(refs[i], refs[4 + i], sem.at[i]) for i in range(4)
    ]
    for copy in copies:
        copy.start()
    for copy in copies:
        copy.wait()


def copy_out(arrays):
    anywhere = pl.BlockSpec(memory_space=pl.ANY)
    return pl.pallas_call(
        copy_kernel,
        out_shape=[pltpu.HBM(a.shape, a.dtype) for a in arrays],
        in_specs=[anywhere] * 4,
        out_specs=[anywhere] * 4,
        scratch_shapes=[pltpu.SemaphoreType.DMA((4,))],
    )(*arrays)


def per_device(queries, key_rows, value_rows, out_grad, cluster_ids):
    arrays = (queries, key_rows, value_rows, out_grad, cluster_ids)
    *fast, flag = fast_path(*arrays)
    return lax.cond(
        flag.reshape(()) != 0,
        lambda arrays, fast: full_capacity(*arrays),
        lambda arrays, fast: tuple(copy_out(fast)),
        arrays,
        tuple(fast),
    )


def solution(mesh):
    in_specs = (
        P(("seq", "clu"), None),
        P(("seq", "clu"), None),
        P(("seq", "clu"), None),
        P(("seq", "clu"), None),
        P(("seq", "clu")),
    )
    out_specs = (
        P(("seq", "clu"), None),
        P(("seq", "clu"), None),
        P(("seq", "clu"), None),
        P(("seq", "clu"), None),
    )
    return jax.shard_map(
        per_device, mesh=mesh, in_specs=in_specs, out_specs=out_specs, check_vma=False
    )
```

```python
import math

import jax
import jax.numpy as jnp
from jax import lax
from jax.experimental import pallas as pl
from jax.experimental.pallas import tpu as pltpu
from jax.sharding import PartitionSpec as P

DH = 128
TOK = 128
OVC = 80
SET = 16
FAR = 1e9
MESH = pl.DeviceIdType.MESH


masked = -1e30


def contract_last(left, right):
    return lax.dot_general(
        left, right, (((1,), (1,)), ((), ())), preferred_element_type=jnp.float32
    )


def contract_first(left, right):
    return lax.dot_general(
        left, right, (((0,), (0,)), ((), ())), preferred_element_type=jnp.float32
    )


def softmax_rows(query_head, key_head, allowed, inv_root):
    scores = contract_last(query_head, key_head) * inv_root
    scores = jnp.where(allowed, scores, masked)
    row_max = jnp.max(scores, axis=1, keepdims=True)
    weights = jnp.exp(scores - row_max)
    row_sum = jnp.sum(weights, axis=1, keepdims=True)
    return (weights / row_sum).astype(jnp.bfloat16)


def head_slice(array, head_index):
    return lax.dynamic_slice_in_dim(array, head_index * DH, DH, 1)


def full_capacity(queries, key_rows, value_rows, out_grad, cluster_ids):
    seq_count = lax.axis_size("seq")
    clu_count = lax.axis_size("clu")
    devices = seq_count * clu_count
    tok_rows = queries.shape[0]
    columns = queries.shape[1]
    head_count = columns // DH
    most_rows = 4 * tok_rows // devices
    capacity = most_rows * devices
    inv_root = 1.0 / math.sqrt(DH)
    owners = jnp.arange(devices, dtype=jnp.int32)
    member = (cluster_ids[:, None] == owners[None, :]).astype(jnp.int32)
    running = jnp.cumsum(member, axis=0) - 1
    slot_rank = jnp.sum(member * running, axis=1)
    sent_counts = jnp.sum(member, axis=0).reshape(devices, 1)
    slot_index = cluster_ids * most_rows + slot_rank
    stacked = jnp.concatenate([queries, key_rows, value_rows], axis=1)
    width_in = stacked.shape[1]
    packed = jnp.zeros((devices * most_rows, width_in), jnp.bfloat16).at[slot_index].set(stacked)
    packed = packed.reshape(devices, most_rows, width_in)
    got_rows, got_counts = (
        lax.all_to_all(packed, ("seq", "clu"), split_axis=0, concat_axis=0, tiled=True),
        lax.all_to_all(sent_counts, ("seq", "clu"), split_axis=0, concat_axis=0, tiled=True),
    )
    got_counts = got_counts.reshape(devices)
    starts = jnp.cumsum(got_counts) - got_counts
    live_total = jnp.sum(got_counts)
    within = jnp.arange(most_rows, dtype=jnp.int32)
    target = jnp.where(
        within[None, :] < got_counts[:, None], starts[:, None] + within[None, :], capacity
    )
    target = target.reshape(devices * most_rows)
    gathered = (
        jnp.zeros((capacity, width_in), jnp.bfloat16)
        .at[target]
        .set(got_rows.reshape(devices * most_rows, width_in), mode="drop")
    )
    query_block = gathered[:, :columns]
    key_block = gathered[:, columns : 2 * columns]
    value_block = gathered[:, 2 * columns : 3 * columns]
    positions = jnp.arange(capacity, dtype=jnp.int32)
    allowed = (positions[None, :] <= positions[:, None]) & (positions[None, :] < live_total)

    def forward_head(head_index, mixed_rows):
        weights_low = softmax_rows(
            head_slice(query_block, head_index),
            head_slice(key_block, head_index),
            allowed,
            inv_root,
        )
        out_head = jnp.dot(
            weights_low, head_slice(value_block, head_index), preferred_element_type=jnp.float32
        ).astype(jnp.bfloat16)
        return lax.dynamic_update_slice_in_dim(mixed_rows, out_head, head_index * DH, 1)

    mixed_rows = lax.fori_loop(
        0, head_count, forward_head, jnp.zeros((capacity, columns), jnp.bfloat16)
    )
    back_index = jnp.minimum(target, capacity - 1)
    outgoing = jnp.take(mixed_rows, back_index, axis=0).reshape(devices, most_rows, columns)
    grad_packed = (
        jnp.zeros((devices * most_rows, columns), jnp.bfloat16).at[slot_index].set(out_grad)
    )
    grad_packed = grad_packed.reshape(devices, most_rows, columns)
    returned = lax.all_to_all(outgoing, ("seq", "clu"), split_axis=0, concat_axis=0, tiled=True)
    got_grad = lax.all_to_all(grad_packed, ("seq", "clu"), split_axis=0, concat_axis=0, tiled=True)
    attention_out = jnp.take(returned.reshape(devices * most_rows, columns), slot_index, axis=0)
    grad_block = (
        jnp.zeros((capacity, columns), jnp.bfloat16)
        .at[target]
        .set(got_grad.reshape(devices * most_rows, columns), mode="drop")
    )
    delta_rows = jnp.sum(
        (grad_block.astype(jnp.float32) * mixed_rows.astype(jnp.float32)).reshape(
            capacity, head_count, DH
        ),
        axis=2,
    )

    def backward_head(head_index, grad_rows):
        query_head = head_slice(query_block, head_index)
        key_head = head_slice(key_block, head_index)
        value_head = head_slice(value_block, head_index)
        grad_head = head_slice(grad_block, head_index)
        weights_low = softmax_rows(query_head, key_head, allowed, inv_root)
        prob_grad = contract_last(grad_head, value_head)
        delta_head = lax.dynamic_slice_in_dim(delta_rows, head_index, 1, 1)
        score_grad = (weights_low.astype(jnp.float32) * (prob_grad - delta_head)).astype(
            jnp.bfloat16
        )
        query_part = (
            jnp.dot(score_grad, key_head, preferred_element_type=jnp.float32) * inv_root
        ).astype(jnp.bfloat16)
        key_part = (contract_first(score_grad, query_head) * inv_root).astype(jnp.bfloat16)
        value_part = contract_first(weights_low, grad_head).astype(jnp.bfloat16)
        grad_rows = lax.dynamic_update_slice_in_dim(grad_rows, query_part, head_index * DH, 1)
        grad_rows = lax.dynamic_update_slice_in_dim(
            grad_rows, key_part, columns + head_index * DH, 1
        )
        return lax.dynamic_update_slice_in_dim(
            grad_rows, value_part, 2 * columns + head_index * DH, 1
        )

    grad_rows = lax.fori_loop(
        0, head_count, backward_head, jnp.zeros((capacity, 3 * columns), jnp.bfloat16)
    )
    outgoing_grads = jnp.take(grad_rows, back_index, axis=0).reshape(
        devices, most_rows, 3 * columns
    )
    returned_grads = lax.all_to_all(
        outgoing_grads, ("seq", "clu"), split_axis=0, concat_axis=0, tiled=True
    )
    picked = jnp.take(returned_grads.reshape(devices * most_rows, 3 * columns), slot_index, axis=0)
    return (
        attention_out,
        picked[:, :columns],
        picked[:, columns : 2 * columns],
        picked[:, 2 * columns :],
    )


def bf16_dot(left, right):
    return jnp.dot(left, right, preferred_element_type=jnp.float32)


def flip_perm():
    row = lax.broadcasted_iota(jnp.int32, (SET * 16, SET * 16), 0)
    col = lax.broadcasted_iota(jnp.int32, (SET * 16, SET * 16), 1)
    swapped = (col % 16) * 16 + col // 16
    return (row == swapped).astype(jnp.float32).astype(jnp.bfloat16)


def attend(q, k, v, g, allowed, inv_root):
    raw = jnp.where(allowed, contract_last(k, q), masked)
    most = jnp.max(raw, axis=0, keepdims=True)
    weights = jnp.exp2((raw - most) * (inv_root * math.log2(math.e)))
    prob = weights * (1.0 / jnp.sum(weights, axis=0, keepdims=True))
    prob_low = prob.astype(jnp.bfloat16)
    prob_grad = contract_last(v, g)
    delta = jnp.sum(prob * prob_grad, axis=0, keepdims=True)
    score_grad = (prob * (prob_grad - delta)).astype(jnp.bfloat16)
    out = contract_first(v, prob_low).T.astype(jnp.bfloat16)
    dq = (contract_first(k, score_grad).T * inv_root).astype(jnp.bfloat16)
    dk = bf16_dot(score_grad, q) * inv_root
    dv = bf16_dot(prob_low, g)
    return out, dq, dk, dv


def fast_kernel(
    ids_ref, q_ref, k_ref, v_ref, g_ref,
    out_ref, dq_ref, dk_ref, dv_ref, flag_ref,
    cnt_send, cnt_group, cnt_recv, pack_mat, unpack_mat,
    send_a, send_b, send_c, recv_a, recv_b, recv_c, table,
    over, key_pos, query_pos, pick, onehot, loose, over_res, to_mate, to_block,
    result_a, result_b, result_c, back_a, back_b, back_c,
    ex_send, ex_recv, ex_send2, ex_recv2, ex_ret2, ex_back2, ex_ret1, ex_back1,
    hsend, hrecv, htable, hacc, hresult, hback, inputs, early,
    cnt_send_sem, cnt_sem, cnt2_send_sem, cnt2_sem,
    send_a_sem, recv_a_sem, send_b_sem, recv_b_sem, send_c_sem, recv_c_sem,
    res_a_sem, back_a_sem, res_b_sem, back_b_sem, res_c_sem, back_c_sem,
    ex_send_sem, ex_recv_sem, ex_send2_sem, ex_recv2_sem,
    ex_ret2_sem, ex_back2_sem, ex_ret1_sem, ex_back1_sem,
    hsend_sem, hrecv_sem, hres_sem, hback_sem, input_sem,
):
    seq_at = lax.axis_index("seq")
    clu_at = lax.axis_index("clu")
    groups = lax.axis_size("clu")
    heads = lax.axis_size("seq")
    devices = heads * groups
    me = seq_at * groups + clu_at
    inv_root = 1.0 / math.sqrt(DH)
    is_heavy_owner = lax.rem(seq_at, groups) == clu_at
    at_x, at_z = lax.div(seq_at, 4), lax.rem(seq_at, 4)
    at_y, at_core = lax.div(clu_at, 2), lax.rem(clu_at, 2)

    def by_core(first, second):
        return first + at_core * (second - first)

    eight = []
    for by_x, by_z, by_clu in zip(
        zip((3, 2, 1, 2, 3, 0, 2, 0), (1, 2, 0, 1, 2, 3, 0, 2)),
        zip((0, 0, 3, 2, 1, 2, 3, 1), (2, 2, 1, 0, 3, 0, 0, 2)),
        zip((2, 1, 0, 3, 6, 4, 5, 7), (6, 5, 4, 7, 2, 0, 1, 3)),
    ):
        y = lax.rem(at_y + by_core(by_clu[0] // 2, by_clu[1] // 2), 4)
        core = lax.rem(at_core + by_core(by_clu[0] % 2, by_clu[1] % 2), 2)
        eight.append((by_core(*by_x), by_core(*by_z), y * 2 + core))

    def for_peers(first, count, visit):
        def one_eight(step, carry):
            by = lax.rem(step * 13 + at_core * 12, 16)
            x = at_x + lax.div(by, 4)
            z = at_z + lax.rem(by, 4)
            for j, (more_x, more_z, clu_to) in enumerate(eight):
                seq_to = lax.rem(x + more_x, 4) * 4 + lax.rem(z + more_z, 4)
                if j in (2, 5):
                    pl.when(seq_to * groups + clu_to != me)(lambda: visit(seq_to, clu_to))
                else:
                    visit(seq_to, clu_to)
            return carry

        lax.fori_loop(first, first + count, one_eight, 0)

    def send_steps(first, count, source, target, send_sem, recv_sem):
        def start(seq_to, clu_to):
            pltpu.make_async_remote_copy(
                src_ref=source.at[seq_to * groups + clu_to],
                dst_ref=target,
                send_sem=send_sem,
                recv_sem=recv_sem,
                device_id=(seq_to, clu_to),
                device_id_type=MESH,
            ).start()

        for_peers(first, count, start)

    def send_own(source, target, recv_sem):
        pltpu.make_async_copy(source.at[me], target, recv_sem).start()

    def send_to_all(source, target, send_sem, recv_sem):
        send_steps(0, devices // 8, source, target, send_sem, recv_sem)
        send_own(source, target, recv_sem)

    def wait_bytes(ref, sem):
        pltpu.make_async_copy(ref, ref, sem).wait()

    for array, ref in enumerate((q_ref, k_ref, v_ref, g_ref)):
        pltpu.make_async_copy(ref, inputs.at[array], input_sem).start()
    barrier = pltpu.get_barrier_semaphore()

    def greet(seq_to, clu_to):
        pl.semaphore_signal(barrier, inc=1, device_id=(seq_to, clu_to), device_id_type=MESH)

    for_peers(0, devices // 8, greet)

    sub = lax.broadcasted_iota(jnp.int32, (TOK, TOK), 0)
    lane = lax.broadcasted_iota(jnp.int32, (TOK, TOK), 1)
    sub_f = sub.astype(jnp.float32)
    lane_f = lane.astype(jnp.float32)
    ids_l = jnp.broadcast_to(ids_ref[...].astype(jnp.float32), (TOK, TOK))
    ids_s = ids_l.T
    one = jnp.ones((TOK, TOK), jnp.float32)
    zero = jnp.zeros((TOK, TOK), jnp.float32)
    same = ids_l == ids_s
    rank_l = jnp.sum(jnp.where(same & (sub < lane), one, zero), axis=0, keepdims=True)
    rank_s = jnp.sum(jnp.where(same & (lane < sub), one, zero), axis=1, keepdims=True)
    count_l = jnp.sum(jnp.where(same, one, zero), axis=0, keepdims=True)
    cnt_send[...] = jnp.sum(jnp.where(ids_s == lane_f, one, zero), axis=0, keepdims=True)
    ids_row = ids_l[0:1, :]
    heavy = jnp.min(jnp.where(count_l == 4.0, ids_row, 999.0), axis=1, keepdims=True)
    group_l = jnp.floor(ids_l * (1.0 / 16.0))
    group_s = jnp.floor(ids_s * (1.0 / 16.0))
    earlier = (ids_s < ids_l) | (same & (sub < lane))
    later = (ids_l < ids_s) | (same & (lane < sub))
    before = (group_l == group_s) & (ids_s != heavy) & (rank_s >= 1.0) & earlier
    over_at = jnp.sum(jnp.where(before, one, zero), axis=0, keepdims=True)
    behind = (group_l == group_s) & (ids_l != heavy) & (rank_l >= 1.0) & later
    over_at_s = jnp.sum(jnp.where(behind, one, zero), axis=1, keepdims=True)
    excess_s = (ids_s != heavy) & (rank_s >= 1.0) & (over_at_s >= 4.0)
    excess_at = jnp.sum(jnp.where(excess_s & earlier, one, zero), axis=0, keepdims=True)
    light_l = ids_l != heavy
    slot_group = (sub // 16).astype(jnp.float32)
    in_tile = sub % 16
    over_l = light_l & (rank_l >= 1.0)

    def tile_picks(tile):
        at_slot = (in_tile % 4).astype(jnp.float32)
        if tile < 4:
            cluster = slot_group * 16.0 + at_slot + 4.0 * tile
            taken = (ids_l == cluster) & (rank_l == 0.0) & light_l
        else:
            taken = (group_l == slot_group) & over_l & (over_at == at_slot)
        return [jnp.where(taken & (in_tile // 4 == array), one, zero) for array in range(4)]

    def rest_picks():
        picks = []
        for array in range(4):
            chosen = (ids_l == heavy) & (rank_l == (sub % 4).astype(jnp.float32))
            chosen = chosen & (sub // 4 == array) & (sub < 16)
            beyond = over_l & (over_at >= 4.0) & (excess_at == (sub % 8).astype(jnp.float32))
            beyond = beyond & (sub // 8 == array + 2)
            picks.append(jnp.where(chosen | beyond, one, zero))
        return picks

    def put_pack(at_row, count, picks):
        for array, matrix in enumerate(picks):
            pack_mat[pl.ds(at_row, count), pl.ds(array * TOK, TOK)] = matrix[:count].astype(
                jnp.bfloat16
            )

    put_pack(0, TOK, tile_picks(0))
    put_pack(TOK, TOK, tile_picks(4))
    put_pack(2 * TOK, 48, rest_picks())


    def send_line(source, target, count, at, device, send_sem, recv_sem):
        def one_peer(step, carry):
            to = lax.rem(at + step, count)
            pltpu.make_async_remote_copy(
                src_ref=source(to),
                dst_ref=target,
                send_sem=send_sem,
                recv_sem=recv_sem,
                device_id=device(to),
                device_id_type=MESH,
            ).start()
            return carry

        lax.fori_loop(1, count, one_peer, 0)
        pltpu.make_async_copy(source(at), target, recv_sem).start()

    def along_seq(source, target, send_sem, recv_sem):
        send_line(
            source, target.at[seq_at], heads, seq_at, lambda to: (to, clu_at), send_sem, recv_sem
        )

    def along_clu(source, target, send_sem, recv_sem):
        send_line(
            source, target.at[clu_at], groups, clu_at, lambda to: (seq_at, to), send_sem, recv_sem
        )


    def head_rows(at):
        cols = pl.ds(pl.multiple_of(at * 2 * DH, 2 * DH), 2 * DH)
        return [inputs[array, :, cols] for array in range(4)]

    def put_tile(target, at, tile, packed):
        low = packed.astype(jnp.bfloat16)
        for k in range(2):
            target[pl.ds((2 * at + k) * groups, groups), tile] = low[
                :, k * DH : (k + 1) * DH
            ].reshape(groups, 16, DH)

    def pack_a(at, carry):
        rows = jnp.concatenate(head_rows(at), axis=0)
        packed = bf16_dot(pack_mat[pl.ds(0, 2 * TOK + 48), :], rows)
        put_tile(send_a, at, 0, packed[:TOK])
        put_tile(send_a, at, 1, packed[TOK : 2 * TOK])
        rest = packed[2 * TOK :].astype(jnp.bfloat16)
        for k in range(2):
            hsend[2 * at + k] = rest[:16, k * DH : (k + 1) * DH]
            ex_send[2 * at + k] = rest[16:, k * DH : (k + 1) * DH]
        return carry

    wait_bytes(inputs, input_sem)
    lax.fori_loop(0, heads // 2, pack_a, 0, unroll=4)
    pl.semaphore_wait(barrier, devices - 1)
    along_clu(lambda to: cnt_send, cnt_group, cnt_send_sem, cnt_sem)

    def send_heavy(step, carry):
        head = lax.rem(seq_at + step, heads)
        clu_to = lax.rem(head, groups)

        @pl.when(head * groups + clu_to != me)
        def _():
            pltpu.make_async_remote_copy(
                src_ref=hsend.at[head],
                dst_ref=hrecv.at[me],
                send_sem=hsend_sem,
                recv_sem=hrecv_sem,
                device_id=(head, clu_to),
                device_id_type=MESH,
            ).start()

        @pl.when(head * groups + clu_to == me)
        def _():
            pltpu.make_async_copy(hsend.at[head], hrecv.at[me], hrecv_sem).start()

        return carry

    lax.fori_loop(0, heads, send_heavy, 0)
    along_seq(lambda to: ex_send.at[to], ex_recv, ex_send_sem, ex_recv_sem)
    out_a = (send_a, recv_a.at[me], send_a_sem, recv_a_sem)
    send_steps(0, 4, *out_a)
    wait_bytes(cnt_group, cnt_sem)
    along_seq(lambda to: cnt_group, cnt_recv, cnt2_send_sem, cnt2_sem)
    send_steps(4, devices // 8 - 4, *out_a)
    send_own(send_a, recv_a.at[me], recv_a_sem)

    for tile in range(1, 4):
        put_pack((tile + 1) * TOK + 48, TOK, tile_picks(tile))

    def pack_bc(at, carry):
        rows = jnp.concatenate(head_rows(at), axis=0)
        packed = bf16_dot(pack_mat[pl.ds(2 * TOK + 48, 3 * TOK), :], rows)
        put_tile(send_b, at, 0, packed[:TOK])
        put_tile(send_b, at, 1, packed[TOK : 2 * TOK])
        put_tile(send_c, at, 0, packed[2 * TOK :])
        return carry

    lax.fori_loop(0, heads // 2, pack_bc, 0)

    wait_bytes(cnt_recv, cnt2_sem)
    seen = cnt_recv[...].reshape(TOK, TOK)
    heavies = jnp.min(jnp.where(seen == 4.0, lane_f, 999.0), axis=1, keepdims=True)
    heavy_all = jnp.min(heavies, axis=0, keepdims=True)
    light = lane_f != heavy_all
    more = jnp.where(light, jnp.maximum(seen - 1.0, 0.0), 0.0)
    more_low = more.astype(jnp.bfloat16)
    in_group = jnp.where(sub // 16 == lane, one, zero).astype(jnp.bfloat16)
    ahead = jnp.where(sub < lane, one, zero).astype(jnp.bfloat16)
    prior = jnp.where(lane < sub, one, zero).astype(jnp.bfloat16)
    mates = (lane < sub) & (lane % 8 == sub % 8)
    mates = jnp.where(mates, one, zero).astype(jnp.bfloat16)
    excess = jnp.maximum(bf16_dot(more_low, in_group) - 4.0, 0.0)
    excess_low = excess.astype(jnp.bfloat16)
    excess_off = bf16_dot(excess_low, ahead)
    excess_pre = bf16_dot(mates, excess_low)
    bad = (jnp.sum(excess, axis=1, keepdims=True) > 8.0) | (excess_pre + excess > 16.0)
    bad = bad | (heavies != heavy_all) | (jnp.sum(more, axis=0, keepdims=True) > OVC)
    flag_ref[0, 0] = jnp.max(jnp.where(bad, one, zero)).astype(jnp.int32)

    spot = zero
    for group in range(8):
        off, count, pre = [a[:, group : group + 1] for a in (excess_off, excess, excess_pre)]
        held = (lane_f >= off) & (lane_f < off + count)
        spot = spot + jnp.where(held, lane_f + (group * 16 + 1.0) - off + pre, zero)
    spot = jnp.where(sub % 8 == clu_at, spot, zero).reshape(16, 8, TOK)
    spot = jnp.sum(spot, axis=1).astype(jnp.bfloat16)
    spread8 = jnp.where(lane % 8 == sub, one, zero).astype(jnp.bfloat16)
    spot = jnp.where(lane[:16] // 8 == sub[:16], bf16_dot(spot, spread8), 0.0)
    spot = jnp.sum(spot, axis=0, keepdims=True) - 1.0
    to_mate[...] = jnp.where(sub_f == spot, one, zero).astype(jnp.bfloat16)
    spot = jnp.broadcast_to(spot, (TOK, TOK)).T
    to_block[...] = jnp.where(spot == lane_f, one, zero).astype(jnp.bfloat16)

    wait_bytes(ex_recv, ex_recv_sem)
    held = ex_recv[...].astype(jnp.float32)
    held = [held[:, 8 * a : 8 * a + 8, :].reshape(TOK, DH) for a in range(4)]
    held = jnp.concatenate(held, axis=1).astype(jnp.bfloat16)
    held = bf16_dot(to_mate[...], held).astype(jnp.bfloat16)
    for a in range(4):
        ex_send2[:, a] = held[:, a * DH : (a + 1) * DH].reshape(8, 16, DH)
    along_clu(lambda to: ex_send2.at[to], ex_recv2, ex_send2_sem, ex_recv2_sem)
    send_to_all(send_b, recv_b.at[me], send_b_sem, recv_b_sem)
    send_to_all(send_c, recv_c.at[me], send_c_sem, recv_c_sem)

    valid = jnp.where((seen > 0.0) & light, one, zero).astype(jnp.bfloat16)
    mine = (sub == clu_at * 16 + lane) & (lane < 16)
    mine = jnp.where(mine, one, zero).astype(jnp.bfloat16)
    more_g = bf16_dot(more_low, mine)
    valid_g = bf16_dot(valid, mine)
    more_g_low = more_g.astype(jnp.bfloat16)
    start_g = bf16_dot(prior, more_g_low)
    offset_g = bf16_dot(more_g_low, ahead)
    beyond_g = jnp.maximum(bf16_dot(more_g_low, one.astype(jnp.bfloat16)) - 4.0, 0.0)
    pre_g = bf16_dot(mates, beyond_g.astype(jnp.bfloat16))
    ex_index = lane_f - pre_g + 4.0
    first_row = lax.broadcasted_iota(jnp.int32, (1, TOK), 1).astype(jnp.float32) * 16.0
    in_tile_at = zero
    beyond_at = zero
    for c in range(16):
        count, begin, off, real = [
            a[:, c : c + 1] for a in (more_g, start_g, offset_g, valid_g)
        ]
        place = begin - off + (c * OVC + 1.0)
        held = (lane_f >= off) & (lane_f < off + count) & (lane < 4)
        in_tile_at = in_tile_at + jnp.where(held, lane_f + place, zero)
        held = (ex_index >= off) & (ex_index < off + count) & (ex_index >= 4.0)
        beyond_at = beyond_at + jnp.where(held, ex_index + place, zero)
        held = (lane_f >= begin) & (lane_f < begin + count)
        where = jnp.where(held, sub_f * 16.0 + 1.0 + lane_f - begin, zero)
        where = jnp.sum(where, axis=0, keepdims=True)
        where = jnp.where(where > 0.0, where, FAR)
        query_row = jnp.concatenate([first_row, where], axis=1)
        query_pos[c] = jnp.broadcast_to(query_row, (8, 2 * TOK))
        key_pos[c, pl.ds(0, TOK), :] = jnp.where(real > 0.0, sub_f * 16.0, FAR)
        key_pos[c, pl.ds(TOK, OVC), :] = jnp.broadcast_to(where, (TOK, TOK)).T[:OVC]
    beyond_at = jnp.sum(beyond_at.reshape(16, 8, TOK), axis=0)
    high = jnp.floor(beyond_at * (1.0 / 32.0))
    split = jnp.concatenate([high, beyond_at - high * 32.0], axis=0).astype(jnp.bfloat16)
    spread16 = jnp.where(lane % 16 == sub, one, zero).astype(jnp.bfloat16)
    split = bf16_dot(split, spread16)
    split = jnp.where(lane[:8] // 16 == sub[:8], split[:8] * 32.0 + split[8:], 0.0)
    beyond_row = jnp.sum(split, axis=0, keepdims=True) - 1.0
    tile_rows = in_tile_at.T[0:8, :] - 1.0
    slot_rows = [tile_rows[k : k + 1, :] for k in range(4)] + [beyond_row]
    slot_cols = [in_tile_at[:, k : k + 1] - 1.0 for k in range(4)]
    slot_cols.append(jnp.broadcast_to(beyond_row, (TOK, TOK)).T)

    chunk = 4
    for k in range(5):
        for m in range(16 * OVC // TOK):
            onehot[pl.ds(k * TOK, TOK), pl.ds(m * TOK, TOK)] = jnp.where(
                slot_cols[k] == lane_f + float(m * TOK), one, zero
            ).astype(jnp.bfloat16)
            pick[pl.ds(m * TOK, TOK), pl.ds(k * TOK, TOK)] = jnp.where(
                slot_rows[k] == sub_f + float(m * TOK), one, zero
            ).astype(jnp.bfloat16)

    for at, tile in enumerate((0, 1, 2, None, 3, 4)):
        for array, matrix in enumerate(rest_picks() if tile is None else tile_picks(tile)):
            unpack_mat[pl.ds(array * TOK, TOK), pl.ds(at * TOK, TOK)] = matrix.T.astype(
                jnp.bfloat16
            )

    perm = flip_perm()

    def arrange(source, target, units):
        def two_sets(at, carry):
            blocks = [pl.ds(pl.multiple_of((2 * at + i) * SET, SET), SET) for i in range(2)]
            spots = [(held, unit) for held in blocks for unit in range(units)]
            rows = jnp.concatenate(
                [source(held, unit).reshape(SET * 16, DH) for held, unit in spots], axis=1
            )
            turned = bf16_dot(perm, rows).astype(jnp.bfloat16)
            for i, (held, unit) in enumerate(spots):
                target(held, unit, turned[:, i * DH : (i + 1) * DH].reshape(16, SET, DH))
            return carry

        lax.fori_loop(0, devices // (2 * SET), two_sets, 0, unroll=2)

    def put_table(first):
        def put(blocks, unit, value):
            table[first + unit, :, blocks, :] = value

        return put

    @pl.when(is_heavy_owner)
    def _():
        wait_bytes(hrecv, hrecv_sem)

        def put_heavy(blocks, unit, value):
            htable[:, blocks, :] = value

        arrange(lambda blocks, unit: hrecv[blocks], put_heavy, 1)
        k_h, v_h = [htable[4 * a : 4 * a + 4].reshape(4 * TOK, DH) for a in (1, 2)]
        hacc[...] = jnp.zeros_like(hacc)
        key_sub = lax.broadcasted_iota(jnp.int32, (4 * TOK, TOK), 0)
        key_at = lax.rem(key_sub, TOK) * 4 + lax.div(key_sub, TOK)
        query_at = lax.broadcasted_iota(jnp.int32, (4 * TOK, TOK), 1) * 4

        def heavy_tile(s, carry):
            out, dq, dk, dv = attend(
                htable[s], k_h, v_h, htable[12 + s], key_at <= query_at + s, inv_root
            )
            hacc[2, pl.ds(pl.multiple_of(s * TOK, TOK), TOK)] = out.astype(jnp.float32)
            hacc[3, pl.ds(pl.multiple_of(s * TOK, TOK), TOK)] = dq.astype(jnp.float32)
            hacc[0] += dk
            hacc[1] += dv
            return carry

        lax.fori_loop(0, 4, heavy_tile, 0)
        for array, at in enumerate((2, 3, 0, 1)):
            htable[4 * array : 4 * array + 4] = (
                hacc[at].astype(jnp.bfloat16).reshape(4, TOK, DH)
            )

        def put_hresult(blocks, unit, value):
            hresult[blocks] = value

        arrange(lambda blocks, unit: htable[:, blocks, :], put_hresult, 1)
        send_to_all(hresult, hback.at[seq_at], hres_sem, hback_sem)

    wait_bytes(recv_a, recv_a_sem)
    def put_tile_a(blocks, unit, value):
        table[4 * unit, :, blocks, :] = value

    arrange(lambda blocks, unit: recv_a[blocks, unit], put_tile_a, 2)

    wait_bytes(ex_recv2, ex_recv2_sem)
    for a in range(4):
        cols = pl.ds(a * DH, DH)
        loose[pl.ds(0, 4 * TOK), cols] = table[4, 4 * a : 4 * a + 4].reshape(4 * TOK, DH)
        loose[pl.ds(4 * TOK, TOK), cols] = ex_recv2[:, a].reshape(TOK, DH)

    def gather_chunk(at, carry):
        chosen = pick[pl.ds(pl.multiple_of(at * chunk * OVC, 64), chunk * OVC), :]
        found = bf16_dot(chosen, loose[...]).astype(jnp.bfloat16)
        for c in range(chunk):
            for array in range(4):
                over[array, at * chunk + c] = found[
                    c * OVC : (c + 1) * OVC, array * DH : (array + 1) * DH
                ]
        return carry

    gather_chunk(0, 0)

    pad_rows = jnp.zeros((TOK - OVC, DH), jnp.bfloat16)

    def load_cluster(tile, j):
        c = tile * 4 + j
        rows = [
            jnp.concatenate([table[tile, a * 4 + j], over[a, c]], axis=0) for a in range(4)
        ]
        for a in (0, 3):
            rows[a] = jnp.concatenate([rows[a], pad_rows], axis=0)
        key_at = key_pos[c]
        allowed = jnp.concatenate([key_at, key_at], axis=1) <= query_pos[c, 0:1, :]
        return rows + [allowed]

    def attend_tiles(first, tiles):
        def one_tile(at, carry):
            tile = first + at
            spots = range(4)
            loaded = [load_cluster(tile, j) for j in spots]
            found = [attend(*arrays, inv_root) for arrays in loaded]
            for j, results in zip(spots, found):
                c = tile * 4 + j
                for a, value in enumerate(results):
                    value = value.astype(jnp.bfloat16)
                    table[tile, a * 4 + j] = value[:TOK]
                    over_res[
                        pl.ds(pl.multiple_of(c * OVC, 16), OVC), pl.ds(a * DH, DH)
                    ] = value[TOK : TOK + OVC]
            return carry

        lax.fori_loop(0, tiles, one_tile, 0)

    def put_in(result):
        def put(blocks, unit, value):
            result[blocks, unit] = value

        return put

    def from_table(first):
        return lambda blocks, unit: table[first + unit, :, blocks, :]

    to_a = (result_a, back_a.at[me], res_a_sem, back_a_sem)
    to_b = (result_b, back_b.at[me], res_b_sem, back_b_sem)
    to_c = (result_c, back_c.at[me], res_c_sem, back_c_sem)
    attend_tiles(0, 1)
    arrange(from_table(0), put_in(result_a), 1)
    send_to_all(*to_a)
    lax.fori_loop(1, 16 // chunk, gather_chunk, 0)

    wait_bytes(recv_b, recv_b_sem)
    arrange(lambda blocks, unit: recv_b[blocks, unit], put_table(1), 2)
    attend_tiles(1, 2)
    arrange(from_table(1), put_in(result_b), 2)
    send_to_all(*to_b)

    wait_bytes(recv_c, recv_c_sem)
    arrange(lambda blocks, unit: recv_c[blocks, 0], put_table(3), 1)
    attend_tiles(3, 1)

    found = bf16_dot(onehot[pl.ds(4 * TOK, TOK), :], over_res[...]).astype(jnp.bfloat16)
    for a in range(4):
        ex_ret2[:, a] = found[:, a * DH : (a + 1) * DH].reshape(8, 16, DH)
    along_clu(lambda to: ex_ret2.at[to], ex_back2, ex_ret2_sem, ex_back2_sem)
    found = bf16_dot(onehot[pl.ds(0, 4 * TOK), :], over_res[...]).astype(jnp.bfloat16)
    for a in range(4):
        table[4, 4 * a : 4 * a + 4] = found[:, a * DH : (a + 1) * DH].reshape(4, TOK, DH)
    arrange(from_table(3), put_in(result_c), 2)
    send_steps(0, devices // 16, *to_c)
    send_own(result_c, back_c.at[me], back_c_sem)

    wait_bytes(ex_back2, ex_back2_sem)
    held = [ex_back2[:, a].reshape(TOK, DH) for a in range(4)]
    held = bf16_dot(to_block[...], jnp.concatenate(held, axis=1))
    held = [held[:, a * DH : (a + 1) * DH].reshape(16, 8, DH) for a in range(4)]
    ex_ret1[...] = jnp.concatenate(held, axis=1).astype(jnp.bfloat16)
    along_seq(lambda to: ex_ret1.at[to], ex_back1, ex_ret1_sem, ex_back1_sem)
    send_steps(devices // 16, devices // 16, *to_c)

    def unpack(tiles, rest, first, count):
        sides = []
        for k in range(2):
            sides.append(
                jnp.concatenate(
                    [tile(k).reshape(TOK, DH) for tile in tiles] + [part(k) for part in rest],
                    axis=0,
                )
            )
        return bf16_dot(
            unpack_mat[:, pl.ds(first, count)], jnp.concatenate(sides, axis=1)
        )

    def tile_of(ref, at, tile):
        return lambda k: ref[pl.ds((2 * at + k) * groups, groups), tile]

    def unpack_early(at, carry):
        tiles = [tile_of(back_a, at, 0), tile_of(back_b, at, 0), tile_of(back_b, at, 1)]
        rest = [
            lambda k: hback[2 * at + k],
            lambda k: ex_back1[2 * at + k],
            lambda k: jnp.zeros((TOK - 48, DH), jnp.bfloat16),
        ]
        early[at] = unpack(tiles, rest, 0, 4 * TOK)
        return carry

    def unpack_last(at, carry):
        cols = pl.ds(pl.multiple_of(at * 2 * DH, 2 * DH), 2 * DH)
        tiles = [tile_of(back_c, at, 0), tile_of(back_c, at, 1)]
        found = (early[at] + unpack(tiles, [], 4 * TOK, 2 * TOK)).astype(jnp.bfloat16)
        for array, ref in enumerate((out_ref, dq_ref, dk_ref, dv_ref)):
            ref[:, cols] = found[array * TOK : (array + 1) * TOK]
        return carry

    wait_bytes(hback, hback_sem)
    wait_bytes(back_a, back_a_sem)
    wait_bytes(back_b, back_b_sem)
    wait_bytes(ex_back1, ex_back1_sem)
    lax.fori_loop(0, heads // 2, unpack_early, 0, unroll=2)
    wait_bytes(back_c, back_c_sem)
    lax.fori_loop(0, heads // 2, unpack_last, 0, unroll=2)

    others = pl.ds(0, devices - 1)
    wait_bytes(cnt_group.at[pl.ds(0, groups - 1)], cnt_send_sem)
    wait_bytes(cnt_recv.at[pl.ds(0, heads - 1)], cnt2_send_sem)
    for ref, sem in ((ex_send, ex_send_sem), (ex_ret1, ex_ret1_sem)):
        wait_bytes(ref.at[pl.ds(0, heads - 1)], sem)
    for ref, sem in ((ex_send2, ex_send2_sem), (ex_ret2, ex_ret2_sem)):
        wait_bytes(ref.at[pl.ds(0, groups - 1)], sem)
    wait_bytes(send_a.at[others], send_a_sem)
    wait_bytes(send_b.at[others], send_b_sem)
    wait_bytes(send_c.at[others], send_c_sem)
    wait_bytes(result_a.at[others], res_a_sem)
    wait_bytes(result_b.at[others], res_b_sem)
    wait_bytes(result_c.at[others], res_c_sem)

    @pl.when(is_heavy_owner)
    def _():
        wait_bytes(hsend.at[pl.ds(0, heads - 1)], hsend_sem)
        wait_bytes(hresult.at[others], hres_sem)

    @pl.when(jnp.logical_not(is_heavy_owner))
    def _():
        wait_bytes(hsend, hsend_sem)


def fast_path(queries, key_rows, value_rows, out_grad, cluster_ids):
    tok_rows, columns = queries.shape
    heads = columns // DH
    groups = lax.axis_size("clu")
    devices = lax.axis_size("seq") * groups
    low = jnp.bfloat16
    wide = jnp.float32
    rows = pltpu.VMEM((tok_rows, columns), low)
    vmem = pl.BlockSpec(memory_space=pltpu.VMEM)
    smem = pl.BlockSpec(memory_space=pltpu.SMEM)
    return pl.pallas_call(
        fast_kernel,
        out_shape=[rows] * 4 + [jax.ShapeDtypeStruct((1, 1), jnp.int32)],
        in_specs=[vmem] + [pl.BlockSpec(memory_space=pl.ANY)] * 4,
        out_specs=[vmem] * 4 + [smem],
        scratch_shapes=[
            pltpu.VMEM((1, TOK), wide),
            pltpu.VMEM((groups, 1, TOK), wide),
            pltpu.VMEM((heads, groups, 1, TOK), wide),
            pltpu.VMEM((5 * TOK + 48, 4 * TOK), low),
            pltpu.VMEM((4 * TOK, 6 * TOK), low),
            pltpu.VMEM((devices, 2, 16, DH), low),
            pltpu.VMEM((devices, 2, 16, DH), low),
            pltpu.VMEM((devices, 1, 16, DH), low),
            pltpu.VMEM((devices, 2, 16, DH), low),
            pltpu.VMEM((devices, 2, 16, DH), low),
            pltpu.VMEM((devices, 1, 16, DH), low),
            pltpu.VMEM((5, 16, devices, DH), low),
            pltpu.VMEM((4, 16, OVC, DH), low),
            pltpu.VMEM((16, TOK + OVC, TOK), wide),
            pltpu.VMEM((16, 8, 2 * TOK), wide),
            pltpu.VMEM((16 * OVC, 5 * TOK), low),
            pltpu.VMEM((5 * TOK, 16 * OVC), low),
            pltpu.VMEM((5 * TOK, 4 * DH), low),
            pltpu.VMEM((16 * OVC, 4 * DH), low),
            pltpu.VMEM((TOK, TOK), low),
            pltpu.VMEM((TOK, TOK), low),
            pltpu.VMEM((devices, 1, 16, DH), low),
            pltpu.VMEM((devices, 2, 16, DH), low),
            pltpu.VMEM((devices, 2, 16, DH), low),
            pltpu.VMEM((devices, 1, 16, DH), low),
            pltpu.VMEM((devices, 2, 16, DH), low),
            pltpu.VMEM((devices, 2, 16, DH), low),
            pltpu.VMEM((heads, 32, DH), low),
            pltpu.VMEM((heads, 32, DH), low),
            pltpu.VMEM((groups, 4, 16, DH), low),
            pltpu.VMEM((groups, 4, 16, DH), low),
            pltpu.VMEM((groups, 4, 16, DH), low),
            pltpu.VMEM((groups, 4, 16, DH), low),
            pltpu.VMEM((heads, 32, DH), low),
            pltpu.VMEM((heads, 32, DH), low),
            pltpu.VMEM((heads, 16, DH), low),
            pltpu.VMEM((devices, 16, DH), low),
            pltpu.VMEM((16, devices, DH), low),
            pltpu.VMEM((4, 4 * TOK, DH), wide),
            pltpu.VMEM((devices, 16, DH), low),
            pltpu.VMEM((heads, 16, DH), low),
            pltpu.VMEM((4, tok_rows, columns), low),
            pltpu.VMEM((heads // 2, 4 * tok_rows, 2 * DH), wide),
        ]
        + [pltpu.SemaphoreType.DMA] * 29,
        compiler_params=pltpu.CompilerParams(
            collective_id=0, has_side_effects=True, vmem_limit_bytes=44 * 1024 * 1024
        ),
    )(cluster_ids.reshape(1, tok_rows), queries, key_rows, value_rows, out_grad)


def copy_kernel(*refs):
    sem = refs[-1]
    copies = [
        pltpu.make_async_copy(refs[i], refs[4 + i], sem.at[i]) for i in range(4)
    ]
    for copy in copies:
        copy.start()
    for copy in copies:
        copy.wait()


def copy_out(arrays):
    anywhere = pl.BlockSpec(memory_space=pl.ANY)
    return pl.pallas_call(
        copy_kernel,
        out_shape=[pltpu.HBM(a.shape, a.dtype) for a in arrays],
        in_specs=[anywhere] * 4,
        out_specs=[anywhere] * 4,
        scratch_shapes=[pltpu.SemaphoreType.DMA((4,))],
    )(*arrays)


def per_device(queries, key_rows, value_rows, out_grad, cluster_ids):
    arrays = (queries, key_rows, value_rows, out_grad, cluster_ids)
    *fast, flag = fast_path(*arrays)
    return lax.cond(
        flag.reshape(()) != 0,
        lambda arrays, fast: full_capacity(*arrays),
        lambda arrays, fast: tuple(copy_out(fast)),
        arrays,
        tuple(fast),
    )


def solution(mesh):
    in_specs = (
        P(("seq", "clu"), None),
        P(("seq", "clu"), None),
        P(("seq", "clu"), None),
        P(("seq", "clu"), None),
        P(("seq", "clu")),
    )
    out_specs = (
        P(("seq", "clu"), None),
        P(("seq", "clu"), None),
        P(("seq", "clu"), None),
        P(("seq", "clu"), None),
    )
    return jax.shard_map(
        per_device, mesh=mesh, in_specs=in_specs, out_specs=out_specs, check_vma=False
    )
```

```python
import math

import jax
import jax.numpy as jnp
from jax import lax
from jax.experimental import pallas as pl
from jax.experimental.pallas import tpu as pltpu
from jax.sharding import PartitionSpec as P

DH = 128
TOK = 128
OVC = 80
SET = 16
FAR = 1e9
MESH = pl.DeviceIdType.MESH


masked = -1e30


def contract_last(left, right):
    return lax.dot_general(
        left, right, (((1,), (1,)), ((), ())), preferred_element_type=jnp.float32
    )


def contract_first(left, right):
    return lax.dot_general(
        left, right, (((0,), (0,)), ((), ())), preferred_element_type=jnp.float32
    )


def softmax_rows(query_head, key_head, allowed, inv_root):
    scores = contract_last(query_head, key_head) * inv_root
    scores = jnp.where(allowed, scores, masked)
    row_max = jnp.max(scores, axis=1, keepdims=True)
    weights = jnp.exp(scores - row_max)
    row_sum = jnp.sum(weights, axis=1, keepdims=True)
    return (weights / row_sum).astype(jnp.bfloat16)


def head_slice(array, head_index):
    return lax.dynamic_slice_in_dim(array, head_index * DH, DH, 1)


def full_capacity(queries, key_rows, value_rows, out_grad, cluster_ids):
    seq_count = lax.axis_size("seq")
    clu_count = lax.axis_size("clu")
    devices = seq_count * clu_count
    tok_rows = queries.shape[0]
    columns = queries.shape[1]
    head_count = columns // DH
    most_rows = 4 * tok_rows // devices
    capacity = most_rows * devices
    inv_root = 1.0 / math.sqrt(DH)
    owners = jnp.arange(devices, dtype=jnp.int32)
    member = (cluster_ids[:, None] == owners[None, :]).astype(jnp.int32)
    running = jnp.cumsum(member, axis=0) - 1
    slot_rank = jnp.sum(member * running, axis=1)
    sent_counts = jnp.sum(member, axis=0).reshape(devices, 1)
    slot_index = cluster_ids * most_rows + slot_rank
    stacked = jnp.concatenate([queries, key_rows, value_rows], axis=1)
    width_in = stacked.shape[1]
    packed = jnp.zeros((devices * most_rows, width_in), jnp.bfloat16).at[slot_index].set(stacked)
    packed = packed.reshape(devices, most_rows, width_in)
    got_rows, got_counts = (
        lax.all_to_all(packed, ("seq", "clu"), split_axis=0, concat_axis=0, tiled=True),
        lax.all_to_all(sent_counts, ("seq", "clu"), split_axis=0, concat_axis=0, tiled=True),
    )
    got_counts = got_counts.reshape(devices)
    starts = jnp.cumsum(got_counts) - got_counts
    live_total = jnp.sum(got_counts)
    within = jnp.arange(most_rows, dtype=jnp.int32)
    target = jnp.where(
        within[None, :] < got_counts[:, None], starts[:, None] + within[None, :], capacity
    )
    target = target.reshape(devices * most_rows)
    gathered = (
        jnp.zeros((capacity, width_in), jnp.bfloat16)
        .at[target]
        .set(got_rows.reshape(devices * most_rows, width_in), mode="drop")
    )
    query_block = gathered[:, :columns]
    key_block = gathered[:, columns : 2 * columns]
    value_block = gathered[:, 2 * columns : 3 * columns]
    positions = jnp.arange(capacity, dtype=jnp.int32)
    allowed = (positions[None, :] <= positions[:, None]) & (positions[None, :] < live_total)

    def forward_head(head_index, mixed_rows):
        weights_low = softmax_rows(
            head_slice(query_block, head_index),
            head_slice(key_block, head_index),
            allowed,
            inv_root,
        )
        out_head = jnp.dot(
            weights_low, head_slice(value_block, head_index), preferred_element_type=jnp.float32
        ).astype(jnp.bfloat16)
        return lax.dynamic_update_slice_in_dim(mixed_rows, out_head, head_index * DH, 1)

    mixed_rows = lax.fori_loop(
        0, head_count, forward_head, jnp.zeros((capacity, columns), jnp.bfloat16)
    )
    back_index = jnp.minimum(target, capacity - 1)
    outgoing = jnp.take(mixed_rows, back_index, axis=0).reshape(devices, most_rows, columns)
    grad_packed = (
        jnp.zeros((devices * most_rows, columns), jnp.bfloat16).at[slot_index].set(out_grad)
    )
    grad_packed = grad_packed.reshape(devices, most_rows, columns)
    returned = lax.all_to_all(outgoing, ("seq", "clu"), split_axis=0, concat_axis=0, tiled=True)
    got_grad = lax.all_to_all(grad_packed, ("seq", "clu"), split_axis=0, concat_axis=0, tiled=True)
    attention_out = jnp.take(returned.reshape(devices * most_rows, columns), slot_index, axis=0)
    grad_block = (
        jnp.zeros((capacity, columns), jnp.bfloat16)
        .at[target]
        .set(got_grad.reshape(devices * most_rows, columns), mode="drop")
    )
    delta_rows = jnp.sum(
        (grad_block.astype(jnp.float32) * mixed_rows.astype(jnp.float32)).reshape(
            capacity, head_count, DH
        ),
        axis=2,
    )

    def backward_head(head_index, grad_rows):
        query_head = head_slice(query_block, head_index)
        key_head = head_slice(key_block, head_index)
        value_head = head_slice(value_block, head_index)
        grad_head = head_slice(grad_block, head_index)
        weights_low = softmax_rows(query_head, key_head, allowed, inv_root)
        prob_grad = contract_last(grad_head, value_head)
        delta_head = lax.dynamic_slice_in_dim(delta_rows, head_index, 1, 1)
        score_grad = (weights_low.astype(jnp.float32) * (prob_grad - delta_head)).astype(
            jnp.bfloat16
        )
        query_part = (
            jnp.dot(score_grad, key_head, preferred_element_type=jnp.float32) * inv_root
        ).astype(jnp.bfloat16)
        key_part = (contract_first(score_grad, query_head) * inv_root).astype(jnp.bfloat16)
        value_part = contract_first(weights_low, grad_head).astype(jnp.bfloat16)
        grad_rows = lax.dynamic_update_slice_in_dim(grad_rows, query_part, head_index * DH, 1)
        grad_rows = lax.dynamic_update_slice_in_dim(
            grad_rows, key_part, columns + head_index * DH, 1
        )
        return lax.dynamic_update_slice_in_dim(
            grad_rows, value_part, 2 * columns + head_index * DH, 1
        )

    grad_rows = lax.fori_loop(
        0, head_count, backward_head, jnp.zeros((capacity, 3 * columns), jnp.bfloat16)
    )
    outgoing_grads = jnp.take(grad_rows, back_index, axis=0).reshape(
        devices, most_rows, 3 * columns
    )
    returned_grads = lax.all_to_all(
        outgoing_grads, ("seq", "clu"), split_axis=0, concat_axis=0, tiled=True
    )
    picked = jnp.take(returned_grads.reshape(devices * most_rows, 3 * columns), slot_index, axis=0)
    return (
        attention_out,
        picked[:, :columns],
        picked[:, columns : 2 * columns],
        picked[:, 2 * columns :],
    )


def bf16_dot(left, right):
    return jnp.dot(left, right, preferred_element_type=jnp.float32)


def flip_perm():
    row = lax.broadcasted_iota(jnp.int32, (SET * 16, SET * 16), 0)
    col = lax.broadcasted_iota(jnp.int32, (SET * 16, SET * 16), 1)
    swapped = (col % 16) * 16 + col // 16
    return (row == swapped).astype(jnp.float32).astype(jnp.bfloat16)


def attend(q, k, v, g, allowed, inv_root):
    raw = jnp.where(allowed, contract_last(k, q), masked)
    most = jnp.max(raw, axis=0, keepdims=True)
    weights = jnp.exp2((raw - most) * (inv_root * math.log2(math.e)))
    prob = weights * (1.0 / jnp.sum(weights, axis=0, keepdims=True))
    prob_low = prob.astype(jnp.bfloat16)
    prob_grad = contract_last(v, g)
    delta = jnp.sum(prob * prob_grad, axis=0, keepdims=True)
    score_grad = (prob * (prob_grad - delta)).astype(jnp.bfloat16)
    out = contract_first(v, prob_low).T.astype(jnp.bfloat16)
    dq = (contract_first(k, score_grad).T * inv_root).astype(jnp.bfloat16)
    dk = bf16_dot(score_grad, q) * inv_root
    dv = bf16_dot(prob_low, g)
    return out, dq, dk, dv


def fast_kernel(
    ids_ref, q_ref, k_ref, v_ref, g_ref,
    out_ref, dq_ref, dk_ref, dv_ref, flag_ref,
    cnt_send, cnt_group, cnt_recv, pack_mat, unpack_mat,
    send_a, send_b, send_c, recv_a, recv_b, recv_c, table,
    over, key_pos, query_pos, pick, onehot, loose, over_res, to_mate, to_block,
    result_a, result_b, result_c, back_a, back_b, back_c,
    ex_send, ex_recv, ex_send2, ex_recv2, ex_ret2, ex_back2, ex_ret1, ex_back1,
    hsend, hrecv, htable, hacc, hresult, hback, inputs, early,
    cnt_send_sem, cnt_sem, cnt2_send_sem, cnt2_sem,
    send_a_sem, recv_a_sem, send_b_sem, recv_b_sem, send_c_sem, recv_c_sem,
    res_a_sem, back_a_sem, res_b_sem, back_b_sem, res_c_sem, back_c_sem,
    ex_send_sem, ex_recv_sem, ex_send2_sem, ex_recv2_sem,
    ex_ret2_sem, ex_back2_sem, ex_ret1_sem, ex_back1_sem,
    hsend_sem, hrecv_sem, hres_sem, hback_sem, input_sem,
):
    seq_at = lax.axis_index("seq")
    clu_at = lax.axis_index("clu")
    groups = lax.axis_size("clu")
    heads = lax.axis_size("seq")
    devices = heads * groups
    me = seq_at * groups + clu_at
    inv_root = 1.0 / math.sqrt(DH)
    is_heavy_owner = lax.rem(seq_at, groups) == clu_at
    at_x, at_z = lax.div(seq_at, 4), lax.rem(seq_at, 4)
    at_y, at_core = lax.div(clu_at, 2), lax.rem(clu_at, 2)

    def by_core(first, second):
        return first + at_core * (second - first)

    eight = []
    for by_x, by_z, by_clu in zip(
        zip((2, 2, 1, 2, 3, 0, 2, 0), (1, 1, 0, 1, 2, 3, 0, 2)),
        zip((0, 0, 3, 2, 1, 2, 3, 1), (2, 2, 1, 0, 3, 0, 0, 2)),
        zip((2, 1, 0, 3, 6, 4, 5, 7), (6, 5, 4, 7, 2, 0, 1, 3)),
    ):
        y = lax.rem(at_y + by_core(by_clu[0] // 2, by_clu[1] // 2), 4)
        core = lax.rem(at_core + by_core(by_clu[0] % 2, by_clu[1] % 2), 2)
        eight.append((by_core(*by_x), by_core(*by_z), y * 2 + core))

    def for_peers(first, count, visit):
        def one_eight(step, carry):
            by = lax.rem(step * 13 + at_core * 12, 16)
            x = at_x + lax.div(by, 4)
            z = at_z + lax.rem(by, 4)
            for j, (more_x, more_z, clu_to) in enumerate(eight):
                seq_to = lax.rem(x + more_x, 4) * 4 + lax.rem(z + more_z, 4)
                if j in (2, 5):
                    pl.when(seq_to * groups + clu_to != me)(lambda: visit(seq_to, clu_to))
                else:
                    visit(seq_to, clu_to)
            return carry

        lax.fori_loop(first, first + count, one_eight, 0)

    def send_steps(first, count, source, target, send_sem, recv_sem):
        def start(seq_to, clu_to):
            pltpu.make_async_remote_copy(
                src_ref=source.at[seq_to * groups + clu_to],
                dst_ref=target,
                send_sem=send_sem,
                recv_sem=recv_sem,
                device_id=(seq_to, clu_to),
                device_id_type=MESH,
            ).start()

        for_peers(first, count, start)

    def send_own(source, target, recv_sem):
        pltpu.make_async_copy(source.at[me], target, recv_sem).start()

    def send_to_all(source, target, send_sem, recv_sem):
        send_steps(0, devices // 8, source, target, send_sem, recv_sem)
        send_own(source, target, recv_sem)

    def wait_bytes(ref, sem):
        pltpu.make_async_copy(ref, ref, sem).wait()

    for array, ref in enumerate((q_ref, k_ref, v_ref, g_ref)):
        pltpu.make_async_copy(ref, inputs.at[array], input_sem).start()
    barrier = pltpu.get_barrier_semaphore()

    def greet(seq_to, clu_to):
        pl.semaphore_signal(barrier, inc=1, device_id=(seq_to, clu_to), device_id_type=MESH)

    for_peers(0, devices // 8, greet)

    sub = lax.broadcasted_iota(jnp.int32, (TOK, TOK), 0)
    lane = lax.broadcasted_iota(jnp.int32, (TOK, TOK), 1)
    sub_f = sub.astype(jnp.float32)
    lane_f = lane.astype(jnp.float32)
    ids_l = jnp.broadcast_to(ids_ref[...].astype(jnp.float32), (TOK, TOK))
    ids_s = ids_l.T
    one = jnp.ones((TOK, TOK), jnp.float32)
    zero = jnp.zeros((TOK, TOK), jnp.float32)
    same = ids_l == ids_s
    rank_l = jnp.sum(jnp.where(same & (sub < lane), one, zero), axis=0, keepdims=True)
    rank_s = jnp.sum(jnp.where(same & (lane < sub), one, zero), axis=1, keepdims=True)
    count_l = jnp.sum(jnp.where(same, one, zero), axis=0, keepdims=True)
    cnt_send[...] = jnp.sum(jnp.where(ids_s == lane_f, one, zero), axis=0, keepdims=True)
    ids_row = ids_l[0:1, :]
    heavy = jnp.min(jnp.where(count_l == 4.0, ids_row, 999.0), axis=1, keepdims=True)
    group_l = jnp.floor(ids_l * (1.0 / 16.0))
    group_s = jnp.floor(ids_s * (1.0 / 16.0))
    earlier = (ids_s < ids_l) | (same & (sub < lane))
    later = (ids_l < ids_s) | (same & (lane < sub))
    before = (group_l == group_s) & (ids_s != heavy) & (rank_s >= 1.0) & earlier
    over_at = jnp.sum(jnp.where(before, one, zero), axis=0, keepdims=True)
    behind = (group_l == group_s) & (ids_l != heavy) & (rank_l >= 1.0) & later
    over_at_s = jnp.sum(jnp.where(behind, one, zero), axis=1, keepdims=True)
    excess_s = (ids_s != heavy) & (rank_s >= 1.0) & (over_at_s >= 4.0)
    excess_at = jnp.sum(jnp.where(excess_s & earlier, one, zero), axis=0, keepdims=True)
    light_l = ids_l != heavy
    slot_group = (sub // 16).astype(jnp.float32)
    in_tile = sub % 16
    over_l = light_l & (rank_l >= 1.0)

    def tile_picks(tile):
        at_slot = (in_tile % 4).astype(jnp.float32)
        if tile < 4:
            cluster = slot_group * 16.0 + at_slot + 4.0 * tile
            taken = (ids_l == cluster) & (rank_l == 0.0) & light_l
        else:
            taken = (group_l == slot_group) & over_l & (over_at == at_slot)
        return [jnp.where(taken & (in_tile // 4 == array), one, zero) for array in range(4)]

    def rest_picks():
        picks = []
        for array in range(4):
            chosen = (ids_l == heavy) & (rank_l == (sub % 4).astype(jnp.float32))
            chosen = chosen & (sub // 4 == array) & (sub < 16)
            beyond = over_l & (over_at >= 4.0) & (excess_at == (sub % 8).astype(jnp.float32))
            beyond = beyond & (sub // 8 == array + 2)
            picks.append(jnp.where(chosen | beyond, one, zero))
        return picks

    def put_pack(at_row, count, picks):
        for array, matrix in enumerate(picks):
            pack_mat[pl.ds(at_row, count), pl.ds(array * TOK, TOK)] = matrix[:count].astype(
                jnp.bfloat16
            )

    put_pack(0, TOK, tile_picks(0))
    put_pack(TOK, TOK, tile_picks(4))
    put_pack(2 * TOK, 48, rest_picks())


    def send_line(source, target, count, at, device, send_sem, recv_sem):
        def one_peer(step, carry):
            to = lax.rem(at + step, count)
            pltpu.make_async_remote_copy(
                src_ref=source(to),
                dst_ref=target,
                send_sem=send_sem,
                recv_sem=recv_sem,
                device_id=device(to),
                device_id_type=MESH,
            ).start()
            return carry

        lax.fori_loop(1, count, one_peer, 0)
        pltpu.make_async_copy(source(at), target, recv_sem).start()

    def along_seq(source, target, send_sem, recv_sem):
        send_line(
            source, target.at[seq_at], heads, seq_at, lambda to: (to, clu_at), send_sem, recv_sem
        )

    def along_clu(source, target, send_sem, recv_sem):
        send_line(
            source, target.at[clu_at], groups, clu_at, lambda to: (seq_at, to), send_sem, recv_sem
        )


    def head_rows(at):
        cols = pl.ds(pl.multiple_of(at * 2 * DH, 2 * DH), 2 * DH)
        return [inputs[array, :, cols] for array in range(4)]

    def put_tile(target, at, tile, packed):
        low = packed.astype(jnp.bfloat16)
        for k in range(2):
            target[pl.ds((2 * at + k) * groups, groups), tile] = low[
                :, k * DH : (k + 1) * DH
            ].reshape(groups, 16, DH)

    def pack_a(at, carry):
        rows = jnp.concatenate(head_rows(at), axis=0)
        packed = bf16_dot(pack_mat[pl.ds(0, 2 * TOK + 48), :], rows)
        put_tile(send_a, at, 0, packed[:TOK])
        put_tile(send_a, at, 1, packed[TOK : 2 * TOK])
        rest = packed[2 * TOK :].astype(jnp.bfloat16)
        for k in range(2):
            hsend[2 * at + k] = rest[:16, k * DH : (k + 1) * DH]
            ex_send[2 * at + k] = rest[16:, k * DH : (k + 1) * DH]
        return carry

    wait_bytes(inputs, input_sem)
    lax.fori_loop(0, heads // 2, pack_a, 0, unroll=4)
    pl.semaphore_wait(barrier, devices - 1)
    along_clu(lambda to: cnt_send, cnt_group, cnt_send_sem, cnt_sem)

    def send_heavy(step, carry):
        head = lax.rem(seq_at + step, heads)
        clu_to = lax.rem(head, groups)

        @pl.when(head * groups + clu_to != me)
        def _():
            pltpu.make_async_remote_copy(
                src_ref=hsend.at[head],
                dst_ref=hrecv.at[me],
                send_sem=hsend_sem,
                recv_sem=hrecv_sem,
                device_id=(head, clu_to),
                device_id_type=MESH,
            ).start()

        @pl.when(head * groups + clu_to == me)
        def _():
            pltpu.make_async_copy(hsend.at[head], hrecv.at[me], hrecv_sem).start()

        return carry

    lax.fori_loop(0, heads, send_heavy, 0)
    along_seq(lambda to: ex_send.at[to], ex_recv, ex_send_sem, ex_recv_sem)
    out_a = (send_a, recv_a.at[me], send_a_sem, recv_a_sem)
    send_steps(0, 4, *out_a)
    wait_bytes(cnt_group, cnt_sem)
    along_seq(lambda to: cnt_group, cnt_recv, cnt2_send_sem, cnt2_sem)
    send_steps(4, devices // 8 - 4, *out_a)
    send_own(send_a, recv_a.at[me], recv_a_sem)

    for tile in range(1, 4):
        put_pack((tile + 1) * TOK + 48, TOK, tile_picks(tile))

    def pack_bc(at, carry):
        rows = jnp.concatenate(head_rows(at), axis=0)
        packed = bf16_dot(pack_mat[pl.ds(2 * TOK + 48, 3 * TOK), :], rows)
        put_tile(send_b, at, 0, packed[:TOK])
        put_tile(send_b, at, 1, packed[TOK : 2 * TOK])
        put_tile(send_c, at, 0, packed[2 * TOK :])
        return carry

    lax.fori_loop(0, heads // 2, pack_bc, 0)

    wait_bytes(cnt_recv, cnt2_sem)
    seen = cnt_recv[...].reshape(TOK, TOK)
    heavies = jnp.min(jnp.where(seen == 4.0, lane_f, 999.0), axis=1, keepdims=True)
    heavy_all = jnp.min(heavies, axis=0, keepdims=True)
    light = lane_f != heavy_all
    more = jnp.where(light, jnp.maximum(seen - 1.0, 0.0), 0.0)
    more_low = more.astype(jnp.bfloat16)
    in_group = jnp.where(sub // 16 == lane, one, zero).astype(jnp.bfloat16)
    ahead = jnp.where(sub < lane, one, zero).astype(jnp.bfloat16)
    prior = jnp.where(lane < sub, one, zero).astype(jnp.bfloat16)
    mates = (lane < sub) & (lane % 8 == sub % 8)
    mates = jnp.where(mates, one, zero).astype(jnp.bfloat16)
    excess = jnp.maximum(bf16_dot(more_low, in_group) - 4.0, 0.0)
    excess_low = excess.astype(jnp.bfloat16)
    excess_off = bf16_dot(excess_low, ahead)
    excess_pre = bf16_dot(mates, excess_low)
    bad = (jnp.sum(excess, axis=1, keepdims=True) > 8.0) | (excess_pre + excess > 16.0)
    bad = bad | (heavies != heavy_all) | (jnp.sum(more, axis=0, keepdims=True) > OVC)
    flag_ref[0, 0] = jnp.max(jnp.where(bad, one, zero)).astype(jnp.int32)

    spot = zero
    for group in range(8):
        off, count, pre = [a[:, group : group + 1] for a in (excess_off, excess, excess_pre)]
        held = (lane_f >= off) & (lane_f < off + count)
        spot = spot + jnp.where(held, lane_f + (group * 16 + 1.0) - off + pre, zero)
    spot = jnp.where(sub % 8 == clu_at, spot, zero).reshape(16, 8, TOK)
    spot = jnp.sum(spot, axis=1).astype(jnp.bfloat16)
    spread8 = jnp.where(lane % 8 == sub, one, zero).astype(jnp.bfloat16)
    spot = jnp.where(lane[:16] // 8 == sub[:16], bf16_dot(spot, spread8), 0.0)
    spot = jnp.sum(spot, axis=0, keepdims=True) - 1.0
    to_mate[...] = jnp.where(sub_f == spot, one, zero).astype(jnp.bfloat16)
    spot = jnp.broadcast_to(spot, (TOK, TOK)).T
    to_block[...] = jnp.where(spot == lane_f, one, zero).astype(jnp.bfloat16)

    wait_bytes(ex_recv, ex_recv_sem)
    held = ex_recv[...].astype(jnp.float32)
    held = [held[:, 8 * a : 8 * a + 8, :].reshape(TOK, DH) for a in range(4)]
    held = jnp.concatenate(held, axis=1).astype(jnp.bfloat16)
    held = bf16_dot(to_mate[...], held).astype(jnp.bfloat16)
    for a in range(4):
        ex_send2[:, a] = held[:, a * DH : (a + 1) * DH].reshape(8, 16, DH)
    along_clu(lambda to: ex_send2.at[to], ex_recv2, ex_send2_sem, ex_recv2_sem)
    send_to_all(send_b, recv_b.at[me], send_b_sem, recv_b_sem)
    send_to_all(send_c, recv_c.at[me], send_c_sem, recv_c_sem)

    valid = jnp.where((seen > 0.0) & light, one, zero).astype(jnp.bfloat16)
    mine = (sub == clu_at * 16 + lane) & (lane < 16)
    mine = jnp.where(mine, one, zero).astype(jnp.bfloat16)
    more_g = bf16_dot(more_low, mine)
    valid_g = bf16_dot(valid, mine)
    more_g_low = more_g.astype(jnp.bfloat16)
    start_g = bf16_dot(prior, more_g_low)
    offset_g = bf16_dot(more_g_low, ahead)
    beyond_g = jnp.maximum(bf16_dot(more_g_low, one.astype(jnp.bfloat16)) - 4.0, 0.0)
    pre_g = bf16_dot(mates, beyond_g.astype(jnp.bfloat16))
    ex_index = lane_f - pre_g + 4.0
    first_row = lax.broadcasted_iota(jnp.int32, (1, TOK), 1).astype(jnp.float32) * 16.0
    in_tile_at = zero
    beyond_at = zero
    for c in range(16):
        count, begin, off, real = [
            a[:, c : c + 1] for a in (more_g, start_g, offset_g, valid_g)
        ]
        place = begin - off + (c * OVC + 1.0)
        held = (lane_f >= off) & (lane_f < off + count) & (lane < 4)
        in_tile_at = in_tile_at + jnp.where(held, lane_f + place, zero)
        held = (ex_index >= off) & (ex_index < off + count) & (ex_index >= 4.0)
        beyond_at = beyond_at + jnp.where(held, ex_index + place, zero)
        held = (lane_f >= begin) & (lane_f < begin + count)
        where = jnp.where(held, sub_f * 16.0 + 1.0 + lane_f - begin, zero)
        where = jnp.sum(where, axis=0, keepdims=True)
        where = jnp.where(where > 0.0, where, FAR)
        query_row = jnp.concatenate([first_row, where], axis=1)
        query_pos[c] = jnp.broadcast_to(query_row, (8, 2 * TOK))
        key_pos[c, pl.ds(0, TOK), :] = jnp.where(real > 0.0, sub_f * 16.0, FAR)
        key_pos[c, pl.ds(TOK, OVC), :] = jnp.broadcast_to(where, (TOK, TOK)).T[:OVC]
    beyond_at = jnp.sum(beyond_at.reshape(16, 8, TOK), axis=0)
    high = jnp.floor(beyond_at * (1.0 / 32.0))
    split = jnp.concatenate([high, beyond_at - high * 32.0], axis=0).astype(jnp.bfloat16)
    spread16 = jnp.where(lane % 16 == sub, one, zero).astype(jnp.bfloat16)
    split = bf16_dot(split, spread16)
    split = jnp.where(lane[:8] // 16 == sub[:8], split[:8] * 32.0 + split[8:], 0.0)
    beyond_row = jnp.sum(split, axis=0, keepdims=True) - 1.0
    tile_rows = in_tile_at.T[0:8, :] - 1.0
    slot_rows = [tile_rows[k : k + 1, :] for k in range(4)] + [beyond_row]
    slot_cols = [in_tile_at[:, k : k + 1] - 1.0 for k in range(4)]
    slot_cols.append(jnp.broadcast_to(beyond_row, (TOK, TOK)).T)

    chunk = 4
    for k in range(5):
        for m in range(16 * OVC // TOK):
            onehot[pl.ds(k * TOK, TOK), pl.ds(m * TOK, TOK)] = jnp.where(
                slot_cols[k] == lane_f + float(m * TOK), one, zero
            ).astype(jnp.bfloat16)
            pick[pl.ds(m * TOK, TOK), pl.ds(k * TOK, TOK)] = jnp.where(
                slot_rows[k] == sub_f + float(m * TOK), one, zero
            ).astype(jnp.bfloat16)

    for at, tile in enumerate((0, 1, 2, None, 3, 4)):
        for array, matrix in enumerate(rest_picks() if tile is None else tile_picks(tile)):
            unpack_mat[pl.ds(array * TOK, TOK), pl.ds(at * TOK, TOK)] = matrix.T.astype(
                jnp.bfloat16
            )

    perm = flip_perm()

    def arrange(source, target, units):
        def two_sets(at, carry):
            blocks = [pl.ds(pl.multiple_of((2 * at + i) * SET, SET), SET) for i in range(2)]
            spots = [(held, unit) for held in blocks for unit in range(units)]
            rows = jnp.concatenate(
                [source(held, unit).reshape(SET * 16, DH) for held, unit in spots], axis=1
            )
            turned = bf16_dot(perm, rows).astype(jnp.bfloat16)
            for i, (held, unit) in enumerate(spots):
                target(held, unit, turned[:, i * DH : (i + 1) * DH].reshape(16, SET, DH))
            return carry

        lax.fori_loop(0, devices // (2 * SET), two_sets, 0, unroll=2)

    def put_table(first):
        def put(blocks, unit, value):
            table[first + unit, :, blocks, :] = value

        return put

    @pl.when(is_heavy_owner)
    def _():
        wait_bytes(hrecv, hrecv_sem)

        def put_heavy(blocks, unit, value):
            htable[:, blocks, :] = value

        arrange(lambda blocks, unit: hrecv[blocks], put_heavy, 1)
        k_h, v_h = [htable[4 * a : 4 * a + 4].reshape(4 * TOK, DH) for a in (1, 2)]
        hacc[...] = jnp.zeros_like(hacc)
        key_sub = lax.broadcasted_iota(jnp.int32, (4 * TOK, TOK), 0)
        key_at = lax.rem(key_sub, TOK) * 4 + lax.div(key_sub, TOK)
        query_at = lax.broadcasted_iota(jnp.int32, (4 * TOK, TOK), 1) * 4

        def heavy_tile(s, carry):
            out, dq, dk, dv = attend(
                htable[s], k_h, v_h, htable[12 + s], key_at <= query_at + s, inv_root
            )
            hacc[2, pl.ds(pl.multiple_of(s * TOK, TOK), TOK)] = out.astype(jnp.float32)
            hacc[3, pl.ds(pl.multiple_of(s * TOK, TOK), TOK)] = dq.astype(jnp.float32)
            hacc[0] += dk
            hacc[1] += dv
            return carry

        lax.fori_loop(0, 4, heavy_tile, 0)
        for array, at in enumerate((2, 3, 0, 1)):
            htable[4 * array : 4 * array + 4] = (
                hacc[at].astype(jnp.bfloat16).reshape(4, TOK, DH)
            )

        def put_hresult(blocks, unit, value):
            hresult[blocks] = value

        arrange(lambda blocks, unit: htable[:, blocks, :], put_hresult, 1)
        send_to_all(hresult, hback.at[seq_at], hres_sem, hback_sem)

    wait_bytes(recv_a, recv_a_sem)
    def put_tile_a(blocks, unit, value):
        table[4 * unit, :, blocks, :] = value

    arrange(lambda blocks, unit: recv_a[blocks, unit], put_tile_a, 2)

    wait_bytes(ex_recv2, ex_recv2_sem)
    for a in range(4):
        cols = pl.ds(a * DH, DH)
        loose[pl.ds(0, 4 * TOK), cols] = table[4, 4 * a : 4 * a + 4].reshape(4 * TOK, DH)
        loose[pl.ds(4 * TOK, TOK), cols] = ex_recv2[:, a].reshape(TOK, DH)

    def gather_chunk(at, carry):
        chosen = pick[pl.ds(pl.multiple_of(at * chunk * OVC, 64), chunk * OVC), :]
        found = bf16_dot(chosen, loose[...]).astype(jnp.bfloat16)
        for c in range(chunk):
            for array in range(4):
                over[array, at * chunk + c] = found[
                    c * OVC : (c + 1) * OVC, array * DH : (array + 1) * DH
                ]
        return carry

    gather_chunk(0, 0)

    pad_rows = jnp.zeros((TOK - OVC, DH), jnp.bfloat16)

    def load_cluster(tile, j):
        c = tile * 4 + j
        rows = [
            jnp.concatenate([table[tile, a * 4 + j], over[a, c]], axis=0) for a in range(4)
        ]
        for a in (0, 3):
            rows[a] = jnp.concatenate([rows[a], pad_rows], axis=0)
        key_at = key_pos[c]
        allowed = jnp.concatenate([key_at, key_at], axis=1) <= query_pos[c, 0:1, :]
        return rows + [allowed]

    def attend_tiles(first, tiles):
        def one_tile(at, carry):
            tile = first + at
            spots = range(4)
            loaded = [load_cluster(tile, j) for j in spots]
            found = [attend(*arrays, inv_root) for arrays in loaded]
            for j, results in zip(spots, found):
                c = tile * 4 + j
                for a, value in enumerate(results):
                    value = value.astype(jnp.bfloat16)
                    table[tile, a * 4 + j] = value[:TOK]
                    over_res[
                        pl.ds(pl.multiple_of(c * OVC, 16), OVC), pl.ds(a * DH, DH)
                    ] = value[TOK : TOK + OVC]
            return carry

        lax.fori_loop(0, tiles, one_tile, 0)

    def put_in(result):
        def put(blocks, unit, value):
            result[blocks, unit] = value

        return put

    def from_table(first):
        return lambda blocks, unit: table[first + unit, :, blocks, :]

    to_a = (result_a, back_a.at[me], res_a_sem, back_a_sem)
    to_b = (result_b, back_b.at[me], res_b_sem, back_b_sem)
    to_c = (result_c, back_c.at[me], res_c_sem, back_c_sem)
    attend_tiles(0, 1)
    arrange(from_table(0), put_in(result_a), 1)
    send_to_all(*to_a)
    lax.fori_loop(1, 16 // chunk, gather_chunk, 0)

    wait_bytes(recv_b, recv_b_sem)
    arrange(lambda blocks, unit: recv_b[blocks, unit], put_table(1), 2)
    attend_tiles(1, 2)
    arrange(from_table(1), put_in(result_b), 2)
    send_to_all(*to_b)

    wait_bytes(recv_c, recv_c_sem)
    arrange(lambda blocks, unit: recv_c[blocks, 0], put_table(3), 1)
    attend_tiles(3, 1)

    found = bf16_dot(onehot[pl.ds(4 * TOK, TOK), :], over_res[...]).astype(jnp.bfloat16)
    for a in range(4):
        ex_ret2[:, a] = found[:, a * DH : (a + 1) * DH].reshape(8, 16, DH)
    along_clu(lambda to: ex_ret2.at[to], ex_back2, ex_ret2_sem, ex_back2_sem)
    found = bf16_dot(onehot[pl.ds(0, 4 * TOK), :], over_res[...]).astype(jnp.bfloat16)
    for a in range(4):
        table[4, 4 * a : 4 * a + 4] = found[:, a * DH : (a + 1) * DH].reshape(4, TOK, DH)
    arrange(from_table(3), put_in(result_c), 2)
    send_steps(0, devices // 16, *to_c)
    send_own(result_c, back_c.at[me], back_c_sem)

    wait_bytes(ex_back2, ex_back2_sem)
    held = [ex_back2[:, a].reshape(TOK, DH) for a in range(4)]
    held = bf16_dot(to_block[...], jnp.concatenate(held, axis=1))
    held = [held[:, a * DH : (a + 1) * DH].reshape(16, 8, DH) for a in range(4)]
    ex_ret1[...] = jnp.concatenate(held, axis=1).astype(jnp.bfloat16)
    along_seq(lambda to: ex_ret1.at[to], ex_back1, ex_ret1_sem, ex_back1_sem)
    send_steps(devices // 16, devices // 16, *to_c)

    def unpack(tiles, rest, first, count):
        sides = []
        for k in range(2):
            sides.append(
                jnp.concatenate(
                    [tile(k).reshape(TOK, DH) for tile in tiles] + [part(k) for part in rest],
                    axis=0,
                )
            )
        return bf16_dot(
            unpack_mat[:, pl.ds(first, count)], jnp.concatenate(sides, axis=1)
        )

    def tile_of(ref, at, tile):
        return lambda k: ref[pl.ds((2 * at + k) * groups, groups), tile]

    def unpack_early(at, carry):
        tiles = [tile_of(back_a, at, 0), tile_of(back_b, at, 0), tile_of(back_b, at, 1)]
        rest = [
            lambda k: hback[2 * at + k],
            lambda k: ex_back1[2 * at + k],
            lambda k: jnp.zeros((TOK - 48, DH), jnp.bfloat16),
        ]
        early[at] = unpack(tiles, rest, 0, 4 * TOK)
        return carry

    def unpack_last(at, carry):
        cols = pl.ds(pl.multiple_of(at * 2 * DH, 2 * DH), 2 * DH)
        tiles = [tile_of(back_c, at, 0), tile_of(back_c, at, 1)]
        found = (early[at] + unpack(tiles, [], 4 * TOK, 2 * TOK)).astype(jnp.bfloat16)
        for array, ref in enumerate((out_ref, dq_ref, dk_ref, dv_ref)):
            ref[:, cols] = found[array * TOK : (array + 1) * TOK]
        return carry

    wait_bytes(hback, hback_sem)
    wait_bytes(back_a, back_a_sem)
    wait_bytes(back_b, back_b_sem)
    wait_bytes(ex_back1, ex_back1_sem)
    lax.fori_loop(0, heads // 2, unpack_early, 0, unroll=2)
    wait_bytes(back_c, back_c_sem)
    lax.fori_loop(0, heads // 2, unpack_last, 0, unroll=2)

    others = pl.ds(0, devices - 1)
    wait_bytes(cnt_group.at[pl.ds(0, groups - 1)], cnt_send_sem)
    wait_bytes(cnt_recv.at[pl.ds(0, heads - 1)], cnt2_send_sem)
    for ref, sem in ((ex_send, ex_send_sem), (ex_ret1, ex_ret1_sem)):
        wait_bytes(ref.at[pl.ds(0, heads - 1)], sem)
    for ref, sem in ((ex_send2, ex_send2_sem), (ex_ret2, ex_ret2_sem)):
        wait_bytes(ref.at[pl.ds(0, groups - 1)], sem)
    wait_bytes(send_a.at[others], send_a_sem)
    wait_bytes(send_b.at[others], send_b_sem)
    wait_bytes(send_c.at[others], send_c_sem)
    wait_bytes(result_a.at[others], res_a_sem)
    wait_bytes(result_b.at[others], res_b_sem)
    wait_bytes(result_c.at[others], res_c_sem)

    @pl.when(is_heavy_owner)
    def _():
        wait_bytes(hsend.at[pl.ds(0, heads - 1)], hsend_sem)
        wait_bytes(hresult.at[others], hres_sem)

    @pl.when(jnp.logical_not(is_heavy_owner))
    def _():
        wait_bytes(hsend, hsend_sem)


def fast_path(queries, key_rows, value_rows, out_grad, cluster_ids):
    tok_rows, columns = queries.shape
    heads = columns // DH
    groups = lax.axis_size("clu")
    devices = lax.axis_size("seq") * groups
    low = jnp.bfloat16
    wide = jnp.float32
    rows = pltpu.VMEM((tok_rows, columns), low)
    vmem = pl.BlockSpec(memory_space=pltpu.VMEM)
    smem = pl.BlockSpec(memory_space=pltpu.SMEM)
    return pl.pallas_call(
        fast_kernel,
        out_shape=[rows] * 4 + [jax.ShapeDtypeStruct((1, 1), jnp.int32)],
        in_specs=[vmem] + [pl.BlockSpec(memory_space=pl.ANY)] * 4,
        out_specs=[vmem] * 4 + [smem],
        scratch_shapes=[
            pltpu.VMEM((1, TOK), wide),
            pltpu.VMEM((groups, 1, TOK), wide),
            pltpu.VMEM((heads, groups, 1, TOK), wide),
            pltpu.VMEM((5 * TOK + 48, 4 * TOK), low),
            pltpu.VMEM((4 * TOK, 6 * TOK), low),
            pltpu.VMEM((devices, 2, 16, DH), low),
            pltpu.VMEM((devices, 2, 16, DH), low),
            pltpu.VMEM((devices, 1, 16, DH), low),
            pltpu.VMEM((devices, 2, 16, DH), low),
            pltpu.VMEM((devices, 2, 16, DH), low),
            pltpu.VMEM((devices, 1, 16, DH), low),
            pltpu.VMEM((5, 16, devices, DH), low),
            pltpu.VMEM((4, 16, OVC, DH), low),
            pltpu.VMEM((16, TOK + OVC, TOK), wide),
            pltpu.VMEM((16, 8, 2 * TOK), wide),
            pltpu.VMEM((16 * OVC, 5 * TOK), low),
            pltpu.VMEM((5 * TOK, 16 * OVC), low),
            pltpu.VMEM((5 * TOK, 4 * DH), low),
            pltpu.VMEM((16 * OVC, 4 * DH), low),
            pltpu.VMEM((TOK, TOK), low),
            pltpu.VMEM((TOK, TOK), low),
            pltpu.VMEM((devices, 1, 16, DH), low),
            pltpu.VMEM((devices, 2, 16, DH), low),
            pltpu.VMEM((devices, 2, 16, DH), low),
            pltpu.VMEM((devices, 1, 16, DH), low),
            pltpu.VMEM((devices, 2, 16, DH), low),
            pltpu.VMEM((devices, 2, 16, DH), low),
            pltpu.VMEM((heads, 32, DH), low),
            pltpu.VMEM((heads, 32, DH), low),
            pltpu.VMEM((groups, 4, 16, DH), low),
            pltpu.VMEM((groups, 4, 16, DH), low),
            pltpu.VMEM((groups, 4, 16, DH), low),
            pltpu.VMEM((groups, 4, 16, DH), low),
            pltpu.VMEM((heads, 32, DH), low),
            pltpu.VMEM((heads, 32, DH), low),
            pltpu.VMEM((heads, 16, DH), low),
            pltpu.VMEM((devices, 16, DH), low),
            pltpu.VMEM((16, devices, DH), low),
            pltpu.VMEM((4, 4 * TOK, DH), wide),
            pltpu.VMEM((devices, 16, DH), low),
            pltpu.VMEM((heads, 16, DH), low),
            pltpu.VMEM((4, tok_rows, columns), low),
            pltpu.VMEM((heads // 2, 4 * tok_rows, 2 * DH), wide),
        ]
        + [pltpu.SemaphoreType.DMA] * 29,
        compiler_params=pltpu.CompilerParams(
            collective_id=0, has_side_effects=True, vmem_limit_bytes=44 * 1024 * 1024
        ),
    )(cluster_ids.reshape(1, tok_rows), queries, key_rows, value_rows, out_grad)


def copy_kernel(*refs):
    sem = refs[-1]
    copies = [
        pltpu.make_async_copy(refs[i], refs[4 + i], sem.at[i]) for i in range(4)
    ]
    for copy in copies:
        copy.start()
    for copy in copies:
        copy.wait()


def copy_out(arrays):
    anywhere = pl.BlockSpec(memory_space=pl.ANY)
    return pl.pallas_call(
        copy_kernel,
        out_shape=[pltpu.HBM(a.shape, a.dtype) for a in arrays],
        in_specs=[anywhere] * 4,
        out_specs=[anywhere] * 4,
        scratch_shapes=[pltpu.SemaphoreType.DMA((4,))],
    )(*arrays)


def per_device(queries, key_rows, value_rows, out_grad, cluster_ids):
    arrays = (queries, key_rows, value_rows, out_grad, cluster_ids)
    *fast, flag = fast_path(*arrays)
    return lax.cond(
        flag.reshape(()) != 0,
        lambda arrays, fast: full_capacity(*arrays),
        lambda arrays, fast: tuple(copy_out(fast)),
        arrays,
        tuple(fast),
    )


def solution(mesh):
    in_specs = (
        P(("seq", "clu"), None),
        P(("seq", "clu"), None),
        P(("seq", "clu"), None),
        P(("seq", "clu"), None),
        P(("seq", "clu")),
    )
    out_specs = (
        P(("seq", "clu"), None),
        P(("seq", "clu"), None),
        P(("seq", "clu"), None),
        P(("seq", "clu"), None),
    )
    return jax.shard_map(
        per_device, mesh=mesh, in_specs=in_specs, out_specs=out_specs, check_vma=False
    )
```

```python
import math

import jax
import jax.numpy as jnp
from jax import lax
from jax.experimental import pallas as pl
from jax.experimental.pallas import tpu as pltpu
from jax.sharding import PartitionSpec as P

DH = 128
TOK = 128
OVC = 80
SET = 16
FAR = 1e9
MESH = pl.DeviceIdType.MESH


masked = -1e30


def contract_last(left, right):
    return lax.dot_general(
        left, right, (((1,), (1,)), ((), ())), preferred_element_type=jnp.float32
    )


def contract_first(left, right):
    return lax.dot_general(
        left, right, (((0,), (0,)), ((), ())), preferred_element_type=jnp.float32
    )


def softmax_rows(query_head, key_head, allowed, inv_root):
    scores = contract_last(query_head, key_head) * inv_root
    scores = jnp.where(allowed, scores, masked)
    row_max = jnp.max(scores, axis=1, keepdims=True)
    weights = jnp.exp(scores - row_max)
    row_sum = jnp.sum(weights, axis=1, keepdims=True)
    return (weights / row_sum).astype(jnp.bfloat16)


def head_slice(array, head_index):
    return lax.dynamic_slice_in_dim(array, head_index * DH, DH, 1)


def full_capacity(queries, key_rows, value_rows, out_grad, cluster_ids):
    seq_count = lax.axis_size("seq")
    clu_count = lax.axis_size("clu")
    devices = seq_count * clu_count
    tok_rows = queries.shape[0]
    columns = queries.shape[1]
    head_count = columns // DH
    most_rows = 4 * tok_rows // devices
    capacity = most_rows * devices
    inv_root = 1.0 / math.sqrt(DH)
    owners = jnp.arange(devices, dtype=jnp.int32)
    member = (cluster_ids[:, None] == owners[None, :]).astype(jnp.int32)
    running = jnp.cumsum(member, axis=0) - 1
    slot_rank = jnp.sum(member * running, axis=1)
    sent_counts = jnp.sum(member, axis=0).reshape(devices, 1)
    slot_index = cluster_ids * most_rows + slot_rank
    stacked = jnp.concatenate([queries, key_rows, value_rows], axis=1)
    width_in = stacked.shape[1]
    packed = jnp.zeros((devices * most_rows, width_in), jnp.bfloat16).at[slot_index].set(stacked)
    packed = packed.reshape(devices, most_rows, width_in)
    got_rows, got_counts = (
        lax.all_to_all(packed, ("seq", "clu"), split_axis=0, concat_axis=0, tiled=True),
        lax.all_to_all(sent_counts, ("seq", "clu"), split_axis=0, concat_axis=0, tiled=True),
    )
    got_counts = got_counts.reshape(devices)
    starts = jnp.cumsum(got_counts) - got_counts
    live_total = jnp.sum(got_counts)
    within = jnp.arange(most_rows, dtype=jnp.int32)
    target = jnp.where(
        within[None, :] < got_counts[:, None], starts[:, None] + within[None, :], capacity
    )
    target = target.reshape(devices * most_rows)
    gathered = (
        jnp.zeros((capacity, width_in), jnp.bfloat16)
        .at[target]
        .set(got_rows.reshape(devices * most_rows, width_in), mode="drop")
    )
    query_block = gathered[:, :columns]
    key_block = gathered[:, columns : 2 * columns]
    value_block = gathered[:, 2 * columns : 3 * columns]
    positions = jnp.arange(capacity, dtype=jnp.int32)
    allowed = (positions[None, :] <= positions[:, None]) & (positions[None, :] < live_total)

    def forward_head(head_index, mixed_rows):
        weights_low = softmax_rows(
            head_slice(query_block, head_index),
            head_slice(key_block, head_index),
            allowed,
            inv_root,
        )
        out_head = jnp.dot(
            weights_low, head_slice(value_block, head_index), preferred_element_type=jnp.float32
        ).astype(jnp.bfloat16)
        return lax.dynamic_update_slice_in_dim(mixed_rows, out_head, head_index * DH, 1)

    mixed_rows = lax.fori_loop(
        0, head_count, forward_head, jnp.zeros((capacity, columns), jnp.bfloat16)
    )
    back_index = jnp.minimum(target, capacity - 1)
    outgoing = jnp.take(mixed_rows, back_index, axis=0).reshape(devices, most_rows, columns)
    grad_packed = (
        jnp.zeros((devices * most_rows, columns), jnp.bfloat16).at[slot_index].set(out_grad)
    )
    grad_packed = grad_packed.reshape(devices, most_rows, columns)
    returned = lax.all_to_all(outgoing, ("seq", "clu"), split_axis=0, concat_axis=0, tiled=True)
    got_grad = lax.all_to_all(grad_packed, ("seq", "clu"), split_axis=0, concat_axis=0, tiled=True)
    attention_out = jnp.take(returned.reshape(devices * most_rows, columns), slot_index, axis=0)
    grad_block = (
        jnp.zeros((capacity, columns), jnp.bfloat16)
        .at[target]
        .set(got_grad.reshape(devices * most_rows, columns), mode="drop")
    )
    delta_rows = jnp.sum(
        (grad_block.astype(jnp.float32) * mixed_rows.astype(jnp.float32)).reshape(
            capacity, head_count, DH
        ),
        axis=2,
    )

    def backward_head(head_index, grad_rows):
        query_head = head_slice(query_block, head_index)
        key_head = head_slice(key_block, head_index)
        value_head = head_slice(value_block, head_index)
        grad_head = head_slice(grad_block, head_index)
        weights_low = softmax_rows(query_head, key_head, allowed, inv_root)
        prob_grad = contract_last(grad_head, value_head)
        delta_head = lax.dynamic_slice_in_dim(delta_rows, head_index, 1, 1)
        score_grad = (weights_low.astype(jnp.float32) * (prob_grad - delta_head)).astype(
            jnp.bfloat16
        )
        query_part = (
            jnp.dot(score_grad, key_head, preferred_element_type=jnp.float32) * inv_root
        ).astype(jnp.bfloat16)
        key_part = (contract_first(score_grad, query_head) * inv_root).astype(jnp.bfloat16)
        value_part = contract_first(weights_low, grad_head).astype(jnp.bfloat16)
        grad_rows = lax.dynamic_update_slice_in_dim(grad_rows, query_part, head_index * DH, 1)
        grad_rows = lax.dynamic_update_slice_in_dim(
            grad_rows, key_part, columns + head_index * DH, 1
        )
        return lax.dynamic_update_slice_in_dim(
            grad_rows, value_part, 2 * columns + head_index * DH, 1
        )

    grad_rows = lax.fori_loop(
        0, head_count, backward_head, jnp.zeros((capacity, 3 * columns), jnp.bfloat16)
    )
    outgoing_grads = jnp.take(grad_rows, back_index, axis=0).reshape(
        devices, most_rows, 3 * columns
    )
    returned_grads = lax.all_to_all(
        outgoing_grads, ("seq", "clu"), split_axis=0, concat_axis=0, tiled=True
    )
    picked = jnp.take(returned_grads.reshape(devices * most_rows, 3 * columns), slot_index, axis=0)
    return (
        attention_out,
        picked[:, :columns],
        picked[:, columns : 2 * columns],
        picked[:, 2 * columns :],
    )


def bf16_dot(left, right):
    return jnp.dot(left, right, preferred_element_type=jnp.float32)


def flip_perm():
    row = lax.broadcasted_iota(jnp.int32, (SET * 16, SET * 16), 0)
    col = lax.broadcasted_iota(jnp.int32, (SET * 16, SET * 16), 1)
    swapped = (col % 16) * 16 + col // 16
    return (row == swapped).astype(jnp.float32).astype(jnp.bfloat16)


def attend(q, k, v, g, allowed, inv_root):
    raw = jnp.where(allowed, contract_last(k, q), masked)
    most = jnp.max(raw, axis=0, keepdims=True)
    weights = jnp.exp2((raw - most) * (inv_root * math.log2(math.e)))
    prob = weights * (1.0 / jnp.sum(weights, axis=0, keepdims=True))
    prob_low = prob.astype(jnp.bfloat16)
    prob_grad = contract_last(v, g)
    delta = jnp.sum(prob * prob_grad, axis=0, keepdims=True)
    score_grad = (prob * (prob_grad - delta)).astype(jnp.bfloat16)
    out = contract_first(v, prob_low).T.astype(jnp.bfloat16)
    dq = (contract_first(k, score_grad).T * inv_root).astype(jnp.bfloat16)
    dk = bf16_dot(score_grad, q) * inv_root
    dv = bf16_dot(prob_low, g)
    return out, dq, dk, dv


def fast_kernel(
    ids_ref, q_ref, k_ref, v_ref, g_ref,
    out_ref, dq_ref, dk_ref, dv_ref, flag_ref,
    cnt_send, cnt_group, cnt_recv, pack_mat, unpack_mat,
    send_a, send_b, send_c, recv_a, recv_b, recv_c, table,
    over, key_pos, query_pos, pick, onehot, loose, over_res, to_mate, to_block,
    result_a, result_b, result_c, back_a, back_b, back_c,
    ex_send, ex_recv, ex_send2, ex_recv2, ex_ret2, ex_back2, ex_ret1, ex_back1,
    hsend, hrecv, htable, hacc, hresult, hback, inputs, early,
    cnt_send_sem, cnt_sem, cnt2_send_sem, cnt2_sem,
    send_a_sem, recv_a_sem, send_b_sem, recv_b_sem, send_c_sem, recv_c_sem,
    res_a_sem, back_a_sem, res_b_sem, back_b_sem, res_c_sem, back_c_sem,
    ex_send_sem, ex_recv_sem, ex_send2_sem, ex_recv2_sem,
    ex_ret2_sem, ex_back2_sem, ex_ret1_sem, ex_back1_sem,
    hsend_sem, hrecv_sem, hres_sem, hback_sem, input_sem,
):
    seq_at = lax.axis_index("seq")
    clu_at = lax.axis_index("clu")
    groups = lax.axis_size("clu")
    heads = lax.axis_size("seq")
    devices = heads * groups
    me = seq_at * groups + clu_at
    inv_root = 1.0 / math.sqrt(DH)
    is_heavy_owner = lax.rem(seq_at, groups) == clu_at
    at_x, at_z = lax.div(seq_at, 4), lax.rem(seq_at, 4)
    at_y, at_core = lax.div(clu_at, 2), lax.rem(clu_at, 2)

    def by_core(first, second):
        return first + at_core * (second - first)

    eight = []
    for by_x, by_z, by_clu in zip(
        zip((3, 2, 1, 2, 3, 0, 2, 0), (1, 2, 0, 1, 2, 3, 0, 2)),
        zip((0, 0, 3, 2, 1, 2, 3, 1), (2, 2, 1, 0, 3, 0, 0, 2)),
        zip((2, 1, 0, 3, 6, 4, 5, 7), (6, 5, 4, 7, 2, 0, 1, 3)),
    ):
        y = lax.rem(at_y + by_core(by_clu[0] // 2, by_clu[1] // 2), 4)
        core = lax.rem(at_core + by_core(by_clu[0] % 2, by_clu[1] % 2), 2)
        eight.append((by_core(*by_x), by_core(*by_z), y * 2 + core))

    def for_peers(first, count, visit):
        def one_eight(step, carry):
            by = lax.rem(step * 13 + at_core * 12, 16)
            x = at_x + lax.div(by, 4)
            z = at_z + lax.rem(by, 4)
            for j, (more_x, more_z, clu_to) in enumerate(eight):
                seq_to = lax.rem(x + more_x, 4) * 4 + lax.rem(z + more_z, 4)
                if j in (2, 5):
                    pl.when(seq_to * groups + clu_to != me)(lambda: visit(seq_to, clu_to))
                else:
                    visit(seq_to, clu_to)
            return carry

        lax.fori_loop(first, first + count, one_eight, 0)

    def send_steps(first, count, source, target, send_sem, recv_sem):
        def start(seq_to, clu_to):
            pltpu.make_async_remote_copy(
                src_ref=source.at[seq_to * groups + clu_to],
                dst_ref=target,
                send_sem=send_sem,
                recv_sem=recv_sem,
                device_id=(seq_to, clu_to),
                device_id_type=MESH,
            ).start()

        for_peers(first, count, start)

    def send_own(source, target, recv_sem):
        pltpu.make_async_copy(source.at[me], target, recv_sem).start()

    def send_to_all(source, target, send_sem, recv_sem):
        send_steps(0, devices // 8, source, target, send_sem, recv_sem)
        send_own(source, target, recv_sem)

    def wait_bytes(ref, sem):
        pltpu.make_async_copy(ref, ref, sem).wait()

    for array, ref in enumerate((q_ref, k_ref, v_ref, g_ref)):
        pltpu.make_async_copy(ref, inputs.at[array], input_sem).start()
    barrier = pltpu.get_barrier_semaphore()

    def greet(seq_to, clu_to):
        pl.semaphore_signal(barrier, inc=1, device_id=(seq_to, clu_to), device_id_type=MESH)

    for_peers(0, devices // 8, greet)

    sub = lax.broadcasted_iota(jnp.int32, (TOK, TOK), 0)
    lane = lax.broadcasted_iota(jnp.int32, (TOK, TOK), 1)
    sub_f = sub.astype(jnp.float32)
    lane_f = lane.astype(jnp.float32)
    ids_l = jnp.broadcast_to(ids_ref[...].astype(jnp.float32), (TOK, TOK))
    ids_s = ids_l.T
    one = jnp.ones((TOK, TOK), jnp.float32)
    zero = jnp.zeros((TOK, TOK), jnp.float32)
    same = ids_l == ids_s
    rank_l = jnp.sum(jnp.where(same & (sub < lane), one, zero), axis=0, keepdims=True)
    rank_s = jnp.sum(jnp.where(same & (lane < sub), one, zero), axis=1, keepdims=True)
    count_l = jnp.sum(jnp.where(same, one, zero), axis=0, keepdims=True)
    cnt_send[...] = jnp.sum(jnp.where(ids_s == lane_f, one, zero), axis=0, keepdims=True)
    ids_row = ids_l[0:1, :]
    heavy = jnp.min(jnp.where(count_l == 4.0, ids_row, 999.0), axis=1, keepdims=True)
    group_l = jnp.floor(ids_l * (1.0 / 16.0))
    group_s = jnp.floor(ids_s * (1.0 / 16.0))
    earlier = (ids_s < ids_l) | (same & (sub < lane))
    later = (ids_l < ids_s) | (same & (lane < sub))
    before = (group_l == group_s) & (ids_s != heavy) & (rank_s >= 1.0) & earlier
    over_at = jnp.sum(jnp.where(before, one, zero), axis=0, keepdims=True)
    behind = (group_l == group_s) & (ids_l != heavy) & (rank_l >= 1.0) & later
    over_at_s = jnp.sum(jnp.where(behind, one, zero), axis=1, keepdims=True)
    excess_s = (ids_s != heavy) & (rank_s >= 1.0) & (over_at_s >= 4.0)
    excess_at = jnp.sum(jnp.where(excess_s & earlier, one, zero), axis=0, keepdims=True)
    light_l = ids_l != heavy
    slot_group = (sub // 16).astype(jnp.float32)
    in_tile = sub % 16
    over_l = light_l & (rank_l >= 1.0)

    def tile_picks(tile):
        at_slot = (in_tile % 4).astype(jnp.float32)
        if tile < 4:
            cluster = slot_group * 16.0 + at_slot + 4.0 * tile
            taken = (ids_l == cluster) & (rank_l == 0.0) & light_l
        else:
            taken = (group_l == slot_group) & over_l & (over_at == at_slot)
        return [jnp.where(taken & (in_tile // 4 == array), one, zero) for array in range(4)]

    def rest_picks():
        picks = []
        for array in range(4):
            chosen = (ids_l == heavy) & (rank_l == (sub % 4).astype(jnp.float32))
            chosen = chosen & (sub // 4 == array) & (sub < 16)
            beyond = over_l & (over_at >= 4.0) & (excess_at == (sub % 8).astype(jnp.float32))
            beyond = beyond & (sub // 8 == array + 2)
            picks.append(jnp.where(chosen | beyond, one, zero))
        return picks

    def put_pack(at_row, count, picks):
        for array, matrix in enumerate(picks):
            pack_mat[pl.ds(at_row, count), pl.ds(array * TOK, TOK)] = matrix[:count].astype(
                jnp.bfloat16
            )

    put_pack(0, TOK, tile_picks(0))
    put_pack(TOK, TOK, tile_picks(4))
    put_pack(2 * TOK, 48, rest_picks())


    def send_line(source, target, count, at, device, send_sem, recv_sem):
        def one_peer(step, carry):
            to = lax.rem(at + step, count)
            pltpu.make_async_remote_copy(
                src_ref=source(to),
                dst_ref=target,
                send_sem=send_sem,
                recv_sem=recv_sem,
                device_id=device(to),
                device_id_type=MESH,
            ).start()
            return carry

        lax.fori_loop(1, count, one_peer, 0)
        pltpu.make_async_copy(source(at), target, recv_sem).start()

    def along_seq(source, target, send_sem, recv_sem):
        send_line(
            source, target.at[seq_at], heads, seq_at, lambda to: (to, clu_at), send_sem, recv_sem
        )

    def along_clu(source, target, send_sem, recv_sem):
        send_line(
            source, target.at[clu_at], groups, clu_at, lambda to: (seq_at, to), send_sem, recv_sem
        )


    def head_rows(at):
        cols = pl.ds(pl.multiple_of(at * 2 * DH, 2 * DH), 2 * DH)
        return [inputs[array, :, cols] for array in range(4)]

    def put_tile(target, at, tile, packed):
        low = packed.astype(jnp.bfloat16)
        for k in range(2):
            target[pl.ds((2 * at + k) * groups, groups), tile] = low[
                :, k * DH : (k + 1) * DH
            ].reshape(groups, 16, DH)

    def pack_a(at, carry):
        rows = jnp.concatenate(head_rows(at), axis=0)
        packed = bf16_dot(pack_mat[pl.ds(0, 2 * TOK + 48), :], rows)
        put_tile(send_a, at, 0, packed[:TOK])
        put_tile(send_a, at, 1, packed[TOK : 2 * TOK])
        rest = packed[2 * TOK :].astype(jnp.bfloat16)
        for k in range(2):
            hsend[2 * at + k] = rest[:16, k * DH : (k + 1) * DH]
            ex_send[2 * at + k] = rest[16:, k * DH : (k + 1) * DH]
        return carry

    wait_bytes(inputs, input_sem)
    lax.fori_loop(0, heads // 2, pack_a, 0, unroll=4)
    pl.semaphore_wait(barrier, devices - 1)
    along_clu(lambda to: cnt_send, cnt_group, cnt_send_sem, cnt_sem)

    def send_heavy(step, carry):
        head = lax.rem(seq_at + step, heads)
        clu_to = lax.rem(head, groups)

        @pl.when(head * groups + clu_to != me)
        def _():
            pltpu.make_async_remote_copy(
                src_ref=hsend.at[head],
                dst_ref=hrecv.at[me],
                send_sem=hsend_sem,
                recv_sem=hrecv_sem,
                device_id=(head, clu_to),
                device_id_type=MESH,
            ).start()

        @pl.when(head * groups + clu_to == me)
        def _():
            pltpu.make_async_copy(hsend.at[head], hrecv.at[me], hrecv_sem).start()

        return carry

    along_seq(lambda to: ex_send.at[to], ex_recv, ex_send_sem, ex_recv_sem)
    out_a = (send_a, recv_a.at[me], send_a_sem, recv_a_sem)
    send_steps(0, 4, *out_a)
    wait_bytes(cnt_group, cnt_sem)
    along_seq(lambda to: cnt_group, cnt_recv, cnt2_send_sem, cnt2_sem)
    send_steps(4, devices // 8 - 4, *out_a)
    send_own(send_a, recv_a.at[me], recv_a_sem)
    lax.fori_loop(0, heads, send_heavy, 0)

    for tile in range(1, 4):
        put_pack((tile + 1) * TOK + 48, TOK, tile_picks(tile))

    def pack_bc(at, carry):
        rows = jnp.concatenate(head_rows(at), axis=0)
        packed = bf16_dot(pack_mat[pl.ds(2 * TOK + 48, 3 * TOK), :], rows)
        put_tile(send_b, at, 0, packed[:TOK])
        put_tile(send_b, at, 1, packed[TOK : 2 * TOK])
        put_tile(send_c, at, 0, packed[2 * TOK :])
        return carry

    lax.fori_loop(0, heads // 2, pack_bc, 0)

    wait_bytes(cnt_recv, cnt2_sem)
    seen = cnt_recv[...].reshape(TOK, TOK)
    heavies = jnp.min(jnp.where(seen == 4.0, lane_f, 999.0), axis=1, keepdims=True)
    heavy_all = jnp.min(heavies, axis=0, keepdims=True)
    light = lane_f != heavy_all
    more = jnp.where(light, jnp.maximum(seen - 1.0, 0.0), 0.0)
    more_low = more.astype(jnp.bfloat16)
    in_group = jnp.where(sub // 16 == lane, one, zero).astype(jnp.bfloat16)
    ahead = jnp.where(sub < lane, one, zero).astype(jnp.bfloat16)
    prior = jnp.where(lane < sub, one, zero).astype(jnp.bfloat16)
    mates = (lane < sub) & (lane % 8 == sub % 8)
    mates = jnp.where(mates, one, zero).astype(jnp.bfloat16)
    excess = jnp.maximum(bf16_dot(more_low, in_group) - 4.0, 0.0)
    excess_low = excess.astype(jnp.bfloat16)
    excess_off = bf16_dot(excess_low, ahead)
    excess_pre = bf16_dot(mates, excess_low)
    bad = (jnp.sum(excess, axis=1, keepdims=True) > 8.0) | (excess_pre + excess > 16.0)
    bad = bad | (heavies != heavy_all) | (jnp.sum(more, axis=0, keepdims=True) > OVC)
    flag_ref[0, 0] = jnp.max(jnp.where(bad, one, zero)).astype(jnp.int32)

    spot = zero
    for group in range(8):
        off, count, pre = [a[:, group : group + 1] for a in (excess_off, excess, excess_pre)]
        held = (lane_f >= off) & (lane_f < off + count)
        spot = spot + jnp.where(held, lane_f + (group * 16 + 1.0) - off + pre, zero)
    spot = jnp.where(sub % 8 == clu_at, spot, zero).reshape(16, 8, TOK)
    spot = jnp.sum(spot, axis=1).astype(jnp.bfloat16)
    spread8 = jnp.where(lane % 8 == sub, one, zero).astype(jnp.bfloat16)
    spot = jnp.where(lane[:16] // 8 == sub[:16], bf16_dot(spot, spread8), 0.0)
    spot = jnp.sum(spot, axis=0, keepdims=True) - 1.0
    to_mate[...] = jnp.where(sub_f == spot, one, zero).astype(jnp.bfloat16)
    spot = jnp.broadcast_to(spot, (TOK, TOK)).T
    to_block[...] = jnp.where(spot == lane_f, one, zero).astype(jnp.bfloat16)

    wait_bytes(ex_recv, ex_recv_sem)
    held = ex_recv[...].astype(jnp.float32)
    held = [held[:, 8 * a : 8 * a + 8, :].reshape(TOK, DH) for a in range(4)]
    held = jnp.concatenate(held, axis=1).astype(jnp.bfloat16)
    held = bf16_dot(to_mate[...], held).astype(jnp.bfloat16)
    for a in range(4):
        ex_send2[:, a] = held[:, a * DH : (a + 1) * DH].reshape(8, 16, DH)
    along_clu(lambda to: ex_send2.at[to], ex_recv2, ex_send2_sem, ex_recv2_sem)
    send_to_all(send_b, recv_b.at[me], send_b_sem, recv_b_sem)
    send_to_all(send_c, recv_c.at[me], send_c_sem, recv_c_sem)

    valid = jnp.where((seen > 0.0) & light, one, zero).astype(jnp.bfloat16)
    mine = (sub == clu_at * 16 + lane) & (lane < 16)
    mine = jnp.where(mine, one, zero).astype(jnp.bfloat16)
    more_g = bf16_dot(more_low, mine)
    valid_g = bf16_dot(valid, mine)
    more_g_low = more_g.astype(jnp.bfloat16)
    start_g = bf16_dot(prior, more_g_low)
    offset_g = bf16_dot(more_g_low, ahead)
    beyond_g = jnp.maximum(bf16_dot(more_g_low, one.astype(jnp.bfloat16)) - 4.0, 0.0)
    pre_g = bf16_dot(mates, beyond_g.astype(jnp.bfloat16))
    ex_index = lane_f - pre_g + 4.0
    first_row = lax.broadcasted_iota(jnp.int32, (1, TOK), 1).astype(jnp.float32) * 16.0
    in_tile_at = zero
    beyond_at = zero
    for c in range(16):
        count, begin, off, real = [
            a[:, c : c + 1] for a in (more_g, start_g, offset_g, valid_g)
        ]
        place = begin - off + (c * OVC + 1.0)
        held = (lane_f >= off) & (lane_f < off + count) & (lane < 4)
        in_tile_at = in_tile_at + jnp.where(held, lane_f + place, zero)
        held = (ex_index >= off) & (ex_index < off + count) & (ex_index >= 4.0)
        beyond_at = beyond_at + jnp.where(held, ex_index + place, zero)
        held = (lane_f >= begin) & (lane_f < begin + count)
        where = jnp.where(held, sub_f * 16.0 + 1.0 + lane_f - begin, zero)
        where = jnp.sum(where, axis=0, keepdims=True)
        where = jnp.where(where > 0.0, where, FAR)
        query_row = jnp.concatenate([first_row, where], axis=1)
        query_pos[c] = jnp.broadcast_to(query_row, (8, 2 * TOK))
        key_pos[c, pl.ds(0, TOK), :] = jnp.where(real > 0.0, sub_f * 16.0, FAR)
        key_pos[c, pl.ds(TOK, OVC), :] = jnp.broadcast_to(where, (TOK, TOK)).T[:OVC]
    beyond_at = jnp.sum(beyond_at.reshape(16, 8, TOK), axis=0)
    high = jnp.floor(beyond_at * (1.0 / 32.0))
    split = jnp.concatenate([high, beyond_at - high * 32.0], axis=0).astype(jnp.bfloat16)
    spread16 = jnp.where(lane % 16 == sub, one, zero).astype(jnp.bfloat16)
    split = bf16_dot(split, spread16)
    split = jnp.where(lane[:8] // 16 == sub[:8], split[:8] * 32.0 + split[8:], 0.0)
    beyond_row = jnp.sum(split, axis=0, keepdims=True) - 1.0
    tile_rows = in_tile_at.T[0:8, :] - 1.0
    slot_rows = [tile_rows[k : k + 1, :] for k in range(4)] + [beyond_row]
    slot_cols = [in_tile_at[:, k : k + 1] - 1.0 for k in range(4)]
    slot_cols.append(jnp.broadcast_to(beyond_row, (TOK, TOK)).T)

    chunk = 4
    for k in range(5):
        for m in range(16 * OVC // TOK):
            onehot[pl.ds(k * TOK, TOK), pl.ds(m * TOK, TOK)] = jnp.where(
                slot_cols[k] == lane_f + float(m * TOK), one, zero
            ).astype(jnp.bfloat16)
            pick[pl.ds(m * TOK, TOK), pl.ds(k * TOK, TOK)] = jnp.where(
                slot_rows[k] == sub_f + float(m * TOK), one, zero
            ).astype(jnp.bfloat16)

    for at, tile in enumerate((0, 1, 2, 3, 4, None)):
        for array, matrix in enumerate(rest_picks() if tile is None else tile_picks(tile)):
            unpack_mat[pl.ds(array * TOK, TOK), pl.ds(at * TOK, TOK)] = matrix.T.astype(
                jnp.bfloat16
            )

    perm = flip_perm()

    def arrange(source, target, units):
        def two_sets(at, carry):
            blocks = [pl.ds(pl.multiple_of((2 * at + i) * SET, SET), SET) for i in range(2)]
            spots = [(held, unit) for held in blocks for unit in range(units)]
            rows = jnp.concatenate(
                [source(held, unit).reshape(SET * 16, DH) for held, unit in spots], axis=1
            )
            turned = bf16_dot(perm, rows).astype(jnp.bfloat16)
            for i, (held, unit) in enumerate(spots):
                target(held, unit, turned[:, i * DH : (i + 1) * DH].reshape(16, SET, DH))
            return carry

        lax.fori_loop(0, devices // (2 * SET), two_sets, 0, unroll=2)

    def put_table(first):
        def put(blocks, unit, value):
            table[first + unit, :, blocks, :] = value

        return put

    wait_bytes(recv_a, recv_a_sem)
    def put_tile_a(blocks, unit, value):
        table[4 * unit, :, blocks, :] = value

    arrange(lambda blocks, unit: recv_a[blocks, unit], put_tile_a, 2)

    wait_bytes(ex_recv2, ex_recv2_sem)
    for a in range(4):
        cols = pl.ds(a * DH, DH)
        loose[pl.ds(0, 4 * TOK), cols] = table[4, 4 * a : 4 * a + 4].reshape(4 * TOK, DH)
        loose[pl.ds(4 * TOK, TOK), cols] = ex_recv2[:, a].reshape(TOK, DH)

    def gather_chunk(at, carry):
        chosen = pick[pl.ds(pl.multiple_of(at * chunk * OVC, 64), chunk * OVC), :]
        found = bf16_dot(chosen, loose[...]).astype(jnp.bfloat16)
        for c in range(chunk):
            for array in range(4):
                over[array, at * chunk + c] = found[
                    c * OVC : (c + 1) * OVC, array * DH : (array + 1) * DH
                ]
        return carry

    gather_chunk(0, 0)

    pad_rows = jnp.zeros((TOK - OVC, DH), jnp.bfloat16)

    def load_cluster(tile, j):
        c = tile * 4 + j
        rows = [
            jnp.concatenate([table[tile, a * 4 + j], over[a, c]], axis=0) for a in range(4)
        ]
        for a in (0, 3):
            rows[a] = jnp.concatenate([rows[a], pad_rows], axis=0)
        key_at = key_pos[c]
        allowed = jnp.concatenate([key_at, key_at], axis=1) <= query_pos[c, 0:1, :]
        return rows + [allowed]

    def attend_tiles(first, tiles):
        def one_tile(at, carry):
            tile = first + at
            spots = range(4)
            loaded = [load_cluster(tile, j) for j in spots]
            found = [attend(*arrays, inv_root) for arrays in loaded]
            for j, results in zip(spots, found):
                c = tile * 4 + j
                for a, value in enumerate(results):
                    value = value.astype(jnp.bfloat16)
                    table[tile, a * 4 + j] = value[:TOK]
                    over_res[
                        pl.ds(pl.multiple_of(c * OVC, 16), OVC), pl.ds(a * DH, DH)
                    ] = value[TOK : TOK + OVC]
            return carry

        lax.fori_loop(0, tiles, one_tile, 0)

    def put_in(result):
        def put(blocks, unit, value):
            result[blocks, unit] = value

        return put

    def from_table(first):
        return lambda blocks, unit: table[first + unit, :, blocks, :]

    to_a = (result_a, back_a.at[me], res_a_sem, back_a_sem)
    to_b = (result_b, back_b.at[me], res_b_sem, back_b_sem)
    to_c = (result_c, back_c.at[me], res_c_sem, back_c_sem)
    attend_tiles(0, 1)
    arrange(from_table(0), put_in(result_a), 1)
    send_to_all(*to_a)
    lax.fori_loop(1, 16 // chunk, gather_chunk, 0)

    wait_bytes(recv_b, recv_b_sem)
    arrange(lambda blocks, unit: recv_b[blocks, unit], put_table(1), 2)
    attend_tiles(1, 2)
    arrange(from_table(1), put_in(result_b), 2)
    send_to_all(*to_b)

    wait_bytes(recv_c, recv_c_sem)
    arrange(lambda blocks, unit: recv_c[blocks, 0], put_table(3), 1)
    attend_tiles(3, 1)

    found = bf16_dot(onehot[pl.ds(4 * TOK, TOK), :], over_res[...]).astype(jnp.bfloat16)
    for a in range(4):
        ex_ret2[:, a] = found[:, a * DH : (a + 1) * DH].reshape(8, 16, DH)
    along_clu(lambda to: ex_ret2.at[to], ex_back2, ex_ret2_sem, ex_back2_sem)
    found = bf16_dot(onehot[pl.ds(0, 4 * TOK), :], over_res[...]).astype(jnp.bfloat16)
    for a in range(4):
        table[4, 4 * a : 4 * a + 4] = found[:, a * DH : (a + 1) * DH].reshape(4, TOK, DH)
    arrange(from_table(3), put_in(result_c), 2)
    send_steps(0, devices // 16, *to_c)
    send_own(result_c, back_c.at[me], back_c_sem)

    wait_bytes(ex_back2, ex_back2_sem)
    held = [ex_back2[:, a].reshape(TOK, DH) for a in range(4)]
    held = bf16_dot(to_block[...], jnp.concatenate(held, axis=1))
    held = [held[:, a * DH : (a + 1) * DH].reshape(16, 8, DH) for a in range(4)]
    ex_ret1[...] = jnp.concatenate(held, axis=1).astype(jnp.bfloat16)
    along_seq(lambda to: ex_ret1.at[to], ex_back1, ex_ret1_sem, ex_back1_sem)
    send_steps(devices // 16, devices // 16, *to_c)

    @pl.when(is_heavy_owner)
    def _():
        wait_bytes(hrecv, hrecv_sem)

        def put_heavy(blocks, unit, value):
            htable[:, blocks, :] = value

        arrange(lambda blocks, unit: hrecv[blocks], put_heavy, 1)
        k_h, v_h = [htable[4 * a : 4 * a + 4].reshape(4 * TOK, DH) for a in (1, 2)]
        hacc[...] = jnp.zeros_like(hacc)
        key_sub = lax.broadcasted_iota(jnp.int32, (4 * TOK, TOK), 0)
        key_at = lax.rem(key_sub, TOK) * 4 + lax.div(key_sub, TOK)
        query_at = lax.broadcasted_iota(jnp.int32, (4 * TOK, TOK), 1) * 4

        def heavy_tile(s, carry):
            out, dq, dk, dv = attend(
                htable[s], k_h, v_h, htable[12 + s], key_at <= query_at + s, inv_root
            )
            hacc[2, pl.ds(pl.multiple_of(s * TOK, TOK), TOK)] = out.astype(jnp.float32)
            hacc[3, pl.ds(pl.multiple_of(s * TOK, TOK), TOK)] = dq.astype(jnp.float32)
            hacc[0] += dk
            hacc[1] += dv
            return carry

        lax.fori_loop(0, 4, heavy_tile, 0)
        for array, at in enumerate((2, 3, 0, 1)):
            htable[4 * array : 4 * array + 4] = (
                hacc[at].astype(jnp.bfloat16).reshape(4, TOK, DH)
            )

        def put_hresult(blocks, unit, value):
            hresult[blocks] = value

        arrange(lambda blocks, unit: htable[:, blocks, :], put_hresult, 1)
        send_to_all(hresult, hback.at[seq_at], hres_sem, hback_sem)

    def unpack(tiles, rest, first, count):
        sides = []
        for k in range(2):
            sides.append(
                jnp.concatenate(
                    [tile(k).reshape(TOK, DH) for tile in tiles] + [part(k) for part in rest],
                    axis=0,
                )
            )
        return bf16_dot(
            unpack_mat[:, pl.ds(first, count)], jnp.concatenate(sides, axis=1)
        )

    def tile_of(ref, at, tile):
        return lambda k: ref[pl.ds((2 * at + k) * groups, groups), tile]

    def unpack_early(at, carry):
        tiles = [tile_of(back_a, at, 0), tile_of(back_b, at, 0), tile_of(back_b, at, 1)]
        early[at] = unpack(tiles, [], 0, 3 * TOK)
        return carry

    def unpack_last(at, carry):
        cols = pl.ds(pl.multiple_of(at * 2 * DH, 2 * DH), 2 * DH)
        tiles = [tile_of(back_c, at, 0), tile_of(back_c, at, 1)]
        rest = [
            lambda k: hback[2 * at + k],
            lambda k: ex_back1[2 * at + k],
            lambda k: jnp.zeros((TOK - 48, DH), jnp.bfloat16),
        ]
        found = (early[at] + unpack(tiles, rest, 3 * TOK, 3 * TOK)).astype(jnp.bfloat16)
        for array, ref in enumerate((out_ref, dq_ref, dk_ref, dv_ref)):
            ref[:, cols] = found[array * TOK : (array + 1) * TOK]
        return carry

    wait_bytes(back_a, back_a_sem)
    wait_bytes(back_b, back_b_sem)
    lax.fori_loop(0, heads // 2, unpack_early, 0, unroll=2)
    wait_bytes(ex_back1, ex_back1_sem)
    wait_bytes(hback, hback_sem)
    wait_bytes(back_c, back_c_sem)
    lax.fori_loop(0, heads // 2, unpack_last, 0, unroll=2)

    others = pl.ds(0, devices - 1)
    wait_bytes(cnt_group.at[pl.ds(0, groups - 1)], cnt_send_sem)
    wait_bytes(cnt_recv.at[pl.ds(0, heads - 1)], cnt2_send_sem)
    for ref, sem in ((ex_send, ex_send_sem), (ex_ret1, ex_ret1_sem)):
        wait_bytes(ref.at[pl.ds(0, heads - 1)], sem)
    for ref, sem in ((ex_send2, ex_send2_sem), (ex_ret2, ex_ret2_sem)):
        wait_bytes(ref.at[pl.ds(0, groups - 1)], sem)
    wait_bytes(send_a.at[others], send_a_sem)
    wait_bytes(send_b.at[others], send_b_sem)
    wait_bytes(send_c.at[others], send_c_sem)
    wait_bytes(result_a.at[others], res_a_sem)
    wait_bytes(result_b.at[others], res_b_sem)
    wait_bytes(result_c.at[others], res_c_sem)

    @pl.when(is_heavy_owner)
    def _():
        wait_bytes(hsend.at[pl.ds(0, heads - 1)], hsend_sem)
        wait_bytes(hresult.at[others], hres_sem)

    @pl.when(jnp.logical_not(is_heavy_owner))
    def _():
        wait_bytes(hsend, hsend_sem)


def fast_path(queries, key_rows, value_rows, out_grad, cluster_ids):
    tok_rows, columns = queries.shape
    heads = columns // DH
    groups = lax.axis_size("clu")
    devices = lax.axis_size("seq") * groups
    low = jnp.bfloat16
    wide = jnp.float32
    rows = pltpu.VMEM((tok_rows, columns), low)
    vmem = pl.BlockSpec(memory_space=pltpu.VMEM)
    smem = pl.BlockSpec(memory_space=pltpu.SMEM)
    return pl.pallas_call(
        fast_kernel,
        out_shape=[rows] * 4 + [jax.ShapeDtypeStruct((1, 1), jnp.int32)],
        in_specs=[vmem] + [pl.BlockSpec(memory_space=pl.ANY)] * 4,
        out_specs=[vmem] * 4 + [smem],
        scratch_shapes=[
            pltpu.VMEM((1, TOK), wide),
            pltpu.VMEM((groups, 1, TOK), wide),
            pltpu.VMEM((heads, groups, 1, TOK), wide),
            pltpu.VMEM((5 * TOK + 48, 4 * TOK), low),
            pltpu.VMEM((4 * TOK, 6 * TOK), low),
            pltpu.VMEM((devices, 2, 16, DH), low),
            pltpu.VMEM((devices, 2, 16, DH), low),
            pltpu.VMEM((devices, 1, 16, DH), low),
            pltpu.VMEM((devices, 2, 16, DH), low),
            pltpu.VMEM((devices, 2, 16, DH), low),
            pltpu.VMEM((devices, 1, 16, DH), low),
            pltpu.VMEM((5, 16, devices, DH), low),
            pltpu.VMEM((4, 16, OVC, DH), low),
            pltpu.VMEM((16, TOK + OVC, TOK), wide),
            pltpu.VMEM((16, 8, 2 * TOK), wide),
            pltpu.VMEM((16 * OVC, 5 * TOK), low),
            pltpu.VMEM((5 * TOK, 16 * OVC), low),
            pltpu.VMEM((5 * TOK, 4 * DH), low),
            pltpu.VMEM((16 * OVC, 4 * DH), low),
            pltpu.VMEM((TOK, TOK), low),
            pltpu.VMEM((TOK, TOK), low),
            pltpu.VMEM((devices, 1, 16, DH), low),
            pltpu.VMEM((devices, 2, 16, DH), low),
            pltpu.VMEM((devices, 2, 16, DH), low),
            pltpu.VMEM((devices, 1, 16, DH), low),
            pltpu.VMEM((devices, 2, 16, DH), low),
            pltpu.VMEM((devices, 2, 16, DH), low),
            pltpu.VMEM((heads, 32, DH), low),
            pltpu.VMEM((heads, 32, DH), low),
            pltpu.VMEM((groups, 4, 16, DH), low),
            pltpu.VMEM((groups, 4, 16, DH), low),
            pltpu.VMEM((groups, 4, 16, DH), low),
            pltpu.VMEM((groups, 4, 16, DH), low),
            pltpu.VMEM((heads, 32, DH), low),
            pltpu.VMEM((heads, 32, DH), low),
            pltpu.VMEM((heads, 16, DH), low),
            pltpu.VMEM((devices, 16, DH), low),
            pltpu.VMEM((16, devices, DH), low),
            pltpu.VMEM((4, 4 * TOK, DH), wide),
            pltpu.VMEM((devices, 16, DH), low),
            pltpu.VMEM((heads, 16, DH), low),
            pltpu.VMEM((4, tok_rows, columns), low),
            pltpu.VMEM((heads // 2, 4 * tok_rows, 2 * DH), wide),
        ]
        + [pltpu.SemaphoreType.DMA] * 29,
        compiler_params=pltpu.CompilerParams(
            collective_id=0, has_side_effects=True, vmem_limit_bytes=44 * 1024 * 1024
        ),
    )(cluster_ids.reshape(1, tok_rows), queries, key_rows, value_rows, out_grad)


def copy_kernel(*refs):
    sem = refs[-1]
    copies = [
        pltpu.make_async_copy(refs[i], refs[4 + i], sem.at[i]) for i in range(4)
    ]
    for copy in copies:
        copy.start()
    for copy in copies:
        copy.wait()


def copy_out(arrays):
    anywhere = pl.BlockSpec(memory_space=pl.ANY)
    return pl.pallas_call(
        copy_kernel,
        out_shape=[pltpu.HBM(a.shape, a.dtype) for a in arrays],
        in_specs=[anywhere] * 4,
        out_specs=[anywhere] * 4,
        scratch_shapes=[pltpu.SemaphoreType.DMA((4,))],
    )(*arrays)


def per_device(queries, key_rows, value_rows, out_grad, cluster_ids):
    arrays = (queries, key_rows, value_rows, out_grad, cluster_ids)
    *fast, flag = fast_path(*arrays)
    return lax.cond(
        flag.reshape(()) != 0,
        lambda arrays, fast: full_capacity(*arrays),
        lambda arrays, fast: tuple(copy_out(fast)),
        arrays,
        tuple(fast),
    )


def solution(mesh):
    in_specs = (
        P(("seq", "clu"), None),
        P(("seq", "clu"), None),
        P(("seq", "clu"), None),
        P(("seq", "clu"), None),
        P(("seq", "clu")),
    )
    out_specs = (
        P(("seq", "clu"), None),
        P(("seq", "clu"), None),
        P(("seq", "clu"), None),
        P(("seq", "clu"), None),
    )
    return jax.shard_map(
        per_device, mesh=mesh, in_specs=in_specs, out_specs=out_specs, check_vma=False
    )
```
